32 devices in a mesh: group: 4 (over x, core), member: 8 (over z, y).
Axes of the slice: x: 2, y: 2, z: 4, core: 2. Of those that a mesh axis runs over, the one named last changes fastest.
Arguments:
- q_rows: bfloat16 [8192, 8192], P(('group', 'member')), may hold values from -36 to 36
- own_kv: bfloat16 [8192, 1024], P(('group', 'member')), may hold values from -6 to 6
- cache: bfloat16 [128, 64, 1024], P(('group', 'member')), may hold values from -6 to 6
- recomp_hidden: bfloat16 [64, 8, 16, 4096], P(('group', 'member')), may hold values from -6 to 6
- w_kv: bfloat16 [4096, 1024], P('member', 'group'), may hold values from -0.09375 to 0.09375
- retrieval: int32 [64, 8], P(('group', 'member')), may hold values from 0 to 31, as said below
- positions: int32 [64, 8, 16], P(('group', 'member')), may hold values from 0 to 63, as said below
Outputs:
- attn_out: bfloat16 [8192, 8192], P(('group', 'member'))
The draws below stay inside these ranges and needn't reach their ends.
Inputs may be any that keep to these rules, and one draw needn't show every extreme that they name: `retrieval`: the 8 passages of one query are different. Passage i of a group's corpus is held by the device of member index i // 4 in that group. The queries of one device name at most 2 passages held by any one device, and this bound is reached. The 16 positions of one retrieved passage are different.
All inputs are finite; a program needn't handle non-finite values.
Results may differ from the reference program's by a relative error of at most 0.0054.
Values may be sent and summed in bfloat16 or wider, within the bound.
No kernel may reach another device: no remote copies, remote signals or barrier semaphores. Data moves between devices by JAX's collectives and lax.ppermute only.
A program may use at most 128 MiB of HBM per device.

```python
import jax
import jax.numpy as jnp
from jax import lax

D = 4096
HQ = 64
KVH = 4
HD = 128
TOPP = 8
QLEN = 128
Q_DEV = 2
PLEN = 64
PASS_DEV = 4
RECOMP = 16
OWNERS = 8
GROUPS = 4
QUERIES = 64
PASSAGES = 128
N_MEMBER = 8


def draw_q_rows(key, part):
    total_rows = QLEN * QUERIES
    result = jnp.clip(jax.random.normal(jax.random.fold_in(key, 1), (total_rows, HQ * HD), jnp.float32), -6.0, 6.0)
    return result.astype(jnp.bfloat16)


def draw_own_kv(key, part):
    total_rows = QLEN * QUERIES
    half_width = KVH * HD
    result = jnp.clip(jax.random.normal(jax.random.fold_in(key, 2), (total_rows, 2 * half_width), jnp.float32), -6.0, 6.0)
    return result.astype(jnp.bfloat16)


def draw_retrieval(key, part):
    requests = Q_DEV * TOPP
    copies = (requests + OWNERS - 1) // OWNERS

    def per_device(device):
        device_key = jax.random.fold_in(key, device)
        hottest = jax.random.randint(jax.random.fold_in(key, 100003 + device // OWNERS), (), 0, OWNERS).astype(jnp.int32)
        sequence = []
        for copy_index in range(copies):
            shuffled = jax.random.permutation(jax.random.fold_in(device_key, copy_index), OWNERS - 1).astype(jnp.int32)
            others = shuffled + (shuffled >= hottest).astype(jnp.int32)
            sequence.append(jnp.concatenate([hottest.reshape(1), others]))
        holders = jnp.concatenate(sequence)[:requests]
        repeats = (jnp.arange(requests) // OWNERS).astype(jnp.int32)
        offsets = jax.random.randint(jax.random.fold_in(device_key, 5000), (OWNERS,), 0, PASS_DEV).astype(jnp.int32)
        inside = (offsets[holders] + repeats) % PASS_DEV
        chosen = holders * PASS_DEV + inside
        mixing = jax.random.permutation(jax.random.fold_in(device_key, 6000), requests)
        return chosen[mixing].reshape(Q_DEV, TOPP)
    drawn = jax.vmap(per_device)(jnp.arange(GROUPS * OWNERS).astype(jnp.int32))
    return drawn.reshape(QUERIES, TOPP).astype(jnp.int32)


def draw_positions(key, part):
    count = QUERIES * TOPP
    split_keys = jax.random.split(key, count)
    picks = jax.vmap(lambda one_key: jax.random.permutation(one_key, PLEN)[:RECOMP])(split_keys)
    return picks.reshape(QUERIES, TOPP, RECOMP).astype(jnp.int32)


def level_of(stream_key, dims, cuts, smallest, largest):
    factor_of, own = 1.0, jax.random.fold_in(stream_key, 6)
    for position, blocks in cuts:
        draws = jnp.exp(jax.random.uniform(jax.random.fold_in(own, position), (blocks,), jnp.float32, smallest / len(cuts), largest / len(cuts)))
        factor_of = factor_of * jnp.repeat(draws, dims[position] // blocks).reshape([-1 if axis == position else 1 for axis in range(len(dims))])
    return factor_of


def gaussian(rng, extent, spread, most, cuts=(), held_as=jnp.bfloat16):
    values = jax.random.normal(rng, extent, jnp.float32) * spread
    if len(cuts) > 0:
        values = level_of(rng, extent, cuts, -0.22, 0.18) * values
    return jnp.clip(values, min=-most, max=most).astype(held_as)


def setup_inputs(seed: int = 0) -> dict:
    key_list = jax.random.split(jax.random.key(seed), 8)
    return {
        "q_rows": draw_q_rows(jax.random.fold_in(key_list[7], 71), 0),
        "own_kv": draw_own_kv(jax.random.fold_in(key_list[7], 71), 0),
        "cache": gaussian(key_list[2], (PASSAGES, PLEN, 2 * KVH * HD), 1.0, 6.0, ((0, 32),)),
        "recomp_hidden": gaussian(key_list[3], (QUERIES, TOPP, RECOMP, D), 1.0, 6.0, ((0, 32),)),
        "w_kv": gaussian(key_list[4], (D, 2 * KVH * HD), D ** -0.5, 0.09375, ((0, 8), (1, 4))),
        "retrieval": draw_retrieval(jax.random.fold_in(key_list[7], 71), 0),
        "positions": draw_positions(jax.random.fold_in(key_list[7], 71), 0),
    }


EPSILON = 1e-06

def reference(q_rows, own_kv, cache, recomp_hidden, w_kv, retrieval, positions):
    query_count = retrieval.shape[0]
    per_group = Q_DEV * N_MEMBER
    corpus_size = PASS_DEV * N_MEMBER
    kv_width = 2 * KVH * HD
    grouped = HQ // KVH
    span_keys = TOPP * PLEN + QLEN
    scale = 1.0 / HD ** 0.5
    weights_full = w_kv.astype(jnp.float32)
    query_all = q_rows.reshape(query_count, QLEN, KVH, grouped, HD)
    own_all = own_kv.reshape(query_count, QLEN, kv_width)
    token_pos = jnp.arange(QLEN)[:, None]
    key_pos = jnp.arange(span_keys)[None, :]
    visible = (key_pos < TOPP * PLEN) | (key_pos - TOPP * PLEN <= token_pos)

    def one_query(query_index):
        group_index = query_index // per_group
        passage_ids = (group_index * corpus_size + retrieval[query_index]).astype(jnp.int32)
        blocks = cache[passage_ids].astype(jnp.float32)
        hidden = recomp_hidden[query_index].astype(jnp.float32)
        normed = (hidden * lax.rsqrt(lax.optimization_barrier(jnp.mean(hidden * hidden, axis=-1, keepdims=True)) + EPSILON)).astype(jnp.bfloat16)
        recomputed = jnp.einsum('jrd,de->jre', normed.astype(jnp.float32), weights_full).astype(jnp.bfloat16)
        onehot = positions[query_index][:, :, None] == jnp.arange(PLEN)[None, None, :]
        covered = jnp.any(onehot, axis=1)
        placed = jnp.einsum('jrp,jre->jpe', onehot.astype(jnp.float32), recomputed.astype(jnp.float32))
        context = jnp.where(covered[:, :, None], placed, blocks).astype(jnp.bfloat16)
        context = jnp.concatenate([context.reshape(TOPP * PLEN, kv_width), own_all[query_index]], axis=0)
        keys = context[:, :KVH * HD].reshape(span_keys, KVH, HD).astype(jnp.float32)
        values = context[:, KVH * HD:].reshape(span_keys, KVH, HD).astype(jnp.float32)
        queries = query_all[query_index].astype(jnp.float32)
        scores = jnp.einsum('tkgd,skd->kgts', queries, keys) * scale
        scores = jnp.where(visible, scores, -jnp.inf)
        peak = lax.optimization_barrier(jnp.max(scores, axis=-1, keepdims=True))
        expd = jnp.exp(scores - peak)
        probs = (expd / lax.optimization_barrier(jnp.sum(expd, axis=-1, keepdims=True))).astype(jnp.bfloat16)
        output = jnp.einsum('kgts,skd->tkgd', probs.astype(jnp.float32), values)
        return output.astype(jnp.bfloat16).reshape(QLEN, HQ * HD)
    results = lax.map(one_query, jnp.arange(query_count).astype(jnp.int32))
    return results.reshape(query_count * QLEN, HQ * HD)
```

```python
import functools

import jax
import jax.numpy as jnp
from jax import lax
from jax.experimental import pallas as pl
from jax.experimental.pallas import tpu as pltpu
from jax.sharding import PartitionSpec as P

D = 4096
HQ = 64
KVH = 4
HD = 128
TOPP = 8
QLEN = 128
PLEN = 64
RECOMP = 16
KEPT = PLEN - RECOMP
GROUPED = HQ // KVH
PAIRS = 2
PAIR_HEADS = KVH // PAIRS
PAIR_WIDTH = PAIR_HEADS * HD
HALF = KVH * HD

EPSILON = 1e-06
LOG2E = 1.4426950408889634
VMEM_BYTES = 56 * 1024 * 1024


def norm_kernel(hidden_ref, normed_ref):
    hidden = hidden_ref[...].astype(jnp.float32)
    mean = jnp.mean(hidden * hidden, axis=1, keepdims=True)
    normed_ref[...] = (hidden * lax.rsqrt(mean + EPSILON)).astype(jnp.bfloat16)


def normalise(hidden):
    rows = hidden.shape[0]
    tile = min(rows, 64)
    return pl.pallas_call(
        norm_kernel,
        grid=(rows // tile,),
        in_specs=[pl.BlockSpec((tile, D), lambda i: (i, 0))],
        out_specs=pl.BlockSpec((tile, D), lambda i: (i, 0)),
        out_shape=jax.ShapeDtypeStruct(hidden.shape, jnp.bfloat16),
        compiler_params=pltpu.CompilerParams(vmem_limit_bytes=VMEM_BYTES),
        cost_estimate=pl.CostEstimate(flops=4 * rows * D, bytes_accessed=4 * rows * D, transcendentals=rows),
        name="normalise",
    )(hidden)


def pick_kernel(
    holders, requests, pass_local, capacity, table_ref, me_ref, cache_ref, first_ref, second_ref, slot_ref, kept_ref
):
    me, pair = me_ref[0], me_ref[1]
    stride = requests * (1 + RECOMP)

    def find(requester, carry):
        base = requester * (capacity + 1)
        for rank in range(capacity + 1):
            slot_ref[base + rank] = 0
        count = jnp.int32(0)
        for k in range(requests):
            wanted = table_ref[requester * stride + k]
            slot_ref[base + count] = k
            mine = (wanted // pass_local == me).astype(jnp.int32)
            count = jnp.minimum(count + mine, capacity)
        return carry

    lax.fori_loop(0, holders, find, 0)
    spot = lax.broadcasted_iota(jnp.int32, (1, PLEN), 1)

    def cover(requester, carry):
        for rank in range(capacity):
            k = slot_ref[requester * (capacity + 1) + rank]
            start = requester * stride + requests + k * RECOMP
            covered = spot < 0
            for r in range(RECOMP):
                covered = covered | (spot == table_ref[start + r])
            kept_ref[pl.ds(requester * capacity + rank, 1), :] = jnp.where(covered, 0.0, 1.0)
        return carry

    lax.fori_loop(0, holders, cover, 0)
    kept = kept_ref[...]
    upto = lax.broadcasted_iota(jnp.int32, (PLEN, PLEN), 0) <= lax.broadcasted_iota(jnp.int32, (PLEN, PLEN), 1)
    rank_of = jnp.dot(
        kept.astype(jnp.bfloat16), upto.astype(jnp.bfloat16), preferred_element_type=jnp.float32
    )
    kept_ref[...] = jnp.where(kept > 0, rank_of, 0.0)
    row = (lax.broadcasted_iota(jnp.int32, (KEPT, PLEN), 0) + 1).astype(jnp.float32)

    def send(requester, carry):
        for rank in range(capacity):
            k = slot_ref[requester * (capacity + 1) + rank]
            passage = lax.rem(table_ref[requester * stride + k], pass_local)
            out = requester * capacity + rank
            select = (kept_ref[pl.ds(out, 1), :] == row).astype(jnp.bfloat16)
            for ref, part in ((first_ref, pair), (second_ref, 1 - pair)):
                for half in range(2):
                    start = pl.multiple_of(half * HALF + part * PAIR_WIDTH, PAIR_WIDTH)
                    ref[out, :, half * PAIR_WIDTH : (half + 1) * PAIR_WIDTH] = jnp.dot(
                        select, cache_ref[passage, :, pl.ds(start, PAIR_WIDTH)], preferred_element_type=jnp.float32
                    ).astype(jnp.bfloat16)
        return carry

    lax.fori_loop(0, holders, send, 0)


def pick_rows(table, me, cache, holders, requests, capacity):
    shape = jax.ShapeDtypeStruct((holders * capacity, KEPT, 2 * PAIR_WIDTH), jnp.bfloat16)
    smem = pl.BlockSpec(memory_space=pltpu.SMEM)
    vmem = pl.BlockSpec(memory_space=pltpu.VMEM)
    return pl.pallas_call(
        functools.partial(pick_kernel, holders, requests, cache.shape[0], capacity),
        in_specs=[smem, smem, vmem],
        out_specs=[vmem, vmem],
        out_shape=[shape, shape],
        scratch_shapes=[
            pltpu.SMEM((holders * (capacity + 1),), jnp.int32),
            pltpu.VMEM((holders * capacity, PLEN), jnp.float32),
        ],
        compiler_params=pltpu.CompilerParams(vmem_limit_bytes=VMEM_BYTES),
        name="pick_rows",
    )(table, me, cache)


def project_kernel(chunks, me_ref, mine_ref, other_ref, *refs):
    weights, outs = refs[: 2 * chunks], refs[2 * chunks :]
    member, x = me_ref[0], me_ref[1]
    depth = D // chunks
    for side, out_ref in ((mine_ref, outs[0]), (other_ref, outs[1])):
        for block in range(2):
            total = None
            for k in range(chunks):
                start = pl.multiple_of((member ^ k) * depth, depth)
                term = jnp.dot(
                    side[:, pl.ds(start, depth)],
                    weights[block * chunks + k][...],
                    preferred_element_type=jnp.float32,
                )
                total = term if total is None else total + term
            place = pl.multiple_of((x ^ block) * PAIR_WIDTH, PAIR_WIDTH)
            out_ref[:, pl.ds(place, PAIR_WIDTH)] = total.astype(jnp.bfloat16)


def project(me, mine, other, weights):
    rows = mine.shape[0]
    vmem = pl.BlockSpec(memory_space=pltpu.VMEM)
    shape = jax.ShapeDtypeStruct((rows, 2 * PAIR_WIDTH), jnp.bfloat16)
    return pl.pallas_call(
        functools.partial(project_kernel, len(weights) // 2),
        in_specs=[pl.BlockSpec(memory_space=pltpu.SMEM)] + [vmem] * (2 + len(weights)),
        out_specs=[vmem, vmem],
        out_shape=[shape, shape],
        compiler_params=pltpu.CompilerParams(vmem_limit_bytes=VMEM_BYTES),
        cost_estimate=pl.CostEstimate(
            flops=8 * rows * D * PAIR_WIDTH, bytes_accessed=4 * rows * D + 4 * D * PAIR_WIDTH, transcendentals=0
        ),
        name="project",
    )(me, mine, other, *weights)


def attend_kernel(
    heads_once, info_ref, q_ref, own_k_ref, own_v_ref, kept_k_ref, kept_v_ref, rec_k_ref, rec_v_ref, *rest
):
    out_ref, key_ref, value_ref = rest[-3:]
    query = pl.program_id(0)
    passage_keys = TOPP * PLEN
    value_ref[:, HD:] = jnp.ones((passage_keys + QLEN, HD), jnp.bfloat16)
    for j in range(TOPP):
        slot = info_ref[1 + query * TOPP + j]
        key_ref[j * KEPT : (j + 1) * KEPT, :] = kept_k_ref[slot]
        value_ref[j * KEPT : (j + 1) * KEPT, :HD] = kept_v_ref[slot]
    key_ref[TOPP * KEPT : passage_keys, :] = rec_k_ref[...]
    value_ref[TOPP * KEPT : passage_keys, :HD] = rec_v_ref[...]
    key_ref[passage_keys:, :] = own_k_ref[...]
    value_ref[passage_keys:, :HD] = own_v_ref[...]
    rows = heads_once * QLEN
    token = lax.broadcasted_iota(jnp.int32, (rows, QLEN), 0) % QLEN
    visible = lax.broadcasted_iota(jnp.int32, (rows, QLEN), 1) <= token
    factor = LOG2E / HD**0.5
    for first in range(0, GROUPED, heads_once):
        block = jnp.concatenate(
            [q_ref[:, (first + i) * HD : (first + i + 1) * HD] for i in range(heads_once)], axis=0
        )
        scores = lax.dot_general(
            block, key_ref[...], (((1,), (1,)), ((), ())), preferred_element_type=jnp.float32
        )
        scores = jnp.concatenate(
            [scores[:, :passage_keys], jnp.where(visible, scores[:, passage_keys:], -jnp.inf)], axis=1
        )
        peak = jnp.max(scores, axis=1, keepdims=True)
        expd = jnp.exp2((scores - peak) * factor).astype(jnp.bfloat16)
        summed = jnp.dot(expd, value_ref[...], preferred_element_type=jnp.float32)
        result = (summed[:, :HD] / summed[:, HD:]).astype(jnp.bfloat16)
        for i in range(heads_once):
            out_ref[:, (first + i) * HD : (first + i + 1) * HD] = result[i * QLEN : (i + 1) * QLEN]


def attend(info, q_rows, own_kv, kept, recomputed, earlier=None):
    rows, width = q_rows.shape
    queries = rows // QLEN
    slots = kept.shape[0]
    span = TOPP * PLEN + QLEN
    wide = GROUPED * HD
    in_specs = [
        pl.BlockSpec((QLEN, wide), lambda n, h, info: (n, info[0] * PAIR_HEADS + h)),
        pl.BlockSpec((QLEN, HD), lambda n, h, info: (n, info[0] * PAIR_HEADS + h)),
        pl.BlockSpec((QLEN, HD), lambda n, h, info: (n, KVH + info[0] * PAIR_HEADS + h)),
        pl.BlockSpec((slots, KEPT, HD), lambda n, h, info: (0, 0, h)),
        pl.BlockSpec((slots, KEPT, HD), lambda n, h, info: (0, 0, PAIR_HEADS + h)),
        pl.BlockSpec((TOPP * RECOMP, HD), lambda n, h, info: (n, h)),
        pl.BlockSpec((TOPP * RECOMP, HD), lambda n, h, info: (n, PAIR_HEADS + h)),
    ]
    operands = [q_rows, own_kv, own_kv, kept, kept, recomputed, recomputed]
    aliases = {}
    if earlier is not None:
        in_specs.append(pl.BlockSpec(memory_space=pl.ANY))
        operands.append(earlier)
        aliases = {len(operands): 0}
    flops = 4 * rows * (HQ // PAIRS) * span * HD
    return pl.pallas_call(
        functools.partial(attend_kernel, 4),
        grid_spec=pltpu.PrefetchScalarGridSpec(
            num_scalar_prefetch=1,
            grid=(queries, PAIR_HEADS),
            in_specs=in_specs,
            out_specs=pl.BlockSpec((QLEN, wide), lambda n, h, info: (n, info[0] * PAIR_HEADS + h)),
            scratch_shapes=[pltpu.VMEM((span, HD), jnp.bfloat16), pltpu.VMEM((span, 2 * HD), jnp.bfloat16)],
        ),
        out_shape=jax.ShapeDtypeStruct((rows, width), jnp.bfloat16),
        input_output_aliases=aliases,
        compiler_params=pltpu.CompilerParams(vmem_limit_bytes=VMEM_BYTES),
        cost_estimate=pl.CostEstimate(
            flops=flops, bytes_accessed=2 * rows * width, transcendentals=rows * (HQ // PAIRS) * span
        ),
        name="attend",
    )(info, *operands)


def swap(array, axis, bits):
    size = lax.axis_size(axis)
    return lax.ppermute(array, axis, [(i, i ^ bits) for i in range(size)])


def recompute_tuned(normed, w_kv, member, group):
    other = swap(normed, "group", 1)
    column = [w_kv] + [swap(w_kv, "member", 2 * k) for k in (1, 2, 3)]
    near, far = column, [swap(part, "member", 1) for part in column]
    blocks = []
    for k in range(4):
        blocks += [near[k], far[k]]
    beyond = [swap(part, "group", 2) for part in blocks]
    me = jnp.stack([member, group // 2]).astype(jnp.int32)
    mine, theirs = project(me, normed, other, blocks + beyond)
    return mine, swap(theirs, "group", 1)


def recompute_general(normed, w_kv, pair):
    whole = lax.all_gather(lax.all_gather(w_kv, "member", axis=0, tiled=True), "group", axis=1, tiled=True)
    result = jnp.dot(normed, whole, preferred_element_type=jnp.float32).astype(jnp.bfloat16)
    result = result.reshape(-1, 2, PAIRS, PAIR_WIDTH)
    parts = [result[:, :, part, :].reshape(-1, 2 * PAIR_WIDTH) for part in range(PAIRS)]
    first = jnp.where(pair == 0, parts[0], parts[1])
    second = jnp.where(pair == 0, parts[1], parts[0])
    return first, second


def local(q_rows, own_kv, cache, recomp_hidden, w_kv, retrieval, positions):
    queries = retrieval.shape[0]
    requests = queries * TOPP
    holders = lax.axis_size("member")
    groups = lax.axis_size("group")
    pass_local = cache.shape[0]
    capacity = -(-requests // holders)
    member = lax.axis_index("member")
    group = lax.axis_index("group")
    pair = group % PAIRS
    wanted = retrieval.reshape(requests)
    request = jnp.concatenate([wanted, positions.reshape(requests * RECOMP)])
    normed = normalise(recomp_hidden.reshape(requests * RECOMP, D))
    if groups == 4 and holders == 8:
        rec_first, rec_second = recompute_tuned(normed, w_kv, member, group)
    else:
        rec_first, rec_second = recompute_general(normed, w_kv, pair)
    table = lax.all_gather(request.reshape(1, -1), "member", axis=0, tiled=True).reshape(-1)
    me = jnp.stack([member, pair]).astype(jnp.int32)
    sent = pick_rows(table, me, cache, holders, requests, capacity)
    shape = (holders, capacity * KEPT, 2 * PAIR_WIDTH)
    arrived = [
        lax.all_to_all(part.reshape(shape), "member", split_axis=0, concat_axis=0, tiled=True).reshape(part.shape)
        for part in sent
    ]
    holder_of = wanted // pass_local
    same = holder_of[:, None] == holder_of[None, :]
    before = jnp.arange(requests)[None, :] < jnp.arange(requests)[:, None]
    slot = holder_of * capacity + jnp.sum((same & before).astype(jnp.int32), axis=1)
    info = jnp.concatenate([pair.reshape(1), slot]).astype(jnp.int32)
    other_info = jnp.concatenate([(1 - pair).reshape(1), slot]).astype(jnp.int32)
    out = attend(info, q_rows, own_kv, arrived[0], rec_first)
    return attend(other_info, q_rows, own_kv, arrived[1], rec_second, out)


def solution(mesh):
    rows = P(("group", "member"), None)
    placed = (
        rows,
        rows,
        P(("group", "member"), None, None),
        P(("group", "member"), None, None, None),
        P("member", "group"),
        rows,
        P(("group", "member"), None, None),
    )
    return jax.shard_map(local, mesh=mesh, in_specs=placed, out_specs=rows, check_vma=False)
```

```python
import functools

import jax
import jax.numpy as jnp
from jax import lax
from jax.experimental import pallas as pl
from jax.experimental.pallas import tpu as pltpu
from jax.sharding import PartitionSpec as P

D = 4096
HQ = 64
KVH = 4
HD = 128
TOPP = 8
QLEN = 128
PLEN = 64
RECOMP = 16
KEPT = PLEN - RECOMP
GROUPED = HQ // KVH
PAIRS = 2
PAIR_HEADS = KVH // PAIRS
PAIR_WIDTH = PAIR_HEADS * HD
HALF = KVH * HD

EPSILON = 1e-06
LOG2E = 1.4426950408889634
VMEM_BYTES = 56 * 1024 * 1024


def norm_kernel(hidden_ref, normed_ref):
    hidden = hidden_ref[...].astype(jnp.float32)
    mean = jnp.mean(hidden * hidden, axis=1, keepdims=True)
    normed_ref[...] = (hidden * lax.rsqrt(mean + EPSILON)).astype(jnp.bfloat16)


def normalise(hidden):
    rows = hidden.shape[0]
    tile = min(rows, 64)
    return pl.pallas_call(
        norm_kernel,
        grid=(rows // tile,),
        in_specs=[pl.BlockSpec((tile, D), lambda i: (i, 0))],
        out_specs=pl.BlockSpec((tile, D), lambda i: (i, 0)),
        out_shape=jax.ShapeDtypeStruct(hidden.shape, jnp.bfloat16),
        compiler_params=pltpu.CompilerParams(vmem_limit_bytes=VMEM_BYTES),
        cost_estimate=pl.CostEstimate(flops=4 * rows * D, bytes_accessed=4 * rows * D, transcendentals=rows),
        name="normalise",
    )(hidden)


def pick_kernel(
    holders, requests, pass_local, capacity, table_ref, me_ref, cache_ref, first_ref, second_ref, slot_ref, kept_ref
):
    me, pair = me_ref[0], me_ref[1]
    stride = table_ref.shape[0] // holders

    def find(requester, carry):
        base = requester * (capacity + 1)
        for rank in range(capacity + 1):
            slot_ref[base + rank] = 0
        count = jnp.int32(0)
        for k in range(requests):
            wanted = table_ref[requester * stride + k]
            slot_ref[base + count] = k
            mine = (wanted // pass_local == me).astype(jnp.int32)
            count = jnp.minimum(count + mine, capacity)
        return carry

    lax.fori_loop(0, holders, find, 0)
    spot = lax.broadcasted_iota(jnp.int32, (1, PLEN), 1)

    def cover(requester, carry):
        for rank in range(capacity):
            k = slot_ref[requester * (capacity + 1) + rank]
            start = requester * stride + requests + k * RECOMP
            covered = spot < 0
            for r in range(RECOMP):
                covered = covered | (spot == table_ref[start + r])
            kept_ref[pl.ds(requester * capacity + rank, 1), :] = jnp.where(covered, 0.0, 1.0)
        return carry

    lax.fori_loop(0, holders, cover, 0)
    kept = kept_ref[...]
    upto = lax.broadcasted_iota(jnp.int32, (PLEN, PLEN), 0) <= lax.broadcasted_iota(jnp.int32, (PLEN, PLEN), 1)
    rank_of = jnp.dot(
        kept.astype(jnp.bfloat16), upto.astype(jnp.bfloat16), preferred_element_type=jnp.float32
    )
    kept_ref[...] = jnp.where(kept > 0, rank_of, 0.0)
    row = (lax.broadcasted_iota(jnp.int32, (KEPT, PLEN), 0) + 1).astype(jnp.float32)

    def send(requester, carry):
        for rank in range(capacity):
            k = slot_ref[requester * (capacity + 1) + rank]
            passage = lax.rem(table_ref[requester * stride + k], pass_local)
            out = requester * capacity + rank
            select = (kept_ref[pl.ds(out, 1), :] == row).astype(jnp.bfloat16)
            for ref, part in ((first_ref, pair), (second_ref, 1 - pair)):
                for half in range(2):
                    start = pl.multiple_of(half * HALF + part * PAIR_WIDTH, PAIR_WIDTH)
                    ref[out, :, half * PAIR_WIDTH : (half + 1) * PAIR_WIDTH] = jnp.dot(
                        select, cache_ref[passage, :, pl.ds(start, PAIR_WIDTH)], preferred_element_type=jnp.float32
                    ).astype(jnp.bfloat16)
        return carry

    lax.fori_loop(0, holders, send, 0)


def pick_rows(table, me, cache, holders, requests, capacity):
    shape = jax.ShapeDtypeStruct((holders * capacity, KEPT, 2 * PAIR_WIDTH), jnp.bfloat16)
    smem = pl.BlockSpec(memory_space=pltpu.SMEM)
    vmem = pl.BlockSpec(memory_space=pltpu.VMEM)
    return pl.pallas_call(
        functools.partial(pick_kernel, holders, requests, cache.shape[0], capacity),
        in_specs=[smem, smem, vmem],
        out_specs=[vmem, vmem],
        out_shape=[shape, shape],
        scratch_shapes=[
            pltpu.SMEM((holders * (capacity + 1),), jnp.int32),
            pltpu.VMEM((holders * capacity, PLEN), jnp.float32),
        ],
        compiler_params=pltpu.CompilerParams(vmem_limit_bytes=VMEM_BYTES),
        name="pick_rows",
    )(table, me, cache)


def project_kernel(chunks, me_ref, mine_ref, other_ref, *refs):
    weights, outs = refs[: 2 * chunks], refs[2 * chunks :]
    member, x = me_ref[0], me_ref[1]
    depth = D // chunks
    for side, out_ref in ((mine_ref, outs[0]), (other_ref, outs[1])):
        for block in range(2):
            total = None
            for k in range(chunks):
                start = pl.multiple_of((member ^ k) * depth, depth)
                term = jnp.dot(
                    side[:, pl.ds(start, depth)],
                    weights[block * chunks + k][...],
                    preferred_element_type=jnp.float32,
                )
                total = term if total is None else total + term
            place = pl.multiple_of((x ^ block) * PAIR_WIDTH, PAIR_WIDTH)
            out_ref[:, pl.ds(place, PAIR_WIDTH)] = total.astype(jnp.bfloat16)


def project(me, mine, other, weights):
    rows = mine.shape[0]
    vmem = pl.BlockSpec(memory_space=pltpu.VMEM)
    shape = jax.ShapeDtypeStruct((rows, 2 * PAIR_WIDTH), jnp.bfloat16)
    return pl.pallas_call(
        functools.partial(project_kernel, len(weights) // 2),
        in_specs=[pl.BlockSpec(memory_space=pltpu.SMEM)] + [vmem] * (2 + len(weights)),
        out_specs=[vmem, vmem],
        out_shape=[shape, shape],
        compiler_params=pltpu.CompilerParams(vmem_limit_bytes=VMEM_BYTES),
        cost_estimate=pl.CostEstimate(
            flops=8 * rows * D * PAIR_WIDTH, bytes_accessed=4 * rows * D + 4 * D * PAIR_WIDTH, transcendentals=0
        ),
        name="project",
    )(me, mine, other, *weights)


def attend_kernel(
    heads_once, info_ref, q_ref, own_k_ref, own_v_ref, kept_k_ref, kept_v_ref, rec_k_ref, rec_v_ref, *rest
):
    out_ref, key_ref, value_ref = rest[-3:]
    query = pl.program_id(0)
    passage_keys = TOPP * PLEN
    value_ref[:, HD:] = jnp.ones((passage_keys + QLEN, HD), jnp.bfloat16)
    for j in range(TOPP):
        slot = info_ref[1 + query * TOPP + j]
        key_ref[j * KEPT : (j + 1) * KEPT, :] = kept_k_ref[slot]
        value_ref[j * KEPT : (j + 1) * KEPT, :HD] = kept_v_ref[slot]
    key_ref[TOPP * KEPT : passage_keys, :] = rec_k_ref[...]
    value_ref[TOPP * KEPT : passage_keys, :HD] = rec_v_ref[...]
    key_ref[passage_keys:, :] = own_k_ref[...]
    value_ref[passage_keys:, :HD] = own_v_ref[...]
    rows = heads_once * QLEN
    token = lax.broadcasted_iota(jnp.int32, (rows, QLEN), 0) % QLEN
    visible = lax.broadcasted_iota(jnp.int32, (rows, QLEN), 1) <= token
    factor = LOG2E / HD**0.5

    def score(first):
        block = jnp.concatenate(
            [q_ref[:, (first + i) * HD : (first + i + 1) * HD] for i in range(heads_once)], axis=0
        )
        return lax.dot_general(
            block, key_ref[...], (((1,), (1,)), ((), ())), preferred_element_type=jnp.float32
        )

    later = score(0)
    for first in range(0, GROUPED, heads_once):
        scores = later
        if first + heads_once < GROUPED:
            later = score(first + heads_once)
        scores = jnp.concatenate(
            [scores[:, :passage_keys], jnp.where(visible, scores[:, passage_keys:], -jnp.inf)], axis=1
        )
        peak = jnp.max(scores, axis=1, keepdims=True)
        expd = jnp.exp2((scores - peak) * factor).astype(jnp.bfloat16)
        summed = jnp.dot(expd, value_ref[...], preferred_element_type=jnp.float32)
        result = (summed[:, :HD] / summed[:, HD:]).astype(jnp.bfloat16)
        for i in range(heads_once):
            out_ref[:, (first + i) * HD : (first + i + 1) * HD] = result[i * QLEN : (i + 1) * QLEN]


def attend(info, q_rows, own_kv, kept, recomputed, earlier=None):
    rows, width = q_rows.shape
    queries = rows // QLEN
    slots = kept.shape[0]
    span = TOPP * PLEN + QLEN
    wide = GROUPED * HD
    in_specs = [
        pl.BlockSpec((QLEN, wide), lambda n, h, info: (n, info[0] * PAIR_HEADS + h)),
        pl.BlockSpec((QLEN, HD), lambda n, h, info: (n, info[0] * PAIR_HEADS + h)),
        pl.BlockSpec((QLEN, HD), lambda n, h, info: (n, KVH + info[0] * PAIR_HEADS + h)),
        pl.BlockSpec((slots, KEPT, HD), lambda n, h, info: (0, 0, h)),
        pl.BlockSpec((slots, KEPT, HD), lambda n, h, info: (0, 0, PAIR_HEADS + h)),
        pl.BlockSpec((TOPP * RECOMP, HD), lambda n, h, info: (n, h)),
        pl.BlockSpec((TOPP * RECOMP, HD), lambda n, h, info: (n, PAIR_HEADS + h)),
    ]
    operands = [q_rows, own_kv, own_kv, kept, kept, recomputed, recomputed]
    aliases = {}
    if earlier is not None:
        in_specs.append(pl.BlockSpec(memory_space=pl.ANY))
        operands.append(earlier)
        aliases = {len(operands): 0}
    flops = 4 * rows * (HQ // PAIRS) * span * HD
    return pl.pallas_call(
        functools.partial(attend_kernel, 2),
        grid_spec=pltpu.PrefetchScalarGridSpec(
            num_scalar_prefetch=1,
            grid=(queries, PAIR_HEADS),
            in_specs=in_specs,
            out_specs=pl.BlockSpec((QLEN, wide), lambda n, h, info: (n, info[0] * PAIR_HEADS + h)),
            scratch_shapes=[pltpu.VMEM((span, HD), jnp.bfloat16), pltpu.VMEM((span, 2 * HD), jnp.bfloat16)],
        ),
        out_shape=jax.ShapeDtypeStruct((rows, width), jnp.bfloat16),
        input_output_aliases=aliases,
        compiler_params=pltpu.CompilerParams(vmem_limit_bytes=VMEM_BYTES),
        cost_estimate=pl.CostEstimate(
            flops=flops, bytes_accessed=2 * rows * width, transcendentals=rows * (HQ // PAIRS) * span
        ),
        name="attend",
    )(info, *operands)


def swap(array, axis, bits):
    size = lax.axis_size(axis)
    return lax.ppermute(array, axis, [(i, i ^ bits) for i in range(size)])


def recompute_tuned(normed, w_kv, member, group):
    other = swap(normed, "group", 1)
    column = [w_kv, swap(w_kv, "member", 2), swap(w_kv, "member", 4)]
    column.append(swap(column[2], "member", 2))
    near, far = column, [swap(part, "member", 1) for part in column]
    blocks = []
    for k in range(4):
        blocks += [near[k], far[k]]
    beyond = [swap(part, "group", 2) for part in blocks]
    me = jnp.stack([member, group // 2]).astype(jnp.int32)
    mine, theirs = project(me, normed, other, blocks + beyond)
    return mine, swap(theirs, "group", 1)


def recompute_general(normed, w_kv, pair):
    whole = lax.all_gather(lax.all_gather(w_kv, "member", axis=0, tiled=True), "group", axis=1, tiled=True)
    result = jnp.dot(normed, whole, preferred_element_type=jnp.float32).astype(jnp.bfloat16)
    result = result.reshape(-1, 2, PAIRS, PAIR_WIDTH)
    parts = [result[:, :, part, :].reshape(-1, 2 * PAIR_WIDTH) for part in range(PAIRS)]
    first = jnp.where(pair == 0, parts[0], parts[1])
    second = jnp.where(pair == 0, parts[1], parts[0])
    return first, second


def local(q_rows, own_kv, cache, recomp_hidden, w_kv, retrieval, positions):
    queries = retrieval.shape[0]
    requests = queries * TOPP
    holders = lax.axis_size("member")
    groups = lax.axis_size("group")
    pass_local = cache.shape[0]
    capacity = -(-requests // holders)
    member = lax.axis_index("member")
    group = lax.axis_index("group")
    pair = group % PAIRS
    wanted = retrieval.reshape(requests)
    request = jnp.concatenate([wanted, positions.reshape(requests * RECOMP)])
    request = jnp.pad(request, (0, -request.shape[0] % 128)).reshape(1, -1, 128)
    request = jnp.broadcast_to(request, (holders,) + request.shape[1:])
    table = lax.all_to_all(request, "member", split_axis=0, concat_axis=0, tiled=True).reshape(-1)
    normed = normalise(recomp_hidden.reshape(requests * RECOMP, D))
    if groups == 4 and holders == 8:
        rec_first, rec_second = recompute_tuned(normed, w_kv, member, group)
    else:
        rec_first, rec_second = recompute_general(normed, w_kv, pair)
    me = jnp.stack([member, pair]).astype(jnp.int32)
    sent = pick_rows(table, me, cache, holders, requests, capacity)
    shape = (holders, capacity * KEPT, 2 * PAIR_WIDTH)
    arrived = [
        lax.all_to_all(part.reshape(shape), "member", split_axis=0, concat_axis=0, tiled=True).reshape(part.shape)
        for part in sent
    ]
    holder_of = wanted // pass_local
    same = holder_of[:, None] == holder_of[None, :]
    before = jnp.arange(requests)[None, :] < jnp.arange(requests)[:, None]
    slot = holder_of * capacity + jnp.sum((same & before).astype(jnp.int32), axis=1)
    info = jnp.concatenate([pair.reshape(1), slot]).astype(jnp.int32)
    other_info = jnp.concatenate([(1 - pair).reshape(1), slot]).astype(jnp.int32)
    out = attend(info, q_rows, own_kv, arrived[0], rec_first)
    return attend(other_info, q_rows, own_kv, arrived[1], rec_second, out)


def solution(mesh):
    rows = P(("group", "member"), None)
    placed = (
        rows,
        rows,
        P(("group", "member"), None, None),
        P(("group", "member"), None, None, None),
        P("member", "group"),
        rows,
        P(("group", "member"), None, None),
    )
    return jax.shard_map(local, mesh=mesh, in_specs=placed, out_specs=rows, check_vma=False)
```

```python
import functools

import jax
import jax.numpy as jnp
from jax import lax
from jax.experimental import pallas as pl
from jax.experimental.pallas import tpu as pltpu
from jax.sharding import PartitionSpec as P

D = 4096
HQ = 64
KVH = 4
HD = 128
TOPP = 8
QLEN = 128
PLEN = 64
RECOMP = 16
KEPT = PLEN - RECOMP
GROUPED = HQ // KVH
PAIRS = 2
PAIR_HEADS = KVH // PAIRS
PAIR_WIDTH = PAIR_HEADS * HD
HALF = KVH * HD

EPSILON = 1e-06
LOG2E = 1.4426950408889634
VMEM_BYTES = 56 * 1024 * 1024


def norm_kernel(hidden_ref, normed_ref):
    hidden = hidden_ref[...].astype(jnp.float32)
    mean = jnp.mean(hidden * hidden, axis=1, keepdims=True)
    normed_ref[...] = (hidden * lax.rsqrt(mean + EPSILON)).astype(jnp.bfloat16)


def normalise(hidden):
    rows = hidden.shape[0]
    tile = min(rows, 64)
    return pl.pallas_call(
        norm_kernel,
        grid=(rows // tile,),
        in_specs=[pl.BlockSpec((tile, D), lambda i: (i, 0))],
        out_specs=pl.BlockSpec((tile, D), lambda i: (i, 0)),
        out_shape=jax.ShapeDtypeStruct(hidden.shape, jnp.bfloat16),
        compiler_params=pltpu.CompilerParams(vmem_limit_bytes=VMEM_BYTES),
        cost_estimate=pl.CostEstimate(flops=4 * rows * D, bytes_accessed=4 * rows * D, transcendentals=rows),
        name="normalise",
    )(hidden)


def pick_kernel(
    holders, requests, pass_local, capacity, table_ref, me_ref, cache_ref, *rest
):
    first_ref, second_ref, slot_ref, kept_ref = rest[-4:]
    me, pair = me_ref[0], me_ref[1]
    stride = table_ref.shape[0] // holders

    def find(requester, carry):
        base = requester * (capacity + 1)
        for rank in range(capacity + 1):
            slot_ref[base + rank] = 0
        count = jnp.int32(0)
        for k in range(requests):
            wanted = table_ref[requester * stride + k]
            slot_ref[base + count] = k
            mine = (wanted // pass_local == me).astype(jnp.int32)
            count = jnp.minimum(count + mine, capacity)
        return carry

    lax.fori_loop(0, holders, find, 0, unroll=4)
    spot = lax.broadcasted_iota(jnp.int32, (1, PLEN), 1)

    def cover(requester, carry):
        for rank in range(capacity):
            k = slot_ref[requester * (capacity + 1) + rank]
            start = requester * stride + requests + k * RECOMP
            covered = spot < 0
            for r in range(RECOMP):
                covered = covered | (spot == table_ref[start + r])
            kept_ref[pl.ds(requester * capacity + rank, 1), :] = jnp.where(covered, 0.0, 1.0)
        return carry

    lax.fori_loop(0, holders, cover, 0, unroll=4)
    kept = kept_ref[...]
    upto = lax.broadcasted_iota(jnp.int32, (PLEN, PLEN), 0) <= lax.broadcasted_iota(jnp.int32, (PLEN, PLEN), 1)
    rank_of = jnp.dot(
        kept.astype(jnp.bfloat16), upto.astype(jnp.bfloat16), preferred_element_type=jnp.float32
    )
    kept_ref[...] = jnp.where(kept > 0, rank_of, 0.0)
    row = (lax.broadcasted_iota(jnp.int32, (KEPT, PLEN), 0) + 1).astype(jnp.float32)

    def send(requester, carry):
        for rank in range(capacity):
            k = slot_ref[requester * (capacity + 1) + rank]
            passage = lax.rem(table_ref[requester * stride + k], pass_local)
            out = requester * capacity + rank
            select = (kept_ref[pl.ds(out, 1), :] == row).astype(jnp.bfloat16)
            for ref, part in ((first_ref, pair), (second_ref, 1 - pair)):
                for half in range(2):
                    start = pl.multiple_of(half * HALF + part * PAIR_WIDTH, PAIR_WIDTH)
                    ref[out, :, half * PAIR_WIDTH : (half + 1) * PAIR_WIDTH] = jnp.dot(
                        select, cache_ref[passage, :, pl.ds(start, PAIR_WIDTH)], preferred_element_type=jnp.float32
                    ).astype(jnp.bfloat16)
        return carry

    lax.fori_loop(0, holders, send, 0, unroll=4)


def pick_rows(table, me, cache, holders, requests, capacity, ahead):
    shape = jax.ShapeDtypeStruct((holders * capacity, KEPT, 2 * PAIR_WIDTH), jnp.bfloat16)
    smem = pl.BlockSpec(memory_space=pltpu.SMEM)
    vmem = pl.BlockSpec(memory_space=pltpu.VMEM)
    return pl.pallas_call(
        functools.partial(pick_kernel, holders, requests, cache.shape[0], capacity),
        in_specs=[smem, smem, vmem] + [pl.BlockSpec(memory_space=pl.ANY)] * len(ahead),
        out_specs=[vmem, vmem],
        out_shape=[shape, shape],
        scratch_shapes=[
            pltpu.SMEM((holders * (capacity + 1),), jnp.int32),
            pltpu.VMEM((holders * capacity, PLEN), jnp.float32),
        ],
        compiler_params=pltpu.CompilerParams(vmem_limit_bytes=VMEM_BYTES),
        name="pick_rows",
    )(table, me, cache, *ahead)


def project_kernel(chunks, member_ref, mine_ref, other_ref, *refs):
    weights, outs = refs[:chunks], refs[chunks:]
    member = member_ref[0]
    depth = D // chunks
    for side, out_ref in ((mine_ref, outs[0]), (other_ref, outs[1])):
        total = None
        for k in range(chunks):
            start = pl.multiple_of((member ^ k) * depth, depth)
            term = jnp.dot(side[:, pl.ds(start, depth)], weights[k][...], preferred_element_type=jnp.float32)
            total = term if total is None else total + term
        out_ref[...] = total.astype(jnp.bfloat16)


def project(member, mine, other, weights):
    rows, width = mine.shape[0], weights[0].shape[1]
    vmem = pl.BlockSpec(memory_space=pltpu.VMEM)
    shape = jax.ShapeDtypeStruct((rows, width), jnp.bfloat16)
    return pl.pallas_call(
        functools.partial(project_kernel, len(weights)),
        in_specs=[pl.BlockSpec(memory_space=pltpu.SMEM)] + [vmem] * (2 + len(weights)),
        out_specs=[vmem, vmem],
        out_shape=[shape, shape],
        compiler_params=pltpu.CompilerParams(vmem_limit_bytes=VMEM_BYTES),
        cost_estimate=pl.CostEstimate(
            flops=4 * rows * D * width, bytes_accessed=4 * rows * D + 2 * D * width, transcendentals=0
        ),
        name="project",
    )(member.reshape(1), mine, other, *weights)


def attend_kernel(
    heads_once, info_ref, q_ref, own_k_ref, own_v_ref, kept_k_ref, kept_v_ref, near_ref, far_ref, *rest
):
    out_ref, key_ref, turned_ref, value_ref = rest[-4:]
    query = pl.program_id(0)
    passage_keys = TOPP * PLEN
    flip = info_ref[1] > 0
    value_ref[:, HD:] = jnp.ones((passage_keys + QLEN, HD), jnp.bfloat16)
    for j in range(TOPP):
        slot = info_ref[2 + query * TOPP + j]
        key_ref[j * KEPT : (j + 1) * KEPT, :] = kept_k_ref[slot]
        value_ref[j * KEPT : (j + 1) * KEPT, :HD] = kept_v_ref[slot]
    key_ref[TOPP * KEPT : passage_keys, :] = jnp.where(flip, far_ref[...], near_ref[...])
    value_ref[TOPP * KEPT : passage_keys, :HD] = jnp.where(flip, near_ref[...], far_ref[...])
    key_ref[passage_keys:, :] = own_k_ref[...]
    value_ref[passage_keys:, :HD] = own_v_ref[...]
    turned_ref[...] = key_ref[...].T
    rows = heads_once * QLEN
    token = lax.broadcasted_iota(jnp.int32, (rows, QLEN), 0) % QLEN
    visible = lax.broadcasted_iota(jnp.int32, (rows, QLEN), 1) <= token
    factor = LOG2E / HD**0.5

    def score(first):
        block = jnp.concatenate(
            [q_ref[:, (first + i) * HD : (first + i + 1) * HD] for i in range(heads_once)], axis=0
        )
        return jnp.dot(block, turned_ref[...], preferred_element_type=jnp.float32)

    later = score(0)
    for first in range(0, GROUPED, heads_once):
        scores = later
        if first + heads_once < GROUPED:
            later = score(first + heads_once)
        scores = jnp.concatenate(
            [scores[:, :passage_keys], jnp.where(visible, scores[:, passage_keys:], -jnp.inf)], axis=1
        )
        peak = jnp.max(scores, axis=1, keepdims=True)
        expd = jnp.exp2((scores - peak) * factor).astype(jnp.bfloat16)
        summed = jnp.dot(expd, value_ref[...], preferred_element_type=jnp.float32)
        result = (summed[:, :HD] / summed[:, HD:]).astype(jnp.bfloat16)
        for i in range(heads_once):
            out_ref[:, (first + i) * HD : (first + i + 1) * HD] = result[i * QLEN : (i + 1) * QLEN]


def attend(info, q_rows, own_kv, kept, near, far, earlier=None):
    rows, width = q_rows.shape
    queries = rows // QLEN
    slots = kept.shape[0]
    span = TOPP * PLEN + QLEN
    wide = GROUPED * HD
    in_specs = [
        pl.BlockSpec((QLEN, wide), lambda n, h, info: (n, info[0] * PAIR_HEADS + h)),
        pl.BlockSpec((QLEN, HD), lambda n, h, info: (n, info[0] * PAIR_HEADS + h)),
        pl.BlockSpec((QLEN, HD), lambda n, h, info: (n, KVH + info[0] * PAIR_HEADS + h)),
        pl.BlockSpec((slots, KEPT, HD), lambda n, h, info: (0, 0, h)),
        pl.BlockSpec((slots, KEPT, HD), lambda n, h, info: (0, 0, PAIR_HEADS + h)),
        pl.BlockSpec((TOPP * RECOMP, HD), lambda n, h, info: (n, h)),
        pl.BlockSpec((TOPP * RECOMP, HD), lambda n, h, info: (n, h)),
    ]
    operands = [q_rows, own_kv, own_kv, kept, kept, near, far]
    aliases = {}
    if earlier is not None:
        in_specs.append(pl.BlockSpec(memory_space=pl.ANY))
        operands.append(earlier)
        aliases = {len(operands): 0}
    flops = 4 * rows * (HQ // PAIRS) * span * HD
    return pl.pallas_call(
        functools.partial(attend_kernel, 2),
        grid_spec=pltpu.PrefetchScalarGridSpec(
            num_scalar_prefetch=1,
            grid=(queries, PAIR_HEADS),
            in_specs=in_specs,
            out_specs=pl.BlockSpec((QLEN, wide), lambda n, h, info: (n, info[0] * PAIR_HEADS + h)),
            scratch_shapes=[
                pltpu.VMEM((span, HD), jnp.bfloat16),
                pltpu.VMEM((HD, span), jnp.bfloat16),
                pltpu.VMEM((span, 2 * HD), jnp.bfloat16),
            ],
        ),
        out_shape=jax.ShapeDtypeStruct((rows, width), jnp.bfloat16),
        input_output_aliases=aliases,
        compiler_params=pltpu.CompilerParams(vmem_limit_bytes=VMEM_BYTES),
        cost_estimate=pl.CostEstimate(
            flops=flops, bytes_accessed=2 * rows * width, transcendentals=rows * (HQ // PAIRS) * span
        ),
        name="attend",
    )(info, *operands)


def swap(array, axis, bits):
    size = lax.axis_size(axis)
    return lax.ppermute(array, axis, [(i, i ^ bits) for i in range(size)])


def gather_columns(w_kv):
    column = [w_kv, swap(w_kv, "member", 2), swap(w_kv, "member", 4)]
    column.append(swap(column[2], "member", 2))
    blocks = []
    for part in column:
        blocks += [part, swap(part, "member", 1)]
    return blocks, [swap(part, "group", 2) for part in blocks]


def recompute_general(normed, w_kv, pair):
    whole = lax.all_gather(lax.all_gather(w_kv, "member", axis=0, tiled=True), "group", axis=1, tiled=True)
    result = jnp.dot(normed, whole, preferred_element_type=jnp.float32).astype(jnp.bfloat16)
    result = result.reshape(-1, 2, PAIRS, PAIR_WIDTH)
    first = jnp.where(pair == 0, result[:, :, 0], result[:, :, 1])
    second = jnp.where(pair == 0, result[:, :, 1], result[:, :, 0])
    return [first[:, 0], first[:, 1]], [second[:, 0], second[:, 1]]


def local(q_rows, own_kv, cache, recomp_hidden, w_kv, retrieval, positions):
    queries = retrieval.shape[0]
    requests = queries * TOPP
    holders = lax.axis_size("member")
    groups = lax.axis_size("group")
    pass_local = cache.shape[0]
    capacity = -(-requests // holders)
    member = lax.axis_index("member")
    group = lax.axis_index("group")
    pair = group % PAIRS
    tuned = groups == 4 and holders == 8
    wanted = retrieval.reshape(requests)
    request = jnp.concatenate([wanted, positions.reshape(requests * RECOMP)])
    request = jnp.pad(request, (0, -request.shape[0] % 128)).reshape(1, -1, 128)
    request = jnp.broadcast_to(request, (holders,) + request.shape[1:])
    table = lax.all_to_all(request, "member", split_axis=0, concat_axis=0, tiled=True).reshape(-1)
    normed = normalise(recomp_hidden.reshape(requests * RECOMP, D))
    ahead = [normed]
    if tuned:
        other = swap(normed, "group", 1)
        blocks, beyond = gather_columns(w_kv)
        ahead += [blocks[1], blocks[2], beyond[0]]
    me = jnp.stack([member, pair]).astype(jnp.int32)
    sent = pick_rows(table, me, cache, holders, requests, capacity, ahead)
    shape = (holders, capacity * KEPT, 2 * PAIR_WIDTH)
    arrived = [
        lax.all_to_all(part.reshape(shape), "member", split_axis=0, concat_axis=0, tiled=True).reshape(part.shape)
        for part in sent
    ]
    if tuned:
        flip = group // 2
        near, near_other = project(member, normed, other, blocks)
        far, far_other = project(member, normed, other, beyond)
        first = [near, far]
        second = [swap(near_other, "group", 1), swap(far_other, "group", 1)]
    else:
        flip = jnp.int32(0)
        first, second = recompute_general(normed, w_kv, pair)
    holder_of = wanted // pass_local
    same = holder_of[:, None] == holder_of[None, :]
    before = jnp.arange(requests)[None, :] < jnp.arange(requests)[:, None]
    slot = holder_of * capacity + jnp.sum((same & before).astype(jnp.int32), axis=1)
    info = jnp.concatenate([jnp.stack([pair, flip]), slot]).astype(jnp.int32)
    other_info = jnp.concatenate([jnp.stack([1 - pair, flip]), slot]).astype(jnp.int32)
    out = attend(info, q_rows, own_kv, arrived[0], *first)
    return attend(other_info, q_rows, own_kv, arrived[1], *second, earlier=out)


def solution(mesh):
    rows = P(("group", "member"), None)
    placed = (
        rows,
        rows,
        P(("group", "member"), None, None),
        P(("group", "member"), None, None, None),
        P("member", "group"),
        rows,
        P(("group", "member"), None, None),
    )
    return jax.shard_map(local, mesh=mesh, in_specs=placed, out_specs=rows, check_vma=False)
```

```python
import functools

import jax
import jax.numpy as jnp
from jax import lax
from jax.experimental import pallas as pl
from jax.experimental.pallas import tpu as pltpu
from jax.sharding import PartitionSpec as P

D = 4096
HQ = 64
KVH = 4
HD = 128
TOPP = 8
QLEN = 128
PLEN = 64
RECOMP = 16
KEPT = PLEN - RECOMP
GROUPED = HQ // KVH
PAIRS = 2
PAIR_HEADS = KVH // PAIRS
PAIR_WIDTH = PAIR_HEADS * HD
HALF = KVH * HD

EPSILON = 1e-06
SCORE_FACTOR = 1.4426950408889634 / HD**0.5
SAFE_EXPONENT = 80.0
VMEM_BYTES = 56 * 1024 * 1024


def norm_kernel(hidden_ref, normed_ref):
    hidden = hidden_ref[...].astype(jnp.float32)
    mean = jnp.mean(hidden * hidden, axis=1, keepdims=True)
    normed_ref[...] = (hidden * lax.rsqrt(mean + EPSILON)).astype(jnp.bfloat16)


def normalise(hidden):
    rows = hidden.shape[0]
    tile = min(rows, 64)
    return pl.pallas_call(
        norm_kernel,
        grid=(rows // tile,),
        in_specs=[pl.BlockSpec((tile, D), lambda i: (i, 0))],
        out_specs=pl.BlockSpec((tile, D), lambda i: (i, 0)),
        out_shape=jax.ShapeDtypeStruct(hidden.shape, jnp.bfloat16),
        compiler_params=pltpu.CompilerParams(vmem_limit_bytes=VMEM_BYTES),
        cost_estimate=pl.CostEstimate(flops=4 * rows * D, bytes_accessed=4 * rows * D, transcendentals=rows),
        name="normalise",
    )(hidden)


def pick_kernel(
    holders, requests, pass_local, capacity, table_ref, me_ref, cache_ref, *rest
):
    out_ref, slot_ref, kept_ref = rest[-3:]
    me, part = me_ref[0], me_ref[1]
    stride = table_ref.shape[0] // holders

    def find(requester, carry):
        base = requester * (capacity + 1)
        for rank in range(capacity + 1):
            slot_ref[base + rank] = 0
        count = jnp.int32(0)
        for k in range(requests):
            wanted = table_ref[requester * stride + k]
            slot_ref[base + count] = k
            mine = (wanted // pass_local == me).astype(jnp.int32)
            count = jnp.minimum(count + mine, capacity)
        return carry

    lax.fori_loop(0, holders, find, 0, unroll=4)
    spot = lax.broadcasted_iota(jnp.int32, (1, PLEN), 1)

    def cover(requester, carry):
        for rank in range(capacity):
            k = slot_ref[requester * (capacity + 1) + rank]
            start = requester * stride + requests + k * RECOMP
            covered = spot < 0
            for r in range(RECOMP):
                covered = covered | (spot == table_ref[start + r])
            kept_ref[pl.ds(requester * capacity + rank, 1), :] = jnp.where(covered, 0.0, 1.0)
        return carry

    lax.fori_loop(0, holders, cover, 0, unroll=4)
    kept = kept_ref[...]
    upto = lax.broadcasted_iota(jnp.int32, (PLEN, PLEN), 0) <= lax.broadcasted_iota(jnp.int32, (PLEN, PLEN), 1)
    rank_of = jnp.dot(
        kept.astype(jnp.bfloat16), upto.astype(jnp.bfloat16), preferred_element_type=jnp.float32
    )
    kept_ref[...] = jnp.where(kept > 0, rank_of, 0.0)
    row = (lax.broadcasted_iota(jnp.int32, (KEPT, PLEN), 0) + 1).astype(jnp.float32)

    def send(requester, carry):
        for rank in range(capacity):
            k = slot_ref[requester * (capacity + 1) + rank]
            passage = lax.rem(table_ref[requester * stride + k], pass_local)
            out = requester * capacity + rank
            select = (kept_ref[pl.ds(out, 1), :] == row).astype(jnp.bfloat16)
            for half in range(2):
                start = pl.multiple_of(half * HALF + part * PAIR_WIDTH, PAIR_WIDTH)
                out_ref[out, :, half * PAIR_WIDTH : (half + 1) * PAIR_WIDTH] = jnp.dot(
                    select, cache_ref[passage, :, pl.ds(start, PAIR_WIDTH)], preferred_element_type=jnp.float32
                ).astype(jnp.bfloat16)
        return carry

    lax.fori_loop(0, holders, send, 0, unroll=4)


def pick_rows(table, me, cache, holders, requests, capacity, ahead):
    shape = jax.ShapeDtypeStruct((holders * capacity, KEPT, 2 * PAIR_WIDTH), jnp.bfloat16)
    smem = pl.BlockSpec(memory_space=pltpu.SMEM)
    vmem = pl.BlockSpec(memory_space=pltpu.VMEM)
    return pl.pallas_call(
        functools.partial(pick_kernel, holders, requests, cache.shape[0], capacity),
        in_specs=[smem, smem, vmem] + [pl.BlockSpec(memory_space=pl.ANY)] * len(ahead),
        out_specs=vmem,
        out_shape=shape,
        scratch_shapes=[
            pltpu.SMEM((holders * (capacity + 1),), jnp.int32),
            pltpu.VMEM((holders * capacity, PLEN), jnp.float32),
        ],
        compiler_params=pltpu.CompilerParams(vmem_limit_bytes=VMEM_BYTES),
        name="pick_rows",
    )(table, me, cache, *ahead)


def project_kernel(chunks, member_ref, mine_ref, other_ref, *refs):
    weights, mine_out, other_out, total_ref = refs[:chunks], refs[-3], refs[-2], refs[-1]
    step = pl.program_id(0)
    rows = mine_ref.shape[0]

    @pl.when(step == 0)
    def clear():
        total_ref[...] = jnp.zeros_like(total_ref)

    both = jnp.concatenate([mine_ref[...], other_ref[...]], axis=0)
    for k in range(chunks):

        @pl.when(step == k)
        def add(k=k):
            total_ref[...] += jnp.dot(both, weights[k][...], preferred_element_type=jnp.float32)

    @pl.when(step == chunks - 1)
    def finish():
        mine_out[...] = total_ref[:rows].astype(jnp.bfloat16)
        other_out[...] = total_ref[rows:].astype(jnp.bfloat16)


def project(member, mine, other, weights):
    rows, width = mine.shape[0], weights[0].shape[1]
    chunks = len(weights)
    shape = jax.ShapeDtypeStruct((rows, width), jnp.bfloat16)
    rows_spec = pl.BlockSpec((rows, D // chunks), lambda k, member: (0, member[0] ^ k))
    weight_spec = pl.BlockSpec((D // chunks, width), lambda k, member: (0, 0))
    out_spec = pl.BlockSpec((rows, width), lambda k, member: (0, 0))
    return pl.pallas_call(
        functools.partial(project_kernel, chunks),
        grid_spec=pltpu.PrefetchScalarGridSpec(
            num_scalar_prefetch=1,
            grid=(chunks,),
            in_specs=[rows_spec, rows_spec] + [weight_spec] * chunks,
            out_specs=[out_spec, out_spec],
            scratch_shapes=[pltpu.VMEM((2 * rows, width), jnp.float32)],
        ),
        out_shape=[shape, shape],
        compiler_params=pltpu.CompilerParams(vmem_limit_bytes=VMEM_BYTES),
        cost_estimate=pl.CostEstimate(
            flops=4 * rows * D * width, bytes_accessed=4 * rows * D + 2 * D * width, transcendentals=0
        ),
        name="project",
    )(member.reshape(1), mine, other, *weights)


def bound_kernel(q_ref, bound_ref):
    @pl.when((pl.program_id(0) == 0) & (pl.program_id(1) == 0))
    def clear():
        bound_ref[...] = jnp.zeros_like(bound_ref)

    peak = jnp.zeros((QLEN, 1), jnp.float32)
    for head in range(GROUPED):
        block = q_ref[:, head * HD : (head + 1) * HD].astype(jnp.float32)
        peak = jnp.maximum(peak, jnp.sum(block * block, axis=1, keepdims=True))
    bound_ref[...] = jnp.maximum(bound_ref[...], jnp.max(peak))


def query_bound(q_rows):
    rows, width = q_rows.shape
    return pl.pallas_call(
        bound_kernel,
        grid=(rows // QLEN, KVH),
        in_specs=[pl.BlockSpec((QLEN, GROUPED * HD), lambda n, h: (n, h))],
        out_specs=pl.BlockSpec((8, HD), lambda n, h: (0, 0)),
        out_shape=jax.ShapeDtypeStruct((8, HD), jnp.float32),
        compiler_params=pltpu.CompilerParams(vmem_limit_bytes=VMEM_BYTES),
        cost_estimate=pl.CostEstimate(flops=3 * rows * width, bytes_accessed=2 * rows * width, transcendentals=0),
        name="query_bound",
    )(q_rows)


def attend_kernel(
    heads_once, info_ref, q_ref, own_k_ref, own_v_ref, kept_k_ref, kept_v_ref, near_ref, far_ref, bound_ref, *rest
):
    out_ref, key_ref, turned_ref, value_ref = rest[-4:]
    query = pl.program_id(0)
    passage_keys = TOPP * PLEN
    flip = info_ref[1] > 0
    value_ref[:, HD:] = jnp.ones((passage_keys + QLEN, HD), jnp.bfloat16)
    for j in range(TOPP):
        slot = info_ref[2 + query * TOPP + j]
        key_ref[j * KEPT : (j + 1) * KEPT, :] = kept_k_ref[slot]
        value_ref[j * KEPT : (j + 1) * KEPT, :HD] = kept_v_ref[slot]
    key_ref[TOPP * KEPT : passage_keys, :] = jnp.where(flip, far_ref[...], near_ref[...])
    value_ref[TOPP * KEPT : passage_keys, :HD] = jnp.where(flip, near_ref[...], far_ref[...])
    key_ref[passage_keys:, :] = own_k_ref[...]
    value_ref[passage_keys:, :HD] = own_v_ref[...]
    scaled = key_ref[...].astype(jnp.float32) * SCORE_FACTOR
    high = scaled.astype(jnp.bfloat16)
    turned_ref[:HD, :] = high.T
    turned_ref[HD:, :] = (scaled - high.astype(jnp.float32)).astype(jnp.bfloat16).T
    key_bound = jnp.max(jnp.sum(scaled * scaled, axis=1, keepdims=True))
    small = jnp.max(bound_ref[...]) * key_bound <= SAFE_EXPONENT**2
    rows = heads_once * QLEN
    token = lax.broadcasted_iota(jnp.int32, (rows, QLEN), 0) % QLEN
    visible = lax.broadcasted_iota(jnp.int32, (rows, QLEN), 1) <= token

    def score(first):
        block = jnp.concatenate(
            [q_ref[:, (first + i) * HD : (first + i + 1) * HD] for i in range(heads_once)], axis=0
        )
        return jnp.dot(
            jnp.concatenate([block, block], axis=1), turned_ref[...], preferred_element_type=jnp.float32
        )

    def store(first, expd):
        summed = jnp.dot(expd, value_ref[...], preferred_element_type=jnp.float32)
        result = (summed[:, :HD] / summed[:, HD:]).astype(jnp.bfloat16)
        for i in range(heads_once):
            out_ref[:, (first + i) * HD : (first + i + 1) * HD] = result[i * QLEN : (i + 1) * QLEN]

    @pl.when(small)
    def unshifted():
        shown = jnp.where(visible, 1.0, 0.0).astype(jnp.bfloat16)
        for first in range(0, GROUPED, heads_once):
            expd = jnp.exp2(score(first)).astype(jnp.bfloat16)
            store(first, jnp.concatenate([expd[:, :passage_keys], expd[:, passage_keys:] * shown], axis=1))

    @pl.when(jnp.logical_not(small))
    def shifted():
        for first in range(0, GROUPED, heads_once):
            scores = score(first)
            scores = jnp.concatenate(
                [scores[:, :passage_keys], jnp.where(visible, scores[:, passage_keys:], -jnp.inf)], axis=1
            )
            peak = jnp.max(scores, axis=1, keepdims=True)
            store(first, jnp.exp2(scores - peak).astype(jnp.bfloat16))


def attend(info, q_rows, own_kv, kept, near, far, bound, earlier=None):
    rows, width = q_rows.shape
    queries = rows // QLEN
    slots = kept.shape[0]
    span = TOPP * PLEN + QLEN
    wide = GROUPED * HD
    in_specs = [
        pl.BlockSpec((QLEN, wide), lambda n, h, info: (n, info[0] * PAIR_HEADS + h)),
        pl.BlockSpec((QLEN, HD), lambda n, h, info: (n, info[0] * PAIR_HEADS + h)),
        pl.BlockSpec((QLEN, HD), lambda n, h, info: (n, KVH + info[0] * PAIR_HEADS + h)),
        pl.BlockSpec((slots, KEPT, HD), lambda n, h, info: (0, 0, h)),
        pl.BlockSpec((slots, KEPT, HD), lambda n, h, info: (0, 0, PAIR_HEADS + h)),
        pl.BlockSpec((TOPP * RECOMP, HD), lambda n, h, info: (n, h)),
        pl.BlockSpec((TOPP * RECOMP, HD), lambda n, h, info: (n, h)),
        pl.BlockSpec((8, HD), lambda n, h, info: (0, 0)),
    ]
    operands = [q_rows, own_kv, own_kv, kept, kept, near, far, bound]
    aliases = {}
    if earlier is not None:
        in_specs.append(pl.BlockSpec(memory_space=pl.ANY))
        operands.append(earlier)
        aliases = {len(operands): 0}
    flops = 4 * rows * (HQ // PAIRS) * span * HD
    return pl.pallas_call(
        functools.partial(attend_kernel, 2),
        grid_spec=pltpu.PrefetchScalarGridSpec(
            num_scalar_prefetch=1,
            grid=(queries, PAIR_HEADS),
            in_specs=in_specs,
            out_specs=pl.BlockSpec((QLEN, wide), lambda n, h, info: (n, info[0] * PAIR_HEADS + h)),
            scratch_shapes=[
                pltpu.VMEM((span, HD), jnp.bfloat16),
                pltpu.VMEM((2 * HD, span), jnp.bfloat16),
                pltpu.VMEM((span, 2 * HD), jnp.bfloat16),
            ],
        ),
        out_shape=jax.ShapeDtypeStruct((rows, width), jnp.bfloat16),
        input_output_aliases=aliases,
        compiler_params=pltpu.CompilerParams(vmem_limit_bytes=VMEM_BYTES),
        cost_estimate=pl.CostEstimate(
            flops=flops, bytes_accessed=2 * rows * width, transcendentals=rows * (HQ // PAIRS) * span
        ),
        name="attend",
    )(info, *operands)


def swap(array, axis, bits):
    size = lax.axis_size(axis)
    return lax.ppermute(array, axis, [(i, i ^ bits) for i in range(size)])


def gather_columns(w_kv):
    column = [w_kv, swap(w_kv, "member", 2), swap(w_kv, "member", 4)]
    column.append(swap(column[2], "member", 2))
    across = [swap(part, "group", 2) for part in column]
    blocks, beyond = [], []
    for k in range(4):
        aside = swap(column[k], "member", 1)
        blocks += [column[k], aside]
        beyond += [across[k], swap(aside, "group", 2) if k % 2 == 0 else swap(across[k], "member", 1)]
    return blocks, beyond


def recompute_general(normed, w_kv, pair):
    whole = lax.all_gather(lax.all_gather(w_kv, "member", axis=0, tiled=True), "group", axis=1, tiled=True)
    result = jnp.dot(normed, whole, preferred_element_type=jnp.float32).astype(jnp.bfloat16)
    result = result.reshape(-1, 2, PAIRS, PAIR_WIDTH)
    first = jnp.where(pair == 0, result[:, :, 0], result[:, :, 1])
    second = jnp.where(pair == 0, result[:, :, 1], result[:, :, 0])
    return [first[:, 0], first[:, 1]], [second[:, 0], second[:, 1]]


def local(q_rows, own_kv, cache, recomp_hidden, w_kv, retrieval, positions):
    queries = retrieval.shape[0]
    requests = queries * TOPP
    holders = lax.axis_size("member")
    groups = lax.axis_size("group")
    pass_local = cache.shape[0]
    capacity = -(-requests // holders)
    member = lax.axis_index("member")
    group = lax.axis_index("group")
    pair = group % PAIRS
    tuned = groups == 4 and holders == 8
    wanted = retrieval.reshape(requests)
    request = jnp.concatenate([wanted, positions.reshape(requests * RECOMP)])
    request = jnp.pad(request, (0, -request.shape[0] % 128)).reshape(1, -1, 128)
    request = jnp.broadcast_to(request, (holders,) + request.shape[1:])
    table = lax.all_to_all(request, "member", split_axis=0, concat_axis=0, tiled=True).reshape(-1)
    normed = normalise(recomp_hidden.reshape(requests * RECOMP, D))
    early, middle = [normed], []
    if tuned:
        other = swap(normed, "group", 1)
        blocks, beyond = gather_columns(w_kv)
        early += [blocks[1], blocks[2], blocks[4], beyond[0]]
        middle += [blocks[3], blocks[5], blocks[6], beyond[1], beyond[2]]
    bound = query_bound(q_rows)
    shape = (holders, capacity * KEPT, 2 * PAIR_WIDTH)
    arrived = []
    for part, ahead in ((pair, early), (1 - pair, middle + [bound])):
        me = jnp.stack([member, part]).astype(jnp.int32)
        sent = pick_rows(table, me, cache, holders, requests, capacity, ahead)
        got = lax.all_to_all(sent.reshape(shape), "member", split_axis=0, concat_axis=0, tiled=True)
        arrived.append(got.reshape(sent.shape))
    if tuned:
        flip = group // 2
        near, near_other = project(member, normed, other, blocks)
        far, far_other = project(member, normed, other, beyond)
        first = [near, far]
        second = [swap(near_other, "group", 1), swap(far_other, "group", 1)]
    else:
        flip = jnp.int32(0)
        first, second = recompute_general(normed, w_kv, pair)
    holder_of = wanted // pass_local
    same = holder_of[:, None] == holder_of[None, :]
    before = jnp.arange(requests)[None, :] < jnp.arange(requests)[:, None]
    slot = holder_of * capacity + jnp.sum((same & before).astype(jnp.int32), axis=1)
    info = jnp.concatenate([jnp.stack([pair, flip]), slot]).astype(jnp.int32)
    other_info = jnp.concatenate([jnp.stack([1 - pair, flip]), slot]).astype(jnp.int32)
    out = attend(info, q_rows, own_kv, arrived[0], *first, bound)
    return attend(other_info, q_rows, own_kv, arrived[1], *second, bound, earlier=out)


def solution(mesh):
    rows = P(("group", "member"), None)
    placed = (
        rows,
        rows,
        P(("group", "member"), None, None),
        P(("group", "member"), None, None, None),
        P("member", "group"),
        rows,
        P(("group", "member"), None, None),
    )
    return jax.shard_map(local, mesh=mesh, in_specs=placed, out_specs=rows, check_vma=False)
```

```python
import functools

import jax
import jax.numpy as jnp
from jax import lax
from jax.experimental import pallas as pl
from jax.experimental.pallas import tpu as pltpu
from jax.sharding import PartitionSpec as P

D = 4096
HQ = 64
KVH = 4
HD = 128
TOPP = 8
QLEN = 128
PLEN = 64
RECOMP = 16
KEPT = PLEN - RECOMP
GROUPED = HQ // KVH
PAIRS = 2
PAIR_HEADS = KVH // PAIRS
PAIR_WIDTH = PAIR_HEADS * HD
HALF = KVH * HD

EPSILON = 1e-06
SCORE_FACTOR = 1.4426950408889634 / HD**0.5
SAFE_EXPONENT = 80.0
VMEM_BYTES = 56 * 1024 * 1024


def norm_kernel(hidden_ref, *rest):
    normed_ref = rest[-1]
    hidden = hidden_ref[...].astype(jnp.float32)
    mean = jnp.mean(hidden * hidden, axis=1, keepdims=True)
    normed_ref[...] = (hidden * lax.rsqrt(mean + EPSILON)).astype(jnp.bfloat16)


def normalise(hidden, ahead):
    rows = hidden.shape[0]
    tile = min(rows, 32)
    return pl.pallas_call(
        norm_kernel,
        grid=(rows // tile,),
        in_specs=[pl.BlockSpec((tile, D), lambda i: (i, 0))] + [pl.BlockSpec(memory_space=pl.ANY)] * len(ahead),
        out_specs=pl.BlockSpec((tile, D), lambda i: (i, 0)),
        out_shape=jax.ShapeDtypeStruct(hidden.shape, jnp.bfloat16),
        compiler_params=pltpu.CompilerParams(vmem_limit_bytes=VMEM_BYTES),
        cost_estimate=pl.CostEstimate(flops=4 * rows * D, bytes_accessed=4 * rows * D, transcendentals=rows),
        name="normalise",
    )(hidden, *ahead)


def pick_kernel(
    holders, requests, pass_local, capacity, table_ref, me_ref, cache_ref, *rest
):
    first_ref, second_ref, slot_ref, kept_ref = rest[-4:]
    me, pair = me_ref[0], me_ref[1]
    stride = table_ref.shape[0] // holders

    def find(requester, carry):
        base = requester * (capacity + 1)
        for rank in range(capacity + 1):
            slot_ref[base + rank] = 0
        count = jnp.int32(0)
        for k in range(requests):
            wanted = table_ref[requester * stride + k]
            slot_ref[base + count] = k
            mine = (wanted // pass_local == me).astype(jnp.int32)
            count = jnp.minimum(count + mine, capacity)
        return carry

    lax.fori_loop(0, holders, find, 0, unroll=4)
    spot = lax.broadcasted_iota(jnp.int32, (1, PLEN), 1)

    def cover(requester, carry):
        for rank in range(capacity):
            k = slot_ref[requester * (capacity + 1) + rank]
            start = requester * stride + requests + k * RECOMP
            covered = spot < 0
            for r in range(RECOMP):
                covered = covered | (spot == table_ref[start + r])
            kept_ref[pl.ds(requester * capacity + rank, 1), :] = jnp.where(covered, 0.0, 1.0)
        return carry

    lax.fori_loop(0, holders, cover, 0, unroll=4)
    kept = kept_ref[...]
    upto = lax.broadcasted_iota(jnp.int32, (PLEN, PLEN), 0) <= lax.broadcasted_iota(jnp.int32, (PLEN, PLEN), 1)
    rank_of = jnp.dot(
        kept.astype(jnp.bfloat16), upto.astype(jnp.bfloat16), preferred_element_type=jnp.float32
    )
    kept_ref[...] = jnp.where(kept > 0, rank_of, 0.0)
    row = (lax.broadcasted_iota(jnp.int32, (KEPT, PLEN), 0) + 1).astype(jnp.float32)

    def send(requester, carry):
        for rank in range(capacity):
            k = slot_ref[requester * (capacity + 1) + rank]
            passage = lax.rem(table_ref[requester * stride + k], pass_local)
            out = requester * capacity + rank
            select = (kept_ref[pl.ds(out, 1), :] == row).astype(jnp.bfloat16)
            for ref, part in ((first_ref, pair), (second_ref, 1 - pair)):
                for half in range(2):
                    start = pl.multiple_of(half * HALF + part * PAIR_WIDTH, PAIR_WIDTH)
                    ref[out, :, half * PAIR_WIDTH : (half + 1) * PAIR_WIDTH] = jnp.dot(
                        select, cache_ref[passage, :, pl.ds(start, PAIR_WIDTH)], preferred_element_type=jnp.float32
                    ).astype(jnp.bfloat16)
        return carry

    lax.fori_loop(0, holders, send, 0, unroll=4)


def pick_rows(table, me, cache, holders, requests, capacity, ahead):
    shape = jax.ShapeDtypeStruct((holders * capacity, KEPT, 2 * PAIR_WIDTH), jnp.bfloat16)
    smem = pl.BlockSpec(memory_space=pltpu.SMEM)
    vmem = pl.BlockSpec(memory_space=pltpu.VMEM)
    return pl.pallas_call(
        functools.partial(pick_kernel, holders, requests, cache.shape[0], capacity),
        in_specs=[smem, smem, vmem] + [pl.BlockSpec(memory_space=pl.ANY)] * len(ahead),
        out_specs=[vmem, vmem],
        out_shape=[shape, shape],
        scratch_shapes=[
            pltpu.SMEM((holders * (capacity + 1),), jnp.int32),
            pltpu.VMEM((holders * capacity, PLEN), jnp.float32),
        ],
        compiler_params=pltpu.CompilerParams(vmem_limit_bytes=VMEM_BYTES),
        name="pick_rows",
    )(table, me, cache, *ahead)


def project_kernel(chunks, member_ref, mine_ref, other_ref, *refs):
    weights, mine_out, other_out = refs[:chunks], refs[-2], refs[-1]
    rows = mine_ref.shape[0]
    depth = D // chunks
    total = None
    for k in range(chunks):
        columns = pl.ds(pl.multiple_of((member_ref[0] ^ k) * depth, depth), depth)
        both = jnp.concatenate([mine_ref[:, columns], other_ref[:, columns]], axis=0)
        term = jnp.dot(both, weights[k][...], preferred_element_type=jnp.float32)
        total = term if total is None else total + term
    mine_out[...] = total[:rows].astype(jnp.bfloat16)
    other_out[...] = total[rows:].astype(jnp.bfloat16)


def project(member, mine, other, weights, ahead):
    rows, width = mine.shape[0], weights[0].shape[1]
    shape = jax.ShapeDtypeStruct((rows, width), jnp.bfloat16)
    vmem = pl.BlockSpec(memory_space=pltpu.VMEM)
    return pl.pallas_call(
        functools.partial(project_kernel, len(weights)),
        in_specs=[pl.BlockSpec(memory_space=pltpu.SMEM)]
        + [vmem] * (2 + len(weights))
        + [pl.BlockSpec(memory_space=pl.ANY)] * len(ahead),
        out_specs=[vmem, vmem],
        out_shape=[shape, shape],
        compiler_params=pltpu.CompilerParams(vmem_limit_bytes=VMEM_BYTES),
        cost_estimate=pl.CostEstimate(
            flops=4 * rows * D * width, bytes_accessed=4 * rows * D + 2 * D * width, transcendentals=0
        ),
        name="project",
    )(member.reshape(1), mine, other, *weights, *ahead)


def bound_kernel(q_ref, *rest):
    bound_ref = rest[-1]

    @pl.when(pl.program_id(0) == 0)
    def clear():
        bound_ref[...] = jnp.zeros_like(bound_ref)

    peak = jnp.zeros((q_ref.shape[0], 1), jnp.float32)
    for first in range(0, GROUPED, 4):
        most = None
        for head in range(first, first + 4):
            block = q_ref[:, head * HD : (head + 1) * HD].astype(jnp.float32)
            most = block * block if most is None else jnp.maximum(most, block * block)
        peak = jnp.maximum(peak, jnp.sum(most, axis=1, keepdims=True))
    bound_ref[...] = jnp.maximum(bound_ref[...], jnp.max(peak))


def query_bound(q_rows, ahead):
    rows, width = q_rows.shape
    return pl.pallas_call(
        bound_kernel,
        grid=(KVH,),
        in_specs=[pl.BlockSpec((rows, GROUPED * HD), lambda h: (0, h))]
        + [pl.BlockSpec(memory_space=pl.ANY)] * len(ahead),
        out_specs=pl.BlockSpec((8, HD), lambda h: (0, 0)),
        out_shape=jax.ShapeDtypeStruct((8, HD), jnp.float32),
        compiler_params=pltpu.CompilerParams(vmem_limit_bytes=VMEM_BYTES),
        cost_estimate=pl.CostEstimate(flops=3 * rows * width, bytes_accessed=2 * rows * width, transcendentals=0),
        name="query_bound",
    )(q_rows, *ahead)


def attend_kernel(
    heads_once, info_ref, q_ref, own_k_ref, own_v_ref, kept_k_ref, kept_v_ref, near_ref, far_ref, bound_ref, *rest
):
    out_ref, key_ref, turned_ref, value_ref = rest[-4:]
    query = pl.program_id(0)
    passage_keys = TOPP * PLEN
    flip = info_ref[1] > 0
    value_ref[:, HD:] = jnp.ones((passage_keys + QLEN, HD), jnp.bfloat16)
    for j in range(TOPP):
        slot = info_ref[2 + query * TOPP + j]
        key_ref[j * KEPT : (j + 1) * KEPT, :] = kept_k_ref[slot]
        value_ref[j * KEPT : (j + 1) * KEPT, :HD] = kept_v_ref[slot]
    key_ref[TOPP * KEPT : passage_keys, :] = jnp.where(flip, far_ref[...], near_ref[...])
    value_ref[TOPP * KEPT : passage_keys, :HD] = jnp.where(flip, near_ref[...], far_ref[...])
    key_ref[passage_keys:, :] = own_k_ref[...]
    value_ref[passage_keys:, :HD] = own_v_ref[...]
    scaled = key_ref[...].astype(jnp.float32) * SCORE_FACTOR
    high = scaled.astype(jnp.bfloat16)
    turned_ref[:HD, :] = high.T
    turned_ref[HD:, :] = (scaled - high.astype(jnp.float32)).astype(jnp.bfloat16).T
    key_bound = jnp.max(jnp.sum(scaled * scaled, axis=1, keepdims=True))
    small = jnp.max(bound_ref[...]) * key_bound <= SAFE_EXPONENT**2
    rows = heads_once * QLEN
    token = lax.broadcasted_iota(jnp.int32, (rows, QLEN), 0) % QLEN
    visible = lax.broadcasted_iota(jnp.int32, (rows, QLEN), 1) <= token

    def score(first):
        block = jnp.concatenate(
            [q_ref[:, (first + i) * HD : (first + i + 1) * HD] for i in range(heads_once)], axis=0
        )
        return jnp.dot(
            jnp.concatenate([block, block], axis=1), turned_ref[...], preferred_element_type=jnp.float32
        )

    def store(first, expd):
        summed = jnp.dot(expd, value_ref[...], preferred_element_type=jnp.float32)
        result = (summed[:, :HD] / summed[:, HD:]).astype(jnp.bfloat16)
        for i in range(heads_once):
            out_ref[:, (first + i) * HD : (first + i + 1) * HD] = result[i * QLEN : (i + 1) * QLEN]

    @pl.when(small)
    def unshifted():
        shown = jnp.where(visible, 1.0, 0.0).astype(jnp.bfloat16)
        for first in range(0, GROUPED, heads_once):
            expd = jnp.exp2(score(first)).astype(jnp.bfloat16)
            store(first, jnp.concatenate([expd[:, :passage_keys], expd[:, passage_keys:] * shown], axis=1))

    @pl.when(jnp.logical_not(small))
    def shifted():
        for first in range(0, GROUPED, heads_once):
            scores = score(first)
            scores = jnp.concatenate(
                [scores[:, :passage_keys], jnp.where(visible, scores[:, passage_keys:], -jnp.inf)], axis=1
            )
            peak = jnp.max(scores, axis=1, keepdims=True)
            store(first, jnp.exp2(scores - peak).astype(jnp.bfloat16))


def attend(info, q_rows, own_kv, kept, near, far, bound, earlier=None):
    rows, width = q_rows.shape
    queries = rows // QLEN
    slots = kept.shape[0]
    span = TOPP * PLEN + QLEN
    wide = GROUPED * HD
    in_specs = [
        pl.BlockSpec((QLEN, wide), lambda n, h, info: (n, info[0] * PAIR_HEADS + h)),
        pl.BlockSpec((QLEN, HD), lambda n, h, info: (n, info[0] * PAIR_HEADS + h)),
        pl.BlockSpec((QLEN, HD), lambda n, h, info: (n, KVH + info[0] * PAIR_HEADS + h)),
        pl.BlockSpec((slots, KEPT, HD), lambda n, h, info: (0, 0, h)),
        pl.BlockSpec((slots, KEPT, HD), lambda n, h, info: (0, 0, PAIR_HEADS + h)),
        pl.BlockSpec((TOPP * RECOMP, HD), lambda n, h, info: (n, h)),
        pl.BlockSpec((TOPP * RECOMP, HD), lambda n, h, info: (n, h)),
        pl.BlockSpec((8, HD), lambda n, h, info: (0, 0)),
    ]
    operands = [q_rows, own_kv, own_kv, kept, kept, near, far, bound]
    aliases = {}
    if earlier is not None:
        in_specs.append(pl.BlockSpec(memory_space=pl.ANY))
        operands.append(earlier)
        aliases = {len(operands): 0}
    flops = 4 * rows * (HQ // PAIRS) * span * HD
    return pl.pallas_call(
        functools.partial(attend_kernel, 8),
        grid_spec=pltpu.PrefetchScalarGridSpec(
            num_scalar_prefetch=1,
            grid=(queries, PAIR_HEADS),
            in_specs=in_specs,
            out_specs=pl.BlockSpec((QLEN, wide), lambda n, h, info: (n, info[0] * PAIR_HEADS + h)),
            scratch_shapes=[
                pltpu.VMEM((span, HD), jnp.bfloat16),
                pltpu.VMEM((2 * HD, span), jnp.bfloat16),
                pltpu.VMEM((span, 2 * HD), jnp.bfloat16),
            ],
        ),
        out_shape=jax.ShapeDtypeStruct((rows, width), jnp.bfloat16),
        input_output_aliases=aliases,
        compiler_params=pltpu.CompilerParams(vmem_limit_bytes=VMEM_BYTES),
        cost_estimate=pl.CostEstimate(
            flops=flops, bytes_accessed=2 * rows * width, transcendentals=rows * (HQ // PAIRS) * span
        ),
        name="attend",
    )(info, *operands)


def swap(array, axis, bits):
    size = lax.axis_size(axis)
    return lax.ppermute(array, axis, [(i, i ^ bits) for i in range(size)])


def gather_columns(w_kv):
    column = [w_kv, swap(w_kv, "member", 2), swap(w_kv, "member", 4)]
    column.append(swap(column[2], "member", 2))
    across = [swap(part, "group", 2) for part in column]
    blocks, beyond = [], []
    for k in range(4):
        aside = swap(column[k], "member", 1)
        blocks += [column[k], aside]
        beyond += [across[k], swap(aside, "group", 2) if k % 2 == 0 else swap(across[k], "member", 1)]
    return blocks, beyond


def recompute_general(normed, w_kv, pair):
    whole = lax.all_gather(lax.all_gather(w_kv, "member", axis=0, tiled=True), "group", axis=1, tiled=True)
    result = jnp.dot(normed, whole, preferred_element_type=jnp.float32).astype(jnp.bfloat16)
    result = result.reshape(-1, 2, PAIRS, PAIR_WIDTH)
    first = jnp.where(pair == 0, result[:, :, 0], result[:, :, 1])
    second = jnp.where(pair == 0, result[:, :, 1], result[:, :, 0])
    return [first[:, 0], first[:, 1]], [second[:, 0], second[:, 1]]


def local(q_rows, own_kv, cache, recomp_hidden, w_kv, retrieval, positions):
    queries = retrieval.shape[0]
    requests = queries * TOPP
    holders = lax.axis_size("member")
    groups = lax.axis_size("group")
    pass_local = cache.shape[0]
    capacity = -(-requests // holders)
    member = lax.axis_index("member")
    group = lax.axis_index("group")
    pair = group % PAIRS
    tuned = groups == 4 and holders == 8
    wanted = retrieval.reshape(requests)
    request = jnp.concatenate([wanted, positions.reshape(requests * RECOMP)])
    request = jnp.pad(request, (0, -request.shape[0] % 128)).reshape(1, -1, 128)
    request = jnp.broadcast_to(request, (holders,) + request.shape[1:])
    table = lax.all_to_all(request, "member", split_axis=0, concat_axis=0, tiled=True).reshape(-1)
    hidden = recomp_hidden.reshape(requests * RECOMP, D)
    hops = [[], [], [], []]
    if tuned:
        blocks, beyond = gather_columns(w_kv)
        hops = [
            [blocks[1], blocks[2], blocks[4], beyond[0]],
            [blocks[3], blocks[6], beyond[2]],
            [blocks[5], beyond[1], beyond[4]],
            [blocks[7], beyond[6]],
        ]
    normed = normalise(hidden, hops[0])
    me = jnp.stack([member, pair]).astype(jnp.int32)
    sent = pick_rows(table, me, cache, holders, requests, capacity, [normed] + hops[1])
    shape = (holders, capacity * KEPT, 2 * PAIR_WIDTH)
    arrived = [
        lax.all_to_all(part.reshape(shape), "member", split_axis=0, concat_axis=0, tiled=True).reshape(part.shape)
        for part in sent
    ]
    bound = query_bound(q_rows, list(sent) + hops[2])
    if tuned:
        flip = group // 2
        other = swap(normed, "group", 1)
        near, near_other = project(member, normed, other, blocks, [bound] + hops[3])
        far, far_other = project(member, normed, other, beyond, [near])
        first = [near, far]
        second = [swap(near_other, "group", 1), swap(far_other, "group", 1)]
    else:
        flip = jnp.int32(0)
        first, second = recompute_general(normed, w_kv, pair)
    holder_of = wanted // pass_local
    same = holder_of[:, None] == holder_of[None, :]
    before = jnp.arange(requests)[None, :] < jnp.arange(requests)[:, None]
    slot = holder_of * capacity + jnp.sum((same & before).astype(jnp.int32), axis=1)
    info = jnp.concatenate([jnp.stack([pair, flip]), slot]).astype(jnp.int32)
    other_info = jnp.concatenate([jnp.stack([1 - pair, flip]), slot]).astype(jnp.int32)
    out = attend(info, q_rows, own_kv, arrived[0], *first, bound)
    return attend(other_info, q_rows, own_kv, arrived[1], *second, bound, earlier=out)


def solution(mesh):
    rows = P(("group", "member"), None)
    placed = (
        rows,
        rows,
        P(("group", "member"), None, None),
        P(("group", "member"), None, None, None),
        P("member", "group"),
        rows,
        P(("group", "member"), None, None),
    )
    return jax.shard_map(local, mesh=mesh, in_specs=placed, out_specs=rows, check_vma=False)
```

```python
import functools

import jax
import jax.numpy as jnp
from jax import lax
from jax.experimental import pallas as pl
from jax.experimental.pallas import tpu as pltpu
from jax.sharding import PartitionSpec as P

D = 4096
HQ = 64
KVH = 4
HD = 128
TOPP = 8
QLEN = 128
PLEN = 64
RECOMP = 16
KEPT = PLEN - RECOMP
GROUPED = HQ // KVH
PAIRS = 2
PAIR_HEADS = KVH // PAIRS
PAIR_WIDTH = PAIR_HEADS * HD
HALF = KVH * HD

EPSILON = 1e-06
SCORE_FACTOR = 1.4426950408889634 / HD**0.5
SAFE_EXPONENT = 48.0
LN2 = 0.6931471805599453
VMEM_BYTES = 56 * 1024 * 1024


def norm_kernel(hidden_ref, *rest):
    normed_ref = rest[-1]
    hidden = hidden_ref[...].astype(jnp.float32)
    mean = jnp.mean(hidden * hidden, axis=1, keepdims=True)
    normed_ref[...] = (hidden * lax.rsqrt(mean + EPSILON)).astype(jnp.bfloat16)


def normalise(hidden, ahead):
    rows = hidden.shape[0]
    tile = min(rows, 64)
    return pl.pallas_call(
        norm_kernel,
        grid=(rows // tile,),
        in_specs=[pl.BlockSpec((tile, D), lambda i: (i, 0))] + [pl.BlockSpec(memory_space=pl.ANY)] * len(ahead),
        out_specs=pl.BlockSpec((tile, D), lambda i: (i, 0)),
        out_shape=jax.ShapeDtypeStruct(hidden.shape, jnp.bfloat16),
        compiler_params=pltpu.CompilerParams(vmem_limit_bytes=VMEM_BYTES),
        cost_estimate=pl.CostEstimate(flops=4 * rows * D, bytes_accessed=4 * rows * D, transcendentals=rows),
        name="normalise",
    )(hidden, *ahead)


def pick_kernel(
    holders, requests, pass_local, capacity, me_ref, cache_ref, *rest
):
    tables, (out_ref, slot_ref, kept_ref) = rest[:holders], rest[-3:]
    me, pair = me_ref[0], me_ref[1]

    for k, table_ref in enumerate(tables):
        base = k * (capacity + 1)
        for rank in range(capacity + 1):
            slot_ref[base + rank] = 0
        count = jnp.int32(0)
        for request in range(requests):
            slot_ref[base + count] = request
            mine = (table_ref[request] // pass_local == me).astype(jnp.int32)
            count = jnp.minimum(count + mine, capacity)
    spot = lax.broadcasted_iota(jnp.int32, (1, PLEN), 1)
    for k, table_ref in enumerate(tables):
        for rank in range(capacity):
            start = requests + slot_ref[k * (capacity + 1) + rank] * RECOMP
            covered = spot < 0
            for r in range(RECOMP):
                covered = covered | (spot == table_ref[start + r])
            kept_ref[k * capacity + rank : k * capacity + rank + 1, :] = jnp.where(covered, 0.0, 1.0)
    kept = kept_ref[...]
    upto = lax.broadcasted_iota(jnp.int32, (PLEN, PLEN), 0) <= lax.broadcasted_iota(jnp.int32, (PLEN, PLEN), 1)
    rank_of = jnp.dot(
        kept.astype(jnp.bfloat16), upto.astype(jnp.bfloat16), preferred_element_type=jnp.float32
    )
    kept_ref[...] = jnp.where(kept > 0, rank_of, 0.0)
    row = (lax.broadcasted_iota(jnp.int32, (KEPT, PLEN), 0) + 1).astype(jnp.float32)

    for k, table_ref in enumerate(tables):
        for rank in range(capacity):
            passage = lax.rem(table_ref[slot_ref[k * (capacity + 1) + rank]], pass_local)
            at = k * capacity + rank
            select = (kept_ref[at : at + 1, :] == row).astype(jnp.bfloat16)
            out = (me ^ k) * capacity + rank
            for place, part in ((0, pair), (1, 1 - pair)):
                for half in range(2):
                    start = pl.multiple_of(half * HALF + part * PAIR_WIDTH, PAIR_WIDTH)
                    end = (place * 2 + half) * PAIR_WIDTH
                    out_ref[out, :, end : end + PAIR_WIDTH] = jnp.dot(
                        select, cache_ref[passage, :, pl.ds(start, PAIR_WIDTH)], preferred_element_type=jnp.float32
                    ).astype(jnp.bfloat16)


def pick_rows(tables, me, cache, requests, capacity, ahead):
    holders = len(tables)
    shape = jax.ShapeDtypeStruct((holders * capacity, KEPT, 2 * HALF), jnp.bfloat16)
    smem = pl.BlockSpec(memory_space=pltpu.SMEM)
    vmem = pl.BlockSpec(memory_space=pltpu.VMEM)
    return pl.pallas_call(
        functools.partial(pick_kernel, holders, requests, cache.shape[0], capacity),
        in_specs=[smem, vmem] + [smem] * holders + [pl.BlockSpec(memory_space=pl.ANY)] * len(ahead),
        out_specs=vmem,
        out_shape=shape,
        scratch_shapes=[
            pltpu.SMEM((holders * (capacity + 1),), jnp.int32),
            pltpu.VMEM((holders * capacity, PLEN), jnp.float32),
        ],
        compiler_params=pltpu.CompilerParams(vmem_limit_bytes=VMEM_BYTES),
        name="pick_rows",
    )(me, cache, *tables, *ahead)


def project_kernel(chunks, member_ref, mine_ref, other_ref, *refs):
    weights, mine_out, other_out = refs[:chunks], refs[-2], refs[-1]
    rows = mine_ref.shape[0]
    depth = D // chunks
    total = None
    for k in range(chunks):
        columns = pl.ds(pl.multiple_of((member_ref[0] ^ k) * depth, depth), depth)
        both = jnp.concatenate([mine_ref[:, columns], other_ref[:, columns]], axis=0)
        term = jnp.dot(both, weights[k][...], preferred_element_type=jnp.float32)
        total = term if total is None else total + term
    mine_out[...] = total[:rows].astype(jnp.bfloat16)
    other_out[...] = total[rows:].astype(jnp.bfloat16)


def project(member, mine, other, weights, ahead):
    rows, width = mine.shape[0], weights[0].shape[1]
    shape = jax.ShapeDtypeStruct((rows, width), jnp.bfloat16)
    vmem = pl.BlockSpec(memory_space=pltpu.VMEM)
    return pl.pallas_call(
        functools.partial(project_kernel, len(weights)),
        in_specs=[pl.BlockSpec(memory_space=pltpu.SMEM)]
        + [vmem] * (2 + len(weights))
        + [pl.BlockSpec(memory_space=pl.ANY)] * len(ahead),
        out_specs=[vmem, vmem],
        out_shape=[shape, shape],
        compiler_params=pltpu.CompilerParams(vmem_limit_bytes=VMEM_BYTES),
        cost_estimate=pl.CostEstimate(
            flops=4 * rows * D * width, bytes_accessed=4 * rows * D + 2 * D * width, transcendentals=0
        ),
        name="project",
    )(member.reshape(1), mine, other, *weights, *ahead)


def bound_kernel(q_ref, *rest):
    bound_ref = rest[-1]

    @pl.when(pl.program_id(0) == 0)
    def clear():
        bound_ref[...] = jnp.zeros_like(bound_ref)

    peak = jnp.zeros((q_ref.shape[0], 1), jnp.float32)
    for first in range(0, GROUPED, 4):
        most = None
        for head in range(first, first + 4):
            block = q_ref[:, head * HD : (head + 1) * HD].astype(jnp.float32)
            most = block * block if most is None else jnp.maximum(most, block * block)
        peak = jnp.maximum(peak, jnp.sum(most, axis=1, keepdims=True))
    bound_ref[...] = jnp.maximum(bound_ref[...], jnp.max(peak))


def query_bound(q_rows, ahead):
    rows, width = q_rows.shape
    return pl.pallas_call(
        bound_kernel,
        grid=(KVH,),
        in_specs=[pl.BlockSpec((rows, GROUPED * HD), lambda h: (0, h))]
        + [pl.BlockSpec(memory_space=pl.ANY)] * len(ahead),
        out_specs=pl.BlockSpec((8, HD), lambda h: (0, 0)),
        out_shape=jax.ShapeDtypeStruct((8, HD), jnp.float32),
        compiler_params=pltpu.CompilerParams(vmem_limit_bytes=VMEM_BYTES),
        cost_estimate=pl.CostEstimate(flops=3 * rows * width, bytes_accessed=2 * rows * width, transcendentals=0),
        name="query_bound",
    )(q_rows, *ahead)


def attend_kernel(
    heads_once, info_ref, q_ref, own_k_ref, own_v_ref, kept_k_ref, kept_v_ref, near_ref, far_ref, bound_ref, *rest
):
    out_ref, key_ref, turned_ref, value_ref = rest[-4:]
    query = pl.program_id(0)
    passage_keys = TOPP * PLEN
    flip = info_ref[1] > 0
    value_ref[:, HD:] = jnp.ones((passage_keys + QLEN, HD), jnp.bfloat16)
    for j in range(TOPP):
        slot = info_ref[2 + query * TOPP + j]
        key_ref[j * KEPT : (j + 1) * KEPT, :] = kept_k_ref[slot]
        value_ref[j * KEPT : (j + 1) * KEPT, :HD] = kept_v_ref[slot]
    key_ref[TOPP * KEPT : passage_keys, :] = jnp.where(flip, far_ref[...], near_ref[...])
    value_ref[TOPP * KEPT : passage_keys, :HD] = jnp.where(flip, near_ref[...], far_ref[...])
    key_ref[passage_keys:, :] = own_k_ref[...]
    value_ref[passage_keys:, :HD] = own_v_ref[...]
    scaled = key_ref[...].astype(jnp.float32) * SCORE_FACTOR
    high = scaled.astype(jnp.bfloat16)
    turned_ref[:HD, :] = high.T
    turned_ref[HD:, :] = (scaled - high.astype(jnp.float32)).astype(jnp.bfloat16).T
    key_bound = jnp.max(jnp.sum(scaled * scaled, axis=1, keepdims=True))
    small = jnp.max(bound_ref[...]) * key_bound <= SAFE_EXPONENT**2
    rows = heads_once * QLEN
    token = lax.broadcasted_iota(jnp.int32, (rows, QLEN), 0) % QLEN
    visible = lax.broadcasted_iota(jnp.int32, (rows, QLEN), 1) <= token

    def score(first):
        block = jnp.concatenate(
            [q_ref[:, (first + i) * HD : (first + i + 1) * HD] for i in range(heads_once)], axis=0
        )
        return jnp.dot(
            jnp.concatenate([block, block], axis=1), turned_ref[...], preferred_element_type=jnp.float32
        )

    def store(first, expd):
        summed = jnp.dot(expd, value_ref[...], preferred_element_type=jnp.float32)
        result = (summed[:, :HD] / summed[:, HD:]).astype(jnp.bfloat16)
        for i in range(heads_once):
            out_ref[:, (first + i) * HD : (first + i + 1) * HD] = result[i * QLEN : (i + 1) * QLEN]

    @pl.when(small)
    def unshifted():
        shown = jnp.where(visible, 1.0, 0.0).astype(jnp.bfloat16)
        for first in range(0, GROUPED, heads_once):
            scores = score(first)
            coarse = scores.astype(jnp.bfloat16)
            fine = ((scores - coarse.astype(jnp.float32)) * LN2).astype(jnp.bfloat16)
            expd = jnp.exp2(coarse)
            expd = expd + expd * fine
            store(first, jnp.concatenate([expd[:, :passage_keys], expd[:, passage_keys:] * shown], axis=1))

    @pl.when(jnp.logical_not(small))
    def shifted():
        for first in range(0, GROUPED, heads_once):
            scores = score(first)
            scores = jnp.concatenate(
                [scores[:, :passage_keys], jnp.where(visible, scores[:, passage_keys:], -jnp.inf)], axis=1
            )
            peak = jnp.max(scores, axis=1, keepdims=True)
            store(first, jnp.exp2(scores - peak).astype(jnp.bfloat16))


def attend(part, info, q_rows, own_kv, kept, near, far, bound, earlier=None):
    rows, width = q_rows.shape
    queries = rows // QLEN
    slots = kept.shape[0]
    span = TOPP * PLEN + QLEN
    wide = GROUPED * HD
    in_specs = [
        pl.BlockSpec((QLEN, wide), lambda n, h, info: (n, info[0] * PAIR_HEADS + h)),
        pl.BlockSpec((QLEN, HD), lambda n, h, info: (n, info[0] * PAIR_HEADS + h)),
        pl.BlockSpec((QLEN, HD), lambda n, h, info: (n, KVH + info[0] * PAIR_HEADS + h)),
        pl.BlockSpec((slots, KEPT, HD), lambda n, h, info: (0, 0, part * KVH + h)),
        pl.BlockSpec((slots, KEPT, HD), lambda n, h, info: (0, 0, part * KVH + PAIR_HEADS + h)),
        pl.BlockSpec((TOPP * RECOMP, HD), lambda n, h, info: (n, h)),
        pl.BlockSpec((TOPP * RECOMP, HD), lambda n, h, info: (n, h)),
        pl.BlockSpec((8, HD), lambda n, h, info: (0, 0)),
    ]
    operands = [q_rows, own_kv, own_kv, kept, kept, near, far, bound]
    aliases = {}
    if earlier is not None:
        in_specs.append(pl.BlockSpec(memory_space=pl.ANY))
        operands.append(earlier)
        aliases = {len(operands): 0}
    flops = 4 * rows * (HQ // PAIRS) * span * HD
    return pl.pallas_call(
        functools.partial(attend_kernel, 8),
        grid_spec=pltpu.PrefetchScalarGridSpec(
            num_scalar_prefetch=1,
            grid=(queries, PAIR_HEADS),
            in_specs=in_specs,
            out_specs=pl.BlockSpec((QLEN, wide), lambda n, h, info: (n, info[0] * PAIR_HEADS + h)),
            scratch_shapes=[
                pltpu.VMEM((span, HD), jnp.bfloat16),
                pltpu.VMEM((2 * HD, span), jnp.bfloat16),
                pltpu.VMEM((span, 2 * HD), jnp.bfloat16),
            ],
        ),
        out_shape=jax.ShapeDtypeStruct((rows, width), jnp.bfloat16),
        input_output_aliases=aliases,
        compiler_params=pltpu.CompilerParams(vmem_limit_bytes=VMEM_BYTES),
        cost_estimate=pl.CostEstimate(
            flops=flops, bytes_accessed=2 * rows * width, transcendentals=rows * (HQ // PAIRS) * span
        ),
        name="attend",
    )(info, *operands)


def swap(array, axis, bits):
    size = lax.axis_size(axis)
    return lax.ppermute(array, axis, [(i, i ^ bits) for i in range(size)])


def gather_columns(w_kv):
    column = [w_kv, swap(w_kv, "member", 2), swap(w_kv, "member", 4)]
    column.append(swap(column[2], "member", 2))
    across = [swap(part, "group", 2) for part in column]
    blocks, beyond = [], []
    for k in range(4):
        aside = swap(column[k], "member", 1)
        blocks += [column[k], aside]
        beyond += [across[k], swap(aside, "group", 2) if k < 3 else swap(across[k], "member", 1)]
    return blocks, beyond


def recompute_general(normed, w_kv, pair):
    whole = lax.all_gather(lax.all_gather(w_kv, "member", axis=0, tiled=True), "group", axis=1, tiled=True)
    result = jnp.dot(normed, whole, preferred_element_type=jnp.float32).astype(jnp.bfloat16)
    result = result.reshape(-1, 2, PAIRS, PAIR_WIDTH)
    first = jnp.where(pair == 0, result[:, :, 0], result[:, :, 1])
    second = jnp.where(pair == 0, result[:, :, 1], result[:, :, 0])
    return [first[:, 0], first[:, 1]], [second[:, 0], second[:, 1]]


def local(q_rows, own_kv, cache, recomp_hidden, w_kv, retrieval, positions):
    queries = retrieval.shape[0]
    requests = queries * TOPP
    holders = lax.axis_size("member")
    groups = lax.axis_size("group")
    pass_local = cache.shape[0]
    capacity = -(-requests // holders)
    member = lax.axis_index("member")
    group = lax.axis_index("group")
    pair = group % PAIRS
    tuned = groups == 4 and holders == 8
    wanted = retrieval.reshape(requests)
    request = jnp.concatenate([wanted, positions.reshape(requests * RECOMP)])
    request = jnp.pad(request, (0, -request.shape[0] % 128))
    tables = [request] + [swap(request, "member", k) for k in range(1, holders)]
    hidden = recomp_hidden.reshape(requests * RECOMP, D)
    hops = [[], []]
    if tuned:
        blocks, beyond = gather_columns(w_kv)
        hops = [[blocks[3], blocks[6], beyond[2]], [blocks[5], beyond[1], beyond[4]]]
    normed = normalise(hidden, [])
    me = jnp.stack([member, pair]).astype(jnp.int32)
    sent = pick_rows(tables, me, cache, requests, capacity, [normed] + hops[0])
    arrived = lax.all_to_all(
        sent.reshape(holders, capacity * KEPT, 2 * HALF), "member", split_axis=0, concat_axis=0, tiled=True
    ).reshape(sent.shape)
    bound = query_bound(q_rows, [sent] + hops[1])
    if tuned:
        flip = group // 2
        other = swap(normed, "group", 1)
        near, near_other = project(member, normed, other, blocks, [bound])
        far, far_other = project(member, normed, other, beyond, [near])
        first = [near, far]
        second = [swap(near_other, "group", 1), swap(far_other, "group", 1)]
    else:
        flip = jnp.int32(0)
        first, second = recompute_general(normed, w_kv, pair)
    holder_of = wanted // pass_local
    same = holder_of[:, None] == holder_of[None, :]
    before = jnp.arange(requests)[None, :] < jnp.arange(requests)[:, None]
    slot = holder_of * capacity + jnp.sum((same & before).astype(jnp.int32), axis=1)
    info = jnp.concatenate([jnp.stack([pair, flip]), slot]).astype(jnp.int32)
    other_info = jnp.concatenate([jnp.stack([1 - pair, flip]), slot]).astype(jnp.int32)
    out = attend(0, info, q_rows, own_kv, arrived, *first, bound)
    return attend(1, other_info, q_rows, own_kv, arrived, *second, bound, earlier=out)


def solution(mesh):
    rows = P(("group", "member"), None)
    placed = (
        rows,
        rows,
        P(("group", "member"), None, None),
        P(("group", "member"), None, None, None),
        P("member", "group"),
        rows,
        P(("group", "member"), None, None),
    )
    return jax.shard_map(local, mesh=mesh, in_specs=placed, out_specs=rows, check_vma=False)
```

```python
import functools

import jax
import jax.numpy as jnp
from jax import lax
from jax.experimental import pallas as pl
from jax.experimental.pallas import tpu as pltpu
from jax.sharding import PartitionSpec as P

D = 4096
HQ = 64
KVH = 4
HD = 128
TOPP = 8
QLEN = 128
PLEN = 64
RECOMP = 16
KEPT = PLEN - RECOMP
GROUPED = HQ // KVH
PAIRS = 2
PAIR_HEADS = KVH // PAIRS
PAIR_WIDTH = PAIR_HEADS * HD
HALF = KVH * HD

EPSILON = 1e-06
SCORE_FACTOR = 1.4426950408889634 / HD**0.5
SAFE_EXPONENT = 80.0
VMEM_BYTES = 56 * 1024 * 1024
LITTLE = pl.CostEstimate(flops=1, bytes_accessed=1, transcendentals=0)


def norm_kernel(hidden_ref, *rest):
    normed_ref = rest[-1]
    hidden = hidden_ref[...].astype(jnp.float32)
    mean = jnp.mean(hidden * hidden, axis=1, keepdims=True)
    normed_ref[...] = (hidden * lax.rsqrt(mean + EPSILON)).astype(jnp.bfloat16)


def normalise(hidden, ahead):
    rows = hidden.shape[0]
    tile = min(rows, 64)
    return pl.pallas_call(
        norm_kernel,
        grid=(rows // tile,),
        in_specs=[pl.BlockSpec((tile, D), lambda i: (i, 0))] + [pl.BlockSpec(memory_space=pl.ANY)] * len(ahead),
        out_specs=pl.BlockSpec((tile, D), lambda i: (i, 0)),
        out_shape=jax.ShapeDtypeStruct(hidden.shape, jnp.bfloat16),
        compiler_params=pltpu.CompilerParams(vmem_limit_bytes=VMEM_BYTES),
        cost_estimate=LITTLE,
        name="normalise",
    )(hidden, *ahead)


def pick_kernel(
    holders, requests, pass_local, capacity, me_ref, table_ref, cache_ref, *rest
):
    out_ref, slot_ref, kept_ref = rest[-3:]
    me, pair = me_ref[0], me_ref[1]
    stride = table_ref.shape[0] // holders

    for k in range(holders):
        base = k * (capacity + 1)
        for rank in range(capacity + 1):
            slot_ref[base + rank] = 0
        count = jnp.int32(0)
        for request in range(requests):
            slot_ref[base + count] = request
            mine = (table_ref[k * stride + request] // pass_local == me).astype(jnp.int32)
            count = jnp.minimum(count + mine, capacity)
    spot = lax.broadcasted_iota(jnp.int32, (1, PLEN), 1)
    for k in range(holders):
        for rank in range(capacity):
            start = k * stride + requests + slot_ref[k * (capacity + 1) + rank] * RECOMP
            covered = spot < 0
            for r in range(RECOMP):
                covered = covered | (spot == table_ref[start + r])
            kept_ref[k * capacity + rank : k * capacity + rank + 1, :] = jnp.where(covered, 0.0, 1.0)
    kept = kept_ref[...]
    upto = lax.broadcasted_iota(jnp.int32, (PLEN, PLEN), 0) <= lax.broadcasted_iota(jnp.int32, (PLEN, PLEN), 1)
    rank_of = jnp.dot(
        kept.astype(jnp.bfloat16), upto.astype(jnp.bfloat16), preferred_element_type=jnp.float32
    )
    kept_ref[...] = jnp.where(kept > 0, rank_of, 0.0)
    row = (lax.broadcasted_iota(jnp.int32, (KEPT, PLEN), 0) + 1).astype(jnp.float32)

    for k in range(holders):
        for rank in range(capacity):
            passage = lax.rem(table_ref[k * stride + slot_ref[k * (capacity + 1) + rank]], pass_local)
            at = k * capacity + rank
            select = (kept_ref[at : at + 1, :] == row).astype(jnp.bfloat16)
            for place, part in ((0, pair), (1, 1 - pair)):
                for half in range(2):
                    start = pl.multiple_of(half * HALF + part * PAIR_WIDTH, PAIR_WIDTH)
                    end = (place * 2 + half) * PAIR_WIDTH
                    out_ref[at, :, end : end + PAIR_WIDTH] = jnp.dot(
                        select, cache_ref[passage, :, pl.ds(start, PAIR_WIDTH)], preferred_element_type=jnp.float32
                    ).astype(jnp.bfloat16)


def pick_rows(table, me, cache, holders, requests, capacity, ahead):
    shape = jax.ShapeDtypeStruct((holders * capacity, KEPT, 2 * HALF), jnp.bfloat16)
    smem = pl.BlockSpec(memory_space=pltpu.SMEM)
    vmem = pl.BlockSpec(memory_space=pltpu.VMEM)
    return pl.pallas_call(
        functools.partial(pick_kernel, holders, requests, cache.shape[0], capacity),
        in_specs=[smem, smem, vmem] + [pl.BlockSpec(memory_space=pl.ANY)] * len(ahead),
        out_specs=vmem,
        out_shape=shape,
        scratch_shapes=[
            pltpu.SMEM((holders * (capacity + 1),), jnp.int32),
            pltpu.VMEM((holders * capacity, PLEN), jnp.float32),
        ],
        compiler_params=pltpu.CompilerParams(vmem_limit_bytes=VMEM_BYTES),
        cost_estimate=LITTLE,
        name="pick_rows",
    )(me, table, cache, *ahead)


def project_kernel(chunks, member_ref, mine_ref, other_ref, *refs):
    weights, mine_out, other_out = refs[:chunks], refs[-2], refs[-1]
    rows = mine_ref.shape[0]
    depth = D // chunks
    total = None
    for k in range(chunks):
        columns = pl.ds(pl.multiple_of((member_ref[0] ^ k) * depth, depth), depth)
        both = jnp.concatenate([mine_ref[:, columns], other_ref[:, columns]], axis=0)
        term = jnp.dot(both, weights[k][...], preferred_element_type=jnp.float32)
        total = term if total is None else total + term
    mine_out[...] = total[:rows].astype(jnp.bfloat16)
    other_out[...] = total[rows:].astype(jnp.bfloat16)


def project(member, mine, other, weights, ahead):
    rows, width = mine.shape[0], weights[0].shape[1]
    shape = jax.ShapeDtypeStruct((rows, width), jnp.bfloat16)
    vmem = pl.BlockSpec(memory_space=pltpu.VMEM)
    return pl.pallas_call(
        functools.partial(project_kernel, len(weights)),
        in_specs=[pl.BlockSpec(memory_space=pltpu.SMEM)]
        + [vmem] * (2 + len(weights))
        + [pl.BlockSpec(memory_space=pl.ANY)] * len(ahead),
        out_specs=[vmem, vmem],
        out_shape=[shape, shape],
        compiler_params=pltpu.CompilerParams(vmem_limit_bytes=VMEM_BYTES),
        cost_estimate=LITTLE,
        name="project",
    )(member.reshape(1), mine, other, *weights, *ahead)


def bound_kernel(q_ref, *rest):
    bound_ref = rest[-1]

    @pl.when(pl.program_id(0) == 0)
    def clear():
        bound_ref[...] = jnp.zeros_like(bound_ref)

    peak = jnp.zeros((q_ref.shape[0], 1), jnp.float32)
    for first in range(0, GROUPED, 4):
        most = None
        for head in range(first, first + 4):
            block = q_ref[:, head * HD : (head + 1) * HD].astype(jnp.float32)
            most = block * block if most is None else jnp.maximum(most, block * block)
        peak = jnp.maximum(peak, jnp.sum(most, axis=1, keepdims=True))
    bound_ref[...] = jnp.maximum(bound_ref[...], jnp.max(peak))


def query_bound(q_rows, ahead):
    rows, width = q_rows.shape
    return pl.pallas_call(
        bound_kernel,
        grid=(KVH,),
        in_specs=[pl.BlockSpec((rows, GROUPED * HD), lambda h: (0, h))]
        + [pl.BlockSpec(memory_space=pl.ANY)] * len(ahead),
        out_specs=pl.BlockSpec((8, HD), lambda h: (0, 0)),
        out_shape=jax.ShapeDtypeStruct((8, HD), jnp.float32),
        compiler_params=pltpu.CompilerParams(vmem_limit_bytes=VMEM_BYTES),
        cost_estimate=LITTLE,
        name="query_bound",
    )(q_rows, *ahead)


def attend_kernel(
    heads_once, info_ref, q_ref, own_k_ref, own_v_ref, kept_ref, near_ref, far_ref, bound_ref, *rest
):
    out_ref, key_ref, turned_ref, value_ref = rest[-4:]
    query = pl.program_id(0)
    key_start = pl.multiple_of(pl.program_id(1) * HD, HD)
    value_start = pl.multiple_of(PAIR_WIDTH + pl.program_id(1) * HD, HD)
    passage_keys = TOPP * PLEN
    flip = info_ref[1] > 0
    value_ref[:, HD:] = jnp.ones((passage_keys + QLEN, HD), jnp.bfloat16)
    for j in range(TOPP):
        slot = info_ref[2 + query * TOPP + j]
        key_ref[j * KEPT : (j + 1) * KEPT, :] = kept_ref[slot, :, pl.ds(key_start, HD)]
        value_ref[j * KEPT : (j + 1) * KEPT, :HD] = kept_ref[slot, :, pl.ds(value_start, HD)]
    key_ref[TOPP * KEPT : passage_keys, :] = jnp.where(flip, far_ref[...], near_ref[...])
    value_ref[TOPP * KEPT : passage_keys, :HD] = jnp.where(flip, near_ref[...], far_ref[...])
    key_ref[passage_keys:, :] = own_k_ref[...]
    value_ref[passage_keys:, :HD] = own_v_ref[...]
    scaled = key_ref[...].astype(jnp.float32) * SCORE_FACTOR
    high = scaled.astype(jnp.bfloat16)
    turned_ref[:HD, :] = high.T
    turned_ref[HD:, :] = (scaled - high.astype(jnp.float32)).astype(jnp.bfloat16).T
    key_bound = jnp.max(jnp.sum(scaled * scaled, axis=1, keepdims=True))
    small = jnp.max(bound_ref[...]) * key_bound <= SAFE_EXPONENT**2
    rows = heads_once * QLEN
    token = lax.broadcasted_iota(jnp.int32, (rows, QLEN), 0) % QLEN
    visible = lax.broadcasted_iota(jnp.int32, (rows, QLEN), 1) <= token

    def score(first):
        block = jnp.concatenate(
            [q_ref[:, (first + i) * HD : (first + i + 1) * HD] for i in range(heads_once)], axis=0
        )
        return jnp.dot(
            jnp.concatenate([block, block], axis=1), turned_ref[...], preferred_element_type=jnp.float32
        )

    def store(first, expd):
        summed = jnp.dot(expd, value_ref[...], preferred_element_type=jnp.float32)
        result = (summed[:, :HD] / summed[:, HD:]).astype(jnp.bfloat16)
        for i in range(heads_once):
            out_ref[:, (first + i) * HD : (first + i + 1) * HD] = result[i * QLEN : (i + 1) * QLEN]

    @pl.when(small)
    def unshifted():
        shown = jnp.where(visible, 1.0, 0.0).astype(jnp.bfloat16)
        for first in range(0, GROUPED, heads_once):
            expd = jnp.exp2(score(first)).astype(jnp.bfloat16)
            store(first, jnp.concatenate([expd[:, :passage_keys], expd[:, passage_keys:] * shown], axis=1))

    @pl.when(jnp.logical_not(small))
    def shifted():
        for first in range(0, GROUPED, heads_once):
            scores = score(first)
            scores = jnp.concatenate(
                [scores[:, :passage_keys], jnp.where(visible, scores[:, passage_keys:], -jnp.inf)], axis=1
            )
            peak = jnp.max(scores, axis=1, keepdims=True)
            store(first, jnp.exp2(scores - peak).astype(jnp.bfloat16))


def attend(part, info, q_rows, own_kv, kept, near, far, bound, earlier=None):
    rows, width = q_rows.shape
    queries = rows // QLEN
    slots = kept.shape[0]
    span = TOPP * PLEN + QLEN
    wide = GROUPED * HD
    in_specs = [
        pl.BlockSpec((QLEN, wide), lambda n, h, info: (n, info[0] * PAIR_HEADS + h)),
        pl.BlockSpec((QLEN, HD), lambda n, h, info: (n, info[0] * PAIR_HEADS + h)),
        pl.BlockSpec((QLEN, HD), lambda n, h, info: (n, KVH + info[0] * PAIR_HEADS + h)),
        pl.BlockSpec((slots, KEPT, HALF), lambda n, h, info: (0, 0, part)),
        pl.BlockSpec((TOPP * RECOMP, HD), lambda n, h, info: (n, h)),
        pl.BlockSpec((TOPP * RECOMP, HD), lambda n, h, info: (n, h)),
        pl.BlockSpec((8, HD), lambda n, h, info: (0, 0)),
    ]
    operands = [q_rows, own_kv, own_kv, kept, near, far, bound]
    aliases = {}
    if earlier is not None:
        in_specs.append(pl.BlockSpec(memory_space=pl.ANY))
        operands.append(earlier)
        aliases = {len(operands): 0}
    return pl.pallas_call(
        functools.partial(attend_kernel, 8),
        grid_spec=pltpu.PrefetchScalarGridSpec(
            num_scalar_prefetch=1,
            grid=(queries, PAIR_HEADS),
            in_specs=in_specs,
            out_specs=pl.BlockSpec((QLEN, wide), lambda n, h, info: (n, info[0] * PAIR_HEADS + h)),
            scratch_shapes=[
                pltpu.VMEM((span, HD), jnp.bfloat16),
                pltpu.VMEM((2 * HD, span), jnp.bfloat16),
                pltpu.VMEM((span, 2 * HD), jnp.bfloat16),
            ],
        ),
        out_shape=jax.ShapeDtypeStruct((rows, width), jnp.bfloat16),
        input_output_aliases=aliases,
        compiler_params=pltpu.CompilerParams(vmem_limit_bytes=VMEM_BYTES),
        cost_estimate=LITTLE,
        name="attend",
    )(info, *operands)


def swap(array, axis, bits):
    size = lax.axis_size(axis)
    return lax.ppermute(array, axis, [(i, i ^ bits) for i in range(size)])


def gather_columns(w_kv):
    column = [w_kv, swap(w_kv, "member", 2), swap(w_kv, "member", 4)]
    column.append(swap(column[2], "member", 2))
    across = [swap(part, "group", 2) for part in column]
    blocks, beyond = [], []
    for k in range(4):
        aside = swap(column[k], "member", 1)
        blocks += [column[k], aside]
        beyond += [across[k], swap(aside, "group", 2) if k < 3 else swap(across[k], "member", 1)]
    return blocks, beyond


def recompute_general(normed, w_kv, pair):
    whole = lax.all_gather(lax.all_gather(w_kv, "member", axis=0, tiled=True), "group", axis=1, tiled=True)
    result = jnp.dot(normed, whole, preferred_element_type=jnp.float32).astype(jnp.bfloat16)
    result = result.reshape(-1, 2, PAIRS, PAIR_WIDTH)
    first = jnp.where(pair == 0, result[:, :, 0], result[:, :, 1])
    second = jnp.where(pair == 0, result[:, :, 1], result[:, :, 0])
    return [first[:, 0], first[:, 1]], [second[:, 0], second[:, 1]]


def local(q_rows, own_kv, cache, recomp_hidden, w_kv, retrieval, positions):
    queries = retrieval.shape[0]
    requests = queries * TOPP
    holders = lax.axis_size("member")
    groups = lax.axis_size("group")
    pass_local = cache.shape[0]
    capacity = -(-requests // holders)
    member = lax.axis_index("member")
    group = lax.axis_index("group")
    pair = group % PAIRS
    tuned = groups == 4 and holders == 8
    wanted = retrieval.reshape(requests)
    request = jnp.concatenate([wanted, positions.reshape(requests * RECOMP)])
    request = jnp.pad(request, (0, -request.shape[0] % 128)).reshape(1, -1, 128)
    request = jnp.broadcast_to(request, (holders,) + request.shape[1:])
    table = lax.all_to_all(request, "member", split_axis=0, concat_axis=0, tiled=True).reshape(-1)
    hidden = recomp_hidden.reshape(requests * RECOMP, D)
    hops = [[], []]
    if tuned:
        blocks, beyond = gather_columns(w_kv)
        hops = [[blocks[3], blocks[6], beyond[2]], [blocks[5], beyond[1], beyond[4]]]
    normed = normalise(hidden, [])
    me = jnp.stack([member, pair]).astype(jnp.int32)
    sent = pick_rows(table, me, cache, holders, requests, capacity, [normed] + hops[0])
    arrived = lax.all_to_all(
        sent.reshape(holders, capacity * KEPT, 2 * HALF), "member", split_axis=0, concat_axis=0, tiled=True
    ).reshape(sent.shape)
    bound = query_bound(q_rows, [sent] + hops[1])
    if tuned:
        flip = group // 2
        other = swap(normed, "group", 1)
        near, near_other = project(member, normed, other, blocks, [bound])
        far, far_other = project(member, normed, other, beyond, [near])
        first = [near, far]
        second = [swap(near_other, "group", 1), swap(far_other, "group", 1)]
    else:
        flip = jnp.int32(0)
        first, second = recompute_general(normed, w_kv, pair)
    holder_of = wanted // pass_local
    same = holder_of[:, None] == holder_of[None, :]
    before = jnp.arange(requests)[None, :] < jnp.arange(requests)[:, None]
    slot = holder_of * capacity + jnp.sum((same & before).astype(jnp.int32), axis=1)
    info = jnp.concatenate([jnp.stack([pair, flip]), slot]).astype(jnp.int32)
    other_info = jnp.concatenate([jnp.stack([1 - pair, flip]), slot]).astype(jnp.int32)
    out = attend(0, info, q_rows, own_kv, arrived, *first, bound)
    return attend(1, other_info, q_rows, own_kv, arrived, *second, bound, earlier=out)


def solution(mesh):
    rows = P(("group", "member"), None)
    placed = (
        rows,
        rows,
        P(("group", "member"), None, None),
        P(("group", "member"), None, None, None),
        P("member", "group"),
        rows,
        P(("group", "member"), None, None),
    )
    return jax.shard_map(local, mesh=mesh, in_specs=placed, out_specs=rows, check_vma=False)
```

```python
import functools

import jax
import jax.numpy as jnp
from jax import lax
from jax.experimental import pallas as pl
from jax.experimental.pallas import tpu as pltpu
from jax.sharding import PartitionSpec as P

D = 4096
HQ = 64
KVH = 4
HD = 128
TOPP = 8
QLEN = 128
PLEN = 64
RECOMP = 16
KEPT = PLEN - RECOMP
GROUPED = HQ // KVH
PAIRS = 2
PAIR_HEADS = KVH // PAIRS
PAIR_WIDTH = PAIR_HEADS * HD
HALF = KVH * HD

EPSILON = 1e-06
SCORE_FACTOR = 1.4426950408889634 / HD**0.5
SAFE_EXPONENT = 80.0
VMEM_BYTES = 56 * 1024 * 1024
LITTLE = pl.CostEstimate(flops=1, bytes_accessed=1, transcendentals=0)
MEDIUM = pl.CostEstimate(flops=1, bytes_accessed=18_000_000, transcendentals=0)
LARGE = pl.CostEstimate(flops=1, bytes_accessed=36_000_000, transcendentals=0)


def norm_kernel(hidden_ref, *rest):
    normed_ref = rest[-1]
    hidden = hidden_ref[...].astype(jnp.float32)
    mean = jnp.mean(hidden * hidden, axis=1, keepdims=True)
    normed_ref[...] = (hidden * lax.rsqrt(mean + EPSILON)).astype(jnp.bfloat16)


def normalise(hidden, ahead):
    rows = hidden.shape[0]
    tile = min(rows, 64)
    return pl.pallas_call(
        norm_kernel,
        grid=(rows // tile,),
        in_specs=[pl.BlockSpec((tile, D), lambda i: (i, 0))] + [pl.BlockSpec(memory_space=pl.ANY)] * len(ahead),
        out_specs=pl.BlockSpec((tile, D), lambda i: (i, 0)),
        out_shape=jax.ShapeDtypeStruct(hidden.shape, jnp.bfloat16),
        compiler_params=pltpu.CompilerParams(vmem_limit_bytes=VMEM_BYTES),
        cost_estimate=LITTLE,
        name="normalise",
    )(hidden, *ahead)


def find_kernel(holders, requests, pass_local, capacity, me_ref, table_ref, rank_ref, passage_ref, slot_ref, kept_ref):
    me = me_ref[0]
    stride = table_ref.shape[0] // holders
    for k in range(holders):
        base = k * (capacity + 1)
        for rank in range(capacity + 1):
            slot_ref[base + rank] = 0
        count = jnp.int32(0)
        for request in range(requests):
            slot_ref[base + count] = request
            mine = (table_ref[k * stride + request] // pass_local == me).astype(jnp.int32)
            count = jnp.minimum(count + mine, capacity)
    spot = lax.broadcasted_iota(jnp.int32, (1, PLEN), 1)
    for k in range(holders):
        for rank in range(capacity):
            at = k * capacity + rank
            request = slot_ref[k * (capacity + 1) + rank]
            passage_ref[at] = lax.rem(table_ref[k * stride + request], pass_local)
            start = k * stride + requests + request * RECOMP
            covered = spot < 0
            for r in range(RECOMP):
                covered = covered | (spot == table_ref[start + r])
            kept_ref[at : at + 1, :] = jnp.where(covered, 0.0, 1.0)
    kept = kept_ref[...]
    upto = lax.broadcasted_iota(jnp.int32, (PLEN, PLEN), 0) <= lax.broadcasted_iota(jnp.int32, (PLEN, PLEN), 1)
    rank_of = jnp.dot(
        kept.astype(jnp.bfloat16), upto.astype(jnp.bfloat16), preferred_element_type=jnp.float32
    )
    rank_ref[...] = jnp.where(kept > 0, rank_of, 0.0)


def find_rows(table, me, holders, requests, pass_local, capacity):
    slots = holders * capacity
    smem = pl.BlockSpec(memory_space=pltpu.SMEM)
    return pl.pallas_call(
        functools.partial(find_kernel, holders, requests, pass_local, capacity),
        in_specs=[smem, smem],
        out_specs=[pl.BlockSpec(memory_space=pltpu.VMEM), smem],
        out_shape=[jax.ShapeDtypeStruct((slots, PLEN), jnp.float32), jax.ShapeDtypeStruct((slots,), jnp.int32)],
        scratch_shapes=[pltpu.SMEM((holders * (capacity + 1),), jnp.int32), pltpu.VMEM((slots, PLEN), jnp.float32)],
        compiler_params=pltpu.CompilerParams(vmem_limit_bytes=VMEM_BYTES),
        cost_estimate=LARGE,
        name="find_rows",
    )(me, table)


def pick_kernel(me_ref, passage_ref, rank_ref, cache_ref, *rest):
    out_ref = rest[-1]
    pair = me_ref[1]
    row = (lax.broadcasted_iota(jnp.int32, (KEPT, PLEN), 0) + 1).astype(jnp.float32)
    for at in range(out_ref.shape[0]):
        passage = passage_ref[at]
        select = (rank_ref[at : at + 1, :] == row).astype(jnp.bfloat16)
        for place, part in ((0, pair), (1, 1 - pair)):
            for half in range(2):
                start = pl.multiple_of(half * HALF + part * PAIR_WIDTH, PAIR_WIDTH)
                end = (place * 2 + half) * PAIR_WIDTH
                out_ref[at, :, end : end + PAIR_WIDTH] = jnp.dot(
                    select, cache_ref[passage, :, pl.ds(start, PAIR_WIDTH)], preferred_element_type=jnp.float32
                ).astype(jnp.bfloat16)


def pick_rows(me, passages, ranks, cache, ahead):
    smem = pl.BlockSpec(memory_space=pltpu.SMEM)
    vmem = pl.BlockSpec(memory_space=pltpu.VMEM)
    return pl.pallas_call(
        pick_kernel,
        in_specs=[smem, smem, vmem, vmem] + [pl.BlockSpec(memory_space=pl.ANY)] * len(ahead),
        out_specs=vmem,
        out_shape=jax.ShapeDtypeStruct((passages.shape[0], KEPT, 2 * HALF), jnp.bfloat16),
        compiler_params=pltpu.CompilerParams(vmem_limit_bytes=VMEM_BYTES),
        cost_estimate=LITTLE,
        name="pick_rows",
    )(me, passages, ranks, cache, *ahead)


def project_kernel(chunks, wanted, carried, last, member_ref, mine_ref, other_ref, *refs):
    weights, total_ref = refs[: len(wanted)], refs[len(wanted)]
    rows = mine_ref.shape[0]
    depth = D // chunks
    total = total_ref[...] if carried else None
    for k, weight_ref in zip(wanted, weights):
        columns = pl.ds(pl.multiple_of((member_ref[0] ^ k) * depth, depth), depth)
        both = jnp.concatenate([mine_ref[:, columns], other_ref[:, columns]], axis=0)
        term = jnp.dot(both, weight_ref[...], preferred_element_type=jnp.float32)
        total = term if total is None else total + term
    if last:
        refs[-2][...] = total[:rows].astype(jnp.bfloat16)
        refs[-1][...] = total[rows:].astype(jnp.bfloat16)
    else:
        refs[-1][...] = total


def project(member, mine, other, weights, wanted, ahead, carry=None, last=True):
    rows, width = mine.shape[0], weights[0].shape[1]
    vmem = pl.BlockSpec(memory_space=pltpu.VMEM)
    carried = [] if carry is None else [carry]
    if last:
        shape = [jax.ShapeDtypeStruct((rows, width), jnp.bfloat16)] * 2
    else:
        shape = [jax.ShapeDtypeStruct((2 * rows, width), jnp.float32)]
    return pl.pallas_call(
        functools.partial(project_kernel, len(weights), wanted, bool(carried), last),
        in_specs=[pl.BlockSpec(memory_space=pltpu.SMEM)]
        + [vmem] * (2 + len(wanted) + len(carried))
        + [pl.BlockSpec(memory_space=pl.ANY)] * len(ahead),
        out_specs=[vmem] * len(shape),
        out_shape=shape,
        compiler_params=pltpu.CompilerParams(vmem_limit_bytes=VMEM_BYTES),
        cost_estimate=MEDIUM,
        name="project",
    )(member.reshape(1), mine, other, *[weights[k] for k in wanted], *carried, *ahead)


def bound_kernel(q_ref, *rest):
    bound_ref = rest[-1]

    @pl.when(pl.program_id(0) == 0)
    def clear():
        bound_ref[...] = jnp.zeros_like(bound_ref)

    peak = jnp.zeros((q_ref.shape[0], 1), jnp.float32)
    for first in range(0, GROUPED, 4):
        most = None
        for head in range(first, first + 4):
            block = q_ref[:, head * HD : (head + 1) * HD].astype(jnp.float32)
            most = block * block if most is None else jnp.maximum(most, block * block)
        peak = jnp.maximum(peak, jnp.sum(most, axis=1, keepdims=True))
    bound_ref[...] = jnp.maximum(bound_ref[...], jnp.max(peak))


def query_bound(q_rows, ahead):
    rows, width = q_rows.shape
    return pl.pallas_call(
        bound_kernel,
        grid=(KVH,),
        in_specs=[pl.BlockSpec((rows, GROUPED * HD), lambda h: (0, h))]
        + [pl.BlockSpec(memory_space=pl.ANY)] * len(ahead),
        out_specs=pl.BlockSpec((8, HD), lambda h: (0, 0)),
        out_shape=jax.ShapeDtypeStruct((8, HD), jnp.float32),
        compiler_params=pltpu.CompilerParams(vmem_limit_bytes=VMEM_BYTES),
        cost_estimate=LITTLE,
        name="query_bound",
    )(q_rows, *ahead)


def attend_kernel(
    heads_once, info_ref, q_ref, own_k_ref, own_v_ref, kept_ref, near_ref, far_ref, bound_ref, *rest
):
    out_ref, key_ref, turned_ref, value_ref = rest[-4:]
    query = pl.program_id(0)
    key_start = pl.multiple_of(pl.program_id(1) * HD, HD)
    value_start = pl.multiple_of(PAIR_WIDTH + pl.program_id(1) * HD, HD)
    passage_keys = TOPP * PLEN
    flip = info_ref[1] > 0
    value_ref[:, HD:] = jnp.ones((passage_keys + QLEN, HD), jnp.bfloat16)
    for j in range(TOPP):
        slot = info_ref[2 + query * TOPP + j]
        key_ref[j * KEPT : (j + 1) * KEPT, :] = kept_ref[slot, :, pl.ds(key_start, HD)]
        value_ref[j * KEPT : (j + 1) * KEPT, :HD] = kept_ref[slot, :, pl.ds(value_start, HD)]
    key_ref[TOPP * KEPT : passage_keys, :] = jnp.where(flip, far_ref[...], near_ref[...])
    value_ref[TOPP * KEPT : passage_keys, :HD] = jnp.where(flip, near_ref[...], far_ref[...])
    key_ref[passage_keys:, :] = own_k_ref[...]
    value_ref[passage_keys:, :HD] = own_v_ref[...]
    scaled = key_ref[...].astype(jnp.float32) * SCORE_FACTOR
    high = scaled.astype(jnp.bfloat16)
    turned_ref[:HD, :] = high.T
    turned_ref[HD:, :] = (scaled - high.astype(jnp.float32)).astype(jnp.bfloat16).T
    key_bound = jnp.max(jnp.sum(scaled * scaled, axis=1, keepdims=True))
    small = jnp.max(bound_ref[...]) * key_bound <= SAFE_EXPONENT**2
    rows = heads_once * QLEN
    token = lax.broadcasted_iota(jnp.int32, (rows, QLEN), 0) % QLEN
    visible = lax.broadcasted_iota(jnp.int32, (rows, QLEN), 1) <= token

    def score(first):
        block = jnp.concatenate(
            [q_ref[:, (first + i) * HD : (first + i + 1) * HD] for i in range(heads_once)], axis=0
        )
        return jnp.dot(
            jnp.concatenate([block, block], axis=1), turned_ref[...], preferred_element_type=jnp.float32
        )

    def store(first, expd):
        summed = jnp.dot(expd, value_ref[...], preferred_element_type=jnp.float32)
        result = (summed[:, :HD] / summed[:, HD:]).astype(jnp.bfloat16)
        for i in range(heads_once):
            out_ref[:, (first + i) * HD : (first + i + 1) * HD] = result[i * QLEN : (i + 1) * QLEN]

    @pl.when(small)
    def unshifted():
        shown = jnp.where(visible, 1.0, 0.0).astype(jnp.bfloat16)
        for first in range(0, GROUPED, heads_once):
            expd = jnp.exp2(score(first)).astype(jnp.bfloat16)
            store(first, jnp.concatenate([expd[:, :passage_keys], expd[:, passage_keys:] * shown], axis=1))

    @pl.when(jnp.logical_not(small))
    def shifted():
        for first in range(0, GROUPED, heads_once):
            scores = score(first)
            scores = jnp.concatenate(
                [scores[:, :passage_keys], jnp.where(visible, scores[:, passage_keys:], -jnp.inf)], axis=1
            )
            peak = jnp.max(scores, axis=1, keepdims=True)
            store(first, jnp.exp2(scores - peak).astype(jnp.bfloat16))


def attend(part, info, q_rows, own_kv, kept, near, far, bound, earlier=None):
    rows, width = q_rows.shape
    queries = rows // QLEN
    slots = kept.shape[0]
    span = TOPP * PLEN + QLEN
    wide = GROUPED * HD
    in_specs = [
        pl.BlockSpec((QLEN, wide), lambda n, h, info: (n, info[0] * PAIR_HEADS + h)),
        pl.BlockSpec((QLEN, HD), lambda n, h, info: (n, info[0] * PAIR_HEADS + h)),
        pl.BlockSpec((QLEN, HD), lambda n, h, info: (n, KVH + info[0] * PAIR_HEADS + h)),
        pl.BlockSpec((slots, KEPT, HALF), lambda n, h, info: (0, 0, part)),
        pl.BlockSpec((TOPP * RECOMP, HD), lambda n, h, info: (n, h)),
        pl.BlockSpec((TOPP * RECOMP, HD), lambda n, h, info: (n, h)),
        pl.BlockSpec((8, HD), lambda n, h, info: (0, 0)),
    ]
    operands = [q_rows, own_kv, own_kv, kept, near, far, bound]
    aliases = {}
    if earlier is not None:
        in_specs.append(pl.BlockSpec(memory_space=pl.ANY))
        operands.append(earlier)
        aliases = {len(operands): 0}
    return pl.pallas_call(
        functools.partial(attend_kernel, 8),
        grid_spec=pltpu.PrefetchScalarGridSpec(
            num_scalar_prefetch=1,
            grid=(queries, PAIR_HEADS),
            in_specs=in_specs,
            out_specs=pl.BlockSpec((QLEN, wide), lambda n, h, info: (n, info[0] * PAIR_HEADS + h)),
            scratch_shapes=[
                pltpu.VMEM((span, HD), jnp.bfloat16),
                pltpu.VMEM((2 * HD, span), jnp.bfloat16),
                pltpu.VMEM((span, 2 * HD), jnp.bfloat16),
            ],
        ),
        out_shape=jax.ShapeDtypeStruct((rows, width), jnp.bfloat16),
        input_output_aliases=aliases,
        compiler_params=pltpu.CompilerParams(vmem_limit_bytes=VMEM_BYTES),
        cost_estimate=LITTLE,
        name="attend",
    )(info, *operands)


def swap(array, axis, bits):
    size = lax.axis_size(axis)
    return lax.ppermute(array, axis, [(i, i ^ bits) for i in range(size)])


def gather_columns(w_kv):
    column = [w_kv, swap(w_kv, "member", 2), swap(w_kv, "member", 4)]
    column.append(swap(column[2], "member", 2))
    across = [swap(part, "group", 2) for part in column]
    blocks, beyond = [], []
    for k in range(4):
        aside = swap(column[k], "member", 1)
        blocks += [column[k], aside]
        beyond += [across[k], swap(aside, "group", 2) if k < 3 else swap(across[k], "member", 1)]
    return blocks, beyond


def recompute_general(normed, w_kv, pair):
    whole = lax.all_gather(lax.all_gather(w_kv, "member", axis=0, tiled=True), "group", axis=1, tiled=True)
    result = jnp.dot(normed, whole, preferred_element_type=jnp.float32).astype(jnp.bfloat16)
    result = result.reshape(-1, 2, PAIRS, PAIR_WIDTH)
    first = jnp.where(pair == 0, result[:, :, 0], result[:, :, 1])
    second = jnp.where(pair == 0, result[:, :, 1], result[:, :, 0])
    return [first[:, 0], first[:, 1]], [second[:, 0], second[:, 1]]


def local(q_rows, own_kv, cache, recomp_hidden, w_kv, retrieval, positions):
    queries = retrieval.shape[0]
    requests = queries * TOPP
    holders = lax.axis_size("member")
    groups = lax.axis_size("group")
    pass_local = cache.shape[0]
    capacity = -(-requests // holders)
    member = lax.axis_index("member")
    group = lax.axis_index("group")
    pair = group % PAIRS
    tuned = groups == 4 and holders == 8
    wanted = retrieval.reshape(requests)
    request = jnp.concatenate([wanted, positions.reshape(requests * RECOMP)])
    request = jnp.pad(request, (0, -request.shape[0] % 128)).reshape(1, -1, 128)
    request = jnp.broadcast_to(request, (holders,) + request.shape[1:])
    table = lax.all_to_all(request, "member", split_axis=0, concat_axis=0, tiled=True).reshape(-1)
    hidden = recomp_hidden.reshape(requests * RECOMP, D)
    normed = normalise(hidden, [])
    ahead = [normed]
    if tuned:
        blocks, beyond = gather_columns(w_kv)
        ahead += [blocks[1], beyond[0], blocks[3], blocks[6], beyond[2]]
    me = jnp.stack([member, pair]).astype(jnp.int32)
    ranks, passages = find_rows(table, me, holders, requests, pass_local, capacity)
    sent = pick_rows(me, passages, ranks, cache, ahead)
    arrived = lax.all_to_all(
        sent.reshape(holders, capacity * KEPT, 2 * HALF), "member", split_axis=0, concat_axis=0, tiled=True
    ).reshape(sent.shape)
    bound = query_bound(q_rows, [sent])
    if tuned:
        flip = group // 2
        other = swap(normed, "group", 1)
        (begun,) = project(member, normed, other, beyond, (0, 2, 1, 4), [sent], last=False)
        near, near_other = project(member, normed, other, blocks, tuple(range(8)), [begun])
        far, far_other = project(member, normed, other, beyond, (6, 3, 5, 7), [near], carry=begun)
        first = [near, far]
        second = [swap(near_other, "group", 1), swap(far_other, "group", 1)]
    else:
        flip = jnp.int32(0)
        first, second = recompute_general(normed, w_kv, pair)
    holder_of = wanted // pass_local
    same = holder_of[:, None] == holder_of[None, :]
    before = jnp.arange(requests)[None, :] < jnp.arange(requests)[:, None]
    slot = holder_of * capacity + jnp.sum((same & before).astype(jnp.int32), axis=1)
    info = jnp.concatenate([jnp.stack([pair, flip]), slot]).astype(jnp.int32)
    other_info = jnp.concatenate([jnp.stack([1 - pair, flip]), slot]).astype(jnp.int32)
    out = attend(0, info, q_rows, own_kv, arrived, *first, bound)
    return attend(1, other_info, q_rows, own_kv, arrived, *second, bound, earlier=out)


def solution(mesh):
    rows = P(("group", "member"), None)
    placed = (
        rows,
        rows,
        P(("group", "member"), None, None),
        P(("group", "member"), None, None, None),
        P("member", "group"),
        rows,
        P(("group", "member"), None, None),
    )
    return jax.shard_map(local, mesh=mesh, in_specs=placed, out_specs=rows, check_vma=False)
```

```python
import functools

import jax
import jax.numpy as jnp
from jax import lax
from jax.experimental import pallas as pl
from jax.experimental.pallas import tpu as pltpu
from jax.sharding import PartitionSpec as P

D = 4096
HQ = 64
KVH = 4
HD = 128
TOPP = 8
QLEN = 128
PLEN = 64
RECOMP = 16
KEPT = PLEN - RECOMP
GROUPED = HQ // KVH
PAIRS = 2
PAIR_HEADS = KVH // PAIRS
PAIR_WIDTH = PAIR_HEADS * HD
HALF = KVH * HD

EPSILON = 1e-06
SCORE_FACTOR = 1.4426950408889634 / HD**0.5
SAFE_EXPONENT = 80.0
VMEM_BYTES = 56 * 1024 * 1024
LITTLE = pl.CostEstimate(flops=1, bytes_accessed=1, transcendentals=0)
MEDIUM = pl.CostEstimate(flops=1, bytes_accessed=18_000_000, transcendentals=0)
LARGE = pl.CostEstimate(flops=1, bytes_accessed=36_000_000, transcendentals=0)


def norm_kernel(hidden_ref, *rest):
    normed_ref = rest[-1]
    hidden = hidden_ref[...].astype(jnp.float32)
    mean = jnp.mean(hidden * hidden, axis=1, keepdims=True)
    normed_ref[...] = (hidden * lax.rsqrt(mean + EPSILON)).astype(jnp.bfloat16)


def normalise(hidden, ahead):
    rows = hidden.shape[0]
    tile = min(rows, 64)
    return pl.pallas_call(
        norm_kernel,
        grid=(rows // tile,),
        in_specs=[pl.BlockSpec((tile, D), lambda i: (i, 0))] + [pl.BlockSpec(memory_space=pl.ANY)] * len(ahead),
        out_specs=pl.BlockSpec((tile, D), lambda i: (i, 0)),
        out_shape=jax.ShapeDtypeStruct(hidden.shape, jnp.bfloat16),
        compiler_params=pltpu.CompilerParams(vmem_limit_bytes=VMEM_BYTES),
        cost_estimate=LITTLE,
        name="normalise",
    )(hidden, *ahead)


def find_kernel(holders, requests, pass_local, capacity, passing, me_ref, table_ref, *rest):
    rank_ref, passage_ref = rest[passing : passing + 2]
    slot_ref, kept_ref = rest[-2:]
    me = me_ref[0]
    stride = table_ref.shape[0] // holders
    for k in range(holders):
        base = k * (capacity + 1)
        for rank in range(capacity + 1):
            slot_ref[base + rank] = 0
        count = jnp.int32(0)
        for request in range(requests):
            slot_ref[base + count] = request
            mine = (table_ref[k * stride + request] // pass_local == me).astype(jnp.int32)
            count = jnp.minimum(count + mine, capacity)
    spot = lax.broadcasted_iota(jnp.int32, (1, PLEN), 1)
    for k in range(holders):
        for rank in range(capacity):
            at = k * capacity + rank
            request = slot_ref[k * (capacity + 1) + rank]
            passage_ref[at] = lax.rem(table_ref[k * stride + request], pass_local)
            start = k * stride + requests + request * RECOMP
            covered = spot < 0
            for r in range(RECOMP):
                covered = covered | (spot == table_ref[start + r])
            kept_ref[at : at + 1, :] = jnp.where(covered, 0.0, 1.0)
    kept = kept_ref[...]
    upto = lax.broadcasted_iota(jnp.int32, (PLEN, PLEN), 0) <= lax.broadcasted_iota(jnp.int32, (PLEN, PLEN), 1)
    rank_of = jnp.dot(
        kept.astype(jnp.bfloat16), upto.astype(jnp.bfloat16), preferred_element_type=jnp.float32
    )
    rank_ref[...] = jnp.where(kept > 0, rank_of, 0.0)


def find_rows(table, me, holders, requests, pass_local, capacity, passing):
    slots = holders * capacity
    smem = pl.BlockSpec(memory_space=pltpu.SMEM)
    whole = pl.BlockSpec(memory_space=pl.ANY)
    return pl.pallas_call(
        functools.partial(find_kernel, holders, requests, pass_local, capacity, len(passing)),
        in_specs=[smem, smem] + [whole] * len(passing),
        out_specs=[pl.BlockSpec(memory_space=pltpu.VMEM), smem] + [whole] * len(passing),
        out_shape=[jax.ShapeDtypeStruct((slots, PLEN), jnp.float32), jax.ShapeDtypeStruct((slots,), jnp.int32)]
        + [jax.ShapeDtypeStruct(part.shape, part.dtype) for part in passing],
        input_output_aliases={2 + i: 2 + i for i in range(len(passing))},
        scratch_shapes=[pltpu.SMEM((holders * (capacity + 1),), jnp.int32), pltpu.VMEM((slots, PLEN), jnp.float32)],
        compiler_params=pltpu.CompilerParams(vmem_limit_bytes=VMEM_BYTES),
        cost_estimate=LARGE,
        name="find_rows",
    )(me, table, *passing)


def pick_kernel(me_ref, passage_ref, rank_ref, cache_ref, *rest):
    out_ref = rest[-1]
    pair = me_ref[1]
    row = (lax.broadcasted_iota(jnp.int32, (KEPT, PLEN), 0) + 1).astype(jnp.float32)
    for at in range(out_ref.shape[0]):
        passage = passage_ref[at]
        select = (rank_ref[at : at + 1, :] == row).astype(jnp.bfloat16)
        for place, part in ((0, pair), (1, 1 - pair)):
            for half in range(2):
                start = pl.multiple_of(half * HALF + part * PAIR_WIDTH, PAIR_WIDTH)
                end = (place * 2 + half) * PAIR_WIDTH
                out_ref[at, :, end : end + PAIR_WIDTH] = jnp.dot(
                    select, cache_ref[passage, :, pl.ds(start, PAIR_WIDTH)], preferred_element_type=jnp.float32
                ).astype(jnp.bfloat16)


def pick_rows(me, passages, ranks, cache, ahead):
    smem = pl.BlockSpec(memory_space=pltpu.SMEM)
    vmem = pl.BlockSpec(memory_space=pltpu.VMEM)
    return pl.pallas_call(
        pick_kernel,
        in_specs=[smem, smem, vmem, vmem] + [pl.BlockSpec(memory_space=pl.ANY)] * len(ahead),
        out_specs=vmem,
        out_shape=jax.ShapeDtypeStruct((passages.shape[0], KEPT, 2 * HALF), jnp.bfloat16),
        compiler_params=pltpu.CompilerParams(vmem_limit_bytes=VMEM_BYTES),
        cost_estimate=LITTLE,
        name="pick_rows",
    )(me, passages, ranks, cache, *ahead)


def project_kernel(chunks, wanted, carried, last, member_ref, mine_ref, other_ref, *refs):
    weights, total_ref = refs[: len(wanted)], refs[len(wanted)]
    rows = mine_ref.shape[0]
    depth = D // chunks
    total = total_ref[...] if carried else None
    for k, weight_ref in zip(wanted, weights):
        columns = pl.ds(pl.multiple_of((member_ref[0] ^ k) * depth, depth), depth)
        both = jnp.concatenate([mine_ref[:, columns], other_ref[:, columns]], axis=0)
        term = jnp.dot(both, weight_ref[...], preferred_element_type=jnp.float32)
        total = term if total is None else total + term
    if last:
        refs[-2][...] = total[:rows].astype(jnp.bfloat16)
        refs[-1][...] = total[rows:].astype(jnp.bfloat16)
    else:
        refs[-1][...] = total


def project(member, mine, other, weights, wanted, ahead, carry=None, last=True):
    rows, width = mine.shape[0], weights[0].shape[1]
    vmem = pl.BlockSpec(memory_space=pltpu.VMEM)
    carried = [] if carry is None else [carry]
    if last:
        shape = [jax.ShapeDtypeStruct((rows, width), jnp.bfloat16)] * 2
    else:
        shape = [jax.ShapeDtypeStruct((2 * rows, width), jnp.float32)]
    return pl.pallas_call(
        functools.partial(project_kernel, len(weights), wanted, bool(carried), last),
        in_specs=[pl.BlockSpec(memory_space=pltpu.SMEM)]
        + [vmem] * (2 + len(wanted) + len(carried))
        + [pl.BlockSpec(memory_space=pl.ANY)] * len(ahead),
        out_specs=[vmem] * len(shape),
        out_shape=shape,
        compiler_params=pltpu.CompilerParams(vmem_limit_bytes=VMEM_BYTES),
        cost_estimate=MEDIUM,
        name="project",
    )(member.reshape(1), mine, other, *[weights[k] for k in wanted], *carried, *ahead)


def scaled_keys(keys, turned_ref):
    scaled = keys.astype(jnp.float32) * SCORE_FACTOR
    high = scaled.astype(jnp.bfloat16)
    turned_ref[:HD, :] = high.T
    turned_ref[HD:, :] = (scaled - high.astype(jnp.float32)).astype(jnp.bfloat16).T
    return jnp.max(jnp.sum(scaled * scaled, axis=1, keepdims=True))


def head_rows(q_ref, first, heads_once):
    block = jnp.concatenate(
        [q_ref[:, (first + i) * HD : (first + i + 1) * HD] for i in range(heads_once)], axis=0
    )
    return jnp.concatenate([block, block], axis=1)


def causal(rows):
    token = lax.broadcasted_iota(jnp.int32, (rows, QLEN), 0) % QLEN
    return lax.broadcasted_iota(jnp.int32, (rows, QLEN), 1) <= token


def own_kernel(heads_once, info_ref, q_ref, key_ref, value_ref, *rest):
    sum_ref, weight_ref, bound_ref, turned_ref, wide_ref = rest[-5:]

    @pl.when((pl.program_id(0) == 0) & (pl.program_id(1) == 0))
    def clear():
        bound_ref[...] = jnp.zeros_like(bound_ref)

    scaled_keys(key_ref[...], turned_ref)
    wide_ref[:, :HD] = value_ref[...]
    wide_ref[:, HD:] = jnp.ones((QLEN, HD), jnp.bfloat16)
    shown = jnp.where(causal(heads_once * QLEN), 1.0, 0.0).astype(jnp.bfloat16)
    lane = lax.broadcasted_iota(jnp.int32, (QLEN, HD), 1)
    weights = jnp.zeros((QLEN, HD), jnp.float32)
    peak = jnp.zeros((QLEN, 1), jnp.float32)
    for first in range(0, GROUPED, heads_once):
        scores = jnp.dot(head_rows(q_ref, first, heads_once), turned_ref[...], preferred_element_type=jnp.float32)
        summed = jnp.dot(
            jnp.exp2(scores).astype(jnp.bfloat16) * shown, wide_ref[...], preferred_element_type=jnp.float32
        )
        for i in range(heads_once):
            rows = slice(i * QLEN, (i + 1) * QLEN)
            sum_ref[:, (first + i) * HD : (first + i + 1) * HD] = summed[rows, :HD].astype(jnp.bfloat16)
            weights = jnp.where(lane == first + i, summed[rows, HD:], weights)
        for pair in range(first, first + heads_once, 4):
            most = None
            for head in range(pair, pair + 4):
                block = q_ref[:, head * HD : (head + 1) * HD].astype(jnp.float32)
                most = block * block if most is None else jnp.maximum(most, block * block)
            peak = jnp.maximum(peak, jnp.sum(most, axis=1, keepdims=True))
    weight_ref[...] = weights
    bound_ref[...] = jnp.maximum(bound_ref[...], jnp.max(peak))


def attend_own(info, q_rows, own_kv, ahead):
    rows = q_rows.shape[0]
    wide = GROUPED * HD
    return pl.pallas_call(
        functools.partial(own_kernel, 8),
        grid_spec=pltpu.PrefetchScalarGridSpec(
            num_scalar_prefetch=1,
            grid=(rows // QLEN, PAIR_HEADS),
            in_specs=[
                pl.BlockSpec((QLEN, wide), lambda n, h, info: (n, info[0] * PAIR_HEADS + h)),
                pl.BlockSpec((QLEN, HD), lambda n, h, info: (n, info[0] * PAIR_HEADS + h)),
                pl.BlockSpec((QLEN, HD), lambda n, h, info: (n, KVH + info[0] * PAIR_HEADS + h)),
            ]
            + [pl.BlockSpec(memory_space=pl.ANY)] * len(ahead),
            out_specs=[
                pl.BlockSpec((QLEN, wide), lambda n, h, info: (n, h)),
                pl.BlockSpec((QLEN, HD), lambda n, h, info: (n, h)),
                pl.BlockSpec((8, HD), lambda n, h, info: (0, 0)),
            ],
            scratch_shapes=[pltpu.VMEM((2 * HD, QLEN), jnp.bfloat16), pltpu.VMEM((QLEN, 2 * HD), jnp.bfloat16)],
        ),
        out_shape=[
            jax.ShapeDtypeStruct((rows, PAIR_HEADS * wide), jnp.bfloat16),
            jax.ShapeDtypeStruct((rows, PAIR_HEADS * HD), jnp.float32),
            jax.ShapeDtypeStruct((8, HD), jnp.float32),
        ],
        compiler_params=pltpu.CompilerParams(vmem_limit_bytes=VMEM_BYTES),
        cost_estimate=LITTLE,
        name="attend_own",
    )(info, q_rows, own_kv, own_kv, *ahead)


def attend_kernel(
    heads_once,
    info_ref,
    q_ref,
    own_k_ref,
    own_v_ref,
    kept_ref,
    near_ref,
    far_ref,
    sum_ref,
    weight_ref,
    bound_ref,
    *rest,
):
    out_ref, key_ref, turned_ref, value_ref = rest[-4:]
    query = pl.program_id(0)
    key_start = pl.multiple_of(pl.program_id(1) * HD, HD)
    value_start = pl.multiple_of(PAIR_WIDTH + pl.program_id(1) * HD, HD)
    passage_keys = TOPP * PLEN
    flip = info_ref[1] > 0
    value_ref[:, HD:] = jnp.ones((passage_keys + QLEN, HD), jnp.bfloat16)
    for j in range(TOPP):
        slot = info_ref[2 + query * TOPP + j]
        key_ref[j * KEPT : (j + 1) * KEPT, :] = kept_ref[slot, :, pl.ds(key_start, HD)]
        value_ref[j * KEPT : (j + 1) * KEPT, :HD] = kept_ref[slot, :, pl.ds(value_start, HD)]
    key_ref[TOPP * KEPT : passage_keys, :] = jnp.where(flip, far_ref[...], near_ref[...])
    value_ref[TOPP * KEPT : passage_keys, :HD] = jnp.where(flip, near_ref[...], far_ref[...])
    key_ref[passage_keys:, :] = own_k_ref[...]
    value_ref[passage_keys:, :HD] = own_v_ref[...]
    key_bound = scaled_keys(key_ref[...], turned_ref)
    small = jnp.max(bound_ref[...]) * key_bound <= SAFE_EXPONENT**2
    rows = heads_once * QLEN

    @pl.when(small)
    def unshifted():
        for first in range(0, GROUPED, heads_once):
            scores = jnp.dot(
                head_rows(q_ref, first, heads_once),
                turned_ref[:, :passage_keys],
                preferred_element_type=jnp.float32,
            )
            summed = jnp.dot(
                jnp.exp2(scores).astype(jnp.bfloat16),
                value_ref[:passage_keys, :],
                preferred_element_type=jnp.float32,
            )
            for i in range(heads_once):
                part = summed[i * QLEN : (i + 1) * QLEN]
                columns = slice((first + i) * HD, (first + i + 1) * HD)
                total = part[:, :HD] + sum_ref[:, columns].astype(jnp.float32)
                weight = part[:, HD:] + weight_ref[:, first + i : first + i + 1]
                out_ref[:, columns] = (total / weight).astype(jnp.bfloat16)

    @pl.when(jnp.logical_not(small))
    def shifted():
        visible = causal(rows)
        for first in range(0, GROUPED, heads_once):
            scores = jnp.dot(
                head_rows(q_ref, first, heads_once), turned_ref[...], preferred_element_type=jnp.float32
            )
            scores = jnp.concatenate(
                [scores[:, :passage_keys], jnp.where(visible, scores[:, passage_keys:], -jnp.inf)], axis=1
            )
            peak = jnp.max(scores, axis=1, keepdims=True)
            expd = jnp.exp2(scores - peak).astype(jnp.bfloat16)
            summed = jnp.dot(expd, value_ref[...], preferred_element_type=jnp.float32)
            result = (summed[:, :HD] / summed[:, HD:]).astype(jnp.bfloat16)
            for i in range(heads_once):
                out_ref[:, (first + i) * HD : (first + i + 1) * HD] = result[i * QLEN : (i + 1) * QLEN]


def attend(part, info, q_rows, own_kv, kept, near, far, own, earlier=None):
    rows, width = q_rows.shape
    queries = rows // QLEN
    slots = kept.shape[0]
    span = TOPP * PLEN + QLEN
    wide = GROUPED * HD
    in_specs = [
        pl.BlockSpec((QLEN, wide), lambda n, h, info: (n, info[0] * PAIR_HEADS + h)),
        pl.BlockSpec((QLEN, HD), lambda n, h, info: (n, info[0] * PAIR_HEADS + h)),
        pl.BlockSpec((QLEN, HD), lambda n, h, info: (n, KVH + info[0] * PAIR_HEADS + h)),
        pl.BlockSpec((slots, KEPT, HALF), lambda n, h, info: (0, 0, part)),
        pl.BlockSpec((TOPP * RECOMP, HD), lambda n, h, info: (n, h)),
        pl.BlockSpec((TOPP * RECOMP, HD), lambda n, h, info: (n, h)),
        pl.BlockSpec((QLEN, wide), lambda n, h, info: (n, h)),
        pl.BlockSpec((QLEN, HD), lambda n, h, info: (n, h)),
        pl.BlockSpec((8, HD), lambda n, h, info: (0, 0)),
    ]
    operands = [q_rows, own_kv, own_kv, kept, near, far, *own]
    aliases = {}
    if earlier is not None:
        in_specs.append(pl.BlockSpec(memory_space=pl.ANY))
        operands.append(earlier)
        aliases = {len(operands): 0}
    return pl.pallas_call(
        functools.partial(attend_kernel, 8),
        grid_spec=pltpu.PrefetchScalarGridSpec(
            num_scalar_prefetch=1,
            grid=(queries, PAIR_HEADS),
            in_specs=in_specs,
            out_specs=pl.BlockSpec((QLEN, wide), lambda n, h, info: (n, info[0] * PAIR_HEADS + h)),
            scratch_shapes=[
                pltpu.VMEM((span, HD), jnp.bfloat16),
                pltpu.VMEM((2 * HD, span), jnp.bfloat16),
                pltpu.VMEM((span, 2 * HD), jnp.bfloat16),
            ],
        ),
        out_shape=jax.ShapeDtypeStruct((rows, width), jnp.bfloat16),
        input_output_aliases=aliases,
        compiler_params=pltpu.CompilerParams(vmem_limit_bytes=VMEM_BYTES),
        cost_estimate=LITTLE,
        name="attend",
    )(info, *operands)


def swap(array, axis, bits):
    size = lax.axis_size(axis)
    return lax.ppermute(array, axis, [(i, i ^ bits) for i in range(size)])


def first_hops(w_kv):
    return [swap(w_kv, "member", 2), swap(w_kv, "member", 4), swap(w_kv, "member", 1)]


def gather_columns(w_kv, beyond, hops):
    one, two, aside = hops
    three = swap(two, "member", 2)
    blocks, beyond = [w_kv, aside], [beyond, swap(aside, "group", 2)]
    for part in (one, two):
        near = swap(part, "member", 1)
        blocks += [part, near]
        beyond += [swap(part, "group", 2), swap(near, "group", 2)]
    blocks += [three, swap(three, "member", 1)]
    across = swap(three, "group", 2)
    return blocks, beyond + [across, swap(across, "member", 1)]


def recompute_general(normed, w_kv, pair):
    whole = lax.all_gather(lax.all_gather(w_kv, "member", axis=0, tiled=True), "group", axis=1, tiled=True)
    result = jnp.dot(normed, whole, preferred_element_type=jnp.float32).astype(jnp.bfloat16)
    result = result.reshape(-1, 2, PAIRS, PAIR_WIDTH)
    first = jnp.where(pair == 0, result[:, :, 0], result[:, :, 1])
    second = jnp.where(pair == 0, result[:, :, 1], result[:, :, 0])
    return [first[:, 0], first[:, 1]], [second[:, 0], second[:, 1]]


def local(q_rows, own_kv, cache, recomp_hidden, w_kv, retrieval, positions):
    queries = retrieval.shape[0]
    requests = queries * TOPP
    holders = lax.axis_size("member")
    groups = lax.axis_size("group")
    pass_local = cache.shape[0]
    capacity = -(-requests // holders)
    member = lax.axis_index("member")
    group = lax.axis_index("group")
    pair = group % PAIRS
    tuned = groups == 4 and holders == 8
    wanted = retrieval.reshape(requests)
    request = jnp.concatenate([wanted, positions.reshape(requests * RECOMP)])
    request = jnp.pad(request, (0, -request.shape[0] % 128)).reshape(1, -1, 128)
    request = jnp.broadcast_to(request, (holders,) + request.shape[1:])
    table = lax.all_to_all(request, "member", split_axis=0, concat_axis=0, tiled=True).reshape(-1)
    hidden = recomp_hidden.reshape(requests * RECOMP, D)
    normed = normalise(hidden, [])
    me = jnp.stack([member, pair]).astype(jnp.int32)
    ahead = [normed]
    hops = first_hops(w_kv) if tuned else []
    ranks, passages, *hops = find_rows(table, me, holders, requests, pass_local, capacity, hops)
    if tuned:
        blocks, beyond = gather_columns(w_kv, swap(w_kv, "group", 2), hops)
        ahead += [beyond[0], blocks[3], blocks[6], beyond[2]]
    sent = pick_rows(me, passages, ranks, cache, ahead)
    arrived = lax.all_to_all(
        sent.reshape(holders, capacity * KEPT, 2 * HALF), "member", split_axis=0, concat_axis=0, tiled=True
    ).reshape(sent.shape)
    holder_of = wanted // pass_local
    same = holder_of[:, None] == holder_of[None, :]
    before = jnp.arange(requests)[None, :] < jnp.arange(requests)[:, None]
    slot = holder_of * capacity + jnp.sum((same & before).astype(jnp.int32), axis=1)
    flip = group // 2 if tuned else jnp.int32(0)
    info = jnp.concatenate([jnp.stack([pair, flip]), slot]).astype(jnp.int32)
    other_info = jnp.concatenate([jnp.stack([1 - pair, flip]), slot]).astype(jnp.int32)
    first_own = attend_own(info, q_rows, own_kv, [sent])
    if tuned:
        other = swap(normed, "group", 1)
        (begun,) = project(member, normed, other, beyond, (0, 2, 1, 4), [first_own[0]], last=False)
        second_own = attend_own(other_info, q_rows, own_kv, [begun])
        near, near_other = project(member, normed, other, blocks, tuple(range(8)), [second_own[0]])
        far, far_other = project(member, normed, other, beyond, (6, 3, 5, 7), [near], carry=begun)
        first = [near, far]
        second = [swap(near_other, "group", 1), swap(far_other, "group", 1)]
    else:
        second_own = attend_own(other_info, q_rows, own_kv, [first_own[0]])
        first, second = recompute_general(normed, w_kv, pair)
    out = attend(0, info, q_rows, own_kv, arrived, *first, first_own)
    return attend(1, other_info, q_rows, own_kv, arrived, *second, second_own, earlier=out)


def solution(mesh):
    rows = P(("group", "member"), None)
    placed = (
        rows,
        rows,
        P(("group", "member"), None, None),
        P(("group", "member"), None, None, None),
        P("member", "group"),
        rows,
        P(("group", "member"), None, None),
    )
    return jax.shard_map(local, mesh=mesh, in_specs=placed, out_specs=rows, check_vma=False)
```

```python
import functools

import jax
import jax.numpy as jnp
from jax import lax
from jax.experimental import pallas as pl
from jax.experimental.pallas import tpu as pltpu
from jax.sharding import PartitionSpec as P

D = 4096
HQ = 64
KVH = 4
HD = 128
TOPP = 8
QLEN = 128
PLEN = 64
RECOMP = 16
KEPT = PLEN - RECOMP
GROUPED = HQ // KVH
PAIRS = 2
PAIR_HEADS = KVH // PAIRS
PAIR_WIDTH = PAIR_HEADS * HD
HALF = KVH * HD

EPSILON = 1e-06
SCORE_FACTOR = 1.4426950408889634 / HD**0.5
SAFE_EXPONENT = 64.0
HALVINGS = 6
POWERS = (1.00000378, 0.693132975, 0.240147805, 0.0555562830, 0.00984230973, 0.00130689140)
SMALL_VMEM = 12 * 1024 * 1024
VMEM_BYTES = 28 * 1024 * 1024
LITTLE = pl.CostEstimate(flops=1, bytes_accessed=1, transcendentals=0)
LARGE = pl.CostEstimate(flops=1, bytes_accessed=36_000_000, transcendentals=0)


def norm_kernel(hidden_ref, *rest):
    normed_ref = rest[-1]
    hidden = hidden_ref[...].astype(jnp.float32)
    mean = jnp.mean(hidden * hidden, axis=1, keepdims=True)
    normed_ref[...] = (hidden * lax.rsqrt(mean + EPSILON)).astype(jnp.bfloat16)


def normalise(hidden, ahead):
    rows = hidden.shape[0]
    tile = min(rows, 64)
    return pl.pallas_call(
        norm_kernel,
        grid=(rows // tile,),
        in_specs=[pl.BlockSpec((tile, D), lambda i: (i, 0))] + [pl.BlockSpec(memory_space=pl.ANY)] * len(ahead),
        out_specs=pl.BlockSpec((tile, D), lambda i: (i, 0)),
        out_shape=jax.ShapeDtypeStruct(hidden.shape, jnp.bfloat16),
        compiler_params=pltpu.CompilerParams(vmem_limit_bytes=SMALL_VMEM),
        cost_estimate=LITTLE,
        name="normalise",
    )(hidden, *ahead)


def find_kernel(holders, requests, pass_local, capacity, passing, me_ref, table_ref, *rest):
    rank_ref, passage_ref = rest[passing + 1 : passing + 3]
    slot_ref, kept_ref = rest[-2:]
    me = me_ref[0]
    stride = table_ref.shape[0] // holders
    for k in range(holders):
        base = k * (capacity + 1)
        for rank in range(capacity + 1):
            slot_ref[base + rank] = 0
        count = jnp.int32(0)
        for request in range(requests):
            slot_ref[base + count] = request
            mine = (table_ref[k * stride + request] // pass_local == me).astype(jnp.int32)
            count = jnp.minimum(count + mine, capacity)
    spot = lax.broadcasted_iota(jnp.int32, (1, PLEN), 1)
    for k in range(holders):
        for rank in range(capacity):
            at = k * capacity + rank
            request = slot_ref[k * (capacity + 1) + rank]
            passage_ref[at] = lax.rem(table_ref[k * stride + request], pass_local)
            start = k * stride + requests + request * RECOMP
            covered = spot < 0
            for r in range(RECOMP):
                covered = covered | (spot == table_ref[start + r])
            kept_ref[at : at + 1, :] = jnp.where(covered, 0.0, 1.0)
    kept = kept_ref[...]
    upto = lax.broadcasted_iota(jnp.int32, (PLEN, PLEN), 0) <= lax.broadcasted_iota(jnp.int32, (PLEN, PLEN), 1)
    rank_of = jnp.dot(
        kept.astype(jnp.bfloat16), upto.astype(jnp.bfloat16), preferred_element_type=jnp.float32
    )
    rank_ref[...] = jnp.where(kept > 0, rank_of, 0.0)


def find_rows(table, me, holders, requests, pass_local, capacity, passing, normed):
    slots = holders * capacity
    smem = pl.BlockSpec(memory_space=pltpu.SMEM)
    whole = pl.BlockSpec(memory_space=pl.ANY)
    return pl.pallas_call(
        functools.partial(find_kernel, holders, requests, pass_local, capacity, len(passing)),
        in_specs=[smem, smem] + [whole] * (len(passing) + 1),
        out_specs=[pl.BlockSpec(memory_space=pltpu.VMEM), smem] + [whole] * len(passing),
        out_shape=[jax.ShapeDtypeStruct((slots, PLEN), jnp.float32), jax.ShapeDtypeStruct((slots,), jnp.int32)]
        + [jax.ShapeDtypeStruct(part.shape, part.dtype) for part in passing],
        input_output_aliases={2 + i: 2 + i for i in range(len(passing))},
        scratch_shapes=[pltpu.SMEM((holders * (capacity + 1),), jnp.int32), pltpu.VMEM((slots, PLEN), jnp.float32)],
        compiler_params=pltpu.CompilerParams(vmem_limit_bytes=SMALL_VMEM),
        cost_estimate=LARGE,
        name="find_rows",
    )(me, table, *passing, normed)


def pick_kernel(me_ref, passage_ref, rank_ref, cache_ref, *rest):
    out_ref = rest[-1]
    pair = me_ref[1]
    row = (lax.broadcasted_iota(jnp.int32, (KEPT, PLEN), 0) + 1).astype(jnp.float32)
    for at in range(out_ref.shape[0]):
        passage = passage_ref[at]
        select = (rank_ref[at : at + 1, :] == row).astype(jnp.bfloat16)
        for place, part in ((0, pair), (1, 1 - pair)):
            for half in range(2):
                start = pl.multiple_of(half * HALF + part * PAIR_WIDTH, PAIR_WIDTH)
                end = (place * 2 + half) * PAIR_WIDTH
                out_ref[at, :, end : end + PAIR_WIDTH] = jnp.dot(
                    select, cache_ref[passage, :, pl.ds(start, PAIR_WIDTH)], preferred_element_type=jnp.float32
                ).astype(jnp.bfloat16)


def pick_rows(me, passages, ranks, cache, ahead):
    smem = pl.BlockSpec(memory_space=pltpu.SMEM)
    vmem = pl.BlockSpec(memory_space=pltpu.VMEM)
    return pl.pallas_call(
        pick_kernel,
        in_specs=[smem, smem, vmem, vmem] + [pl.BlockSpec(memory_space=pl.ANY)] * len(ahead),
        out_specs=vmem,
        out_shape=jax.ShapeDtypeStruct((passages.shape[0], KEPT, 2 * HALF), jnp.bfloat16),
        compiler_params=pltpu.CompilerParams(vmem_limit_bytes=SMALL_VMEM),
        cost_estimate=LITTLE,
        name="pick_rows",
    )(me, passages, ranks, cache, *ahead)


def project_kernel(chunks, member_ref, mine_ref, other_ref, *refs):
    weights, mine_out, other_out = refs[:chunks], refs[-2], refs[-1]
    rows = mine_ref.shape[0]
    depth = D // chunks
    total = None
    for k in range(chunks):
        columns = pl.ds(pl.multiple_of((member_ref[0] ^ k) * depth, depth), depth)
        both = jnp.concatenate([mine_ref[:, columns], other_ref[:, columns]], axis=0)
        term = jnp.dot(both, weights[k][...], preferred_element_type=jnp.float32)
        total = term if total is None else total + term
    mine_out[...] = total[:rows].astype(jnp.bfloat16)
    other_out[...] = total[rows:].astype(jnp.bfloat16)


def project(member, mine, other, weights, ahead):
    rows, width = mine.shape[0], weights[0].shape[1]
    shape = jax.ShapeDtypeStruct((rows, width), jnp.bfloat16)
    vmem = pl.BlockSpec(memory_space=pltpu.VMEM)
    return pl.pallas_call(
        functools.partial(project_kernel, len(weights)),
        in_specs=[pl.BlockSpec(memory_space=pltpu.SMEM)]
        + [vmem] * (2 + len(weights))
        + [pl.BlockSpec(memory_space=pl.ANY)] * len(ahead),
        out_specs=[vmem, vmem],
        out_shape=[shape, shape],
        compiler_params=pltpu.CompilerParams(vmem_limit_bytes=SMALL_VMEM),
        cost_estimate=LITTLE,
        name="project",
    )(member.reshape(1), mine, other, *weights, *ahead)


def power(exponent):
    result = jnp.full_like(exponent, POWERS[-1] / 2.0 ** (HALVINGS * (len(POWERS) - 1)))
    for degree in range(len(POWERS) - 2, -1, -1):
        result = result * exponent + POWERS[degree] / 2.0 ** (HALVINGS * degree)
    for _ in range(HALVINGS):
        result = result * result
    return result


def scaled_keys(keys, turned_ref):
    scaled = keys.astype(jnp.float32) * SCORE_FACTOR
    high = scaled.astype(jnp.bfloat16)
    turned_ref[:HD, :] = high.T
    turned_ref[HD:, :] = (scaled - high.astype(jnp.float32)).astype(jnp.bfloat16).T
    return jnp.max(jnp.sum(scaled * scaled, axis=1, keepdims=True))


def head_rows(q_ref, first, heads_once):
    block = jnp.concatenate(
        [q_ref[:, (first + i) * HD : (first + i + 1) * HD] for i in range(heads_once)], axis=0
    )
    return jnp.concatenate([block, block], axis=1)


def causal(rows):
    token = lax.broadcasted_iota(jnp.int32, (rows, QLEN), 0) % QLEN
    return lax.broadcasted_iota(jnp.int32, (rows, QLEN), 1) <= token


def own_kernel(heads_once, info_ref, q_ref, key_ref, value_ref, *rest):
    sum_ref, weight_ref, bound_ref, turned_ref, wide_ref = rest[-5:]

    @pl.when((pl.program_id(0) == 0) & (pl.program_id(1) == 0))
    def clear():
        bound_ref[...] = jnp.zeros_like(bound_ref)

    scaled_keys(key_ref[...], turned_ref)
    wide_ref[:, :HD] = value_ref[...]
    wide_ref[:, HD:] = jnp.ones((QLEN, HD), jnp.bfloat16)
    shown = jnp.where(causal(heads_once * QLEN), 1.0, 0.0).astype(jnp.bfloat16)
    lane = lax.broadcasted_iota(jnp.int32, (QLEN, HD), 1)
    weights = jnp.zeros((QLEN, HD), jnp.float32)
    peak = jnp.zeros((QLEN, 1), jnp.float32)
    for first in range(0, GROUPED, heads_once):
        scores = jnp.dot(head_rows(q_ref, first, heads_once), turned_ref[...], preferred_element_type=jnp.float32)
        middle = heads_once * QLEN // 2
        expd = jnp.concatenate([jnp.exp2(scores[:middle]), power(scores[middle:])], axis=0)
        summed = jnp.dot(
            expd.astype(jnp.bfloat16) * shown, wide_ref[...], preferred_element_type=jnp.float32
        )
        for i in range(heads_once):
            rows = slice(i * QLEN, (i + 1) * QLEN)
            sum_ref[:, (first + i) * HD : (first + i + 1) * HD] = summed[rows, :HD].astype(jnp.bfloat16)
            weights = jnp.where(lane == first + i, summed[rows, HD:], weights)
        for pair in range(first, first + heads_once, 4):
            most = None
            for head in range(pair, pair + 4):
                block = q_ref[:, head * HD : (head + 1) * HD].astype(jnp.float32)
                most = block * block if most is None else jnp.maximum(most, block * block)
            peak = jnp.maximum(peak, jnp.sum(most, axis=1, keepdims=True))
    weight_ref[...] = weights
    bound_ref[...] = jnp.maximum(bound_ref[...], jnp.max(peak))


def attend_own(info, q_rows, own_kv, ahead):
    rows = q_rows.shape[0]
    wide = GROUPED * HD
    return pl.pallas_call(
        functools.partial(own_kernel, 8),
        grid_spec=pltpu.PrefetchScalarGridSpec(
            num_scalar_prefetch=1,
            grid=(rows // QLEN, PAIR_HEADS),
            in_specs=[
                pl.BlockSpec((QLEN, wide), lambda n, h, info: (n, info[0] * PAIR_HEADS + h)),
                pl.BlockSpec((QLEN, HD), lambda n, h, info: (n, info[0] * PAIR_HEADS + h)),
                pl.BlockSpec((QLEN, HD), lambda n, h, info: (n, KVH + info[0] * PAIR_HEADS + h)),
            ]
            + [pl.BlockSpec(memory_space=pl.ANY)] * len(ahead),
            out_specs=[
                pl.BlockSpec((QLEN, wide), lambda n, h, info: (n, h)),
                pl.BlockSpec((QLEN, HD), lambda n, h, info: (n, h)),
                pl.BlockSpec((8, HD), lambda n, h, info: (0, 0)),
            ],
            scratch_shapes=[pltpu.VMEM((2 * HD, QLEN), jnp.bfloat16), pltpu.VMEM((QLEN, 2 * HD), jnp.bfloat16)],
        ),
        out_shape=[
            jax.ShapeDtypeStruct((rows, PAIR_HEADS * wide), jnp.bfloat16),
            jax.ShapeDtypeStruct((rows, PAIR_HEADS * HD), jnp.float32),
            jax.ShapeDtypeStruct((8, HD), jnp.float32),
        ],
        compiler_params=pltpu.CompilerParams(vmem_limit_bytes=VMEM_BYTES),
        cost_estimate=LITTLE,
        name="attend_own",
    )(info, q_rows, own_kv, own_kv, *ahead)


def attend_kernel(
    heads_once,
    info_ref,
    q_ref,
    own_k_ref,
    own_v_ref,
    kept_ref,
    near_ref,
    far_ref,
    sum_ref,
    weight_ref,
    bound_ref,
    *rest,
):
    out_ref, key_ref, turned_ref, value_ref = rest[-4:]
    query = pl.program_id(0)
    key_start = pl.multiple_of(pl.program_id(1) * HD, HD)
    value_start = pl.multiple_of(PAIR_WIDTH + pl.program_id(1) * HD, HD)
    passage_keys = TOPP * PLEN
    flip = info_ref[1] > 0
    value_ref[:, HD:] = jnp.ones((passage_keys + QLEN, HD), jnp.bfloat16)
    for j in range(TOPP):
        slot = info_ref[2 + query * TOPP + j]
        key_ref[j * KEPT : (j + 1) * KEPT, :] = kept_ref[slot, :, pl.ds(key_start, HD)]
        value_ref[j * KEPT : (j + 1) * KEPT, :HD] = kept_ref[slot, :, pl.ds(value_start, HD)]
    key_ref[TOPP * KEPT : passage_keys, :] = jnp.where(flip, far_ref[...], near_ref[...])
    value_ref[TOPP * KEPT : passage_keys, :HD] = jnp.where(flip, near_ref[...], far_ref[...])
    key_ref[passage_keys:, :] = own_k_ref[...]
    value_ref[passage_keys:, :HD] = own_v_ref[...]
    key_bound = scaled_keys(key_ref[...], turned_ref)
    small = jnp.max(bound_ref[...]) * key_bound <= SAFE_EXPONENT**2
    rows = heads_once * QLEN

    @pl.when(small)
    def unshifted():
        middle = passage_keys // 2
        lane = lax.broadcasted_iota(jnp.int32, (QLEN, HD), 1)
        for first in range(0, GROUPED, heads_once):
            scores = jnp.dot(
                head_rows(q_ref, first, heads_once),
                turned_ref[:, :passage_keys],
                preferred_element_type=jnp.float32,
            )
            expd = jnp.concatenate([jnp.exp2(scores[:, :middle]), power(scores[:, middle:])], axis=1)
            summed = jnp.dot(
                expd.astype(jnp.bfloat16), value_ref[:passage_keys, :], preferred_element_type=jnp.float32
            )
            weights = jnp.ones((QLEN, HD), jnp.float32)
            for i in range(heads_once):
                part = summed[i * QLEN : (i + 1) * QLEN, HD:]
                weights = jnp.where(lane == first + i, part + weight_ref[...], weights)
            inverse = 1.0 / weights
            for i in range(heads_once):
                columns = slice((first + i) * HD, (first + i + 1) * HD)
                total = summed[i * QLEN : (i + 1) * QLEN, :HD] + sum_ref[:, columns].astype(jnp.float32)
                out_ref[:, columns] = (total * inverse[:, first + i : first + i + 1]).astype(jnp.bfloat16)

    @pl.when(jnp.logical_not(small))
    def shifted():
        visible = causal(rows)
        for first in range(0, GROUPED, heads_once):
            scores = jnp.dot(
                head_rows(q_ref, first, heads_once), turned_ref[...], preferred_element_type=jnp.float32
            )
            scores = jnp.concatenate(
                [scores[:, :passage_keys], jnp.where(visible, scores[:, passage_keys:], -jnp.inf)], axis=1
            )
            peak = jnp.max(scores, axis=1, keepdims=True)
            expd = jnp.exp2(scores - peak).astype(jnp.bfloat16)
            summed = jnp.dot(expd, value_ref[...], preferred_element_type=jnp.float32)
            result = (summed[:, :HD] / summed[:, HD:]).astype(jnp.bfloat16)
            for i in range(heads_once):
                out_ref[:, (first + i) * HD : (first + i + 1) * HD] = result[i * QLEN : (i + 1) * QLEN]


def attend(part, info, q_rows, own_kv, kept, near, far, own, earlier=None):
    rows, width = q_rows.shape
    queries = rows // QLEN
    slots = kept.shape[0]
    span = TOPP * PLEN + QLEN
    wide = GROUPED * HD
    in_specs = [
        pl.BlockSpec((QLEN, wide), lambda n, h, info: (n, info[0] * PAIR_HEADS + h)),
        pl.BlockSpec((QLEN, HD), lambda n, h, info: (n, info[0] * PAIR_HEADS + h)),
        pl.BlockSpec((QLEN, HD), lambda n, h, info: (n, KVH + info[0] * PAIR_HEADS + h)),
        pl.BlockSpec((slots, KEPT, HALF), lambda n, h, info: (0, 0, part)),
        pl.BlockSpec((TOPP * RECOMP, HD), lambda n, h, info: (n, h)),
        pl.BlockSpec((TOPP * RECOMP, HD), lambda n, h, info: (n, h)),
        pl.BlockSpec((QLEN, wide), lambda n, h, info: (n, h)),
        pl.BlockSpec((QLEN, HD), lambda n, h, info: (n, h)),
        pl.BlockSpec((8, HD), lambda n, h, info: (0, 0)),
    ]
    operands = [q_rows, own_kv, own_kv, kept, near, far, *own]
    aliases = {}
    if earlier is not None:
        in_specs.append(pl.BlockSpec(memory_space=pl.ANY))
        operands.append(earlier)
        aliases = {len(operands): 0}
    return pl.pallas_call(
        functools.partial(attend_kernel, 8),
        grid_spec=pltpu.PrefetchScalarGridSpec(
            num_scalar_prefetch=1,
            grid=(queries, PAIR_HEADS),
            in_specs=in_specs,
            out_specs=pl.BlockSpec((QLEN, wide), lambda n, h, info: (n, info[0] * PAIR_HEADS + h)),
            scratch_shapes=[
                pltpu.VMEM((span, HD), jnp.bfloat16),
                pltpu.VMEM((2 * HD, span), jnp.bfloat16),
                pltpu.VMEM((span, 2 * HD), jnp.bfloat16),
            ],
        ),
        out_shape=jax.ShapeDtypeStruct((rows, width), jnp.bfloat16),
        input_output_aliases=aliases,
        compiler_params=pltpu.CompilerParams(vmem_limit_bytes=VMEM_BYTES),
        cost_estimate=LITTLE,
        name="attend",
    )(info, *operands)


def swap(array, axis, bits):
    size = lax.axis_size(axis)
    return lax.ppermute(array, axis, [(i, i ^ bits) for i in range(size)])


def first_hops(w_kv):
    return [swap(w_kv, "member", 2), swap(w_kv, "member", 4), swap(w_kv, "member", 1)]


def gather_columns(w_kv, beyond, hops):
    one, two, aside = hops
    three = swap(two, "member", 2)
    blocks, beyond = [w_kv, aside], [beyond, swap(aside, "group", 2)]
    for part in (one, two):
        near = swap(part, "member", 1)
        blocks += [part, near]
        beyond += [swap(part, "group", 2), swap(near, "group", 2)]
    blocks += [three, swap(three, "member", 1)]
    across = swap(three, "group", 2)
    return blocks, beyond + [across, swap(across, "member", 1)]


def recompute_general(normed, w_kv, pair):
    whole = lax.all_gather(lax.all_gather(w_kv, "member", axis=0, tiled=True), "group", axis=1, tiled=True)
    result = jnp.dot(normed, whole, preferred_element_type=jnp.float32).astype(jnp.bfloat16)
    result = result.reshape(-1, 2, PAIRS, PAIR_WIDTH)
    first = jnp.where(pair == 0, result[:, :, 0], result[:, :, 1])
    second = jnp.where(pair == 0, result[:, :, 1], result[:, :, 0])
    return [first[:, 0], first[:, 1]], [second[:, 0], second[:, 1]]


def local(q_rows, own_kv, cache, recomp_hidden, w_kv, retrieval, positions):
    queries = retrieval.shape[0]
    requests = queries * TOPP
    holders = lax.axis_size("member")
    groups = lax.axis_size("group")
    pass_local = cache.shape[0]
    capacity = -(-requests // holders)
    member = lax.axis_index("member")
    group = lax.axis_index("group")
    pair = group % PAIRS
    tuned = groups == 4 and holders == 8
    wanted = retrieval.reshape(requests)
    request = jnp.concatenate([wanted, positions.reshape(requests * RECOMP)])
    request = jnp.pad(request, (0, -request.shape[0] % 128)).reshape(1, -1, 128)
    request = jnp.broadcast_to(request, (holders,) + request.shape[1:])
    table = lax.all_to_all(request, "member", split_axis=0, concat_axis=0, tiled=True).reshape(-1)
    hidden = recomp_hidden.reshape(requests * RECOMP, D)
    normed = normalise(hidden, [])
    me = jnp.stack([member, pair]).astype(jnp.int32)
    ahead = []
    hops = first_hops(w_kv) if tuned else []
    ranks, passages, *hops = find_rows(table, me, holders, requests, pass_local, capacity, hops, normed)
    if tuned:
        blocks, beyond = gather_columns(w_kv, swap(w_kv, "group", 2), hops)
        ahead += [beyond[0], blocks[3], blocks[6], beyond[2]]
    sent = pick_rows(me, passages, ranks, cache, ahead)
    arrived = lax.all_to_all(
        sent.reshape(holders, capacity * KEPT, 2 * HALF), "member", split_axis=0, concat_axis=0, tiled=True
    ).reshape(sent.shape)
    holder_of = wanted // pass_local
    same = holder_of[:, None] == holder_of[None, :]
    before = jnp.arange(requests)[None, :] < jnp.arange(requests)[:, None]
    slot = holder_of * capacity + jnp.sum((same & before).astype(jnp.int32), axis=1)
    flip = group // 2 if tuned else jnp.int32(0)
    info = jnp.concatenate([jnp.stack([pair, flip]), slot]).astype(jnp.int32)
    other_info = jnp.concatenate([jnp.stack([1 - pair, flip]), slot]).astype(jnp.int32)
    first_own = attend_own(info, q_rows, own_kv, [sent])
    if tuned:
        other = swap(normed, "group", 1)
        near, near_other = project(member, normed, other, blocks, [first_own[0]])
        second_own = attend_own(other_info, q_rows, own_kv, [near])
        far, far_other = project(member, normed, other, beyond, [second_own[0]])
        first = [near, far]
        second = [swap(near_other, "group", 1), swap(far_other, "group", 1)]
    else:
        second_own = attend_own(other_info, q_rows, own_kv, [first_own[0]])
        first, second = recompute_general(normed, w_kv, pair)
    out = attend(0, info, q_rows, own_kv, arrived, *first, first_own)
    return attend(1, other_info, q_rows, own_kv, arrived, *second, second_own, earlier=out)


def solution(mesh):
    rows = P(("group", "member"), None)
    placed = (
        rows,
        rows,
        P(("group", "member"), None, None),
        P(("group", "member"), None, None, None),
        P("member", "group"),
        rows,
        P(("group", "member"), None, None),
    )
    return jax.shard_map(local, mesh=mesh, in_specs=placed, out_specs=rows, check_vma=False)
```

```python
import functools

import jax
import jax.numpy as jnp
from jax import lax
from jax.experimental import pallas as pl
from jax.experimental.pallas import tpu as pltpu
from jax.sharding import PartitionSpec as P

D = 4096
HQ = 64
KVH = 4
HD = 128
TOPP = 8
QLEN = 128
PLEN = 64
RECOMP = 16
KEPT = PLEN - RECOMP
GROUPED = HQ // KVH
PAIRS = 2
PAIR_HEADS = KVH // PAIRS
PAIR_WIDTH = PAIR_HEADS * HD
HALF = KVH * HD

EPSILON = 1e-06
SCORE_FACTOR = 1.0 / HD**0.5
SAFE_EXPONENT = 60.0
SMALL_VMEM = 12 * 1024 * 1024
VMEM_BYTES = 56 * 1024 * 1024
LITTLE = pl.CostEstimate(flops=1, bytes_accessed=1, transcendentals=0)
LARGE = pl.CostEstimate(flops=1, bytes_accessed=36_000_000, transcendentals=0)


def norm_kernel(hidden_ref, *rest):
    normed_ref = rest[-1]
    hidden = hidden_ref[...].astype(jnp.float32)
    mean = jnp.mean(hidden * hidden, axis=1, keepdims=True)
    normed_ref[...] = (hidden * lax.rsqrt(mean + EPSILON)).astype(jnp.bfloat16)


def normalise(hidden, ahead):
    rows = hidden.shape[0]
    tile = min(rows, 64)
    return pl.pallas_call(
        norm_kernel,
        grid=(rows // tile,),
        in_specs=[pl.BlockSpec((tile, D), lambda i: (i, 0))] + [pl.BlockSpec(memory_space=pl.ANY)] * len(ahead),
        out_specs=pl.BlockSpec((tile, D), lambda i: (i, 0)),
        out_shape=jax.ShapeDtypeStruct(hidden.shape, jnp.bfloat16),
        compiler_params=pltpu.CompilerParams(vmem_limit_bytes=SMALL_VMEM),
        cost_estimate=LITTLE,
        name="normalise",
    )(hidden, *ahead)


def find_kernel(holders, requests, pass_local, capacity, passing, me_ref, table_ref, *rest):
    rank_ref, passage_ref = rest[passing + 1 : passing + 3]
    slot_ref, kept_ref = rest[-2:]
    me = me_ref[0]
    stride = table_ref.shape[0] // holders
    for k in range(holders):
        base = k * (capacity + 1)
        for rank in range(capacity + 1):
            slot_ref[base + rank] = 0
        count = jnp.int32(0)
        for request in range(requests):
            slot_ref[base + count] = request
            mine = (table_ref[k * stride + request] // pass_local == me).astype(jnp.int32)
            count = jnp.minimum(count + mine, capacity)
    spot = lax.broadcasted_iota(jnp.int32, (1, PLEN), 1)
    for k in range(holders):
        for rank in range(capacity):
            at = k * capacity + rank
            request = slot_ref[k * (capacity + 1) + rank]
            passage_ref[at] = lax.rem(table_ref[k * stride + request], pass_local)
            start = k * stride + requests + request * RECOMP
            covered = spot < 0
            for r in range(RECOMP):
                covered = covered | (spot == table_ref[start + r])
            kept_ref[at : at + 1, :] = jnp.where(covered, 0.0, 1.0)
    kept = kept_ref[...]
    upto = lax.broadcasted_iota(jnp.int32, (PLEN, PLEN), 0) <= lax.broadcasted_iota(jnp.int32, (PLEN, PLEN), 1)
    rank_of = jnp.dot(
        kept.astype(jnp.bfloat16), upto.astype(jnp.bfloat16), preferred_element_type=jnp.float32
    )
    rank_ref[...] = jnp.where(kept > 0, rank_of, 0.0)


def find_rows(table, me, holders, requests, pass_local, capacity, passing, normed):
    slots = holders * capacity
    smem = pl.BlockSpec(memory_space=pltpu.SMEM)
    whole = pl.BlockSpec(memory_space=pl.ANY)
    return pl.pallas_call(
        functools.partial(find_kernel, holders, requests, pass_local, capacity, len(passing)),
        in_specs=[smem, smem] + [whole] * (len(passing) + 1),
        out_specs=[pl.BlockSpec(memory_space=pltpu.VMEM), smem] + [whole] * len(passing),
        out_shape=[jax.ShapeDtypeStruct((slots, PLEN), jnp.float32), jax.ShapeDtypeStruct((slots,), jnp.int32)]
        + [jax.ShapeDtypeStruct(part.shape, part.dtype) for part in passing],
        input_output_aliases={2 + i: 2 + i for i in range(len(passing))},
        scratch_shapes=[pltpu.SMEM((holders * (capacity + 1),), jnp.int32), pltpu.VMEM((slots, PLEN), jnp.float32)],
        compiler_params=pltpu.CompilerParams(vmem_limit_bytes=SMALL_VMEM),
        cost_estimate=LARGE,
        name="find_rows",
    )(me, table, *passing, normed)


def pick_kernel(me_ref, passage_ref, rank_ref, cache_ref, *rest):
    out_ref = rest[-1]
    pair = me_ref[1]
    row = (lax.broadcasted_iota(jnp.int32, (KEPT, PLEN), 0) + 1).astype(jnp.float32)
    for at in range(out_ref.shape[0]):
        passage = passage_ref[at]
        select = (rank_ref[at : at + 1, :] == row).astype(jnp.bfloat16)
        for place, part in ((0, pair), (1, 1 - pair)):
            for half in range(2):
                start = pl.multiple_of(half * HALF + part * PAIR_WIDTH, PAIR_WIDTH)
                end = (place * 2 + half) * PAIR_WIDTH
                out_ref[at, :, end : end + PAIR_WIDTH] = jnp.dot(
                    select, cache_ref[passage, :, pl.ds(start, PAIR_WIDTH)], preferred_element_type=jnp.float32
                ).astype(jnp.bfloat16)


def pick_rows(me, passages, ranks, cache, ahead):
    smem = pl.BlockSpec(memory_space=pltpu.SMEM)
    vmem = pl.BlockSpec(memory_space=pltpu.VMEM)
    return pl.pallas_call(
        pick_kernel,
        in_specs=[smem, smem, vmem, vmem] + [pl.BlockSpec(memory_space=pl.ANY)] * len(ahead),
        out_specs=vmem,
        out_shape=jax.ShapeDtypeStruct((passages.shape[0], KEPT, 2 * HALF), jnp.bfloat16),
        compiler_params=pltpu.CompilerParams(vmem_limit_bytes=SMALL_VMEM),
        cost_estimate=LITTLE,
        name="pick_rows",
    )(me, passages, ranks, cache, *ahead)


def project_kernel(chunks, member_ref, mine_ref, other_ref, *refs):
    weights, mine_out, other_out = refs[:chunks], refs[-2], refs[-1]
    rows = mine_ref.shape[0]
    depth = D // chunks
    total = None
    for k in range(chunks):
        columns = pl.ds(pl.multiple_of((member_ref[0] ^ k) * depth, depth), depth)
        both = jnp.concatenate([mine_ref[:, columns], other_ref[:, columns]], axis=0)
        term = jnp.dot(both, weights[k][...], preferred_element_type=jnp.float32)
        total = term if total is None else total + term
    mine_out[...] = total[:rows].astype(jnp.bfloat16)
    other_out[...] = total[rows:].astype(jnp.bfloat16)


def project(member, mine, other, weights, ahead):
    rows, width = mine.shape[0], weights[0].shape[1]
    shape = jax.ShapeDtypeStruct((rows, width), jnp.bfloat16)
    vmem = pl.BlockSpec(memory_space=pltpu.VMEM)
    return pl.pallas_call(
        functools.partial(project_kernel, len(weights)),
        in_specs=[pl.BlockSpec(memory_space=pltpu.SMEM)]
        + [vmem] * (2 + len(weights))
        + [pl.BlockSpec(memory_space=pl.ANY)] * len(ahead),
        out_specs=[vmem, vmem],
        out_shape=[shape, shape],
        compiler_params=pltpu.CompilerParams(vmem_limit_bytes=SMALL_VMEM),
        cost_estimate=LITTLE,
        name="project",
    )(member.reshape(1), mine, other, *weights, *ahead)


def scaled_keys(keys, turned_ref):
    scaled = keys.astype(jnp.float32) * SCORE_FACTOR
    high = scaled.astype(jnp.bfloat16)
    turned_ref[:HD, :] = high.T
    turned_ref[HD:, :] = (scaled - high.astype(jnp.float32)).astype(jnp.bfloat16).T
    return jnp.max(jnp.sum(scaled * scaled, axis=1, keepdims=True))


def head_rows(q_ref, first, heads_once):
    block = jnp.concatenate(
        [q_ref[:, (first + i) * HD : (first + i + 1) * HD] for i in range(heads_once)], axis=0
    )
    return jnp.concatenate([block, block], axis=1)


def causal(rows):
    token = lax.broadcasted_iota(jnp.int32, (rows, QLEN), 0) % QLEN
    return lax.broadcasted_iota(jnp.int32, (rows, QLEN), 1) <= token


def own_kernel(heads_once, passing, info_ref, q_ref, key_ref, value_ref, *rest):
    sum_ref, weight_ref, bound_ref = rest[passing + 1 : passing + 4]
    turned_ref, wide_ref = rest[-2:]

    @pl.when((pl.program_id(0) == 0) & (pl.program_id(1) == 0))
    def clear():
        bound_ref[...] = jnp.zeros_like(bound_ref)

    scaled_keys(key_ref[...], turned_ref)
    wide_ref[:, :HD] = value_ref[...]
    wide_ref[:, HD:] = jnp.ones((QLEN, HD), jnp.bfloat16)
    shown = jnp.where(causal(heads_once * QLEN), 1.0, 0.0).astype(jnp.bfloat16)
    lane = lax.broadcasted_iota(jnp.int32, (QLEN, HD), 1)
    weights = jnp.zeros((QLEN, HD), jnp.float32)
    peak = jnp.zeros((QLEN, 1), jnp.float32)
    for first in range(0, GROUPED, heads_once):
        scores = jnp.dot(head_rows(q_ref, first, heads_once), turned_ref[...], preferred_element_type=jnp.float32)
        summed = jnp.dot(
            jnp.exp(scores).astype(jnp.bfloat16) * shown, wide_ref[...], preferred_element_type=jnp.float32
        )
        for i in range(heads_once):
            rows = slice(i * QLEN, (i + 1) * QLEN)
            sum_ref[:, (first + i) * HD : (first + i + 1) * HD] = summed[rows, :HD].astype(jnp.bfloat16)
            weights = jnp.where(lane == first + i, summed[rows, HD:], weights)
        for pair in range(first, first + heads_once, 4):
            most = None
            for head in range(pair, pair + 4):
                block = q_ref[:, head * HD : (head + 1) * HD].astype(jnp.float32)
                most = block * block if most is None else jnp.maximum(most, block * block)
            peak = jnp.maximum(peak, jnp.sum(most, axis=1, keepdims=True))
    weight_ref[...] = weights
    bound_ref[...] = jnp.maximum(bound_ref[...], jnp.max(peak))


def attend_own(info, q_rows, own_kv, ahead, passing):
    rows = q_rows.shape[0]
    whole = pl.BlockSpec(memory_space=pl.ANY)
    wide = GROUPED * HD
    return pl.pallas_call(
        functools.partial(own_kernel, 8, len(passing)),
        grid_spec=pltpu.PrefetchScalarGridSpec(
            num_scalar_prefetch=1,
            grid=(rows // QLEN, PAIR_HEADS),
            in_specs=[
                pl.BlockSpec((QLEN, wide), lambda n, h, info: (n, info[0] * PAIR_HEADS + h)),
                pl.BlockSpec((QLEN, HD), lambda n, h, info: (n, info[0] * PAIR_HEADS + h)),
                pl.BlockSpec((QLEN, HD), lambda n, h, info: (n, KVH + info[0] * PAIR_HEADS + h)),
            ]
            + [whole] * (1 + len(passing)),
            out_specs=[
                pl.BlockSpec((QLEN, wide), lambda n, h, info: (n, h)),
                pl.BlockSpec((QLEN, HD), lambda n, h, info: (n, h)),
                pl.BlockSpec((8, HD), lambda n, h, info: (0, 0)),
            ]
            + [whole] * len(passing),
            scratch_shapes=[pltpu.VMEM((2 * HD, QLEN), jnp.bfloat16), pltpu.VMEM((QLEN, 2 * HD), jnp.bfloat16)],
        ),
        out_shape=[
            jax.ShapeDtypeStruct((rows, PAIR_HEADS * wide), jnp.bfloat16),
            jax.ShapeDtypeStruct((rows, PAIR_HEADS * HD), jnp.float32),
            jax.ShapeDtypeStruct((8, HD), jnp.float32),
        ]
        + [jax.ShapeDtypeStruct(part.shape, part.dtype) for part in passing],
        input_output_aliases={5 + i: 3 + i for i in range(len(passing))},
        compiler_params=pltpu.CompilerParams(vmem_limit_bytes=VMEM_BYTES),
        cost_estimate=LITTLE,
        name="attend_own",
    )(info, q_rows, own_kv, own_kv, ahead, *passing)


def attend_kernel(
    heads_once,
    info_ref,
    q_ref,
    own_k_ref,
    own_v_ref,
    kept_ref,
    near_ref,
    far_ref,
    sum_ref,
    weight_ref,
    bound_ref,
    *rest,
):
    out_ref, key_ref, turned_ref, value_ref = rest[-4:]
    query = pl.program_id(0)
    key_start = pl.multiple_of(pl.program_id(1) * HD, HD)
    value_start = pl.multiple_of(PAIR_WIDTH + pl.program_id(1) * HD, HD)
    passage_keys = TOPP * PLEN
    flip = info_ref[1] > 0
    value_ref[:, HD:] = jnp.ones((passage_keys + QLEN, HD), jnp.bfloat16)
    for j in range(TOPP):
        slot = info_ref[2 + query * TOPP + j]
        key_ref[j * KEPT : (j + 1) * KEPT, :] = kept_ref[slot, :, pl.ds(key_start, HD)]
        value_ref[j * KEPT : (j + 1) * KEPT, :HD] = kept_ref[slot, :, pl.ds(value_start, HD)]
    key_ref[TOPP * KEPT : passage_keys, :] = jnp.where(flip, far_ref[...], near_ref[...])
    value_ref[TOPP * KEPT : passage_keys, :HD] = jnp.where(flip, near_ref[...], far_ref[...])
    key_ref[passage_keys:, :] = own_k_ref[...]
    value_ref[passage_keys:, :HD] = own_v_ref[...]
    key_bound = scaled_keys(key_ref[...], turned_ref)
    small = jnp.max(bound_ref[...]) * key_bound <= SAFE_EXPONENT**2
    rows = heads_once * QLEN

    @pl.when(small)
    def unshifted():
        lane = lax.broadcasted_iota(jnp.int32, (QLEN, HD), 1)
        for first in range(0, GROUPED, heads_once):
            scores = jnp.dot(
                head_rows(q_ref, first, heads_once),
                turned_ref[:, :passage_keys],
                preferred_element_type=jnp.float32,
            )
            summed = jnp.dot(
                jnp.exp(scores).astype(jnp.bfloat16), value_ref[:passage_keys, :], preferred_element_type=jnp.float32
            )
            weights = jnp.ones((QLEN, HD), jnp.float32)
            for i in range(heads_once):
                part = summed[i * QLEN : (i + 1) * QLEN, HD:]
                weights = jnp.where(lane == first + i, part + weight_ref[...], weights)
            inverse = 1.0 / weights
            for i in range(heads_once):
                columns = slice((first + i) * HD, (first + i + 1) * HD)
                total = summed[i * QLEN : (i + 1) * QLEN, :HD] + sum_ref[:, columns].astype(jnp.float32)
                out_ref[:, columns] = (total * inverse[:, first + i : first + i + 1]).astype(jnp.bfloat16)

    @pl.when(jnp.logical_not(small))
    def shifted():
        visible = causal(rows)
        for first in range(0, GROUPED, heads_once):
            scores = jnp.dot(
                head_rows(q_ref, first, heads_once), turned_ref[...], preferred_element_type=jnp.float32
            )
            scores = jnp.concatenate(
                [scores[:, :passage_keys], jnp.where(visible, scores[:, passage_keys:], -jnp.inf)], axis=1
            )
            peak = jnp.max(scores, axis=1, keepdims=True)
            expd = jnp.exp(scores - peak).astype(jnp.bfloat16)
            summed = jnp.dot(expd, value_ref[...], preferred_element_type=jnp.float32)
            result = (summed[:, :HD] / summed[:, HD:]).astype(jnp.bfloat16)
            for i in range(heads_once):
                out_ref[:, (first + i) * HD : (first + i + 1) * HD] = result[i * QLEN : (i + 1) * QLEN]


def attend(part, info, q_rows, own_kv, kept, near, far, own, earlier=None):
    rows, width = q_rows.shape
    queries = rows // QLEN
    slots = kept.shape[0]
    span = TOPP * PLEN + QLEN
    wide = GROUPED * HD
    in_specs = [
        pl.BlockSpec((QLEN, wide), lambda n, h, info: (n, info[0] * PAIR_HEADS + h)),
        pl.BlockSpec((QLEN, HD), lambda n, h, info: (n, info[0] * PAIR_HEADS + h)),
        pl.BlockSpec((QLEN, HD), lambda n, h, info: (n, KVH + info[0] * PAIR_HEADS + h)),
        pl.BlockSpec((slots, KEPT, HALF), lambda n, h, info: (0, 0, part)),
        pl.BlockSpec((TOPP * RECOMP, HD), lambda n, h, info: (n, h)),
        pl.BlockSpec((TOPP * RECOMP, HD), lambda n, h, info: (n, h)),
        pl.BlockSpec((QLEN, wide), lambda n, h, info: (n, h)),
        pl.BlockSpec((QLEN, HD), lambda n, h, info: (n, h)),
        pl.BlockSpec((8, HD), lambda n, h, info: (0, 0)),
    ]
    operands = [q_rows, own_kv, own_kv, kept, near, far, *own]
    aliases = {}
    if earlier is not None:
        in_specs.append(pl.BlockSpec(memory_space=pl.ANY))
        operands.append(earlier)
        aliases = {len(operands): 0}
    return pl.pallas_call(
        functools.partial(attend_kernel, 8),
        grid_spec=pltpu.PrefetchScalarGridSpec(
            num_scalar_prefetch=1,
            grid=(queries, PAIR_HEADS),
            in_specs=in_specs,
            out_specs=pl.BlockSpec((QLEN, wide), lambda n, h, info: (n, info[0] * PAIR_HEADS + h)),
            scratch_shapes=[
                pltpu.VMEM((span, HD), jnp.bfloat16),
                pltpu.VMEM((2 * HD, span), jnp.bfloat16),
                pltpu.VMEM((span, 2 * HD), jnp.bfloat16),
            ],
        ),
        out_shape=jax.ShapeDtypeStruct((rows, width), jnp.bfloat16),
        input_output_aliases=aliases,
        compiler_params=pltpu.CompilerParams(vmem_limit_bytes=VMEM_BYTES),
        cost_estimate=LITTLE,
        name="attend",
    )(info, *operands)


def swap(array, axis, bits):
    size = lax.axis_size(axis)
    return lax.ppermute(array, axis, [(i, i ^ bits) for i in range(size)])


def first_hops(w_kv):
    return [swap(w_kv, "member", 2), swap(w_kv, "member", 4), swap(w_kv, "member", 1)]


def gather_columns(w_kv, beyond, hops):
    one, two, aside = hops
    blocks, beyond = [w_kv, aside], [beyond, swap(aside, "group", 2)]
    for part in (one, two):
        near = swap(part, "member", 1)
        blocks += [part, near]
        beyond += [swap(part, "group", 2), swap(near, "group", 2)]
    return blocks, beyond


def last_columns(three):
    across = swap(three, "group", 2)
    return [three, swap(three, "member", 1)], [across, swap(across, "member", 1)]


def recompute_general(normed, w_kv, pair):
    whole = lax.all_gather(lax.all_gather(w_kv, "member", axis=0, tiled=True), "group", axis=1, tiled=True)
    result = jnp.dot(normed, whole, preferred_element_type=jnp.float32).astype(jnp.bfloat16)
    result = result.reshape(-1, 2, PAIRS, PAIR_WIDTH)
    first = jnp.where(pair == 0, result[:, :, 0], result[:, :, 1])
    second = jnp.where(pair == 0, result[:, :, 1], result[:, :, 0])
    return [first[:, 0], first[:, 1]], [second[:, 0], second[:, 1]]


def local(q_rows, own_kv, cache, recomp_hidden, w_kv, retrieval, positions):
    queries = retrieval.shape[0]
    requests = queries * TOPP
    holders = lax.axis_size("member")
    groups = lax.axis_size("group")
    pass_local = cache.shape[0]
    capacity = -(-requests // holders)
    member = lax.axis_index("member")
    group = lax.axis_index("group")
    pair = group % PAIRS
    tuned = groups == 4 and holders == 8
    wanted = retrieval.reshape(requests)
    request = jnp.concatenate([wanted, positions.reshape(requests * RECOMP)])
    request = jnp.pad(request, (0, -request.shape[0] % 128)).reshape(1, -1, 128)
    request = jnp.broadcast_to(request, (holders,) + request.shape[1:])
    table = lax.all_to_all(request, "member", split_axis=0, concat_axis=0, tiled=True).reshape(-1)
    hidden = recomp_hidden.reshape(requests * RECOMP, D)
    normed = normalise(hidden, [])
    me = jnp.stack([member, pair]).astype(jnp.int32)
    ahead = []
    hops = first_hops(w_kv) if tuned else []
    ranks, passages, *hops = find_rows(table, me, holders, requests, pass_local, capacity, hops, normed)
    holder_of = wanted // pass_local
    same = holder_of[:, None] == holder_of[None, :]
    before = jnp.arange(requests)[None, :] < jnp.arange(requests)[:, None]
    slot = holder_of * capacity + jnp.sum((same & before).astype(jnp.int32), axis=1)
    flip = group // 2 if tuned else jnp.int32(0)
    info = jnp.concatenate([jnp.stack([pair, flip]), slot]).astype(jnp.int32)
    other_info = jnp.concatenate([jnp.stack([1 - pair, flip]), slot]).astype(jnp.int32)
    first_own = attend_own(info, q_rows, own_kv, ranks, [])
    ahead += [first_own[0]]
    three = []
    if tuned:
        three = [swap(hops[1], "member", 2)]
        blocks, beyond = gather_columns(w_kv, swap(w_kv, "group", 2), hops)
        ahead += [beyond[0], blocks[3], beyond[2], three[0]]
    sent = pick_rows(me, passages, ranks, cache, ahead)
    arrived = lax.all_to_all(
        sent.reshape(holders, capacity * KEPT, 2 * HALF), "member", split_axis=0, concat_axis=0, tiled=True
    ).reshape(sent.shape)
    second_own = attend_own(other_info, q_rows, own_kv, sent, three)
    if tuned:
        other = swap(normed, "group", 1)
        last_near, last_far = last_columns(second_own[3])
        near, near_other = project(member, normed, other, blocks + last_near, [second_own[0]])
        far, far_other = project(member, normed, other, beyond + last_far, [near])
        first = [near, far]
        second = [swap(near_other, "group", 1), swap(far_other, "group", 1)]
    else:
        first, second = recompute_general(normed, w_kv, pair)
    out = attend(0, info, q_rows, own_kv, arrived, *first, first_own)
    return attend(1, other_info, q_rows, own_kv, arrived, *second, second_own[:3], earlier=out)


def solution(mesh):
    rows = P(("group", "member"), None)
    placed = (
        rows,
        rows,
        P(("group", "member"), None, None),
        P(("group", "member"), None, None, None),
        P("member", "group"),
        rows,
        P(("group", "member"), None, None),
    )
    return jax.shard_map(local, mesh=mesh, in_specs=placed, out_specs=rows, check_vma=False)
```

```python
import functools

import jax
import jax.numpy as jnp
from jax import lax
from jax.experimental import pallas as pl
from jax.experimental.pallas import tpu as pltpu
from jax.sharding import PartitionSpec as P

D = 4096
HQ = 64
KVH = 4
HD = 128
TOPP = 8
QLEN = 128
PLEN = 64
RECOMP = 16
KEPT = PLEN - RECOMP
GROUPED = HQ // KVH
PAIRS = 2
PAIR_HEADS = KVH // PAIRS
PAIR_WIDTH = PAIR_HEADS * HD
HALF = KVH * HD

EPSILON = 1e-06
SCORE_FACTOR = 1.4426950408889634 / HD**0.5
SAFE_EXPONENT = 80.0
SMALL_VMEM = 12 * 1024 * 1024
VMEM_BYTES = 56 * 1024 * 1024
LITTLE = pl.CostEstimate(flops=1, bytes_accessed=1, transcendentals=0)
LARGE = pl.CostEstimate(flops=1, bytes_accessed=36_000_000, transcendentals=0)


def norm_kernel(hidden_ref, *rest):
    normed_ref = rest[-1]
    hidden = hidden_ref[...].astype(jnp.float32)
    mean = jnp.mean(hidden * hidden, axis=1, keepdims=True)
    normed_ref[...] = (hidden * lax.rsqrt(mean + EPSILON)).astype(jnp.bfloat16)


def normalise(hidden, ahead):
    rows = hidden.shape[0]
    tile = min(rows, 64)
    return pl.pallas_call(
        norm_kernel,
        grid=(rows // tile,),
        in_specs=[pl.BlockSpec((tile, D), lambda i: (i, 0))] + [pl.BlockSpec(memory_space=pl.ANY)] * len(ahead),
        out_specs=pl.BlockSpec((tile, D), lambda i: (i, 0)),
        out_shape=jax.ShapeDtypeStruct(hidden.shape, jnp.bfloat16),
        compiler_params=pltpu.CompilerParams(vmem_limit_bytes=SMALL_VMEM),
        cost_estimate=LITTLE,
        name="normalise",
    )(hidden, *ahead)


def find_kernel(holders, requests, pass_local, capacity, passing, me_ref, table_ref, *rest):
    rank_ref, passage_ref = rest[passing + 1 : passing + 3]
    slot_ref, kept_ref = rest[-2:]
    me = me_ref[0]
    stride = table_ref.shape[0] // holders
    for k in range(holders):
        base = k * (capacity + 1)
        for rank in range(capacity + 1):
            slot_ref[base + rank] = 0
        count = jnp.int32(0)
        for request in range(requests):
            slot_ref[base + count] = request
            mine = (table_ref[k * stride + request] // pass_local == me).astype(jnp.int32)
            count = jnp.minimum(count + mine, capacity)
    spot = lax.broadcasted_iota(jnp.int32, (1, PLEN), 1)
    for k in range(holders):
        for rank in range(capacity):
            at = k * capacity + rank
            request = slot_ref[k * (capacity + 1) + rank]
            passage_ref[at] = lax.rem(table_ref[k * stride + request], pass_local)
            start = k * stride + requests + request * RECOMP
            covered = spot < 0
            for r in range(RECOMP):
                covered = covered | (spot == table_ref[start + r])
            kept_ref[at : at + 1, :] = jnp.where(covered, 0.0, 1.0)
    kept = kept_ref[...]
    upto = lax.broadcasted_iota(jnp.int32, (PLEN, PLEN), 0) <= lax.broadcasted_iota(jnp.int32, (PLEN, PLEN), 1)
    rank_of = jnp.dot(
        kept.astype(jnp.bfloat16), upto.astype(jnp.bfloat16), preferred_element_type=jnp.float32
    )
    rank_ref[...] = jnp.where(kept > 0, rank_of, 0.0)


def find_rows(table, me, holders, requests, pass_local, capacity, passing, normed):
    slots = holders * capacity
    smem = pl.BlockSpec(memory_space=pltpu.SMEM)
    whole = pl.BlockSpec(memory_space=pl.ANY)
    return pl.pallas_call(
        functools.partial(find_kernel, holders, requests, pass_local, capacity, len(passing)),
        in_specs=[smem, smem] + [whole] * (len(passing) + 1),
        out_specs=[pl.BlockSpec(memory_space=pltpu.VMEM), smem] + [whole] * len(passing),
        out_shape=[jax.ShapeDtypeStruct((slots, PLEN), jnp.float32), jax.ShapeDtypeStruct((slots,), jnp.int32)]
        + [jax.ShapeDtypeStruct(part.shape, part.dtype) for part in passing],
        input_output_aliases={2 + i: 2 + i for i in range(len(passing))},
        scratch_shapes=[pltpu.SMEM((holders * (capacity + 1),), jnp.int32), pltpu.VMEM((slots, PLEN), jnp.float32)],
        compiler_params=pltpu.CompilerParams(vmem_limit_bytes=SMALL_VMEM),
        cost_estimate=LARGE,
        name="find_rows",
    )(me, table, *passing, normed)


def pick_kernel(me_ref, passage_ref, rank_ref, cache_ref, *rest):
    out_ref = rest[-1]
    pair = me_ref[1]
    row = (lax.broadcasted_iota(jnp.int32, (KEPT, PLEN), 0) + 1).astype(jnp.float32)
    for at in range(out_ref.shape[0]):
        passage = passage_ref[at]
        select = (rank_ref[at : at + 1, :] == row).astype(jnp.bfloat16)
        for place, part in ((0, pair), (1, 1 - pair)):
            for half in range(2):
                start = pl.multiple_of(half * HALF + part * PAIR_WIDTH, PAIR_WIDTH)
                end = (place * 2 + half) * PAIR_WIDTH
                out_ref[at, :, end : end + PAIR_WIDTH] = jnp.dot(
                    select, cache_ref[passage, :, pl.ds(start, PAIR_WIDTH)], preferred_element_type=jnp.float32
                ).astype(jnp.bfloat16)


def pick_rows(me, passages, ranks, cache, ahead):
    smem = pl.BlockSpec(memory_space=pltpu.SMEM)
    vmem = pl.BlockSpec(memory_space=pltpu.VMEM)
    return pl.pallas_call(
        pick_kernel,
        in_specs=[smem, smem, vmem, vmem] + [pl.BlockSpec(memory_space=pl.ANY)] * len(ahead),
        out_specs=vmem,
        out_shape=jax.ShapeDtypeStruct((passages.shape[0], KEPT, 2 * HALF), jnp.bfloat16),
        compiler_params=pltpu.CompilerParams(vmem_limit_bytes=SMALL_VMEM),
        cost_estimate=LITTLE,
        name="pick_rows",
    )(me, passages, ranks, cache, *ahead)


def project_kernel(chunks, member_ref, mine_ref, other_ref, *refs):
    weights, mine_out, other_out = refs[:chunks], refs[-2], refs[-1]
    rows = mine_ref.shape[0]
    depth = D // chunks
    total = None
    for k in range(chunks):
        columns = pl.ds(pl.multiple_of((member_ref[0] ^ k) * depth, depth), depth)
        both = jnp.concatenate([mine_ref[:, columns], other_ref[:, columns]], axis=0)
        term = jnp.dot(both, weights[k][...], preferred_element_type=jnp.float32)
        total = term if total is None else total + term
    mine_out[...] = total[:rows].astype(jnp.bfloat16)
    other_out[...] = total[rows:].astype(jnp.bfloat16)


def project(member, mine, other, weights, ahead):
    rows, width = mine.shape[0], weights[0].shape[1]
    shape = jax.ShapeDtypeStruct((rows, width), jnp.bfloat16)
    vmem = pl.BlockSpec(memory_space=pltpu.VMEM)
    return pl.pallas_call(
        functools.partial(project_kernel, len(weights)),
        in_specs=[pl.BlockSpec(memory_space=pltpu.SMEM)]
        + [vmem] * (2 + len(weights))
        + [pl.BlockSpec(memory_space=pl.ANY)] * len(ahead),
        out_specs=[vmem, vmem],
        out_shape=[shape, shape],
        compiler_params=pltpu.CompilerParams(vmem_limit_bytes=SMALL_VMEM),
        cost_estimate=LITTLE,
        name="project",
    )(member.reshape(1), mine, other, *weights, *ahead)


def scaled_keys(keys, turned_ref):
    scaled = keys.astype(jnp.float32) * SCORE_FACTOR
    high = scaled.astype(jnp.bfloat16)
    turned_ref[:HD, :] = high.T
    turned_ref[HD:, :] = (scaled - high.astype(jnp.float32)).astype(jnp.bfloat16).T
    return jnp.max(jnp.sum(scaled * scaled, axis=1, keepdims=True))


def head_rows(q_ref, first, heads_once):
    block = jnp.concatenate(
        [q_ref[:, (first + i) * HD : (first + i + 1) * HD] for i in range(heads_once)], axis=0
    )
    return jnp.concatenate([block, block], axis=1)


def causal(rows):
    token = lax.broadcasted_iota(jnp.int32, (rows, QLEN), 0) % QLEN
    return lax.broadcasted_iota(jnp.int32, (rows, QLEN), 1) <= token


def own_kernel(heads_once, passing, info_ref, q_ref, key_ref, value_ref, *rest):
    sum_ref, weight_ref, bound_ref = rest[-5 - passing : -2 - passing]
    turned_ref, wide_ref = rest[-2:]

    @pl.when((pl.program_id(0) == 0) & (pl.program_id(1) == 0))
    def clear():
        bound_ref[...] = jnp.zeros_like(bound_ref)

    scaled_keys(key_ref[...], turned_ref)
    wide_ref[:, :HD] = value_ref[...]
    wide_ref[:, HD:] = jnp.ones((QLEN, HD), jnp.bfloat16)
    shown = jnp.where(causal(heads_once * QLEN), 1.0, 0.0).astype(jnp.bfloat16)
    lane = lax.broadcasted_iota(jnp.int32, (QLEN, HD), 1)
    weights = jnp.zeros((QLEN, HD), jnp.float32)
    peak = jnp.zeros((QLEN, 1), jnp.float32)
    for first in range(0, GROUPED, heads_once):
        scores = jnp.dot(head_rows(q_ref, first, heads_once), turned_ref[...], preferred_element_type=jnp.float32)
        summed = jnp.dot(
            jnp.exp2(scores).astype(jnp.bfloat16) * shown, wide_ref[...], preferred_element_type=jnp.float32
        )
        for i in range(heads_once):
            rows = slice(i * QLEN, (i + 1) * QLEN)
            sum_ref[:, (first + i) * HD : (first + i + 1) * HD] = summed[rows, :HD].astype(jnp.bfloat16)
            weights = jnp.where(lane == first + i, summed[rows, HD:], weights)
        for pair in range(first, first + heads_once, 4):
            most = None
            for head in range(pair, pair + 4):
                block = q_ref[:, head * HD : (head + 1) * HD].astype(jnp.float32)
                most = block * block if most is None else jnp.maximum(most, block * block)
            peak = jnp.maximum(peak, jnp.sum(most, axis=1, keepdims=True))
    weight_ref[...] = weights
    bound_ref[...] = jnp.maximum(bound_ref[...], jnp.max(peak))


def attend_own(info, q_rows, own_kv, ahead, passing):
    rows = q_rows.shape[0]
    whole = pl.BlockSpec(memory_space=pl.ANY)
    wide = GROUPED * HD
    return pl.pallas_call(
        functools.partial(own_kernel, 8, len(passing)),
        grid_spec=pltpu.PrefetchScalarGridSpec(
            num_scalar_prefetch=1,
            grid=(rows // QLEN, PAIR_HEADS),
            in_specs=[
                pl.BlockSpec((QLEN, wide), lambda n, h, info: (n, info[0] * PAIR_HEADS + h)),
                pl.BlockSpec((QLEN, HD), lambda n, h, info: (n, info[0] * PAIR_HEADS + h)),
                pl.BlockSpec((QLEN, HD), lambda n, h, info: (n, KVH + info[0] * PAIR_HEADS + h)),
            ]
            + [whole] * (len(passing) + len(ahead)),
            out_specs=[
                pl.BlockSpec((QLEN, wide), lambda n, h, info: (n, h)),
                pl.BlockSpec((QLEN, HD), lambda n, h, info: (n, h)),
                pl.BlockSpec((8, HD), lambda n, h, info: (0, 0)),
            ]
            + [whole] * len(passing),
            scratch_shapes=[pltpu.VMEM((2 * HD, QLEN), jnp.bfloat16), pltpu.VMEM((QLEN, 2 * HD), jnp.bfloat16)],
        ),
        out_shape=[
            jax.ShapeDtypeStruct((rows, PAIR_HEADS * wide), jnp.bfloat16),
            jax.ShapeDtypeStruct((rows, PAIR_HEADS * HD), jnp.float32),
            jax.ShapeDtypeStruct((8, HD), jnp.float32),
        ]
        + [jax.ShapeDtypeStruct(part.shape, part.dtype) for part in passing],
        input_output_aliases={4 + i: 3 + i for i in range(len(passing))},
        compiler_params=pltpu.CompilerParams(vmem_limit_bytes=VMEM_BYTES),
        cost_estimate=LITTLE,
        name="attend_own",
    )(info, q_rows, own_kv, own_kv, *passing, *ahead)


def attend_kernel(
    heads_once,
    info_ref,
    q_ref,
    own_k_ref,
    own_v_ref,
    kept_ref,
    near_ref,
    far_ref,
    sum_ref,
    weight_ref,
    bound_ref,
    *rest,
):
    out_ref, key_ref, turned_ref, value_ref, score_ref, expd_ref = rest[-6:]
    query = pl.program_id(0)
    key_start = pl.multiple_of(pl.program_id(1) * HD, HD)
    value_start = pl.multiple_of(PAIR_WIDTH + pl.program_id(1) * HD, HD)
    passage_keys = TOPP * PLEN
    flip = info_ref[1] > 0
    value_ref[:, HD:] = jnp.ones((passage_keys + QLEN, HD), jnp.bfloat16)
    for j in range(TOPP):
        slot = info_ref[2 + query * TOPP + j]
        key_ref[j * KEPT : (j + 1) * KEPT, :] = kept_ref[slot, :, pl.ds(key_start, HD)]
        value_ref[j * KEPT : (j + 1) * KEPT, :HD] = kept_ref[slot, :, pl.ds(value_start, HD)]
    key_ref[TOPP * KEPT : passage_keys, :] = jnp.where(flip, far_ref[...], near_ref[...])
    value_ref[TOPP * KEPT : passage_keys, :HD] = jnp.where(flip, near_ref[...], far_ref[...])
    key_ref[passage_keys:, :] = own_k_ref[...]
    value_ref[passage_keys:, :HD] = own_v_ref[...]
    key_bound = scaled_keys(key_ref[...], turned_ref)
    small = jnp.max(bound_ref[...]) * key_bound <= SAFE_EXPONENT**2
    rows = heads_once * QLEN

    groups = GROUPED // heads_once

    def score(group):
        score_ref[group % 2] = jnp.dot(
            head_rows(q_ref, group * heads_once, heads_once),
            turned_ref[:, :passage_keys],
            preferred_element_type=jnp.float32,
        )

    def soften(group):
        expd_ref[group % 2] = jnp.exp2(score_ref[group % 2]).astype(jnp.bfloat16)

    def finish(group):
        summed = jnp.dot(expd_ref[group % 2], value_ref[:passage_keys, :], preferred_element_type=jnp.float32)
        for i in range(heads_once):
            head = group * heads_once + i
            part = summed[i * QLEN : (i + 1) * QLEN]
            columns = slice(head * HD, (head + 1) * HD)
            weight = part[:, HD:] + weight_ref[:, head : head + 1]
            inverse = pl.reciprocal(weight, approx=True)
            inverse = inverse * (2.0 - weight * inverse)
            total = part[:, :HD] + sum_ref[:, columns].astype(jnp.float32)
            out_ref[:, columns] = (total * inverse).astype(jnp.bfloat16)

    @pl.when(small)
    def unshifted():
        score(0)
        for group in range(groups):
            if group + 1 < groups:
                score(group + 1)
            soften(group)
            if group > 0:
                finish(group - 1)
        finish(groups - 1)

    @pl.when(jnp.logical_not(small))
    def shifted():
        visible = causal(rows)
        for first in range(0, GROUPED, heads_once):
            scores = jnp.dot(
                head_rows(q_ref, first, heads_once), turned_ref[...], preferred_element_type=jnp.float32
            )
            scores = jnp.concatenate(
                [scores[:, :passage_keys], jnp.where(visible, scores[:, passage_keys:], -jnp.inf)], axis=1
            )
            peak = jnp.max(scores, axis=1, keepdims=True)
            expd = jnp.exp2(scores - peak).astype(jnp.bfloat16)
            summed = jnp.dot(expd, value_ref[...], preferred_element_type=jnp.float32)
            result = (summed[:, :HD] / summed[:, HD:]).astype(jnp.bfloat16)
            for i in range(heads_once):
                out_ref[:, (first + i) * HD : (first + i + 1) * HD] = result[i * QLEN : (i + 1) * QLEN]


def attend(part, info, q_rows, own_kv, kept, near, far, own, earlier=None):
    rows, width = q_rows.shape
    queries = rows // QLEN
    slots = kept.shape[0]
    span = TOPP * PLEN + QLEN
    wide = GROUPED * HD
    heads_once = 2
    in_specs = [
        pl.BlockSpec((QLEN, wide), lambda n, h, info: (n, info[0] * PAIR_HEADS + h)),
        pl.BlockSpec((QLEN, HD), lambda n, h, info: (n, info[0] * PAIR_HEADS + h)),
        pl.BlockSpec((QLEN, HD), lambda n, h, info: (n, KVH + info[0] * PAIR_HEADS + h)),
        pl.BlockSpec((slots, KEPT, HALF), lambda n, h, info: (0, 0, part)),
        pl.BlockSpec((TOPP * RECOMP, HD), lambda n, h, info: (n, h)),
        pl.BlockSpec((TOPP * RECOMP, HD), lambda n, h, info: (n, h)),
        pl.BlockSpec((QLEN, wide), lambda n, h, info: (n, h)),
        pl.BlockSpec((QLEN, HD), lambda n, h, info: (n, h)),
        pl.BlockSpec((8, HD), lambda n, h, info: (0, 0)),
    ]
    operands = [q_rows, own_kv, own_kv, kept, near, far, *own]
    aliases = {}
    if earlier is not None:
        in_specs.append(pl.BlockSpec(memory_space=pl.ANY))
        operands.append(earlier)
        aliases = {len(operands): 0}
    return pl.pallas_call(
        functools.partial(attend_kernel, heads_once),
        grid_spec=pltpu.PrefetchScalarGridSpec(
            num_scalar_prefetch=1,
            grid=(queries, PAIR_HEADS),
            in_specs=in_specs,
            out_specs=pl.BlockSpec((QLEN, wide), lambda n, h, info: (n, info[0] * PAIR_HEADS + h)),
            scratch_shapes=[
                pltpu.VMEM((span, HD), jnp.bfloat16),
                pltpu.VMEM((2 * HD, span), jnp.bfloat16),
                pltpu.VMEM((span, 2 * HD), jnp.bfloat16),
                pltpu.VMEM((2, heads_once * QLEN, TOPP * PLEN), jnp.float32),
                pltpu.VMEM((2, heads_once * QLEN, TOPP * PLEN), jnp.bfloat16),
            ],
        ),
        out_shape=jax.ShapeDtypeStruct((rows, width), jnp.bfloat16),
        input_output_aliases=aliases,
        compiler_params=pltpu.CompilerParams(vmem_limit_bytes=VMEM_BYTES),
        cost_estimate=LITTLE,
        name="attend",
    )(info, *operands)


def swap(array, axis, bits):
    size = lax.axis_size(axis)
    return lax.ppermute(array, axis, [(i, i ^ bits) for i in range(size)])


def first_hops(w_kv):
    return [swap(w_kv, "member", 2), swap(w_kv, "member", 4), swap(w_kv, "member", 1)]


def recompute_general(normed, w_kv, pair):
    whole = lax.all_gather(lax.all_gather(w_kv, "member", axis=0, tiled=True), "group", axis=1, tiled=True)
    result = jnp.dot(normed, whole, preferred_element_type=jnp.float32).astype(jnp.bfloat16)
    result = result.reshape(-1, 2, PAIRS, PAIR_WIDTH)
    first = jnp.where(pair == 0, result[:, :, 0], result[:, :, 1])
    second = jnp.where(pair == 0, result[:, :, 1], result[:, :, 0])
    return [first[:, 0], first[:, 1]], [second[:, 0], second[:, 1]]


def local(q_rows, own_kv, cache, recomp_hidden, w_kv, retrieval, positions):
    queries = retrieval.shape[0]
    requests = queries * TOPP
    holders = lax.axis_size("member")
    groups = lax.axis_size("group")
    pass_local = cache.shape[0]
    capacity = -(-requests // holders)
    member = lax.axis_index("member")
    group = lax.axis_index("group")
    pair = group % PAIRS
    tuned = groups == 4 and holders == 8
    wanted = retrieval.reshape(requests)
    request = jnp.concatenate([wanted, positions.reshape(requests * RECOMP)])
    request = jnp.pad(request, (0, -request.shape[0] % 128)).reshape(1, -1, 128)
    request = jnp.broadcast_to(request, (holders,) + request.shape[1:])
    table = lax.all_to_all(request, "member", split_axis=0, concat_axis=0, tiled=True).reshape(-1)
    hidden = recomp_hidden.reshape(requests * RECOMP, D)
    normed = normalise(hidden, [])
    me = jnp.stack([member, pair]).astype(jnp.int32)
    ahead = []
    hops = first_hops(w_kv) if tuned else []
    ranks, passages, *hops = find_rows(table, me, holders, requests, pass_local, capacity, hops, normed)
    holder_of = wanted // pass_local
    same = holder_of[:, None] == holder_of[None, :]
    before = jnp.arange(requests)[None, :] < jnp.arange(requests)[:, None]
    slot = holder_of * capacity + jnp.sum((same & before).astype(jnp.int32), axis=1)
    flip = group // 2 if tuned else jnp.int32(0)
    info = jnp.concatenate([jnp.stack([pair, flip]), slot]).astype(jnp.int32)
    other_info = jnp.concatenate([jnp.stack([1 - pair, flip]), slot]).astype(jnp.int32)
    if tuned:
        one, two, aside = hops
        three = swap(two, "member", 2)
        beside_one, beside_two = swap(one, "member", 1), swap(two, "member", 1)
        across, across_one, across_two = swap(w_kv, "group", 2), swap(one, "group", 2), swap(two, "group", 2)
        across_aside = swap(aside, "group", 2)
        ahead += [across, beside_one, across_one, three]
    sent = pick_rows(me, passages, ranks, cache, ahead)
    arrived = lax.all_to_all(
        sent.reshape(holders, capacity * KEPT, 2 * HALF), "member", split_axis=0, concat_axis=0, tiled=True
    ).reshape(sent.shape)
    if tuned:
        first_own = attend_own(info, q_rows, own_kv, [sent, across_two, across_aside, beside_two], [beside_one])
        far_one, far_two = swap(first_own[3], "group", 2), swap(beside_two, "group", 2)
        beside_three, across_three = swap(three, "member", 1), swap(three, "group", 2)
        second_own = attend_own(
            other_info, q_rows, own_kv, [first_own[0], far_one, beside_three], [across_three]
        )
        far_three = swap(second_own[3], "member", 1)
        blocks = [w_kv, aside, one, first_own[3], two, beside_two, three, beside_three]
        beyond = [across, across_aside, across_one, far_one, across_two, far_two, second_own[3], far_three]
        other = swap(normed, "group", 1)
        near, near_other = project(member, normed, other, blocks, [second_own[0]])
        far, far_other = project(member, normed, other, beyond, [near])
        first = [near, far]
        second = [swap(near_other, "group", 1), swap(far_other, "group", 1)]
    else:
        first_own = attend_own(info, q_rows, own_kv, [sent], [])
        second_own = attend_own(other_info, q_rows, own_kv, [first_own[0]], [])
        first, second = recompute_general(normed, w_kv, pair)
    out = attend(0, info, q_rows, own_kv, arrived, *first, first_own[:3])
    return attend(1, other_info, q_rows, own_kv, arrived, *second, second_own[:3], earlier=out)


def solution(mesh):
    rows = P(("group", "member"), None)
    placed = (
        rows,
        rows,
        P(("group", "member"), None, None),
        P(("group", "member"), None, None, None),
        P("member", "group"),
        rows,
        P(("group", "member"), None, None),
    )
    return jax.shard_map(local, mesh=mesh, in_specs=placed, out_specs=rows, check_vma=False)
```

```python
import functools

import jax
import jax.numpy as jnp
from jax import lax
from jax.experimental import pallas as pl
from jax.experimental.pallas import tpu as pltpu
from jax.sharding import PartitionSpec as P

D = 4096
HQ = 64
KVH = 4
HD = 128
TOPP = 8
QLEN = 128
PLEN = 64
RECOMP = 16
KEPT = PLEN - RECOMP
GROUPED = HQ // KVH
PAIRS = 2
PAIR_HEADS = KVH // PAIRS
PAIR_WIDTH = PAIR_HEADS * HD
HALF = KVH * HD

EPSILON = 1e-06
SCORE_FACTOR = 1.4426950408889634 / HD**0.5
SAFE_EXPONENT = 80.0
SMALL_VMEM = 12 * 1024 * 1024
VMEM_BYTES = 24 * 1024 * 1024
LITTLE = pl.CostEstimate(flops=1, bytes_accessed=1, transcendentals=0)
LARGE = pl.CostEstimate(flops=1, bytes_accessed=36_000_000, transcendentals=0)


def norm_kernel(hidden_ref, *rest):
    normed_ref = rest[-1]
    hidden = hidden_ref[...].astype(jnp.float32)
    mean = jnp.mean(hidden * hidden, axis=1, keepdims=True)
    normed_ref[...] = (hidden * lax.rsqrt(mean + EPSILON)).astype(jnp.bfloat16)


def normalise(hidden, ahead):
    rows = hidden.shape[0]
    tile = min(rows, 64)
    return pl.pallas_call(
        norm_kernel,
        grid=(rows // tile,),
        in_specs=[pl.BlockSpec((tile, D), lambda i: (i, 0))] + [pl.BlockSpec(memory_space=pl.ANY)] * len(ahead),
        out_specs=pl.BlockSpec((tile, D), lambda i: (i, 0)),
        out_shape=jax.ShapeDtypeStruct(hidden.shape, jnp.bfloat16),
        compiler_params=pltpu.CompilerParams(vmem_limit_bytes=SMALL_VMEM),
        cost_estimate=LITTLE,
        name="normalise",
    )(hidden, *ahead)


def find_kernel(holders, requests, pass_local, capacity, passing, me_ref, table_ref, *rest):
    rank_ref, passage_ref = rest[passing + 1 : passing + 3]
    slot_ref, kept_ref = rest[-2:]
    me = me_ref[0]
    stride = table_ref.shape[0] // holders
    for k in range(holders):
        base = k * (capacity + 1)
        for rank in range(capacity + 1):
            slot_ref[base + rank] = 0
        count = jnp.int32(0)
        for request in range(requests):
            slot_ref[base + count] = request
            mine = (table_ref[k * stride + request] // pass_local == me).astype(jnp.int32)
            count = jnp.minimum(count + mine, capacity)
    spot = lax.broadcasted_iota(jnp.int32, (1, PLEN), 1)
    for k in range(holders):
        for rank in range(capacity):
            at = k * capacity + rank
            request = slot_ref[k * (capacity + 1) + rank]
            passage_ref[at] = lax.rem(table_ref[k * stride + request], pass_local)
            start = k * stride + requests + request * RECOMP
            covered = spot < 0
            for r in range(RECOMP):
                covered = covered | (spot == table_ref[start + r])
            kept_ref[at : at + 1, :] = jnp.where(covered, 0.0, 1.0)
    kept = kept_ref[...]
    upto = lax.broadcasted_iota(jnp.int32, (PLEN, PLEN), 0) <= lax.broadcasted_iota(jnp.int32, (PLEN, PLEN), 1)
    rank_of = jnp.dot(
        kept.astype(jnp.bfloat16), upto.astype(jnp.bfloat16), preferred_element_type=jnp.float32
    )
    rank_ref[...] = jnp.where(kept > 0, rank_of, 0.0)


def find_rows(table, me, holders, requests, pass_local, capacity, passing, normed):
    slots = holders * capacity
    smem = pl.BlockSpec(memory_space=pltpu.SMEM)
    whole = pl.BlockSpec(memory_space=pl.ANY)
    return pl.pallas_call(
        functools.partial(find_kernel, holders, requests, pass_local, capacity, len(passing)),
        in_specs=[smem, smem] + [whole] * (len(passing) + 1),
        out_specs=[pl.BlockSpec(memory_space=pltpu.VMEM), smem] + [whole] * len(passing),
        out_shape=[jax.ShapeDtypeStruct((slots, PLEN), jnp.float32), jax.ShapeDtypeStruct((slots,), jnp.int32)]
        + [jax.ShapeDtypeStruct(part.shape, part.dtype) for part in passing],
        input_output_aliases={2 + i: 2 + i for i in range(len(passing))},
        scratch_shapes=[pltpu.SMEM((holders * (capacity + 1),), jnp.int32), pltpu.VMEM((slots, PLEN), jnp.float32)],
        compiler_params=pltpu.CompilerParams(vmem_limit_bytes=SMALL_VMEM),
        cost_estimate=LARGE,
        name="find_rows",
    )(me, table, *passing, normed)


def pick_kernel(me_ref, passage_ref, rank_ref, cache_ref, *rest):
    out_ref = rest[-1]
    pair = me_ref[1]
    row = (lax.broadcasted_iota(jnp.int32, (KEPT, PLEN), 0) + 1).astype(jnp.float32)
    for at in range(out_ref.shape[0]):
        passage = passage_ref[at]
        select = (rank_ref[at : at + 1, :] == row).astype(jnp.bfloat16)
        for place, part in ((0, pair), (1, 1 - pair)):
            for half in range(2):
                start = pl.multiple_of(half * HALF + part * PAIR_WIDTH, PAIR_WIDTH)
                end = (place * 2 + half) * PAIR_WIDTH
                out_ref[at, :, end : end + PAIR_WIDTH] = jnp.dot(
                    select, cache_ref[passage, :, pl.ds(start, PAIR_WIDTH)], preferred_element_type=jnp.float32
                ).astype(jnp.bfloat16)


def pick_rows(me, passages, ranks, cache, ahead):
    smem = pl.BlockSpec(memory_space=pltpu.SMEM)
    vmem = pl.BlockSpec(memory_space=pltpu.VMEM)
    return pl.pallas_call(
        pick_kernel,
        in_specs=[smem, smem, vmem, vmem] + [pl.BlockSpec(memory_space=pl.ANY)] * len(ahead),
        out_specs=vmem,
        out_shape=jax.ShapeDtypeStruct((passages.shape[0], KEPT, 2 * HALF), jnp.bfloat16),
        compiler_params=pltpu.CompilerParams(vmem_limit_bytes=SMALL_VMEM),
        cost_estimate=LITTLE,
        name="pick_rows",
    )(me, passages, ranks, cache, *ahead)


def project_kernel(chunks, member_ref, mine_ref, other_ref, *refs):
    weights, mine_out, other_out = refs[:chunks], refs[-2], refs[-1]
    rows = mine_ref.shape[0]
    depth = D // chunks
    total = None
    for k in range(chunks):
        columns = pl.ds(pl.multiple_of((member_ref[0] ^ k) * depth, depth), depth)
        both = jnp.concatenate([mine_ref[:, columns], other_ref[:, columns]], axis=0)
        term = jnp.dot(both, weights[k][...], preferred_element_type=jnp.float32)
        total = term if total is None else total + term
    mine_out[...] = total[:rows].astype(jnp.bfloat16)
    other_out[...] = total[rows:].astype(jnp.bfloat16)


def project(member, mine, other, weights, ahead):
    rows, width = mine.shape[0], weights[0].shape[1]
    shape = jax.ShapeDtypeStruct((rows, width), jnp.bfloat16)
    vmem = pl.BlockSpec(memory_space=pltpu.VMEM)
    return pl.pallas_call(
        functools.partial(project_kernel, len(weights)),
        in_specs=[pl.BlockSpec(memory_space=pltpu.SMEM)]
        + [vmem] * (2 + len(weights))
        + [pl.BlockSpec(memory_space=pl.ANY)] * len(ahead),
        out_specs=[vmem, vmem],
        out_shape=[shape, shape],
        compiler_params=pltpu.CompilerParams(vmem_limit_bytes=SMALL_VMEM),
        cost_estimate=LITTLE,
        name="project",
    )(member.reshape(1), mine, other, *weights, *ahead)


def scaled_keys(keys, turned_ref):
    scaled = keys.astype(jnp.float32) * SCORE_FACTOR
    high = scaled.astype(jnp.bfloat16)
    turned_ref[:HD, :] = high.T
    turned_ref[HD:, :] = (scaled - high.astype(jnp.float32)).astype(jnp.bfloat16).T
    return jnp.max(jnp.sum(scaled * scaled, axis=1, keepdims=True))


def head_rows(q_ref, rows, column, heads_once):
    block = jnp.concatenate(
        [q_ref[rows, pl.ds(pl.multiple_of(column + i * HD, HD), HD)] for i in range(heads_once)], axis=0
    )
    return jnp.concatenate([block, block], axis=1)


def causal(rows):
    token = lax.broadcasted_iota(jnp.int32, (rows, QLEN), 0) % QLEN
    return lax.broadcasted_iota(jnp.int32, (rows, QLEN), 1) <= token


def place(step, pair):
    query, head = step // PAIR_HEADS, step % PAIR_HEADS
    rows = pl.ds(pl.multiple_of(query * QLEN, QLEN), QLEN)
    return query, head, rows, pair * PAIR_HEADS + head


def columns(start, width=HD):
    return pl.ds(pl.multiple_of(start, HD), width)


def own_kernel(steps, heads_once, passing, info_ref, q_ref, own_ref, *rest):
    sum_ref, weight_ref, bound_ref = rest[-5 - passing : -2 - passing]
    turned_ref, wide_ref = rest[-2:]
    bound_ref[...] = jnp.zeros_like(bound_ref)
    shown = jnp.where(causal(heads_once * QLEN), 1.0, 0.0).astype(jnp.bfloat16)
    lane = lax.broadcasted_iota(jnp.int32, (QLEN, HD), 1)

    def one(step, carry):
        _, head, rows, column = place(step, info_ref[0])
        scaled_keys(own_ref[rows, columns(column * HD)], turned_ref)
        wide_ref[:, :HD] = own_ref[rows, columns(HALF + column * HD)]
        wide_ref[:, HD:] = jnp.ones((QLEN, HD), jnp.bfloat16)
        weights = jnp.zeros((QLEN, HD), jnp.float32)
        peak = jnp.zeros((QLEN, 1), jnp.float32)
        for first in range(0, GROUPED, heads_once):
            start = (column * GROUPED + first) * HD
            scores = jnp.dot(
                head_rows(q_ref, rows, start, heads_once), turned_ref[...], preferred_element_type=jnp.float32
            )
            summed = jnp.dot(
                jnp.exp2(scores).astype(jnp.bfloat16) * shown, wide_ref[...], preferred_element_type=jnp.float32
            )
            for i in range(heads_once):
                part = summed[i * QLEN : (i + 1) * QLEN]
                sum_ref[rows, columns((head * GROUPED + first + i) * HD)] = part[:, :HD].astype(jnp.bfloat16)
                weights = jnp.where(lane == first + i, part[:, HD:], weights)
            most = None
            for i in range(heads_once):
                block = q_ref[rows, columns(start + i * HD)].astype(jnp.float32)
                most = block * block if most is None else jnp.maximum(most, block * block)
            peak = jnp.maximum(peak, jnp.sum(most, axis=1, keepdims=True))
        weight_ref[rows, columns(head * HD)] = weights
        bound_ref[...] = jnp.maximum(bound_ref[...], jnp.max(peak))
        return carry

    lax.fori_loop(0, steps, one, 0)


def attend_own(info, q_rows, own_kv, ahead, passing):
    rows = q_rows.shape[0]
    whole = pl.BlockSpec(memory_space=pl.ANY)
    vmem = pl.BlockSpec(memory_space=pltpu.VMEM)
    return pl.pallas_call(
        functools.partial(own_kernel, rows // QLEN * PAIR_HEADS, 4, len(passing)),
        in_specs=[pl.BlockSpec(memory_space=pltpu.SMEM), vmem, vmem] + [whole] * (len(passing) + len(ahead)),
        out_specs=[vmem] * 3 + [whole] * len(passing),
        out_shape=[
            jax.ShapeDtypeStruct((rows, PAIR_HEADS * GROUPED * HD), jnp.bfloat16),
            jax.ShapeDtypeStruct((rows, PAIR_HEADS * HD), jnp.float32),
            jax.ShapeDtypeStruct((8, HD), jnp.float32),
        ]
        + [jax.ShapeDtypeStruct(part.shape, part.dtype) for part in passing],
        scratch_shapes=[pltpu.VMEM((2 * HD, QLEN), jnp.bfloat16), pltpu.VMEM((QLEN, 2 * HD), jnp.bfloat16)],
        input_output_aliases={3 + i: 3 + i for i in range(len(passing))},
        compiler_params=pltpu.CompilerParams(vmem_limit_bytes=VMEM_BYTES),
        cost_estimate=LITTLE,
        name="attend_own",
    )(info, q_rows, own_kv, *passing, *ahead)


def attend_kernel(
    steps,
    heads_once,
    part,
    info_ref,
    q_ref,
    own_ref,
    kept_ref,
    near_ref,
    far_ref,
    sum_ref,
    weight_ref,
    bound_ref,
    *rest,
):
    out_ref, key_ref, turned_ref, value_ref, score_ref, expd_ref, result_ref, done_ref = rest[-8:]
    passage_keys = TOPP * PLEN
    wide = GROUPED * HD
    groups = GROUPED // heads_once
    flip = info_ref[1] > 0
    value_ref[:, HD:] = jnp.ones((passage_keys + QLEN, HD), jnp.bfloat16)

    def leave(step):
        _, _, rows, column = place(step, info_ref[0])
        slot = step % 2
        return pltpu.make_async_copy(
            result_ref.at[slot], out_ref.at[rows, columns(column * wide, wide)], done_ref.at[slot]
        )

    def one(step, carry):
        query, head, rows, column = place(step, info_ref[0])
        slot = step % 2

        @pl.when(step >= 2)
        def free():
            leave(step - 2).wait()

        offset = part * HALF + head * HD
        for j in range(TOPP):
            block = info_ref[2 + query * TOPP + j]
            key_ref[j * KEPT : (j + 1) * KEPT, :] = kept_ref[block, :, columns(offset)]
            value_ref[j * KEPT : (j + 1) * KEPT, :HD] = kept_ref[block, :, columns(offset + PAIR_WIDTH)]
        near, far = near_ref[rows, columns(head * HD)], far_ref[rows, columns(head * HD)]
        key_ref[TOPP * KEPT : passage_keys, :] = jnp.where(flip, far, near)
        value_ref[TOPP * KEPT : passage_keys, :HD] = jnp.where(flip, near, far)
        key_ref[passage_keys:, :] = own_ref[rows, columns(column * HD)]
        value_ref[passage_keys:, :HD] = own_ref[rows, columns(HALF + column * HD)]
        key_bound = scaled_keys(key_ref[...], turned_ref)
        small = jnp.max(bound_ref[...]) * key_bound <= SAFE_EXPONENT**2

        def score(group):
            score_ref[group % 2] = jnp.dot(
                head_rows(q_ref, rows, column * wide + group * heads_once * HD, heads_once),
                turned_ref[:, :passage_keys],
                preferred_element_type=jnp.float32,
            )

        def soften(group):
            expd_ref[group % 2] = jnp.exp2(score_ref[group % 2]).astype(jnp.bfloat16)

        def finish(group):
            summed = jnp.dot(
                expd_ref[group % 2], value_ref[:passage_keys, :], preferred_element_type=jnp.float32
            )
            weights = weight_ref[rows, columns(head * HD)]
            for i in range(heads_once):
                at = group * heads_once + i
                both = summed[i * QLEN : (i + 1) * QLEN]
                weight = both[:, HD:] + weights[:, at : at + 1]
                inverse = pl.reciprocal(weight, approx=True)
                inverse = inverse * (2.0 - weight * inverse)
                total = both[:, :HD] + sum_ref[rows, columns(head * wide + at * HD)].astype(jnp.float32)
                result_ref[slot, :, at * HD : (at + 1) * HD] = (total * inverse).astype(jnp.bfloat16)

        @pl.when(small)
        def unshifted():
            score(0)
            for group in range(groups):
                if group + 1 < groups:
                    score(group + 1)
                soften(group)
                if group > 0:
                    finish(group - 1)
            finish(groups - 1)

        @pl.when(jnp.logical_not(small))
        def shifted():
            visible = causal(heads_once * QLEN)
            for group in range(groups):
                scores = jnp.dot(
                    head_rows(q_ref, rows, column * wide + group * heads_once * HD, heads_once),
                    turned_ref[...],
                    preferred_element_type=jnp.float32,
                )
                scores = jnp.concatenate(
                    [scores[:, :passage_keys], jnp.where(visible, scores[:, passage_keys:], -jnp.inf)], axis=1
                )
                peak = jnp.max(scores, axis=1, keepdims=True)
                expd = jnp.exp2(scores - peak).astype(jnp.bfloat16)
                summed = jnp.dot(expd, value_ref[...], preferred_element_type=jnp.float32)
                ratio = (summed[:, :HD] / summed[:, HD:]).astype(jnp.bfloat16)
                for i in range(heads_once):
                    at = group * heads_once + i
                    result_ref[slot, :, at * HD : (at + 1) * HD] = ratio[i * QLEN : (i + 1) * QLEN]

        leave(step).start()
        return carry

    lax.fori_loop(0, steps, one, 0)
    for step in range(max(steps - 2, 0), steps):
        leave(step).wait()


def attend(part, info, q_rows, own_kv, kept, near, far, own, earlier=None):
    rows, width = q_rows.shape
    span = TOPP * PLEN + QLEN
    heads_once = 2
    vmem = pl.BlockSpec(memory_space=pltpu.VMEM)
    whole = pl.BlockSpec(memory_space=pl.ANY)
    operands = [info, q_rows, own_kv, kept, near, far, *own]
    aliases = {}
    if earlier is not None:
        aliases = {len(operands): 0}
        operands.append(earlier)
    return pl.pallas_call(
        functools.partial(attend_kernel, rows // QLEN * PAIR_HEADS, heads_once, part),
        in_specs=[pl.BlockSpec(memory_space=pltpu.SMEM)] + [vmem] * 8 + [whole] * len(aliases),
        out_specs=whole,
        out_shape=jax.ShapeDtypeStruct((rows, width), jnp.bfloat16),
        scratch_shapes=[
            pltpu.VMEM((span, HD), jnp.bfloat16),
            pltpu.VMEM((2 * HD, span), jnp.bfloat16),
            pltpu.VMEM((span, 2 * HD), jnp.bfloat16),
            pltpu.VMEM((2, heads_once * QLEN, TOPP * PLEN), jnp.float32),
            pltpu.VMEM((2, heads_once * QLEN, TOPP * PLEN), jnp.bfloat16),
            pltpu.VMEM((2, QLEN, GROUPED * HD), jnp.bfloat16),
            pltpu.SemaphoreType.DMA((2,)),
        ],
        input_output_aliases=aliases,
        compiler_params=pltpu.CompilerParams(vmem_limit_bytes=VMEM_BYTES),
        cost_estimate=LITTLE,
        name="attend",
    )(*operands)


def swap(array, axis, bits):
    size = lax.axis_size(axis)
    return lax.ppermute(array, axis, [(i, i ^ bits) for i in range(size)])


def first_hops(w_kv):
    return [swap(w_kv, "member", 2), swap(w_kv, "member", 4), swap(w_kv, "member", 1)]


def gather_columns(w_kv, beyond, hops):
    one, two, aside = hops
    blocks, beyond = [w_kv, aside], [beyond, swap(aside, "group", 2)]
    for part in (one, two):
        near = swap(part, "member", 1)
        blocks += [part, near]
        beyond += [swap(part, "group", 2), swap(near, "group", 2)]
    return blocks, beyond


def last_columns(three):
    across = swap(three, "group", 2)
    return [three, swap(three, "member", 1)], [across, swap(across, "member", 1)]


def recompute_general(normed, w_kv, pair):
    whole = lax.all_gather(lax.all_gather(w_kv, "member", axis=0, tiled=True), "group", axis=1, tiled=True)
    result = jnp.dot(normed, whole, preferred_element_type=jnp.float32).astype(jnp.bfloat16)
    result = result.reshape(-1, 2, PAIRS, PAIR_WIDTH)
    first = jnp.where(pair == 0, result[:, :, 0], result[:, :, 1])
    second = jnp.where(pair == 0, result[:, :, 1], result[:, :, 0])
    return [first[:, 0], first[:, 1]], [second[:, 0], second[:, 1]]


def local(q_rows, own_kv, cache, recomp_hidden, w_kv, retrieval, positions):
    queries = retrieval.shape[0]
    requests = queries * TOPP
    holders = lax.axis_size("member")
    groups = lax.axis_size("group")
    pass_local = cache.shape[0]
    capacity = -(-requests // holders)
    member = lax.axis_index("member")
    group = lax.axis_index("group")
    pair = group % PAIRS
    tuned = groups == 4 and holders == 8
    wanted = retrieval.reshape(requests)
    request = jnp.concatenate([wanted, positions.reshape(requests * RECOMP)])
    request = jnp.pad(request, (0, -request.shape[0] % 128)).reshape(1, -1, 128)
    request = jnp.broadcast_to(request, (holders,) + request.shape[1:])
    table = lax.all_to_all(request, "member", split_axis=0, concat_axis=0, tiled=True).reshape(-1)
    hidden = recomp_hidden.reshape(requests * RECOMP, D)
    normed = normalise(hidden, [])
    me = jnp.stack([member, pair]).astype(jnp.int32)
    ahead = []
    hops = first_hops(w_kv) if tuned else []
    ranks, passages, *hops = find_rows(table, me, holders, requests, pass_local, capacity, hops, normed)
    holder_of = wanted // pass_local
    same = holder_of[:, None] == holder_of[None, :]
    before = jnp.arange(requests)[None, :] < jnp.arange(requests)[:, None]
    slot = holder_of * capacity + jnp.sum((same & before).astype(jnp.int32), axis=1)
    flip = group // 2 if tuned else jnp.int32(0)
    info = jnp.concatenate([jnp.stack([pair, flip]), slot]).astype(jnp.int32)
    other_info = jnp.concatenate([jnp.stack([1 - pair, flip]), slot]).astype(jnp.int32)
    first_own = attend_own(info, q_rows, own_kv, [ranks], [])
    ahead += [first_own[0]]
    three = []
    if tuned:
        three = [swap(hops[1], "member", 2)]
        blocks, beyond = gather_columns(w_kv, swap(w_kv, "group", 2), hops)
        ahead += [beyond[0], blocks[3], beyond[2], three[0]]
    sent = pick_rows(me, passages, ranks, cache, ahead)
    arrived = lax.all_to_all(
        sent.reshape(holders, capacity * KEPT, 2 * HALF), "member", split_axis=0, concat_axis=0, tiled=True
    ).reshape(sent.shape)
    second_own = attend_own(other_info, q_rows, own_kv, [sent], three)
    if tuned:
        other = swap(normed, "group", 1)
        last_near, last_far = last_columns(second_own[3])
        near, near_other = project(member, normed, other, blocks + last_near, [second_own[0]])
        far, far_other = project(member, normed, other, beyond + last_far, [near])
        first = [near, far]
        second = [swap(near_other, "group", 1), swap(far_other, "group", 1)]
    else:
        first, second = recompute_general(normed, w_kv, pair)
    out = attend(0, info, q_rows, own_kv, arrived, *first, first_own[:3])
    return attend(1, other_info, q_rows, own_kv, arrived, *second, second_own[:3], earlier=out)


def solution(mesh):
    rows = P(("group", "member"), None)
    placed = (
        rows,
        rows,
        P(("group", "member"), None, None),
        P(("group", "member"), None, None, None),
        P("member", "group"),
        rows,
        P(("group", "member"), None, None),
    )
    return jax.shard_map(local, mesh=mesh, in_specs=placed, out_specs=rows, check_vma=False)
```

```python
import functools

import jax
import jax.numpy as jnp
from jax import lax
from jax.experimental import pallas as pl
from jax.experimental.pallas import tpu as pltpu
from jax.sharding import PartitionSpec as P

D = 4096
HQ = 64
KVH = 4
HD = 128
TOPP = 8
QLEN = 128
PLEN = 64
RECOMP = 16
KEPT = PLEN - RECOMP
GROUPED = HQ // KVH
PAIRS = 2
PAIR_HEADS = KVH // PAIRS
PAIR_WIDTH = PAIR_HEADS * HD
HALF = KVH * HD

EPSILON = 1e-06
SCORE_FACTOR = 1.4426950408889634 / HD**0.5
SAFE_EXPONENT = 80.0
SMALL_VMEM = 12 * 1024 * 1024
VMEM_BYTES = 24 * 1024 * 1024
LITTLE = pl.CostEstimate(flops=1, bytes_accessed=1, transcendentals=0)
LARGE = pl.CostEstimate(flops=1, bytes_accessed=36_000_000, transcendentals=0)


def norm_kernel(tile, hops, hidden_ref, *rest):
    outs = rest[hops:]

    def one(step, carry):
        rows = pl.ds(pl.multiple_of(step * tile, tile), tile)
        hidden = hidden_ref[rows, :].astype(jnp.float32)
        mean = jnp.mean(hidden * hidden, axis=1, keepdims=True)
        outs[0][rows, :] = (hidden * lax.rsqrt(mean + EPSILON)).astype(jnp.bfloat16)
        return carry

    lax.fori_loop(0, hidden_ref.shape[0] // tile, one, 0)
    if hops:
        depth = rest[0].shape[0]
        outs[1][:depth, :] = rest[0][...]
        outs[1][depth:, :] = rest[1][...]
        outs[2][...] = rest[1][...]


def normalise(hidden, hops):
    shapes = [jax.ShapeDtypeStruct(hidden.shape, jnp.bfloat16)]
    if hops:
        depth, width = hops[0].shape
        shapes += [jax.ShapeDtypeStruct((rows, width), jnp.bfloat16) for rows in (2 * depth, depth)]
    vmem = pl.BlockSpec(memory_space=pltpu.VMEM)
    return pl.pallas_call(
        functools.partial(norm_kernel, 32, len(hops)),
        in_specs=[vmem] * (1 + len(hops)),
        out_specs=[vmem] * len(shapes),
        out_shape=shapes,
        compiler_params=pltpu.CompilerParams(vmem_limit_bytes=SMALL_VMEM),
        cost_estimate=LITTLE,
        name="normalise",
    )(hidden, *hops)


def find_kernel(holders, requests, pass_local, capacity, me_ref, table_ref, *rest):
    rank_ref, passage_ref, slot_ref, kept_ref = rest[-4:]
    me = me_ref[0]
    stride = table_ref.shape[0] // holders
    for k in range(holders):
        base = k * (capacity + 1)
        for rank in range(capacity + 1):
            slot_ref[base + rank] = 0
        count = jnp.int32(0)
        for request in range(requests):
            slot_ref[base + count] = request
            mine = (table_ref[k * stride + request] // pass_local == me).astype(jnp.int32)
            count = jnp.minimum(count + mine, capacity)
    spot = lax.broadcasted_iota(jnp.int32, (1, PLEN), 1)
    for k in range(holders):
        for rank in range(capacity):
            at = k * capacity + rank
            request = slot_ref[k * (capacity + 1) + rank]
            passage_ref[at] = lax.rem(table_ref[k * stride + request], pass_local)
            start = k * stride + requests + request * RECOMP
            covered = spot < 0
            for r in range(RECOMP):
                covered = covered | (spot == table_ref[start + r])
            kept_ref[at : at + 1, :] = jnp.where(covered, 0.0, 1.0)
    kept = kept_ref[...]
    upto = lax.broadcasted_iota(jnp.int32, (PLEN, PLEN), 0) <= lax.broadcasted_iota(jnp.int32, (PLEN, PLEN), 1)
    rank_of = jnp.dot(
        kept.astype(jnp.bfloat16), upto.astype(jnp.bfloat16), preferred_element_type=jnp.float32
    )
    rank_ref[...] = jnp.where(kept > 0, rank_of, 0.0)


def find_rows(table, me, holders, requests, pass_local, capacity, normed):
    slots = holders * capacity
    smem = pl.BlockSpec(memory_space=pltpu.SMEM)
    whole = pl.BlockSpec(memory_space=pl.ANY)
    return pl.pallas_call(
        functools.partial(find_kernel, holders, requests, pass_local, capacity),
        in_specs=[smem, smem, whole],
        out_specs=[pl.BlockSpec(memory_space=pltpu.VMEM), smem],
        out_shape=[jax.ShapeDtypeStruct((slots, PLEN), jnp.float32), jax.ShapeDtypeStruct((slots,), jnp.int32)],
        scratch_shapes=[pltpu.SMEM((holders * (capacity + 1),), jnp.int32), pltpu.VMEM((slots, PLEN), jnp.float32)],
        compiler_params=pltpu.CompilerParams(vmem_limit_bytes=SMALL_VMEM),
        cost_estimate=LARGE,
        name="find_rows",
    )(me, table, normed)


def pick_kernel(pieces, me_ref, passage_ref, rank_ref, cache_ref, *rest):
    out_ref = rest[-2] if pieces else rest[-1]
    start = 0
    for piece in rest[:pieces]:
        rest[-1][start : start + piece.shape[0], :] = piece[...]
        start += piece.shape[0]
    pair = me_ref[1]
    row = (lax.broadcasted_iota(jnp.int32, (KEPT, PLEN), 0) + 1).astype(jnp.float32)
    for at in range(out_ref.shape[0]):
        passage = passage_ref[at]
        select = (rank_ref[at : at + 1, :] == row).astype(jnp.bfloat16)
        for place, part in ((0, pair), (1, 1 - pair)):
            for half in range(2):
                start = pl.multiple_of(half * HALF + part * PAIR_WIDTH, PAIR_WIDTH)
                end = (place * 2 + half) * PAIR_WIDTH
                out_ref[at, :, end : end + PAIR_WIDTH] = jnp.dot(
                    select, cache_ref[passage, :, pl.ds(start, PAIR_WIDTH)], preferred_element_type=jnp.float32
                ).astype(jnp.bfloat16)


def pick_rows(me, passages, ranks, cache, pieces, ahead):
    shapes = [jax.ShapeDtypeStruct((passages.shape[0], KEPT, 2 * HALF), jnp.bfloat16)]
    if pieces:
        rows = sum(piece.shape[0] for piece in pieces)
        shapes.append(jax.ShapeDtypeStruct((rows, pieces[0].shape[1]), jnp.bfloat16))
    smem = pl.BlockSpec(memory_space=pltpu.SMEM)
    vmem = pl.BlockSpec(memory_space=pltpu.VMEM)
    return pl.pallas_call(
        functools.partial(pick_kernel, len(pieces)),
        in_specs=[smem, smem] + [vmem] * (2 + len(pieces)) + [pl.BlockSpec(memory_space=pl.ANY)] * len(ahead),
        out_specs=[vmem] * len(shapes),
        out_shape=shapes,
        compiler_params=pltpu.CompilerParams(vmem_limit_bytes=SMALL_VMEM),
        cost_estimate=LITTLE,
        name="pick_rows",
    )(me, passages, ranks, cache, *pieces, *ahead)


def project_kernel(layout, member_ref, mine_ref, other_ref, *refs):
    mine_out, other_out = refs[-2:]
    rows = mine_ref.shape[0]
    depth = D // len(layout)
    total = None
    for k, (array, start) in enumerate(layout):
        chunk = pl.ds(pl.multiple_of((member_ref[0] ^ k) * depth, depth), depth)
        both = jnp.concatenate([mine_ref[:, chunk], other_ref[:, chunk]], axis=0)
        weights = refs[array][start * depth : (start + 1) * depth, :]
        term = jnp.dot(both, weights, preferred_element_type=jnp.float32)
        total = term if total is None else total + term
    mine_out[...] = total[:rows].astype(jnp.bfloat16)
    other_out[...] = total[rows:].astype(jnp.bfloat16)


def project(member, mine, other, arrays, layout, ahead):
    rows, width = mine.shape[0], arrays[0].shape[1]
    shape = jax.ShapeDtypeStruct((rows, width), jnp.bfloat16)
    vmem = pl.BlockSpec(memory_space=pltpu.VMEM)
    return pl.pallas_call(
        functools.partial(project_kernel, layout),
        in_specs=[pl.BlockSpec(memory_space=pltpu.SMEM)]
        + [vmem] * (2 + len(arrays))
        + [pl.BlockSpec(memory_space=pl.ANY)] * len(ahead),
        out_specs=[vmem, vmem],
        out_shape=[shape, shape],
        compiler_params=pltpu.CompilerParams(vmem_limit_bytes=SMALL_VMEM),
        cost_estimate=LITTLE,
        name="project",
    )(member.reshape(1), mine, other, *arrays, *ahead)


def scaled_keys(keys, turned_ref):
    scaled = keys.astype(jnp.float32) * SCORE_FACTOR
    high = scaled.astype(jnp.bfloat16)
    turned_ref[:HD, :] = high.T
    turned_ref[HD:, :] = (scaled - high.astype(jnp.float32)).astype(jnp.bfloat16).T
    return jnp.max(jnp.sum(scaled * scaled, axis=1, keepdims=True))


def head_rows(q_ref, slot, first, heads_once):
    block = jnp.concatenate(
        [q_ref[slot, :, (first + i) * HD : (first + i + 1) * HD] for i in range(heads_once)], axis=0
    )
    return jnp.concatenate([block, block], axis=1)


def causal(rows):
    token = lax.broadcasted_iota(jnp.int32, (rows, QLEN), 0) % QLEN
    return lax.broadcasted_iota(jnp.int32, (rows, QLEN), 1) <= token


def place(step, pair):
    query, head = step // PAIR_HEADS, step % PAIR_HEADS
    rows = pl.ds(pl.multiple_of(query * QLEN, QLEN), QLEN)
    return query, head, rows, pair * PAIR_HEADS + head


def columns(start, width=HD):
    return pl.ds(pl.multiple_of(start, HD), width)


def fetch(step, pair, q_ref, block_ref, arrived_ref):
    _, _, rows, column = place(step, pair)
    wide = GROUPED * HD
    slot = step % 2
    return pltpu.make_async_copy(
        q_ref.at[rows, columns(column * wide, wide)], block_ref.at[slot], arrived_ref.at[slot]
    )


def own_kernel(steps, heads_once, passing, info_ref, q_ref, own_ref, *rest):
    sum_ref, weight_ref, bound_ref = rest[-7 - passing : -4 - passing]
    turned_ref, wide_ref, block_ref, arrived_ref = rest[-4:]
    fetch(0, info_ref[0], q_ref, block_ref, arrived_ref).start()
    bound_ref[...] = jnp.zeros_like(bound_ref)
    shown = jnp.where(causal(heads_once * QLEN), 1.0, 0.0).astype(jnp.bfloat16)
    lane = lax.broadcasted_iota(jnp.int32, (QLEN, HD), 1)

    def one(step, carry):
        _, head, rows, column = place(step, info_ref[0])
        slot = step % 2

        @pl.when(step + 1 < steps)
        def prefetch():
            fetch(step + 1, info_ref[0], q_ref, block_ref, arrived_ref).start()

        scaled_keys(own_ref[rows, columns(column * HD)], turned_ref)
        wide_ref[:, :HD] = own_ref[rows, columns(HALF + column * HD)]
        wide_ref[:, HD:] = jnp.ones((QLEN, HD), jnp.bfloat16)
        weights = jnp.zeros((QLEN, HD), jnp.float32)
        peak = jnp.zeros((QLEN, 1), jnp.float32)
        fetch(step, info_ref[0], q_ref, block_ref, arrived_ref).wait()
        for first in range(0, GROUPED, heads_once):
            scores = jnp.dot(
                head_rows(block_ref, slot, first, heads_once), turned_ref[...], preferred_element_type=jnp.float32
            )
            summed = jnp.dot(
                jnp.exp2(scores).astype(jnp.bfloat16) * shown, wide_ref[...], preferred_element_type=jnp.float32
            )
            for i in range(heads_once):
                part = summed[i * QLEN : (i + 1) * QLEN]
                sum_ref[rows, columns((head * GROUPED + first + i) * HD)] = part[:, :HD].astype(jnp.bfloat16)
                weights = jnp.where(lane == first + i, part[:, HD:], weights)
            most = None
            for i in range(heads_once):
                block = block_ref[slot, :, (first + i) * HD : (first + i + 1) * HD].astype(jnp.float32)
                most = block * block if most is None else jnp.maximum(most, block * block)
            peak = jnp.maximum(peak, jnp.sum(most, axis=1, keepdims=True))
        weight_ref[rows, columns(head * HD)] = weights
        bound_ref[...] = jnp.maximum(bound_ref[...], jnp.max(peak))
        return carry

    lax.fori_loop(0, steps, one, 0)


def attend_own(info, q_rows, own_kv, ahead, passing):
    rows = q_rows.shape[0]
    whole = pl.BlockSpec(memory_space=pl.ANY)
    vmem = pl.BlockSpec(memory_space=pltpu.VMEM)
    return pl.pallas_call(
        functools.partial(own_kernel, rows // QLEN * PAIR_HEADS, 4, len(passing)),
        in_specs=[pl.BlockSpec(memory_space=pltpu.SMEM), whole, vmem] + [whole] * (len(passing) + len(ahead)),
        out_specs=[vmem] * 3 + [whole] * len(passing),
        out_shape=[
            jax.ShapeDtypeStruct((rows, PAIR_HEADS * GROUPED * HD), jnp.bfloat16),
            jax.ShapeDtypeStruct((rows, PAIR_HEADS * HD), jnp.float32),
            jax.ShapeDtypeStruct((8, HD), jnp.float32),
        ]
        + [jax.ShapeDtypeStruct(part.shape, part.dtype) for part in passing],
        scratch_shapes=[
            pltpu.VMEM((2 * HD, QLEN), jnp.bfloat16),
            pltpu.VMEM((QLEN, 2 * HD), jnp.bfloat16),
            pltpu.VMEM((2, QLEN, GROUPED * HD), jnp.bfloat16),
            pltpu.SemaphoreType.DMA((2,)),
        ],
        input_output_aliases={3 + i: 3 + i for i in range(len(passing))},
        compiler_params=pltpu.CompilerParams(vmem_limit_bytes=VMEM_BYTES),
        cost_estimate=LITTLE,
        name="attend_own",
    )(info, q_rows, own_kv, *passing, *ahead)


def attend_kernel(
    steps,
    heads_once,
    part,
    info_ref,
    q_ref,
    own_ref,
    kept_ref,
    near_ref,
    far_ref,
    sum_ref,
    weight_ref,
    bound_ref,
    *rest,
):
    out_ref, key_ref, turned_ref, value_ref, score_ref, expd_ref, result_ref, done_ref = rest[-12:-4]
    block_ref, arrived_ref, cut_ref, cut_done_ref = rest[-4:]
    passage_keys = TOPP * PLEN
    wide = GROUPED * HD
    groups = GROUPED // heads_once
    flip = info_ref[1] > 0
    cut = pltpu.make_async_copy(kept_ref.at[:, :, part * HALF : (part + 1) * HALF], cut_ref, cut_done_ref)
    cut.start()
    fetch(0, info_ref[0], q_ref, block_ref, arrived_ref).start()
    value_ref[:, HD:] = jnp.ones((passage_keys + QLEN, HD), jnp.bfloat16)
    cut.wait()

    def leave(step):
        _, _, rows, column = place(step, info_ref[0])
        slot = step % 2
        return pltpu.make_async_copy(
            result_ref.at[slot], out_ref.at[rows, columns(column * wide, wide)], done_ref.at[slot]
        )

    def one(step, carry):
        query, head, rows, column = place(step, info_ref[0])
        slot = step % 2

        @pl.when(step >= 2)
        def free():
            leave(step - 2).wait()

        @pl.when(step + 1 < steps)
        def prefetch():
            fetch(step + 1, info_ref[0], q_ref, block_ref, arrived_ref).start()

        offset = head * HD
        for j in range(TOPP):
            block = info_ref[2 + query * TOPP + j]
            key_ref[j * KEPT : (j + 1) * KEPT, :] = cut_ref[block, :, columns(offset)]
            value_ref[j * KEPT : (j + 1) * KEPT, :HD] = cut_ref[block, :, columns(offset + PAIR_WIDTH)]
        near, far = near_ref[rows, columns(head * HD)], far_ref[rows, columns(head * HD)]
        key_ref[TOPP * KEPT : passage_keys, :] = jnp.where(flip, far, near)
        value_ref[TOPP * KEPT : passage_keys, :HD] = jnp.where(flip, near, far)
        key_ref[passage_keys:, :] = own_ref[rows, columns(column * HD)]
        value_ref[passage_keys:, :HD] = own_ref[rows, columns(HALF + column * HD)]
        key_bound = scaled_keys(key_ref[...], turned_ref)
        small = jnp.max(bound_ref[...]) * key_bound <= SAFE_EXPONENT**2

        fetch(step, info_ref[0], q_ref, block_ref, arrived_ref).wait()

        def score(group):
            score_ref[group % 2] = jnp.dot(
                head_rows(block_ref, slot, group * heads_once, heads_once),
                turned_ref[:, :passage_keys],
                preferred_element_type=jnp.float32,
            )

        def soften(group):
            expd_ref[group % 2] = jnp.exp2(score_ref[group % 2]).astype(jnp.bfloat16)

        def finish(group):
            summed = jnp.dot(
                expd_ref[group % 2], value_ref[:passage_keys, :], preferred_element_type=jnp.float32
            )
            weights = weight_ref[rows, columns(head * HD)]
            for i in range(heads_once):
                at = group * heads_once + i
                both = summed[i * QLEN : (i + 1) * QLEN]
                weight = both[:, HD:] + weights[:, at : at + 1]
                inverse = pl.reciprocal(weight, approx=True)
                inverse = inverse * (2.0 - weight * inverse)
                total = both[:, :HD] + sum_ref[rows, columns(head * wide + at * HD)].astype(jnp.float32)
                result_ref[slot, :, at * HD : (at + 1) * HD] = (total * inverse).astype(jnp.bfloat16)

        @pl.when(small)
        def unshifted():
            score(0)
            for group in range(groups):
                if group + 1 < groups:
                    score(group + 1)
                soften(group)
                if group > 0:
                    finish(group - 1)
            finish(groups - 1)

        @pl.when(jnp.logical_not(small))
        def shifted():
            visible = causal(heads_once * QLEN)
            for group in range(groups):
                scores = jnp.dot(
                    head_rows(block_ref, slot, group * heads_once, heads_once),
                    turned_ref[...],
                    preferred_element_type=jnp.float32,
                )
                scores = jnp.concatenate(
                    [scores[:, :passage_keys], jnp.where(visible, scores[:, passage_keys:], -jnp.inf)], axis=1
                )
                peak = jnp.max(scores, axis=1, keepdims=True)
                expd = jnp.exp2(scores - peak).astype(jnp.bfloat16)
                summed = jnp.dot(expd, value_ref[...], preferred_element_type=jnp.float32)
                ratio = (summed[:, :HD] / summed[:, HD:]).astype(jnp.bfloat16)
                for i in range(heads_once):
                    at = group * heads_once + i
                    result_ref[slot, :, at * HD : (at + 1) * HD] = ratio[i * QLEN : (i + 1) * QLEN]

        leave(step).start()
        return carry

    lax.fori_loop(0, steps, one, 0)
    for step in range(max(steps - 2, 0), steps):
        leave(step).wait()


def attend(part, info, q_rows, own_kv, kept, near, far, own, earlier=None):
    rows, width = q_rows.shape
    span = TOPP * PLEN + QLEN
    heads_once = 2
    vmem = pl.BlockSpec(memory_space=pltpu.VMEM)
    whole = pl.BlockSpec(memory_space=pl.ANY)
    operands = [info, q_rows, own_kv, kept, near, far, *own]
    aliases = {}
    if earlier is not None:
        aliases = {len(operands): 0}
        operands.append(earlier)
    return pl.pallas_call(
        functools.partial(attend_kernel, rows // QLEN * PAIR_HEADS, heads_once, part),
        in_specs=[pl.BlockSpec(memory_space=pltpu.SMEM), whole, vmem, whole] + [vmem] * 5 + [whole] * len(aliases),
        out_specs=whole,
        out_shape=jax.ShapeDtypeStruct((rows, width), jnp.bfloat16),
        scratch_shapes=[
            pltpu.VMEM((span, HD), jnp.bfloat16),
            pltpu.VMEM((2 * HD, span), jnp.bfloat16),
            pltpu.VMEM((span, 2 * HD), jnp.bfloat16),
            pltpu.VMEM((2, heads_once * QLEN, TOPP * PLEN), jnp.float32),
            pltpu.VMEM((2, heads_once * QLEN, TOPP * PLEN), jnp.bfloat16),
            pltpu.VMEM((2, QLEN, GROUPED * HD), jnp.bfloat16),
            pltpu.SemaphoreType.DMA((2,)),
            pltpu.VMEM((2, QLEN, GROUPED * HD), jnp.bfloat16),
            pltpu.SemaphoreType.DMA((2,)),
            pltpu.VMEM((kept.shape[0], KEPT, HALF), jnp.bfloat16),
            pltpu.SemaphoreType.DMA,
        ],
        input_output_aliases=aliases,
        compiler_params=pltpu.CompilerParams(vmem_limit_bytes=VMEM_BYTES),
        cost_estimate=LITTLE,
        name="attend",
    )(*operands)


def swap(array, axis, bits):
    size = lax.axis_size(axis)
    return lax.ppermute(array, axis, [(i, i ^ bits) for i in range(size)])


def recompute_general(normed, w_kv, pair):
    whole = lax.all_gather(lax.all_gather(w_kv, "member", axis=0, tiled=True), "group", axis=1, tiled=True)
    result = jnp.dot(normed, whole, preferred_element_type=jnp.float32).astype(jnp.bfloat16)
    result = result.reshape(-1, 2, PAIRS, PAIR_WIDTH)
    first = jnp.where(pair == 0, result[:, :, 0], result[:, :, 1])
    second = jnp.where(pair == 0, result[:, :, 1], result[:, :, 0])
    return [first[:, 0], first[:, 1]], [second[:, 0], second[:, 1]]


def local(q_rows, own_kv, cache, recomp_hidden, w_kv, retrieval, positions):
    queries = retrieval.shape[0]
    requests = queries * TOPP
    holders = lax.axis_size("member")
    groups = lax.axis_size("group")
    pass_local = cache.shape[0]
    capacity = -(-requests // holders)
    member = lax.axis_index("member")
    group = lax.axis_index("group")
    pair = group % PAIRS
    tuned = groups == 4 and holders == 8
    wanted = retrieval.reshape(requests)
    request = jnp.concatenate([wanted, positions.reshape(requests * RECOMP)])
    request = jnp.pad(request, (0, -request.shape[0] % 128)).reshape(1, -1, 128)
    request = jnp.broadcast_to(request, (holders,) + request.shape[1:])
    table = lax.all_to_all(request, "member", split_axis=0, concat_axis=0, tiled=True).reshape(-1)
    hidden = recomp_hidden.reshape(requests * RECOMP, D)
    hops = [swap(w_kv, "member", bits) for bits in (2, 4)] if tuned else []
    normed, *hops = normalise(hidden, hops)
    me = jnp.stack([member, pair]).astype(jnp.int32)
    ranks, passages = find_rows(table, me, holders, requests, pass_local, capacity, normed)
    holder_of = wanted // pass_local
    same = holder_of[:, None] == holder_of[None, :]
    before = jnp.arange(requests)[None, :] < jnp.arange(requests)[:, None]
    slot = holder_of * capacity + jnp.sum((same & before).astype(jnp.int32), axis=1)
    flip = group // 2 if tuned else jnp.int32(0)
    info = jnp.concatenate([jnp.stack([pair, flip]), slot]).astype(jnp.int32)
    other_info = jnp.concatenate([jnp.stack([1 - pair, flip]), slot]).astype(jnp.int32)
    first_own = attend_own(info, q_rows, own_kv, [ranks], [])
    pieces, ahead, three = [], [first_own[0]], []
    if tuned:
        stack, two = hops
        aside, across = swap(w_kv, "member", 1), swap(w_kv, "group", 2)
        three = [swap(two, "member", 2)]
        stack_aside, stack_across = swap(stack, "member", 1), swap(stack, "group", 2)
        pieces = [aside, stack_aside, three[0]]
        ahead += [across, stack_across]
    sent, *rest = pick_rows(me, passages, ranks, cache, pieces, ahead)
    arrived = lax.all_to_all(
        sent.reshape(holders, capacity * KEPT, 2 * HALF), "member", split_axis=0, concat_axis=0, tiled=True
    ).reshape(sent.shape)
    second_own = attend_own(other_info, q_rows, own_kv, [sent], three)
    if tuned:
        other = swap(normed, "group", 1)
        rest_across = swap(rest[0], "group", 2)
        beside_three = swap(second_own[3], "member", 1)
        far_three = swap(beside_three, "group", 2)
        near, near_other = project(
            member,
            normed,
            other,
            [w_kv, aside, stack, stack_aside, second_own[3], beside_three],
            ((0, 0), (1, 0), (2, 0), (3, 0), (2, 1), (3, 1), (4, 0), (5, 0)),
            [second_own[0]],
        )
        far, far_other = project(
            member,
            normed,
            other,
            [across, stack_across, rest_across, far_three],
            ((0, 0), (2, 0), (1, 0), (2, 1), (1, 1), (2, 2), (2, 3), (3, 0)),
            [near],
        )
        first = [near, far]
        second = [swap(near_other, "group", 1), swap(far_other, "group", 1)]
    else:
        first, second = recompute_general(normed, w_kv, pair)
    out = attend(0, info, q_rows, own_kv, arrived, *first, first_own[:3])
    return attend(1, other_info, q_rows, own_kv, arrived, *second, second_own[:3], earlier=out)


def solution(mesh):
    rows = P(("group", "member"), None)
    placed = (
        rows,
        rows,
        P(("group", "member"), None, None),
        P(("group", "member"), None, None, None),
        P("member", "group"),
        rows,
        P(("group", "member"), None, None),
    )
    return jax.shard_map(local, mesh=mesh, in_specs=placed, out_specs=rows, check_vma=False)
```

```python
import functools

import jax
import jax.numpy as jnp
from jax import lax
from jax.experimental import pallas as pl
from jax.experimental.pallas import tpu as pltpu
from jax.sharding import PartitionSpec as P

D = 4096
HQ = 64
KVH = 4
HD = 128
TOPP = 8
QLEN = 128
PLEN = 64
RECOMP = 16
KEPT = PLEN - RECOMP
GROUPED = HQ // KVH
PAIRS = 2
PAIR_HEADS = KVH // PAIRS
PAIR_WIDTH = PAIR_HEADS * HD
HALF = KVH * HD

EPSILON = 1e-06
SCORE_FACTOR = 1.4426950408889634 / HD**0.5
SAFE_EXPONENT = 80.0
SMALL_VMEM = 12 * 1024 * 1024
VMEM_BYTES = 58 * 1024 * 1024
LITTLE = pl.CostEstimate(flops=1, bytes_accessed=1, transcendentals=0)
LARGE = pl.CostEstimate(flops=1, bytes_accessed=36_000_000, transcendentals=0)


def norm_kernel(tile, hidden_ref, *rest):
    normed_ref = rest[-1]

    def one(step, carry):
        rows = pl.ds(pl.multiple_of(step * tile, tile), tile)
        hidden = hidden_ref[rows, :].astype(jnp.float32)
        mean = jnp.mean(hidden * hidden, axis=1, keepdims=True)
        normed_ref[rows, :] = (hidden * lax.rsqrt(mean + EPSILON)).astype(jnp.bfloat16)
        return carry

    lax.fori_loop(0, hidden_ref.shape[0] // tile, one, 0)


def normalise(hidden, ahead):
    vmem = pl.BlockSpec(memory_space=pltpu.VMEM)
    return pl.pallas_call(
        functools.partial(norm_kernel, 32),
        in_specs=[vmem] + [pl.BlockSpec(memory_space=pl.ANY)] * len(ahead),
        out_specs=vmem,
        out_shape=jax.ShapeDtypeStruct(hidden.shape, jnp.bfloat16),
        compiler_params=pltpu.CompilerParams(vmem_limit_bytes=SMALL_VMEM),
        cost_estimate=LITTLE,
        name="normalise",
    )(hidden, *ahead)


def stack_kernel(one_ref, two_ref, stack_ref, copy_ref):
    depth = one_ref.shape[0]
    stack_ref[:depth, :] = one_ref[...]
    stack_ref[depth:, :] = two_ref[...]
    copy_ref[...] = two_ref[...]


def stack_hops(one, two):
    depth, width = one.shape
    vmem = pl.BlockSpec(memory_space=pltpu.VMEM)
    return pl.pallas_call(
        stack_kernel,
        in_specs=[vmem, vmem],
        out_specs=[vmem, vmem],
        out_shape=[jax.ShapeDtypeStruct((rows, width), jnp.bfloat16) for rows in (2 * depth, depth)],
        compiler_params=pltpu.CompilerParams(vmem_limit_bytes=SMALL_VMEM),
        cost_estimate=LITTLE,
        name="stack_hops",
    )(one, two)


def find_kernel(holders, requests, pass_local, capacity, me_ref, table_ref, *rest):
    rank_ref, passage_ref, slot_ref, kept_ref = rest[-4:]
    me = me_ref[0]
    stride = table_ref.shape[0] // holders
    for k in range(holders):
        base = k * (capacity + 1)
        for rank in range(capacity + 1):
            slot_ref[base + rank] = 0
        count = jnp.int32(0)
        for request in range(requests):
            slot_ref[base + count] = request
            mine = (table_ref[k * stride + request] // pass_local == me).astype(jnp.int32)
            count = jnp.minimum(count + mine, capacity)
    spot = lax.broadcasted_iota(jnp.int32, (1, PLEN), 1)
    for k in range(holders):
        for rank in range(capacity):
            at = k * capacity + rank
            request = slot_ref[k * (capacity + 1) + rank]
            passage_ref[at] = lax.rem(table_ref[k * stride + request], pass_local)
            start = k * stride + requests + request * RECOMP
            covered = spot < 0
            for r in range(RECOMP):
                covered = covered | (spot == table_ref[start + r])
            kept_ref[at : at + 1, :] = jnp.where(covered, 0.0, 1.0)
    kept = kept_ref[...]
    upto = lax.broadcasted_iota(jnp.int32, (PLEN, PLEN), 0) <= lax.broadcasted_iota(jnp.int32, (PLEN, PLEN), 1)
    rank_of = jnp.dot(
        kept.astype(jnp.bfloat16), upto.astype(jnp.bfloat16), preferred_element_type=jnp.float32
    )
    rank_ref[...] = jnp.where(kept > 0, rank_of, 0.0)


def find_rows(table, me, holders, requests, pass_local, capacity, normed):
    slots = holders * capacity
    smem = pl.BlockSpec(memory_space=pltpu.SMEM)
    whole = pl.BlockSpec(memory_space=pl.ANY)
    return pl.pallas_call(
        functools.partial(find_kernel, holders, requests, pass_local, capacity),
        in_specs=[smem, smem, whole],
        out_specs=[pl.BlockSpec(memory_space=pltpu.VMEM), smem],
        out_shape=[jax.ShapeDtypeStruct((slots, PLEN), jnp.float32), jax.ShapeDtypeStruct((slots,), jnp.int32)],
        scratch_shapes=[pltpu.SMEM((holders * (capacity + 1),), jnp.int32), pltpu.VMEM((slots, PLEN), jnp.float32)],
        compiler_params=pltpu.CompilerParams(vmem_limit_bytes=SMALL_VMEM),
        cost_estimate=LARGE,
        name="find_rows",
    )(me, table, normed)


def pick_kernel(pieces, me_ref, passage_ref, rank_ref, cache_ref, *rest):
    out_ref = rest[-2] if pieces else rest[-1]
    start = 0
    for piece in rest[:pieces]:
        rest[-1][start : start + piece.shape[0], :] = piece[...]
        start += piece.shape[0]
    pair = me_ref[1]
    row = (lax.broadcasted_iota(jnp.int32, (KEPT, PLEN), 0) + 1).astype(jnp.float32)
    for at in range(out_ref.shape[0]):
        passage = passage_ref[at]
        select = (rank_ref[at : at + 1, :] == row).astype(jnp.bfloat16)
        for place, part in ((0, pair), (1, 1 - pair)):
            for half in range(2):
                start = pl.multiple_of(half * HALF + part * PAIR_WIDTH, PAIR_WIDTH)
                end = (place * 2 + half) * PAIR_WIDTH
                out_ref[at, :, end : end + PAIR_WIDTH] = jnp.dot(
                    select, cache_ref[passage, :, pl.ds(start, PAIR_WIDTH)], preferred_element_type=jnp.float32
                ).astype(jnp.bfloat16)


def pick_rows(me, passages, ranks, cache, pieces, ahead):
    shapes = [jax.ShapeDtypeStruct((passages.shape[0], KEPT, 2 * HALF), jnp.bfloat16)]
    if pieces:
        rows = sum(piece.shape[0] for piece in pieces)
        shapes.append(jax.ShapeDtypeStruct((rows, pieces[0].shape[1]), jnp.bfloat16))
    smem = pl.BlockSpec(memory_space=pltpu.SMEM)
    vmem = pl.BlockSpec(memory_space=pltpu.VMEM)
    return pl.pallas_call(
        functools.partial(pick_kernel, len(pieces)),
        in_specs=[smem, smem] + [vmem] * (2 + len(pieces)) + [pl.BlockSpec(memory_space=pl.ANY)] * len(ahead),
        out_specs=[vmem] * len(shapes),
        out_shape=shapes,
        compiler_params=pltpu.CompilerParams(vmem_limit_bytes=SMALL_VMEM),
        cost_estimate=LITTLE,
        name="pick_rows",
    )(me, passages, ranks, cache, *pieces, *ahead)


def project_kernel(layout, member_ref, mine_ref, other_ref, *refs):
    mine_out, other_out = refs[-2:]
    rows = mine_ref.shape[0]
    depth = D // len(layout)
    total = None
    for k, (array, start) in enumerate(layout):
        chunk = pl.ds(pl.multiple_of((member_ref[0] ^ k) * depth, depth), depth)
        both = jnp.concatenate([mine_ref[:, chunk], other_ref[:, chunk]], axis=0)
        weights = refs[array][start * depth : (start + 1) * depth, :]
        term = jnp.dot(both, weights, preferred_element_type=jnp.float32)
        total = term if total is None else total + term
    mine_out[...] = total[:rows].astype(jnp.bfloat16)
    other_out[...] = total[rows:].astype(jnp.bfloat16)


def project(member, mine, other, arrays, layout, ahead):
    rows, width = mine.shape[0], arrays[0].shape[1]
    shape = jax.ShapeDtypeStruct((rows, width), jnp.bfloat16)
    vmem = pl.BlockSpec(memory_space=pltpu.VMEM)
    return pl.pallas_call(
        functools.partial(project_kernel, layout),
        in_specs=[pl.BlockSpec(memory_space=pltpu.SMEM)]
        + [vmem] * (2 + len(arrays))
        + [pl.BlockSpec(memory_space=pl.ANY)] * len(ahead),
        out_specs=[vmem, vmem],
        out_shape=[shape, shape],
        compiler_params=pltpu.CompilerParams(vmem_limit_bytes=SMALL_VMEM),
        cost_estimate=LITTLE,
        name="project",
    )(member.reshape(1), mine, other, *arrays, *ahead)


def scaled_keys(keys, turned_ref):
    scaled = keys.astype(jnp.float32) * SCORE_FACTOR
    high = scaled.astype(jnp.bfloat16)
    turned_ref[:HD, :] = high.T
    turned_ref[HD:, :] = (scaled - high.astype(jnp.float32)).astype(jnp.bfloat16).T
    return jnp.max(jnp.sum(scaled * scaled, axis=1, keepdims=True))


def head_rows(q_ref, slot, first, heads_once):
    block = jnp.concatenate(
        [q_ref[slot, :, (first + i) * HD : (first + i + 1) * HD] for i in range(heads_once)], axis=0
    )
    return jnp.concatenate([block, block], axis=1)


def causal(rows):
    token = lax.broadcasted_iota(jnp.int32, (rows, QLEN), 0) % QLEN
    return lax.broadcasted_iota(jnp.int32, (rows, QLEN), 1) <= token


def place(step, pair):
    query, head = step // PAIR_HEADS, step % PAIR_HEADS
    rows = pl.ds(pl.multiple_of(query * QLEN, QLEN), QLEN)
    return query, head, rows, pair * PAIR_HEADS + head


def columns(start, width=HD):
    return pl.ds(pl.multiple_of(start, HD), width)


def fetch(step, start, array_ref, block_ref, arrived_ref):
    _, _, rows, _ = place(step, 0)
    wide, slot = GROUPED * HD, step % 2
    column = start + (step % PAIR_HEADS) * wide
    return pltpu.make_async_copy(
        array_ref.at[rows, columns(column, wide)], block_ref.at[slot], arrived_ref.at[slot]
    )


def leave(step, start, block_ref, array_ref, done_ref):
    _, _, rows, _ = place(step, 0)
    wide, slot = GROUPED * HD, step % 2
    column = start + (step % PAIR_HEADS) * wide
    return pltpu.make_async_copy(
        block_ref.at[slot], array_ref.at[rows, columns(column, wide)], done_ref.at[slot]
    )


def own_kernel(steps, heads_once, passing, info_ref, q_ref, own_hbm_ref, *rest):
    sum_ref, weight_ref, bound_ref = rest[-11 - passing : -8 - passing]
    turned_ref, wide_ref, block_ref, arrived_ref, own_ref, own_done_ref, part_ref, part_done_ref = rest[-8:]
    start = info_ref[0] * (PAIR_HEADS * GROUPED * HD)
    own = pltpu.make_async_copy(own_hbm_ref, own_ref, own_done_ref)
    own.start()
    fetch(0, start, q_ref, block_ref, arrived_ref).start()
    bound_ref[...] = jnp.zeros_like(bound_ref)
    shown = jnp.where(causal(heads_once * QLEN), 1.0, 0.0).astype(jnp.bfloat16)
    lane = lax.broadcasted_iota(jnp.int32, (QLEN, HD), 1)
    own.wait()

    def one(step, carry):
        _, head, rows, column = place(step, info_ref[0])
        slot = step % 2

        @pl.when(step + 1 < steps)
        def prefetch():
            fetch(step + 1, start, q_ref, block_ref, arrived_ref).start()

        @pl.when(step >= 2)
        def free():
            leave(step - 2, 0, part_ref, sum_ref, part_done_ref).wait()

        scaled_keys(own_ref[rows, columns(column * HD)], turned_ref)
        wide_ref[:, :HD] = own_ref[rows, columns(HALF + column * HD)]
        wide_ref[:, HD:] = jnp.ones((QLEN, HD), jnp.bfloat16)
        weights = jnp.zeros((QLEN, HD), jnp.float32)
        peak = jnp.zeros((QLEN, 1), jnp.float32)
        fetch(step, start, q_ref, block_ref, arrived_ref).wait()
        for first in range(0, GROUPED, heads_once):
            scores = jnp.dot(
                head_rows(block_ref, slot, first, heads_once), turned_ref[...], preferred_element_type=jnp.float32
            )
            summed = jnp.dot(
                jnp.exp2(scores).astype(jnp.bfloat16) * shown, wide_ref[...], preferred_element_type=jnp.float32
            )
            for i in range(heads_once):
                part = summed[i * QLEN : (i + 1) * QLEN]
                part_ref[slot, :, (first + i) * HD : (first + i + 1) * HD] = part[:, :HD].astype(jnp.bfloat16)
                weights = jnp.where(lane == first + i, part[:, HD:], weights)
            most = None
            for i in range(heads_once):
                block = block_ref[slot, :, (first + i) * HD : (first + i + 1) * HD].astype(jnp.float32)
                most = block * block if most is None else jnp.maximum(most, block * block)
            peak = jnp.maximum(peak, jnp.sum(most, axis=1, keepdims=True))
        weight_ref[rows, columns(head * HD)] = weights
        bound_ref[...] = jnp.maximum(bound_ref[...], jnp.max(peak))
        leave(step, 0, part_ref, sum_ref, part_done_ref).start()
        return carry

    lax.fori_loop(0, steps, one, 0)
    for step in range(max(steps - 2, 0), steps):
        leave(step, 0, part_ref, sum_ref, part_done_ref).wait()


def attend_own(info, q_rows, own_kv, ahead, passing):
    rows = q_rows.shape[0]
    whole = pl.BlockSpec(memory_space=pl.ANY)
    hbm = pl.BlockSpec(memory_space=pltpu.HBM)
    vmem = pl.BlockSpec(memory_space=pltpu.VMEM)
    return pl.pallas_call(
        functools.partial(own_kernel, rows // QLEN * PAIR_HEADS, 4, len(passing)),
        in_specs=[pl.BlockSpec(memory_space=pltpu.SMEM), hbm, hbm] + [whole] * (len(passing) + len(ahead)),
        out_specs=[hbm, vmem, vmem] + [whole] * len(passing),
        out_shape=[
            jax.ShapeDtypeStruct((rows, PAIR_HEADS * GROUPED * HD), jnp.bfloat16),
            jax.ShapeDtypeStruct((rows, PAIR_HEADS * HD), jnp.float32),
            jax.ShapeDtypeStruct((8, HD), jnp.float32),
        ]
        + [jax.ShapeDtypeStruct(part.shape, part.dtype) for part in passing],
        scratch_shapes=[
            pltpu.VMEM((2 * HD, QLEN), jnp.bfloat16),
            pltpu.VMEM((QLEN, 2 * HD), jnp.bfloat16),
            pltpu.VMEM((2, QLEN, GROUPED * HD), jnp.bfloat16),
            pltpu.SemaphoreType.DMA((2,)),
            pltpu.VMEM(own_kv.shape, jnp.bfloat16),
            pltpu.SemaphoreType.DMA,
            pltpu.VMEM((2, QLEN, GROUPED * HD), jnp.bfloat16),
            pltpu.SemaphoreType.DMA((2,)),
        ],
        input_output_aliases={3 + i: 3 + i for i in range(len(passing))},
        compiler_params=pltpu.CompilerParams(vmem_limit_bytes=VMEM_BYTES),
        cost_estimate=LITTLE,
        name="attend_own",
    )(info, q_rows, own_kv, *passing, *ahead)


def attend_kernel(
    steps,
    heads_once,
    part,
    info_ref,
    q_ref,
    own_hbm_ref,
    kept_ref,
    near_ref,
    far_ref,
    sum_ref,
    weight_ref,
    bound_ref,
    *rest,
):
    out_ref, key_ref, turned_ref, value_ref, score_ref, expd_ref, result_ref, done_ref = rest[-16:-8]
    block_ref, arrived_ref, cut_ref, cut_done_ref, own_ref, own_done_ref, part_ref, part_done_ref = rest[-8:]
    passage_keys = TOPP * PLEN
    wide = GROUPED * HD
    groups = GROUPED // heads_once
    flip = info_ref[1] > 0
    cut = pltpu.make_async_copy(kept_ref.at[:, :, part * HALF : (part + 1) * HALF], cut_ref, cut_done_ref)
    cut.start()
    own = pltpu.make_async_copy(own_hbm_ref, own_ref, own_done_ref)
    own.start()
    start = info_ref[0] * (PAIR_HEADS * wide)
    fetch(0, start, q_ref, block_ref, arrived_ref).start()
    fetch(0, 0, sum_ref, part_ref, part_done_ref).start()
    value_ref[:, HD:] = jnp.ones((passage_keys + QLEN, HD), jnp.bfloat16)
    cut.wait()
    own.wait()

    def one(step, carry):
        query, head, rows, column = place(step, info_ref[0])
        slot = step % 2

        @pl.when(step >= 2)
        def free():
            leave(step - 2, start, result_ref, out_ref, done_ref).wait()

        @pl.when(step + 1 < steps)
        def prefetch():
            fetch(step + 1, start, q_ref, block_ref, arrived_ref).start()
            fetch(step + 1, 0, sum_ref, part_ref, part_done_ref).start()

        offset = head * HD
        for j in range(TOPP):
            block = info_ref[2 + query * TOPP + j]
            key_ref[j * KEPT : (j + 1) * KEPT, :] = cut_ref[block, :, columns(offset)]
            value_ref[j * KEPT : (j + 1) * KEPT, :HD] = cut_ref[block, :, columns(offset + PAIR_WIDTH)]
        near, far = near_ref[rows, columns(head * HD)], far_ref[rows, columns(head * HD)]
        key_ref[TOPP * KEPT : passage_keys, :] = jnp.where(flip, far, near)
        value_ref[TOPP * KEPT : passage_keys, :HD] = jnp.where(flip, near, far)
        key_ref[passage_keys:, :] = own_ref[rows, columns(column * HD)]
        value_ref[passage_keys:, :HD] = own_ref[rows, columns(HALF + column * HD)]
        key_bound = scaled_keys(key_ref[...], turned_ref)
        small = jnp.max(bound_ref[...]) * key_bound <= SAFE_EXPONENT**2

        fetch(step, start, q_ref, block_ref, arrived_ref).wait()
        fetch(step, 0, sum_ref, part_ref, part_done_ref).wait()

        def score(group):
            score_ref[group % 2] = jnp.dot(
                head_rows(block_ref, slot, group * heads_once, heads_once),
                turned_ref[:, :passage_keys],
                preferred_element_type=jnp.float32,
            )

        def soften(group):
            expd_ref[group % 2] = jnp.exp2(score_ref[group % 2]).astype(jnp.bfloat16)

        def finish(group):
            summed = jnp.dot(
                expd_ref[group % 2], value_ref[:passage_keys, :], preferred_element_type=jnp.float32
            )
            weights = weight_ref[rows, columns(head * HD)]
            for i in range(heads_once):
                at = group * heads_once + i
                both = summed[i * QLEN : (i + 1) * QLEN]
                weight = both[:, HD:] + weights[:, at : at + 1]
                inverse = pl.reciprocal(weight, approx=True)
                inverse = inverse * (2.0 - weight * inverse)
                total = both[:, :HD] + part_ref[slot, :, at * HD : (at + 1) * HD].astype(jnp.float32)
                result_ref[slot, :, at * HD : (at + 1) * HD] = (total * inverse).astype(jnp.bfloat16)

        @pl.when(small)
        def unshifted():
            score(0)
            for group in range(groups):
                if group + 1 < groups:
                    score(group + 1)
                soften(group)
                if group > 0:
                    finish(group - 1)
            finish(groups - 1)

        @pl.when(jnp.logical_not(small))
        def shifted():
            visible = causal(heads_once * QLEN)
            for group in range(groups):
                scores = jnp.dot(
                    head_rows(block_ref, slot, group * heads_once, heads_once),
                    turned_ref[...],
                    preferred_element_type=jnp.float32,
                )
                scores = jnp.concatenate(
                    [scores[:, :passage_keys], jnp.where(visible, scores[:, passage_keys:], -jnp.inf)], axis=1
                )
                peak = jnp.max(scores, axis=1, keepdims=True)
                expd = jnp.exp2(scores - peak).astype(jnp.bfloat16)
                summed = jnp.dot(expd, value_ref[...], preferred_element_type=jnp.float32)
                ratio = (summed[:, :HD] / summed[:, HD:]).astype(jnp.bfloat16)
                for i in range(heads_once):
                    at = group * heads_once + i
                    result_ref[slot, :, at * HD : (at + 1) * HD] = ratio[i * QLEN : (i + 1) * QLEN]

        leave(step, start, result_ref, out_ref, done_ref).start()
        return carry

    lax.fori_loop(0, steps, one, 0)
    for step in range(max(steps - 2, 0), steps):
        leave(step, start, result_ref, out_ref, done_ref).wait()


def attend(part, info, q_rows, own_kv, kept, near, far, own, earlier=None):
    rows, width = q_rows.shape
    span = TOPP * PLEN + QLEN
    heads_once = 2
    vmem = pl.BlockSpec(memory_space=pltpu.VMEM)
    whole = pl.BlockSpec(memory_space=pl.ANY)
    hbm = pl.BlockSpec(memory_space=pltpu.HBM)
    operands = [info, q_rows, own_kv, kept, near, far, *own]
    aliases = {}
    if earlier is not None:
        aliases = {len(operands): 0}
        operands.append(earlier)
    return pl.pallas_call(
        functools.partial(attend_kernel, rows // QLEN * PAIR_HEADS, heads_once, part),
        in_specs=[pl.BlockSpec(memory_space=pltpu.SMEM)] + [hbm] * 3
        + [vmem] * 2
        + [hbm]
        + [vmem] * 2
        + [whole] * len(aliases),
        out_specs=whole,
        out_shape=jax.ShapeDtypeStruct((rows, width), jnp.bfloat16),
        scratch_shapes=[
            pltpu.VMEM((span, HD), jnp.bfloat16),
            pltpu.VMEM((2 * HD, span), jnp.bfloat16),
            pltpu.VMEM((span, 2 * HD), jnp.bfloat16),
            pltpu.VMEM((2, heads_once * QLEN, TOPP * PLEN), jnp.float32),
            pltpu.VMEM((2, heads_once * QLEN, TOPP * PLEN), jnp.bfloat16),
            pltpu.VMEM((2, QLEN, GROUPED * HD), jnp.bfloat16),
            pltpu.SemaphoreType.DMA((2,)),
            pltpu.VMEM((2, QLEN, GROUPED * HD), jnp.bfloat16),
            pltpu.SemaphoreType.DMA((2,)),
            pltpu.VMEM((kept.shape[0], KEPT, HALF), jnp.bfloat16),
            pltpu.SemaphoreType.DMA,
            pltpu.VMEM(own_kv.shape, jnp.bfloat16),
            pltpu.SemaphoreType.DMA,
            pltpu.VMEM((2, QLEN, GROUPED * HD), jnp.bfloat16),
            pltpu.SemaphoreType.DMA((2,)),
        ],
        input_output_aliases=aliases,
        compiler_params=pltpu.CompilerParams(vmem_limit_bytes=VMEM_BYTES),
        cost_estimate=LITTLE,
        name="attend",
    )(*operands)


def swap(array, axis, bits):
    size = lax.axis_size(axis)
    return lax.ppermute(array, axis, [(i, i ^ bits) for i in range(size)])


def recompute_general(normed, w_kv, pair):
    whole = lax.all_gather(lax.all_gather(w_kv, "member", axis=0, tiled=True), "group", axis=1, tiled=True)
    result = jnp.dot(normed, whole, preferred_element_type=jnp.float32).astype(jnp.bfloat16)
    result = result.reshape(-1, 2, PAIRS, PAIR_WIDTH)
    first = jnp.where(pair == 0, result[:, :, 0], result[:, :, 1])
    second = jnp.where(pair == 0, result[:, :, 1], result[:, :, 0])
    return [first[:, 0], first[:, 1]], [second[:, 0], second[:, 1]]


def local(q_rows, own_kv, cache, recomp_hidden, w_kv, retrieval, positions):
    queries = retrieval.shape[0]
    requests = queries * TOPP
    holders = lax.axis_size("member")
    groups = lax.axis_size("group")
    pass_local = cache.shape[0]
    capacity = -(-requests // holders)
    member = lax.axis_index("member")
    group = lax.axis_index("group")
    pair = group % PAIRS
    tuned = groups == 4 and holders == 8
    wanted = retrieval.reshape(requests)
    request = jnp.concatenate([wanted, positions.reshape(requests * RECOMP)])
    request = jnp.pad(request, (0, -request.shape[0] % 128)).reshape(1, -1, 128)
    request = jnp.broadcast_to(request, (holders,) + request.shape[1:])
    table = lax.all_to_all(request, "member", split_axis=0, concat_axis=0, tiled=True).reshape(-1)
    hidden = recomp_hidden.reshape(requests * RECOMP, D)
    hops = stack_hops(swap(w_kv, "member", 2), swap(w_kv, "member", 4)) if tuned else []
    normed = normalise(hidden, hops[:1])
    me = jnp.stack([member, pair]).astype(jnp.int32)
    ranks, passages = find_rows(table, me, holders, requests, pass_local, capacity, normed)
    holder_of = wanted // pass_local
    same = holder_of[:, None] == holder_of[None, :]
    before = jnp.arange(requests)[None, :] < jnp.arange(requests)[:, None]
    slot = holder_of * capacity + jnp.sum((same & before).astype(jnp.int32), axis=1)
    flip = group // 2 if tuned else jnp.int32(0)
    info = jnp.concatenate([jnp.stack([pair, flip]), slot]).astype(jnp.int32)
    other_info = jnp.concatenate([jnp.stack([1 - pair, flip]), slot]).astype(jnp.int32)
    first_own = attend_own(info, q_rows, own_kv, [ranks], [])
    pieces, ahead, beside_three = [], [first_own[0]], []
    if tuned:
        stack, two = hops
        aside, across = swap(w_kv, "member", 1), swap(w_kv, "group", 2)
        three = [swap(two, "member", 2)]
        stack_aside, stack_across = swap(stack, "member", 1), swap(stack, "group", 2)
        pieces = [aside, stack_aside, three[0]]
        ahead += [across, stack_across]
    sent, *rest = pick_rows(me, passages, ranks, cache, pieces, ahead)
    arrived = lax.all_to_all(
        sent.reshape(holders, capacity * KEPT, 2 * HALF), "member", split_axis=0, concat_axis=0, tiled=True
    ).reshape(sent.shape)
    if tuned:
        beside_three = [swap(three[0], "member", 1)]
    second_own = attend_own(other_info, q_rows, own_kv, [sent], beside_three)
    if tuned:
        other = swap(normed, "group", 1)
        rest_across = swap(rest[0], "group", 2)
        far_three = swap(second_own[3], "group", 2)
        near, near_other = project(
            member,
            normed,
            other,
            [w_kv, aside, stack, stack_aside, three[0], second_own[3]],
            ((0, 0), (1, 0), (2, 0), (3, 0), (2, 1), (3, 1), (4, 0), (5, 0)),
            [second_own[0]],
        )
        far, far_other = project(
            member,
            normed,
            other,
            [across, stack_across, rest_across, far_three],
            ((0, 0), (2, 0), (1, 0), (2, 1), (1, 1), (2, 2), (2, 3), (3, 0)),
            [near],
        )
        first = [near, far]
        second = [swap(near_other, "group", 1), swap(far_other, "group", 1)]
    else:
        first, second = recompute_general(normed, w_kv, pair)
    out = attend(0, info, q_rows, own_kv, arrived, *first, first_own[:3])
    return attend(1, other_info, q_rows, own_kv, arrived, *second, second_own[:3], earlier=out)


def solution(mesh):
    rows = P(("group", "member"), None)
    placed = (
        rows,
        rows,
        P(("group", "member"), None, None),
        P(("group", "member"), None, None, None),
        P("member", "group"),
        rows,
        P(("group", "member"), None, None),
    )
    return jax.shard_map(local, mesh=mesh, in_specs=placed, out_specs=rows, check_vma=False)
```

```python
import functools

import jax
import jax.numpy as jnp
from jax import lax
from jax.experimental import pallas as pl
from jax.experimental.pallas import tpu as pltpu
from jax.sharding import PartitionSpec as P

D = 4096
HQ = 64
KVH = 4
HD = 128
TOPP = 8
QLEN = 128
PLEN = 64
RECOMP = 16
KEPT = PLEN - RECOMP
GROUPED = HQ // KVH
PAIRS = 2
PAIR_HEADS = KVH // PAIRS
PAIR_WIDTH = PAIR_HEADS * HD
HALF = KVH * HD

EPSILON = 1e-06
SCORE_FACTOR = 1.4426950408889634 / HD**0.5
SAFE_EXPONENT = 80.0
SMALL_VMEM = 12 * 1024 * 1024
VMEM_BYTES = 56 * 1024 * 1024
PIECES = 4
LITTLE = pl.CostEstimate(flops=1, bytes_accessed=1, transcendentals=0)
LARGE = pl.CostEstimate(flops=1, bytes_accessed=36_000_000, transcendentals=0)


def norm_kernel(tile, hidden_ref, *rest):
    normed_ref = rest[-1]

    def one(step, carry):
        rows = pl.ds(pl.multiple_of(step * tile, tile), tile)
        hidden = hidden_ref[rows, :].astype(jnp.float32)
        mean = jnp.mean(hidden * hidden, axis=1, keepdims=True)
        normed_ref[rows, :] = (hidden * lax.rsqrt(mean + EPSILON)).astype(jnp.bfloat16)
        return carry

    lax.fori_loop(0, hidden_ref.shape[0] // tile, one, 0)


def normalise(hidden, ahead):
    vmem = pl.BlockSpec(memory_space=pltpu.VMEM)
    return pl.pallas_call(
        functools.partial(norm_kernel, 32),
        in_specs=[vmem] + [pl.BlockSpec(memory_space=pl.ANY)] * len(ahead),
        out_specs=vmem,
        out_shape=jax.ShapeDtypeStruct(hidden.shape, jnp.bfloat16),
        compiler_params=pltpu.CompilerParams(vmem_limit_bytes=SMALL_VMEM),
        cost_estimate=LITTLE,
        name="normalise",
    )(hidden, *ahead)


def stack_kernel(one_ref, two_ref, stack_ref, copy_ref):
    depth = one_ref.shape[0]
    stack_ref[:depth, :] = one_ref[...]
    stack_ref[depth:, :] = two_ref[...]
    copy_ref[...] = two_ref[...]


def stack_hops(one, two):
    depth, width = one.shape
    vmem = pl.BlockSpec(memory_space=pltpu.VMEM)
    return pl.pallas_call(
        stack_kernel,
        in_specs=[vmem, vmem],
        out_specs=[vmem, vmem],
        out_shape=[jax.ShapeDtypeStruct((rows, width), jnp.bfloat16) for rows in (2 * depth, depth)],
        compiler_params=pltpu.CompilerParams(vmem_limit_bytes=SMALL_VMEM),
        cost_estimate=LITTLE,
        name="stack_hops",
    )(one, two)


def find_kernel(holders, requests, pass_local, capacity, me_ref, table_ref, *rest):
    rank_ref, passage_ref, slot_ref, kept_ref = rest[-4:]
    me = me_ref[0]
    stride = table_ref.shape[0] // holders
    for k in range(holders):
        base = k * (capacity + 1)
        for rank in range(capacity + 1):
            slot_ref[base + rank] = 0
        count = jnp.int32(0)
        for request in range(requests):
            slot_ref[base + count] = request
            mine = (table_ref[k * stride + request] // pass_local == me).astype(jnp.int32)
            count = jnp.minimum(count + mine, capacity)
    spot = lax.broadcasted_iota(jnp.int32, (1, PLEN), 1)
    for k in range(holders):
        for rank in range(capacity):
            at = k * capacity + rank
            request = slot_ref[k * (capacity + 1) + rank]
            passage_ref[at] = lax.rem(table_ref[k * stride + request], pass_local)
            start = k * stride + requests + request * RECOMP
            covered = spot < 0
            for r in range(RECOMP):
                covered = covered | (spot == table_ref[start + r])
            kept_ref[at : at + 1, :] = jnp.where(covered, 0.0, 1.0)
    kept = kept_ref[...]
    upto = lax.broadcasted_iota(jnp.int32, (PLEN, PLEN), 0) <= lax.broadcasted_iota(jnp.int32, (PLEN, PLEN), 1)
    rank_of = jnp.dot(
        kept.astype(jnp.bfloat16), upto.astype(jnp.bfloat16), preferred_element_type=jnp.float32
    )
    rank_ref[...] = jnp.where(kept > 0, rank_of, 0.0)


def find_rows(table, me, holders, requests, pass_local, capacity, normed):
    slots = holders * capacity
    smem = pl.BlockSpec(memory_space=pltpu.SMEM)
    whole = pl.BlockSpec(memory_space=pl.ANY)
    return pl.pallas_call(
        functools.partial(find_kernel, holders, requests, pass_local, capacity),
        in_specs=[smem, smem, whole],
        out_specs=[pl.BlockSpec(memory_space=pltpu.VMEM), smem],
        out_shape=[jax.ShapeDtypeStruct((slots, PLEN), jnp.float32), jax.ShapeDtypeStruct((slots,), jnp.int32)],
        scratch_shapes=[pltpu.SMEM((holders * (capacity + 1),), jnp.int32), pltpu.VMEM((slots, PLEN), jnp.float32)],
        compiler_params=pltpu.CompilerParams(vmem_limit_bytes=SMALL_VMEM),
        cost_estimate=LARGE,
        name="find_rows",
    )(me, table, normed)


def pick_kernel(pieces, me_ref, passage_ref, rank_ref, cache_ref, *rest):
    out_ref, sent_ref = rest[-2:]
    sent_hbm_ref = rest[-4] if pieces else rest[-3]
    copies = []
    pair = me_ref[1]
    row = (lax.broadcasted_iota(jnp.int32, (KEPT, PLEN), 0) + 1).astype(jnp.float32)
    for at in range(out_ref.shape[0]):
        passage = passage_ref[at]
        select = (rank_ref[at : at + 1, :] == row).astype(jnp.bfloat16)
        for place, part in ((0, pair), (1, 1 - pair)):
            for half in range(2):
                start = pl.multiple_of(half * HALF + part * PAIR_WIDTH, PAIR_WIDTH)
                end = (place * 2 + half) * PAIR_WIDTH
                out_ref[at, :, end : end + PAIR_WIDTH] = jnp.dot(
                    select, cache_ref[passage, :, pl.ds(start, PAIR_WIDTH)], preferred_element_type=jnp.float32
                ).astype(jnp.bfloat16)
        copies.append(pltpu.make_async_copy(out_ref.at[at], sent_hbm_ref.at[at], sent_ref.at[at]))
        copies[-1].start()
    start = 0
    for piece in rest[:pieces]:
        rest[-3][start : start + piece.shape[0], :] = piece[...]
        start += piece.shape[0]
    for copy in copies:
        copy.wait()


def pick_rows(me, passages, ranks, cache, pieces, ahead):
    shapes = [jax.ShapeDtypeStruct((passages.shape[0], KEPT, 2 * HALF), jnp.bfloat16)]
    if pieces:
        rows = sum(piece.shape[0] for piece in pieces)
        shapes.append(jax.ShapeDtypeStruct((rows, pieces[0].shape[1]), jnp.bfloat16))
    smem = pl.BlockSpec(memory_space=pltpu.SMEM)
    vmem = pl.BlockSpec(memory_space=pltpu.VMEM)
    return pl.pallas_call(
        functools.partial(pick_kernel, len(pieces)),
        in_specs=[smem, smem] + [vmem] * (2 + len(pieces)) + [pl.BlockSpec(memory_space=pl.ANY)] * len(ahead),
        out_specs=[pl.BlockSpec(memory_space=pl.ANY)] + [vmem] * (len(shapes) - 1),
        out_shape=shapes,
        scratch_shapes=[
            pltpu.VMEM(shapes[0].shape, jnp.bfloat16),
            pltpu.SemaphoreType.DMA((passages.shape[0],)),
        ],
        compiler_params=pltpu.CompilerParams(vmem_limit_bytes=SMALL_VMEM),
        cost_estimate=LITTLE,
        name="pick_rows",
    )(me, passages, ranks, cache, *pieces, *ahead)


def project_kernel(layout, member_ref, mine_ref, other_ref, *refs):
    mine_out, other_out = refs[-2:]
    rows = mine_ref.shape[0]
    depth = D // len(layout)
    total = None
    for k, (array, start) in enumerate(layout):
        chunk = pl.ds(pl.multiple_of((member_ref[0] ^ k) * depth, depth), depth)
        both = jnp.concatenate([mine_ref[:, chunk], other_ref[:, chunk]], axis=0)
        weights = refs[array][start * depth : (start + 1) * depth, :]
        term = jnp.dot(both, weights, preferred_element_type=jnp.float32)
        total = term if total is None else total + term
    mine_out[...] = total[:rows].astype(jnp.bfloat16)
    other_out[...] = total[rows:].astype(jnp.bfloat16)


def project(member, mine, other, arrays, layout, ahead):
    rows, width = mine.shape[0], arrays[0].shape[1]
    shape = jax.ShapeDtypeStruct((rows, width), jnp.bfloat16)
    vmem = pl.BlockSpec(memory_space=pltpu.VMEM)
    return pl.pallas_call(
        functools.partial(project_kernel, layout),
        in_specs=[pl.BlockSpec(memory_space=pltpu.SMEM)]
        + [vmem] * (2 + len(arrays))
        + [pl.BlockSpec(memory_space=pl.ANY)] * len(ahead),
        out_specs=[vmem, vmem],
        out_shape=[shape, shape],
        compiler_params=pltpu.CompilerParams(vmem_limit_bytes=SMALL_VMEM),
        cost_estimate=LITTLE,
        name="project",
    )(member.reshape(1), mine, other, *arrays, *ahead)


def scaled_keys(keys, turned_ref):
    scaled = keys.astype(jnp.float32) * SCORE_FACTOR
    high = scaled.astype(jnp.bfloat16)
    turned_ref[:HD, :] = high.T
    turned_ref[HD:, :] = (scaled - high.astype(jnp.float32)).astype(jnp.bfloat16).T
    return jnp.max(jnp.sum(scaled * scaled, axis=1, keepdims=True))


def head_rows(q_ref, slot, first, heads_once):
    block = jnp.concatenate(
        [q_ref[slot, :, (first + i) * HD : (first + i + 1) * HD] for i in range(heads_once)], axis=0
    )
    return jnp.concatenate([block, block], axis=1)


def causal(rows):
    token = lax.broadcasted_iota(jnp.int32, (rows, QLEN), 0) % QLEN
    return lax.broadcasted_iota(jnp.int32, (rows, QLEN), 1) <= token


def place(step, pair):
    query, head = step // PAIR_HEADS, step % PAIR_HEADS
    rows = pl.ds(pl.multiple_of(query * QLEN, QLEN), QLEN)
    return query, head, rows, pair * PAIR_HEADS + head


def columns(start, width=HD):
    return pl.ds(pl.multiple_of(start, HD), width)


def block_copies(step, start, array_ref, block_ref, signal_ref, inward):
    wide, slot = GROUPED * HD, step % 2
    column = columns(start + (step % PAIR_HEADS) * wide, wide)
    height = QLEN // PIECES
    copies = []
    for i in range(PIECES):
        outer = array_ref.at[pl.ds(pl.multiple_of(step // PAIR_HEADS * QLEN + i * height, height), height), column]
        inner = block_ref.at[slot, i * height : (i + 1) * height]
        ends = (outer, inner) if inward else (inner, outer)
        copies.append(pltpu.make_async_copy(*ends, signal_ref.at[slot, i]))
    return copies


def start_all(copies):
    for copy in copies:
        copy.start()


def wait_all(copies):
    for copy in copies:
        copy.wait()


def bound_kernel(q_ref, *rest):
    bound_ref = rest[-1]

    @pl.when(pl.program_id(0) == 0)
    def clear():
        bound_ref[...] = jnp.zeros_like(bound_ref)

    peak = jnp.zeros((q_ref.shape[0], 1), jnp.float32)
    for first in range(0, GROUPED, 4):
        most = None
        for head in range(first, first + 4):
            block = q_ref[:, head * HD : (head + 1) * HD].astype(jnp.float32)
            most = block * block if most is None else jnp.maximum(most, block * block)
        peak = jnp.maximum(peak, jnp.sum(most, axis=1, keepdims=True))
    bound_ref[...] = jnp.maximum(bound_ref[...], jnp.max(peak))


def query_bound(q_rows, ahead):
    rows = q_rows.shape[0]
    return pl.pallas_call(
        bound_kernel,
        grid=(KVH,),
        in_specs=[pl.BlockSpec((rows, GROUPED * HD), lambda h: (0, h))]
        + [pl.BlockSpec(memory_space=pl.ANY)] * len(ahead),
        out_specs=pl.BlockSpec((8, HD), lambda h: (0, 0)),
        out_shape=jax.ShapeDtypeStruct((8, HD), jnp.float32),
        compiler_params=pltpu.CompilerParams(vmem_limit_bytes=SMALL_VMEM),
        cost_estimate=LITTLE,
        name="query_bound",
    )(q_rows, *ahead)


def attend_kernel(
    steps,
    heads_once,
    part,
    info_ref,
    q_ref,
    own_hbm_ref,
    kept_ref,
    near_ref,
    far_ref,
    bound_ref,
    *rest,
):
    out_ref, key_ref, turned_ref, value_ref, score_ref, expd_ref, result_ref, done_ref = rest[-14:-6]
    block_ref, arrived_ref, cut_ref, cut_done_ref, own_ref, own_done_ref = rest[-6:]
    passage_keys = TOPP * PLEN
    wide = GROUPED * HD
    groups = GROUPED // heads_once
    flip = info_ref[1] > 0
    cut = pltpu.make_async_copy(kept_ref.at[:, :, part * HALF : (part + 1) * HALF], cut_ref, cut_done_ref)
    cut.start()
    own = pltpu.make_async_copy(own_hbm_ref, own_ref, own_done_ref)
    own.start()
    start = info_ref[0] * (PAIR_HEADS * wide)

    def fetch(step):
        return block_copies(step, start, q_ref, block_ref, arrived_ref, True)

    def leave(step):
        return block_copies(step, start, out_ref, result_ref, done_ref, False)

    start_all(fetch(0))
    shown = jnp.where(causal(heads_once * QLEN), 1.0, 0.0).astype(jnp.bfloat16)
    value_ref[:, HD:] = jnp.ones((passage_keys + QLEN, HD), jnp.bfloat16)
    cut.wait()
    own.wait()

    def one(step, carry):
        query, head, rows, column = place(step, info_ref[0])
        slot = step % 2

        @pl.when(step >= 2)
        def free():
            wait_all(leave(step - 2))

        @pl.when(step + 1 < steps)
        def prefetch():
            start_all(fetch(step + 1))

        offset = head * HD
        for j in range(TOPP):
            block = info_ref[2 + query * TOPP + j]
            key_ref[j * KEPT : (j + 1) * KEPT, :] = cut_ref[block, :, columns(offset)]
            value_ref[j * KEPT : (j + 1) * KEPT, :HD] = cut_ref[block, :, columns(offset + PAIR_WIDTH)]
        near, far = near_ref[rows, columns(head * HD)], far_ref[rows, columns(head * HD)]
        key_ref[TOPP * KEPT : passage_keys, :] = jnp.where(flip, far, near)
        value_ref[TOPP * KEPT : passage_keys, :HD] = jnp.where(flip, near, far)
        key_ref[passage_keys:, :] = own_ref[rows, columns(column * HD)]
        value_ref[passage_keys:, :HD] = own_ref[rows, columns(HALF + column * HD)]
        key_bound = scaled_keys(key_ref[...], turned_ref)
        small = jnp.max(bound_ref[...]) * key_bound <= SAFE_EXPONENT**2

        wait_all(fetch(step))

        def score(group):
            score_ref[group % 2] = jnp.dot(
                head_rows(block_ref, slot, group * heads_once, heads_once),
                turned_ref[...],
                preferred_element_type=jnp.float32,
            )

        def soften(group):
            expd = jnp.exp2(score_ref[group % 2]).astype(jnp.bfloat16)
            expd_ref[group % 2, :, :passage_keys] = expd[:, :passage_keys]
            expd_ref[group % 2, :, passage_keys:] = expd[:, passage_keys:] * shown

        def finish(group):
            summed = jnp.dot(expd_ref[group % 2], value_ref[...], preferred_element_type=jnp.float32)
            for i in range(heads_once):
                at = group * heads_once + i
                both = summed[i * QLEN : (i + 1) * QLEN]
                weight = both[:, HD:]
                inverse = pl.reciprocal(weight, approx=True)
                inverse = inverse * (2.0 - weight * inverse)
                result_ref[slot, :, at * HD : (at + 1) * HD] = (both[:, :HD] * inverse).astype(jnp.bfloat16)

        @pl.when(small)
        def unshifted():
            score(0)
            for group in range(groups):
                if group + 1 < groups:
                    score(group + 1)
                soften(group)
                if group > 0:
                    finish(group - 1)
            finish(groups - 1)

        @pl.when(jnp.logical_not(small))
        def shifted():
            visible = causal(heads_once * QLEN)
            for group in range(groups):
                scores = jnp.dot(
                    head_rows(block_ref, slot, group * heads_once, heads_once),
                    turned_ref[...],
                    preferred_element_type=jnp.float32,
                )
                scores = jnp.concatenate(
                    [scores[:, :passage_keys], jnp.where(visible, scores[:, passage_keys:], -jnp.inf)], axis=1
                )
                peak = jnp.max(scores, axis=1, keepdims=True)
                expd = jnp.exp2(scores - peak).astype(jnp.bfloat16)
                summed = jnp.dot(expd, value_ref[...], preferred_element_type=jnp.float32)
                ratio = (summed[:, :HD] / summed[:, HD:]).astype(jnp.bfloat16)
                for i in range(heads_once):
                    at = group * heads_once + i
                    result_ref[slot, :, at * HD : (at + 1) * HD] = ratio[i * QLEN : (i + 1) * QLEN]

        start_all(leave(step))
        return carry

    lax.fori_loop(0, steps, one, 0)
    for step in range(max(steps - 2, 0), steps):
        wait_all(leave(step))


def attend(part, info, q_rows, own_kv, kept, near, far, bound, earlier=None):
    rows, width = q_rows.shape
    span = TOPP * PLEN + QLEN
    heads_once = 2
    vmem = pl.BlockSpec(memory_space=pltpu.VMEM)
    whole = pl.BlockSpec(memory_space=pl.ANY)
    hbm = pl.BlockSpec(memory_space=pltpu.HBM)
    operands = [info, q_rows, own_kv, kept, near, far, bound]
    aliases = {}
    if earlier is not None:
        aliases = {len(operands): 0}
        operands.append(earlier)
    return pl.pallas_call(
        functools.partial(attend_kernel, rows // QLEN * PAIR_HEADS, heads_once, part),
        in_specs=[pl.BlockSpec(memory_space=pltpu.SMEM)] + [hbm] * 3
        + [vmem] * 3
        + [whole] * len(aliases),
        out_specs=whole,
        out_shape=jax.ShapeDtypeStruct((rows, width), jnp.bfloat16),
        scratch_shapes=[
            pltpu.VMEM((span, HD), jnp.bfloat16),
            pltpu.VMEM((2 * HD, span), jnp.bfloat16),
            pltpu.VMEM((span, 2 * HD), jnp.bfloat16),
            pltpu.VMEM((2, heads_once * QLEN, span), jnp.float32),
            pltpu.VMEM((2, heads_once * QLEN, span), jnp.bfloat16),
            pltpu.VMEM((2, QLEN, GROUPED * HD), jnp.bfloat16),
            pltpu.SemaphoreType.DMA((2, PIECES)),
            pltpu.VMEM((2, QLEN, GROUPED * HD), jnp.bfloat16),
            pltpu.SemaphoreType.DMA((2, PIECES)),
            pltpu.VMEM((kept.shape[0], KEPT, HALF), jnp.bfloat16),
            pltpu.SemaphoreType.DMA,
            pltpu.VMEM(own_kv.shape, jnp.bfloat16),
            pltpu.SemaphoreType.DMA,
        ],
        input_output_aliases=aliases,
        compiler_params=pltpu.CompilerParams(vmem_limit_bytes=VMEM_BYTES),
        cost_estimate=LITTLE,
        name="attend",
    )(*operands)


def swap(array, axis, bits):
    size = lax.axis_size(axis)
    return lax.ppermute(array, axis, [(i, i ^ bits) for i in range(size)])


def recompute_general(normed, w_kv, pair):
    whole = lax.all_gather(lax.all_gather(w_kv, "member", axis=0, tiled=True), "group", axis=1, tiled=True)
    result = jnp.dot(normed, whole, preferred_element_type=jnp.float32).astype(jnp.bfloat16)
    result = result.reshape(-1, 2, PAIRS, PAIR_WIDTH)
    first = jnp.where(pair == 0, result[:, :, 0], result[:, :, 1])
    second = jnp.where(pair == 0, result[:, :, 1], result[:, :, 0])
    return [first[:, 0], first[:, 1]], [second[:, 0], second[:, 1]]


def local(q_rows, own_kv, cache, recomp_hidden, w_kv, retrieval, positions):
    queries = retrieval.shape[0]
    requests = queries * TOPP
    holders = lax.axis_size("member")
    groups = lax.axis_size("group")
    pass_local = cache.shape[0]
    capacity = -(-requests // holders)
    member = lax.axis_index("member")
    group = lax.axis_index("group")
    pair = group % PAIRS
    tuned = groups == 4 and holders == 8
    wanted = retrieval.reshape(requests)
    request = jnp.concatenate([wanted, positions.reshape(requests * RECOMP)])
    request = jnp.pad(request, (0, -request.shape[0] % 128)).reshape(1, -1, 128)
    request = jnp.broadcast_to(request, (holders,) + request.shape[1:])
    table = lax.all_to_all(request, "member", split_axis=0, concat_axis=0, tiled=True).reshape(-1)
    hidden = recomp_hidden.reshape(requests * RECOMP, D)
    hops = stack_hops(swap(w_kv, "member", 2), swap(w_kv, "member", 4)) if tuned else []
    normed = normalise(hidden, hops[:1])
    me = jnp.stack([member, pair]).astype(jnp.int32)
    ranks, passages = find_rows(table, me, holders, requests, pass_local, capacity, normed)
    holder_of = wanted // pass_local
    same = holder_of[:, None] == holder_of[None, :]
    before = jnp.arange(requests)[None, :] < jnp.arange(requests)[:, None]
    slot = holder_of * capacity + jnp.sum((same & before).astype(jnp.int32), axis=1)
    flip = group // 2 if tuned else jnp.int32(0)
    info = jnp.concatenate([jnp.stack([pair, flip]), slot]).astype(jnp.int32)
    other_info = jnp.concatenate([jnp.stack([1 - pair, flip]), slot]).astype(jnp.int32)
    bound = query_bound(q_rows, [ranks])
    pieces, ahead = [], [bound]
    if tuned:
        stack, two = hops
        aside, across = swap(w_kv, "member", 1), swap(w_kv, "group", 2)
        three = swap(two, "member", 2)
        stack_aside, stack_across = swap(stack, "member", 1), swap(stack, "group", 2)
        pieces = [aside, stack_aside, three]
        ahead += [across, stack_across]
    sent, *rest = pick_rows(me, passages, ranks, cache, pieces, ahead)
    arrived = lax.all_to_all(
        sent.reshape(holders, capacity * KEPT, 2 * HALF), "member", split_axis=0, concat_axis=0, tiled=True
    ).reshape(sent.shape)
    if tuned:
        beside_three = swap(three, "member", 1)
        other = swap(normed, "group", 1)
        rest_across = swap(rest[0], "group", 2)
        far_three = swap(beside_three, "group", 2)
        near, near_other = project(
            member,
            normed,
            other,
            [w_kv, aside, stack, stack_aside, three, beside_three],
            ((0, 0), (1, 0), (2, 0), (3, 0), (2, 1), (3, 1), (4, 0), (5, 0)),
            [],
        )
        far, far_other = project(
            member,
            normed,
            other,
            [across, stack_across, rest_across, far_three],
            ((0, 0), (2, 0), (1, 0), (2, 1), (1, 1), (2, 2), (2, 3), (3, 0)),
            [near],
        )
        first = [near, far]
        second = [swap(near_other, "group", 1), swap(far_other, "group", 1)]
    else:
        first, second = recompute_general(normed, w_kv, pair)
    out = attend(0, info, q_rows, own_kv, arrived, *first, bound)
    return attend(1, other_info, q_rows, own_kv, arrived, *second, bound, earlier=out)


def solution(mesh):
    rows = P(("group", "member"), None)
    placed = (
        rows,
        rows,
        P(("group", "member"), None, None),
        P(("group", "member"), None, None, None),
        P("member", "group"),
        rows,
        P(("group", "member"), None, None),
    )
    return jax.shard_map(local, mesh=mesh, in_specs=placed, out_specs=rows, check_vma=False)
```

```python
import functools

import jax
import jax.numpy as jnp
from jax import lax
from jax.experimental import pallas as pl
from jax.experimental.pallas import tpu as pltpu
from jax.sharding import PartitionSpec as P

D = 4096
HQ = 64
KVH = 4
HD = 128
TOPP = 8
QLEN = 128
PLEN = 64
RECOMP = 16
KEPT = PLEN - RECOMP
GROUPED = HQ // KVH
PAIRS = 2
PAIR_HEADS = KVH // PAIRS
PAIR_WIDTH = PAIR_HEADS * HD
HALF = KVH * HD

EPSILON = 1e-06
SCORE_FACTOR = 1.4426950408889634 / HD**0.5
SAFE_EXPONENT = 80.0
SMALL_VMEM = 12 * 1024 * 1024
VMEM_BYTES = 24 * 1024 * 1024
LITTLE = pl.CostEstimate(flops=1, bytes_accessed=1, transcendentals=0)
LARGE = pl.CostEstimate(flops=1, bytes_accessed=36_000_000, transcendentals=0)


def norm_kernel(tile, hidden_ref, *rest):
    normed_ref = rest[-1]

    def one(step, carry):
        rows = pl.ds(pl.multiple_of(step * tile, tile), tile)
        hidden = hidden_ref[rows, :].astype(jnp.float32)
        mean = jnp.mean(hidden * hidden, axis=1, keepdims=True)
        normed_ref[rows, :] = (hidden * lax.rsqrt(mean + EPSILON)).astype(jnp.bfloat16)
        return carry

    lax.fori_loop(0, hidden_ref.shape[0] // tile, one, 0)


def normalise(hidden, ahead):
    vmem = pl.BlockSpec(memory_space=pltpu.VMEM)
    return pl.pallas_call(
        functools.partial(norm_kernel, 32),
        in_specs=[vmem] + [pl.BlockSpec(memory_space=pl.ANY)] * len(ahead),
        out_specs=vmem,
        out_shape=jax.ShapeDtypeStruct(hidden.shape, jnp.bfloat16),
        compiler_params=pltpu.CompilerParams(vmem_limit_bytes=SMALL_VMEM),
        cost_estimate=LITTLE,
        name="normalise",
    )(hidden, *ahead)


def stack_kernel(one_ref, two_ref, stack_ref, copy_ref):
    depth = one_ref.shape[0]
    stack_ref[:depth, :] = one_ref[...]
    stack_ref[depth:, :] = two_ref[...]
    copy_ref[...] = two_ref[...]


def stack_hops(one, two):
    depth, width = one.shape
    vmem = pl.BlockSpec(memory_space=pltpu.VMEM)
    return pl.pallas_call(
        stack_kernel,
        in_specs=[vmem, vmem],
        out_specs=[vmem, vmem],
        out_shape=[jax.ShapeDtypeStruct((rows, width), jnp.bfloat16) for rows in (2 * depth, depth)],
        compiler_params=pltpu.CompilerParams(vmem_limit_bytes=SMALL_VMEM),
        cost_estimate=LITTLE,
        name="stack_hops",
    )(one, two)


def find_kernel(holders, requests, pass_local, capacity, me_ref, table_ref, *rest):
    rank_ref, passage_ref, slot_ref, kept_ref = rest[-4:]
    me = me_ref[0]
    stride = table_ref.shape[0] // holders
    for k in range(holders):
        base = k * (capacity + 1)
        for rank in range(capacity + 1):
            slot_ref[base + rank] = 0
        count = jnp.int32(0)
        for request in range(requests):
            slot_ref[base + count] = request
            mine = (table_ref[k * stride + request] // pass_local == me).astype(jnp.int32)
            count = jnp.minimum(count + mine, capacity)
    spot = lax.broadcasted_iota(jnp.int32, (1, PLEN), 1)
    for k in range(holders):
        for rank in range(capacity):
            at = k * capacity + rank
            request = slot_ref[k * (capacity + 1) + rank]
            passage_ref[at] = lax.rem(table_ref[k * stride + request], pass_local)
            start = k * stride + requests + request * RECOMP
            covered = spot < 0
            for r in range(RECOMP):
                covered = covered | (spot == table_ref[start + r])
            kept_ref[at : at + 1, :] = jnp.where(covered, 0.0, 1.0)
    kept = kept_ref[...]
    upto = lax.broadcasted_iota(jnp.int32, (PLEN, PLEN), 0) <= lax.broadcasted_iota(jnp.int32, (PLEN, PLEN), 1)
    rank_of = jnp.dot(
        kept.astype(jnp.bfloat16), upto.astype(jnp.bfloat16), preferred_element_type=jnp.float32
    )
    rank_ref[...] = jnp.where(kept > 0, rank_of, 0.0)


def find_rows(table, me, holders, requests, pass_local, capacity, normed):
    slots = holders * capacity
    smem = pl.BlockSpec(memory_space=pltpu.SMEM)
    whole = pl.BlockSpec(memory_space=pl.ANY)
    return pl.pallas_call(
        functools.partial(find_kernel, holders, requests, pass_local, capacity),
        in_specs=[smem, smem, whole],
        out_specs=[pl.BlockSpec(memory_space=pltpu.VMEM), smem],
        out_shape=[jax.ShapeDtypeStruct((slots, PLEN), jnp.float32), jax.ShapeDtypeStruct((slots,), jnp.int32)],
        scratch_shapes=[pltpu.SMEM((holders * (capacity + 1),), jnp.int32), pltpu.VMEM((slots, PLEN), jnp.float32)],
        compiler_params=pltpu.CompilerParams(vmem_limit_bytes=SMALL_VMEM),
        cost_estimate=LARGE,
        name="find_rows",
    )(me, table, normed)


def pick_kernel(pieces, me_ref, passage_ref, rank_ref, cache_ref, *rest):
    out_ref = rest[-2] if pieces else rest[-1]
    start = 0
    for piece in rest[:pieces]:
        rest[-1][start : start + piece.shape[0], :] = piece[...]
        start += piece.shape[0]
    pair = me_ref[1]
    row = (lax.broadcasted_iota(jnp.int32, (KEPT, PLEN), 0) + 1).astype(jnp.float32)
    for at in range(out_ref.shape[0]):
        passage = passage_ref[at]
        select = (rank_ref[at : at + 1, :] == row).astype(jnp.bfloat16)
        for place, part in ((0, pair), (1, 1 - pair)):
            for half in range(2):
                start = pl.multiple_of(half * HALF + part * PAIR_WIDTH, PAIR_WIDTH)
                end = (place * 2 + half) * PAIR_WIDTH
                out_ref[at, :, end : end + PAIR_WIDTH] = jnp.dot(
                    select, cache_ref[passage, :, pl.ds(start, PAIR_WIDTH)], preferred_element_type=jnp.float32
                ).astype(jnp.bfloat16)


def pick_rows(me, passages, ranks, cache, pieces, ahead):
    shapes = [jax.ShapeDtypeStruct((passages.shape[0], KEPT, 2 * HALF), jnp.bfloat16)]
    if pieces:
        rows = sum(piece.shape[0] for piece in pieces)
        shapes.append(jax.ShapeDtypeStruct((rows, pieces[0].shape[1]), jnp.bfloat16))
    smem = pl.BlockSpec(memory_space=pltpu.SMEM)
    vmem = pl.BlockSpec(memory_space=pltpu.VMEM)
    return pl.pallas_call(
        functools.partial(pick_kernel, len(pieces)),
        in_specs=[smem, smem] + [vmem] * (2 + len(pieces)) + [pl.BlockSpec(memory_space=pl.ANY)] * len(ahead),
        out_specs=[vmem] * len(shapes),
        out_shape=shapes,
        compiler_params=pltpu.CompilerParams(vmem_limit_bytes=SMALL_VMEM),
        cost_estimate=LITTLE,
        name="pick_rows",
    )(me, passages, ranks, cache, *pieces, *ahead)


def project_kernel(layout, member_ref, mine_ref, other_ref, *refs):
    mine_out, other_out = refs[-2:]
    rows = mine_ref.shape[0]
    depth = D // len(layout)
    total = None
    for k, (array, start) in enumerate(layout):
        chunk = pl.ds(pl.multiple_of((member_ref[0] ^ k) * depth, depth), depth)
        both = jnp.concatenate([mine_ref[:, chunk], other_ref[:, chunk]], axis=0)
        weights = refs[array][start * depth : (start + 1) * depth, :]
        term = jnp.dot(both, weights, preferred_element_type=jnp.float32)
        total = term if total is None else total + term
    mine_out[...] = total[:rows].astype(jnp.bfloat16)
    other_out[...] = total[rows:].astype(jnp.bfloat16)


def project(member, mine, other, arrays, layout, ahead):
    rows, width = mine.shape[0], arrays[0].shape[1]
    shape = jax.ShapeDtypeStruct((rows, width), jnp.bfloat16)
    vmem = pl.BlockSpec(memory_space=pltpu.VMEM)
    return pl.pallas_call(
        functools.partial(project_kernel, layout),
        in_specs=[pl.BlockSpec(memory_space=pltpu.SMEM)]
        + [vmem] * (2 + len(arrays))
        + [pl.BlockSpec(memory_space=pl.ANY)] * len(ahead),
        out_specs=[vmem, vmem],
        out_shape=[shape, shape],
        compiler_params=pltpu.CompilerParams(vmem_limit_bytes=SMALL_VMEM),
        cost_estimate=LITTLE,
        name="project",
    )(member.reshape(1), mine, other, *arrays, *ahead)


def scaled_keys(keys, turned_ref):
    scaled = keys.astype(jnp.float32) * SCORE_FACTOR
    high = scaled.astype(jnp.bfloat16)
    turned_ref[:HD, :] = high.T
    turned_ref[HD:, :] = (scaled - high.astype(jnp.float32)).astype(jnp.bfloat16).T
    return jnp.max(jnp.sum(scaled * scaled, axis=1, keepdims=True))


def head_rows(q_ref, rows, column, heads_once):
    block = jnp.concatenate(
        [q_ref[rows, pl.ds(pl.multiple_of(column + i * HD, HD), HD)] for i in range(heads_once)], axis=0
    )
    return jnp.concatenate([block, block], axis=1)


def causal(rows):
    token = lax.broadcasted_iota(jnp.int32, (rows, QLEN), 0) % QLEN
    return lax.broadcasted_iota(jnp.int32, (rows, QLEN), 1) <= token


def place(step, pair):
    query, head = step // PAIR_HEADS, step % PAIR_HEADS
    rows = pl.ds(pl.multiple_of(query * QLEN, QLEN), QLEN)
    return query, head, rows, pair * PAIR_HEADS + head


def columns(start, width=HD):
    return pl.ds(pl.multiple_of(start, HD), width)


def own_kernel(steps, heads_once, passing, info_ref, q_ref, own_ref, *rest):
    sum_ref, weight_ref, bound_ref = rest[-5 - passing : -2 - passing]
    turned_ref, wide_ref = rest[-2:]
    bound_ref[...] = jnp.zeros_like(bound_ref)
    shown = jnp.where(causal(heads_once * QLEN), 1.0, 0.0).astype(jnp.bfloat16)
    lane = lax.broadcasted_iota(jnp.int32, (QLEN, HD), 1)

    def one(step, carry):
        _, head, rows, column = place(step, info_ref[0])
        scaled_keys(own_ref[rows, columns(column * HD)], turned_ref)
        wide_ref[:, :HD] = own_ref[rows, columns(HALF + column * HD)]
        wide_ref[:, HD:] = jnp.ones((QLEN, HD), jnp.bfloat16)
        weights = jnp.zeros((QLEN, HD), jnp.float32)
        peak = jnp.zeros((QLEN, 1), jnp.float32)
        for first in range(0, GROUPED, heads_once):
            start = (column * GROUPED + first) * HD
            scores = jnp.dot(
                head_rows(q_ref, rows, start, heads_once), turned_ref[...], preferred_element_type=jnp.float32
            )
            summed = jnp.dot(
                jnp.exp2(scores).astype(jnp.bfloat16) * shown, wide_ref[...], preferred_element_type=jnp.float32
            )
            for i in range(heads_once):
                part = summed[i * QLEN : (i + 1) * QLEN]
                sum_ref[rows, columns((head * GROUPED + first + i) * HD)] = part[:, :HD].astype(jnp.bfloat16)
                weights = jnp.where(lane == first + i, part[:, HD:], weights)
            most = None
            for i in range(heads_once):
                block = q_ref[rows, columns(start + i * HD)].astype(jnp.float32)
                most = block * block if most is None else jnp.maximum(most, block * block)
            peak = jnp.maximum(peak, jnp.sum(most, axis=1, keepdims=True))
        weight_ref[rows, columns(head * HD)] = weights
        bound_ref[...] = jnp.maximum(bound_ref[...], jnp.max(peak))
        return carry

    lax.fori_loop(0, steps, one, 0)


def attend_own(info, q_rows, own_kv, ahead, passing):
    rows = q_rows.shape[0]
    whole = pl.BlockSpec(memory_space=pl.ANY)
    vmem = pl.BlockSpec(memory_space=pltpu.VMEM)
    return pl.pallas_call(
        functools.partial(own_kernel, rows // QLEN * PAIR_HEADS, 4, len(passing)),
        in_specs=[pl.BlockSpec(memory_space=pltpu.SMEM), vmem, vmem] + [whole] * (len(passing) + len(ahead)),
        out_specs=[vmem] * 3 + [whole] * len(passing),
        out_shape=[
            jax.ShapeDtypeStruct((rows, PAIR_HEADS * GROUPED * HD), jnp.bfloat16),
            jax.ShapeDtypeStruct((rows, PAIR_HEADS * HD), jnp.float32),
            jax.ShapeDtypeStruct((8, HD), jnp.float32),
        ]
        + [jax.ShapeDtypeStruct(part.shape, part.dtype) for part in passing],
        scratch_shapes=[pltpu.VMEM((2 * HD, QLEN), jnp.bfloat16), pltpu.VMEM((QLEN, 2 * HD), jnp.bfloat16)],
        input_output_aliases={3 + i: 3 + i for i in range(len(passing))},
        compiler_params=pltpu.CompilerParams(vmem_limit_bytes=VMEM_BYTES),
        cost_estimate=LITTLE,
        name="attend_own",
    )(info, q_rows, own_kv, *passing, *ahead)


def attend_kernel(
    steps,
    heads_once,
    part,
    info_ref,
    q_ref,
    own_ref,
    kept_ref,
    near_ref,
    far_ref,
    sum_ref,
    weight_ref,
    bound_ref,
    *rest,
):
    out_ref, key_ref, turned_ref, value_ref, score_ref, expd_ref, result_ref, done_ref = rest[-8:]
    passage_keys = TOPP * PLEN
    wide = GROUPED * HD
    groups = GROUPED // heads_once
    flip = info_ref[1] > 0
    value_ref[:, HD:] = jnp.ones((passage_keys + QLEN, HD), jnp.bfloat16)

    def leave(step):
        _, _, rows, column = place(step, info_ref[0])
        slot = step % 2
        return pltpu.make_async_copy(
            result_ref.at[slot], out_ref.at[rows, columns(column * wide, wide)], done_ref.at[slot]
        )

    def one(step, carry):
        query, head, rows, column = place(step, info_ref[0])
        slot = step % 2

        @pl.when(step >= 2)
        def free():
            leave(step - 2).wait()

        offset = part * HALF + head * HD
        for j in range(TOPP):
            block = info_ref[2 + query * TOPP + j]
            key_ref[j * KEPT : (j + 1) * KEPT, :] = kept_ref[block, :, columns(offset)]
            value_ref[j * KEPT : (j + 1) * KEPT, :HD] = kept_ref[block, :, columns(offset + PAIR_WIDTH)]
        near, far = near_ref[rows, columns(head * HD)], far_ref[rows, columns(head * HD)]
        key_ref[TOPP * KEPT : passage_keys, :] = jnp.where(flip, far, near)
        value_ref[TOPP * KEPT : passage_keys, :HD] = jnp.where(flip, near, far)
        key_ref[passage_keys:, :] = own_ref[rows, columns(column * HD)]
        value_ref[passage_keys:, :HD] = own_ref[rows, columns(HALF + column * HD)]
        key_bound = scaled_keys(key_ref[...], turned_ref)
        small = jnp.max(bound_ref[...]) * key_bound <= SAFE_EXPONENT**2

        def score(group):
            score_ref[group % 2] = jnp.dot(
                head_rows(q_ref, rows, column * wide + group * heads_once * HD, heads_once),
                turned_ref[:, :passage_keys],
                preferred_element_type=jnp.float32,
            )

        def soften(group):
            expd_ref[group % 2] = jnp.exp2(score_ref[group % 2]).astype(jnp.bfloat16)

        def finish(group):
            summed = jnp.dot(
                expd_ref[group % 2], value_ref[:passage_keys, :], preferred_element_type=jnp.float32
            )
            weights = weight_ref[rows, columns(head * HD)]
            for i in range(heads_once):
                at = group * heads_once + i
                both = summed[i * QLEN : (i + 1) * QLEN]
                weight = both[:, HD:] + weights[:, at : at + 1]
                inverse = pl.reciprocal(weight, approx=True)
                inverse = inverse * (2.0 - weight * inverse)
                total = both[:, :HD] + sum_ref[rows, columns(head * wide + at * HD)].astype(jnp.float32)
                result_ref[slot, :, at * HD : (at + 1) * HD] = (total * inverse).astype(jnp.bfloat16)

        @pl.when(small)
        def unshifted():
            score(0)
            for group in range(groups):
                if group + 1 < groups:
                    score(group + 1)
                soften(group)
                if group > 0:
                    finish(group - 1)
            finish(groups - 1)

        @pl.when(jnp.logical_not(small))
        def shifted():
            visible = causal(heads_once * QLEN)
            for group in range(groups):
                scores = jnp.dot(
                    head_rows(q_ref, rows, column * wide + group * heads_once * HD, heads_once),
                    turned_ref[...],
                    preferred_element_type=jnp.float32,
                )
                scores = jnp.concatenate(
                    [scores[:, :passage_keys], jnp.where(visible, scores[:, passage_keys:], -jnp.inf)], axis=1
                )
                peak = jnp.max(scores, axis=1, keepdims=True)
                expd = jnp.exp2(scores - peak).astype(jnp.bfloat16)
                summed = jnp.dot(expd, value_ref[...], preferred_element_type=jnp.float32)
                ratio = (summed[:, :HD] / summed[:, HD:]).astype(jnp.bfloat16)
                for i in range(heads_once):
                    at = group * heads_once + i
                    result_ref[slot, :, at * HD : (at + 1) * HD] = ratio[i * QLEN : (i + 1) * QLEN]

        leave(step).start()
        return carry

    lax.fori_loop(0, steps, one, 0)
    for step in range(max(steps - 2, 0), steps):
        leave(step).wait()


def attend(part, info, q_rows, own_kv, kept, near, far, own, earlier=None):
    rows, width = q_rows.shape
    span = TOPP * PLEN + QLEN
    heads_once = 2
    vmem = pl.BlockSpec(memory_space=pltpu.VMEM)
    whole = pl.BlockSpec(memory_space=pl.ANY)
    operands = [info, q_rows, own_kv, kept, near, far, *own]
    aliases = {}
    if earlier is not None:
        aliases = {len(operands): 0}
        operands.append(earlier)
    return pl.pallas_call(
        functools.partial(attend_kernel, rows // QLEN * PAIR_HEADS, heads_once, part),
        in_specs=[pl.BlockSpec(memory_space=pltpu.SMEM)] + [vmem] * 8 + [whole] * len(aliases),
        out_specs=whole,
        out_shape=jax.ShapeDtypeStruct((rows, width), jnp.bfloat16),
        scratch_shapes=[
            pltpu.VMEM((span, HD), jnp.bfloat16),
            pltpu.VMEM((2 * HD, span), jnp.bfloat16),
            pltpu.VMEM((span, 2 * HD), jnp.bfloat16),
            pltpu.VMEM((2, heads_once * QLEN, TOPP * PLEN), jnp.float32),
            pltpu.VMEM((2, heads_once * QLEN, TOPP * PLEN), jnp.bfloat16),
            pltpu.VMEM((2, QLEN, GROUPED * HD), jnp.bfloat16),
            pltpu.SemaphoreType.DMA((2,)),
        ],
        input_output_aliases=aliases,
        compiler_params=pltpu.CompilerParams(vmem_limit_bytes=VMEM_BYTES),
        cost_estimate=LITTLE,
        name="attend",
    )(*operands)


def swap(array, axis, bits):
    size = lax.axis_size(axis)
    return lax.ppermute(array, axis, [(i, i ^ bits) for i in range(size)])


def recompute_general(normed, w_kv, pair):
    whole = lax.all_gather(lax.all_gather(w_kv, "member", axis=0, tiled=True), "group", axis=1, tiled=True)
    result = jnp.dot(normed, whole, preferred_element_type=jnp.float32).astype(jnp.bfloat16)
    result = result.reshape(-1, 2, PAIRS, PAIR_WIDTH)
    first = jnp.where(pair == 0, result[:, :, 0], result[:, :, 1])
    second = jnp.where(pair == 0, result[:, :, 1], result[:, :, 0])
    return [first[:, 0], first[:, 1]], [second[:, 0], second[:, 1]]


def local(q_rows, own_kv, cache, recomp_hidden, w_kv, retrieval, positions):
    queries = retrieval.shape[0]
    requests = queries * TOPP
    holders = lax.axis_size("member")
    groups = lax.axis_size("group")
    pass_local = cache.shape[0]
    capacity = -(-requests // holders)
    member = lax.axis_index("member")
    group = lax.axis_index("group")
    pair = group % PAIRS
    tuned = groups == 4 and holders == 8
    wanted = retrieval.reshape(requests)
    request = jnp.concatenate([wanted, positions.reshape(requests * RECOMP)])
    request = jnp.pad(request, (0, -request.shape[0] % 128)).reshape(1, -1, 128)
    request = jnp.broadcast_to(request, (holders,) + request.shape[1:])
    table = lax.all_to_all(request, "member", split_axis=0, concat_axis=0, tiled=True).reshape(-1)
    hidden = recomp_hidden.reshape(requests * RECOMP, D)
    hops = stack_hops(swap(w_kv, "member", 2), swap(w_kv, "member", 4)) if tuned else []
    normed = normalise(hidden, hops[:1])
    me = jnp.stack([member, pair]).astype(jnp.int32)
    ranks, passages = find_rows(table, me, holders, requests, pass_local, capacity, normed)
    holder_of = wanted // pass_local
    same = holder_of[:, None] == holder_of[None, :]
    before = jnp.arange(requests)[None, :] < jnp.arange(requests)[:, None]
    slot = holder_of * capacity + jnp.sum((same & before).astype(jnp.int32), axis=1)
    flip = group // 2 if tuned else jnp.int32(0)
    info = jnp.concatenate([jnp.stack([pair, flip]), slot]).astype(jnp.int32)
    other_info = jnp.concatenate([jnp.stack([1 - pair, flip]), slot]).astype(jnp.int32)
    first_own = attend_own(info, q_rows, own_kv, [ranks], [])
    pieces, ahead = [], [first_own[0]]
    if tuned:
        stack, two = hops
        aside, across = swap(w_kv, "member", 1), swap(w_kv, "group", 2)
        three = swap(two, "member", 2)
        stack_aside, stack_across = swap(stack, "member", 1), swap(stack, "group", 2)
        pieces = [aside, stack_aside, three]
        ahead += [across, stack_across]
    sent, *rest = pick_rows(me, passages, ranks, cache, pieces, ahead)
    arrived = lax.all_to_all(
        sent.reshape(holders, capacity * KEPT, 2 * HALF), "member", split_axis=0, concat_axis=0, tiled=True
    ).reshape(sent.shape)
    second_own = attend_own(other_info, q_rows, own_kv, [sent], [normed])
    normed = second_own[3]
    if tuned:
        other = swap(normed, "group", 1)
        rest_across = swap(rest[0], "group", 2)
        beside_three = swap(three, "member", 1)
        far_three = swap(beside_three, "group", 2)
        near, near_other = project(
            member,
            normed,
            other,
            [w_kv, aside, stack, stack_aside, three, beside_three],
            ((0, 0), (1, 0), (2, 0), (3, 0), (2, 1), (3, 1), (4, 0), (5, 0)),
            [],
        )
        far, far_other = project(
            member,
            normed,
            other,
            [across, stack_across, rest_across, far_three],
            ((0, 0), (2, 0), (1, 0), (2, 1), (1, 1), (2, 2), (2, 3), (3, 0)),
            [near],
        )
        first = [near, far]
        second = [swap(near_other, "group", 1), swap(far_other, "group", 1)]
    else:
        first, second = recompute_general(normed, w_kv, pair)
    out = attend(0, info, q_rows, own_kv, arrived, *first, first_own[:3])
    return attend(1, other_info, q_rows, own_kv, arrived, *second, second_own[:3], earlier=out)


def solution(mesh):
    rows = P(("group", "member"), None)
    placed = (
        rows,
        rows,
        P(("group", "member"), None, None),
        P(("group", "member"), None, None, None),
        P("member", "group"),
        rows,
        P(("group", "member"), None, None),
    )
    return jax.shard_map(local, mesh=mesh, in_specs=placed, out_specs=rows, check_vma=False)
```

```python
import functools

import jax
import jax.numpy as jnp
from jax import lax
from jax.experimental import pallas as pl
from jax.experimental.pallas import tpu as pltpu
from jax.sharding import PartitionSpec as P

D = 4096
HQ = 64
KVH = 4
HD = 128
TOPP = 8
QLEN = 128
PLEN = 64
RECOMP = 16
KEPT = PLEN - RECOMP
GROUPED = HQ // KVH
PAIRS = 2
PAIR_HEADS = KVH // PAIRS
PAIR_WIDTH = PAIR_HEADS * HD
HALF = KVH * HD

EPSILON = 1e-06
SCORE_FACTOR = 1.4426950408889634 / HD**0.5
SAFE_EXPONENT = 80.0
SMALL_VMEM = 12 * 1024 * 1024
VMEM_BYTES = 24 * 1024 * 1024
LITTLE = pl.CostEstimate(flops=1, bytes_accessed=1, transcendentals=0)
LARGE = pl.CostEstimate(flops=1, bytes_accessed=36_000_000, transcendentals=0)


def norm_kernel(tile, hidden_ref, *rest):
    normed_ref = rest[-1]

    def one(step, carry):
        rows = pl.ds(pl.multiple_of(step * tile, tile), tile)
        hidden = hidden_ref[rows, :].astype(jnp.float32)
        mean = jnp.mean(hidden * hidden, axis=1, keepdims=True)
        normed_ref[rows, :] = (hidden * lax.rsqrt(mean + EPSILON)).astype(jnp.bfloat16)
        return carry

    lax.fori_loop(0, hidden_ref.shape[0] // tile, one, 0)


def normalise(hidden, ahead):
    vmem = pl.BlockSpec(memory_space=pltpu.VMEM)
    return pl.pallas_call(
        functools.partial(norm_kernel, 32),
        in_specs=[vmem] + [pl.BlockSpec(memory_space=pl.ANY)] * len(ahead),
        out_specs=vmem,
        out_shape=jax.ShapeDtypeStruct(hidden.shape, jnp.bfloat16),
        compiler_params=pltpu.CompilerParams(vmem_limit_bytes=SMALL_VMEM),
        cost_estimate=LITTLE,
        name="normalise",
    )(hidden, *ahead)


def stack_kernel(one_ref, two_ref, stack_ref, copy_ref):
    depth = one_ref.shape[0]
    stack_ref[:depth, :] = one_ref[...]
    stack_ref[depth:, :] = two_ref[...]
    copy_ref[...] = two_ref[...]


def stack_hops(one, two):
    depth, width = one.shape
    vmem = pl.BlockSpec(memory_space=pltpu.VMEM)
    return pl.pallas_call(
        stack_kernel,
        in_specs=[vmem, vmem],
        out_specs=[vmem, vmem],
        out_shape=[jax.ShapeDtypeStruct((rows, width), jnp.bfloat16) for rows in (2 * depth, depth)],
        compiler_params=pltpu.CompilerParams(vmem_limit_bytes=SMALL_VMEM),
        cost_estimate=LITTLE,
        name="stack_hops",
    )(one, two)


def find_kernel(holders, requests, pass_local, capacity, me_ref, table_ref, *rest):
    rank_ref, passage_ref, slot_ref, kept_ref = rest[-4:]
    me = me_ref[0]
    stride = table_ref.shape[0] // holders
    for k in range(holders):
        base = k * (capacity + 1)
        for rank in range(capacity + 1):
            slot_ref[base + rank] = 0
        count = jnp.int32(0)
        for request in range(requests):
            slot_ref[base + count] = request
            mine = (table_ref[k * stride + request] // pass_local == me).astype(jnp.int32)
            count = jnp.minimum(count + mine, capacity)
    spot = lax.broadcasted_iota(jnp.int32, (1, PLEN), 1)
    for k in range(holders):
        for rank in range(capacity):
            at = k * capacity + rank
            request = slot_ref[k * (capacity + 1) + rank]
            passage_ref[at] = lax.rem(table_ref[k * stride + request], pass_local)
            start = k * stride + requests + request * RECOMP
            covered = spot < 0
            for r in range(RECOMP):
                covered = covered | (spot == table_ref[start + r])
            kept_ref[at : at + 1, :] = jnp.where(covered, 0.0, 1.0)
    kept = kept_ref[...]
    upto = lax.broadcasted_iota(jnp.int32, (PLEN, PLEN), 0) <= lax.broadcasted_iota(jnp.int32, (PLEN, PLEN), 1)
    rank_of = jnp.dot(
        kept.astype(jnp.bfloat16), upto.astype(jnp.bfloat16), preferred_element_type=jnp.float32
    )
    rank_ref[...] = jnp.where(kept > 0, rank_of, 0.0)


def find_rows(table, me, holders, requests, pass_local, capacity, normed):
    slots = holders * capacity
    smem = pl.BlockSpec(memory_space=pltpu.SMEM)
    whole = pl.BlockSpec(memory_space=pl.ANY)
    return pl.pallas_call(
        functools.partial(find_kernel, holders, requests, pass_local, capacity),
        in_specs=[smem, smem, whole],
        out_specs=[pl.BlockSpec(memory_space=pltpu.VMEM), smem],
        out_shape=[jax.ShapeDtypeStruct((slots, PLEN), jnp.float32), jax.ShapeDtypeStruct((slots,), jnp.int32)],
        scratch_shapes=[pltpu.SMEM((holders * (capacity + 1),), jnp.int32), pltpu.VMEM((slots, PLEN), jnp.float32)],
        compiler_params=pltpu.CompilerParams(vmem_limit_bytes=SMALL_VMEM),
        cost_estimate=LARGE,
        name="find_rows",
    )(me, table, normed)


def pick_kernel(pieces, me_ref, passage_ref, rank_ref, cache_ref, *rest):
    out_ref = rest[-2] if pieces else rest[-1]
    start = 0
    for piece in rest[:pieces]:
        rest[-1][start : start + piece.shape[0], :] = piece[...]
        start += piece.shape[0]
    pair = me_ref[1]
    row = (lax.broadcasted_iota(jnp.int32, (KEPT, PLEN), 0) + 1).astype(jnp.float32)
    for at in range(out_ref.shape[0]):
        passage = passage_ref[at]
        select = (rank_ref[at : at + 1, :] == row).astype(jnp.bfloat16)
        for place, part in ((0, pair), (1, 1 - pair)):
            for half in range(2):
                start = pl.multiple_of(half * HALF + part * PAIR_WIDTH, PAIR_WIDTH)
                end = (place * 2 + half) * PAIR_WIDTH
                out_ref[at, :, end : end + PAIR_WIDTH] = jnp.dot(
                    select, cache_ref[passage, :, pl.ds(start, PAIR_WIDTH)], preferred_element_type=jnp.float32
                ).astype(jnp.bfloat16)


def pick_rows(me, passages, ranks, cache, pieces, ahead):
    shapes = [jax.ShapeDtypeStruct((passages.shape[0], KEPT, 2 * HALF), jnp.bfloat16)]
    if pieces:
        rows = sum(piece.shape[0] for piece in pieces)
        shapes.append(jax.ShapeDtypeStruct((rows, pieces[0].shape[1]), jnp.bfloat16))
    smem = pl.BlockSpec(memory_space=pltpu.SMEM)
    vmem = pl.BlockSpec(memory_space=pltpu.VMEM)
    return pl.pallas_call(
        functools.partial(pick_kernel, len(pieces)),
        in_specs=[smem, smem] + [vmem] * (2 + len(pieces)) + [pl.BlockSpec(memory_space=pl.ANY)] * len(ahead),
        out_specs=[vmem] * len(shapes),
        out_shape=shapes,
        compiler_params=pltpu.CompilerParams(vmem_limit_bytes=SMALL_VMEM),
        cost_estimate=LITTLE,
        name="pick_rows",
    )(me, passages, ranks, cache, *pieces, *ahead)


def project_kernel(layout, member_ref, mine_ref, other_ref, *refs):
    mine_out, other_out = refs[-2:]
    rows = mine_ref.shape[0]
    depth = D // len(layout)
    total = None
    for k, (array, start) in enumerate(layout):
        chunk = pl.ds(pl.multiple_of((member_ref[0] ^ k) * depth, depth), depth)
        both = jnp.concatenate([mine_ref[:, chunk], other_ref[:, chunk]], axis=0)
        weights = refs[array][start * depth : (start + 1) * depth, :]
        term = jnp.dot(both, weights, preferred_element_type=jnp.float32)
        total = term if total is None else total + term
    mine_out[...] = total[:rows].astype(jnp.bfloat16)
    other_out[...] = total[rows:].astype(jnp.bfloat16)


def project(member, mine, other, arrays, layout, ahead):
    rows, width = mine.shape[0], arrays[0].shape[1]
    shape = jax.ShapeDtypeStruct((rows, width), jnp.bfloat16)
    vmem = pl.BlockSpec(memory_space=pltpu.VMEM)
    return pl.pallas_call(
        functools.partial(project_kernel, layout),
        in_specs=[pl.BlockSpec(memory_space=pltpu.SMEM)]
        + [vmem] * (2 + len(arrays))
        + [pl.BlockSpec(memory_space=pl.ANY)] * len(ahead),
        out_specs=[vmem, vmem],
        out_shape=[shape, shape],
        compiler_params=pltpu.CompilerParams(vmem_limit_bytes=SMALL_VMEM),
        cost_estimate=LITTLE,
        name="project",
    )(member.reshape(1), mine, other, *arrays, *ahead)


def scaled_keys(keys, turned_ref):
    scaled = keys.astype(jnp.float32) * SCORE_FACTOR
    high = scaled.astype(jnp.bfloat16)
    turned_ref[:HD, :] = high.T
    turned_ref[HD:, :] = (scaled - high.astype(jnp.float32)).astype(jnp.bfloat16).T
    return jnp.max(jnp.sum(scaled * scaled, axis=1, keepdims=True))


def head_rows(q_ref, rows, column, heads_once):
    block = jnp.concatenate(
        [q_ref[rows, pl.ds(pl.multiple_of(column + i * HD, HD), HD)] for i in range(heads_once)], axis=0
    )
    return jnp.concatenate([block, block], axis=1)


def causal(rows):
    token = lax.broadcasted_iota(jnp.int32, (rows, QLEN), 0) % QLEN
    return lax.broadcasted_iota(jnp.int32, (rows, QLEN), 1) <= token


def place(step, pair):
    query, head = step // PAIR_HEADS, step % PAIR_HEADS
    rows = pl.ds(pl.multiple_of(query * QLEN, QLEN), QLEN)
    return query, head, rows, pair * PAIR_HEADS + head


def columns(start, width=HD):
    return pl.ds(pl.multiple_of(start, HD), width)


def own_kernel(steps, heads_once, passing, info_ref, q_ref, own_ref, *rest):
    sum_ref, weight_ref, bound_ref = rest[-7 - passing : -4 - passing]
    turned_ref, wide_ref = rest[-2:]
    bound_ref[...] = jnp.zeros_like(bound_ref)
    shown = jnp.where(causal(heads_once * QLEN), 1.0, 0.0).astype(jnp.bfloat16)
    lane = lax.broadcasted_iota(jnp.int32, (QLEN, HD), 1)

    def one(step, carry):
        _, head, rows, column = place(step, info_ref[0])
        scaled_keys(own_ref[rows, columns(column * HD)], turned_ref)
        wide_ref[:, :HD] = own_ref[rows, columns(HALF + column * HD)]
        wide_ref[:, HD:] = jnp.ones((QLEN, HD), jnp.bfloat16)
        weights = jnp.zeros((QLEN, HD), jnp.float32)
        peak = jnp.zeros((QLEN, 1), jnp.float32)
        for first in range(0, GROUPED, heads_once):
            start = (column * GROUPED + first) * HD
            scores = jnp.dot(
                head_rows(q_ref, rows, start, heads_once), turned_ref[...], preferred_element_type=jnp.float32
            )
            summed = jnp.dot(
                jnp.exp2(scores).astype(jnp.bfloat16) * shown, wide_ref[...], preferred_element_type=jnp.float32
            )
            for i in range(heads_once):
                part = summed[i * QLEN : (i + 1) * QLEN]
                sum_ref[rows, columns((head * GROUPED + first + i) * HD)] = part[:, :HD].astype(jnp.bfloat16)
                weights = jnp.where(lane == first + i, part[:, HD:], weights)
            most = None
            for i in range(heads_once):
                block = q_ref[rows, columns(start + i * HD)].astype(jnp.float32)
                most = block * block if most is None else jnp.maximum(most, block * block)
            peak = jnp.maximum(peak, jnp.sum(most, axis=1, keepdims=True))
        weight_ref[rows, columns(head * HD)] = weights
        bound_ref[...] = jnp.maximum(bound_ref[...], jnp.max(peak))
        return carry

    lax.fori_loop(0, steps, one, 0)


def attend_own(info, q_rows, own_kv, ahead, passing):
    rows = q_rows.shape[0]
    whole = pl.BlockSpec(memory_space=pl.ANY)
    vmem = pl.BlockSpec(memory_space=pltpu.VMEM)
    return pl.pallas_call(
        functools.partial(own_kernel, rows // QLEN * PAIR_HEADS, 4, len(passing)),
        in_specs=[pl.BlockSpec(memory_space=pltpu.SMEM), vmem, vmem] + [whole] * (len(passing) + len(ahead)),
        out_specs=[vmem] * 5 + [whole] * len(passing),
        out_shape=[
            jax.ShapeDtypeStruct((rows, PAIR_HEADS * GROUPED * HD), jnp.bfloat16),
            jax.ShapeDtypeStruct((rows, PAIR_HEADS * HD), jnp.float32),
            jax.ShapeDtypeStruct((8, HD), jnp.float32),
        ]
        + [jax.ShapeDtypeStruct(part.shape, part.dtype) for part in (q_rows, own_kv, *passing)],
        scratch_shapes=[pltpu.VMEM((2 * HD, QLEN), jnp.bfloat16), pltpu.VMEM((QLEN, 2 * HD), jnp.bfloat16)],
        input_output_aliases={1 + i: 3 + i for i in range(2 + len(passing))},
        compiler_params=pltpu.CompilerParams(vmem_limit_bytes=VMEM_BYTES),
        cost_estimate=LITTLE,
        name="attend_own",
    )(info, q_rows, own_kv, *passing, *ahead)


def attend_kernel(
    steps,
    heads_once,
    part,
    info_ref,
    q_ref,
    own_ref,
    kept_ref,
    near_ref,
    far_ref,
    sum_ref,
    weight_ref,
    bound_ref,
    *rest,
):
    out_ref, key_ref, turned_ref, value_ref, score_ref, expd_ref, result_ref, done_ref = rest[-8:]
    passage_keys = TOPP * PLEN
    wide = GROUPED * HD
    groups = GROUPED // heads_once
    flip = info_ref[1] > 0
    value_ref[:, HD:] = jnp.ones((passage_keys + QLEN, HD), jnp.bfloat16)

    def leave(step):
        _, _, rows, column = place(step, info_ref[0])
        slot = step % 2
        return pltpu.make_async_copy(
            result_ref.at[slot], out_ref.at[rows, columns(column * wide, wide)], done_ref.at[slot]
        )

    def one(step, carry):
        query, head, rows, column = place(step, info_ref[0])
        slot = step % 2

        @pl.when(step >= 2)
        def free():
            leave(step - 2).wait()

        offset = part * HALF + head * HD
        for j in range(TOPP):
            block = info_ref[2 + query * TOPP + j]
            key_ref[j * KEPT : (j + 1) * KEPT, :] = kept_ref[block, :, columns(offset)]
            value_ref[j * KEPT : (j + 1) * KEPT, :HD] = kept_ref[block, :, columns(offset + PAIR_WIDTH)]
        near, far = near_ref[rows, columns(head * HD)], far_ref[rows, columns(head * HD)]
        key_ref[TOPP * KEPT : passage_keys, :] = jnp.where(flip, far, near)
        value_ref[TOPP * KEPT : passage_keys, :HD] = jnp.where(flip, near, far)
        key_ref[passage_keys:, :] = own_ref[rows, columns(column * HD)]
        value_ref[passage_keys:, :HD] = own_ref[rows, columns(HALF + column * HD)]
        key_bound = scaled_keys(key_ref[...], turned_ref)
        small = jnp.max(bound_ref[...]) * key_bound <= SAFE_EXPONENT**2

        def score(group):
            score_ref[group % 2] = jnp.dot(
                head_rows(q_ref, rows, column * wide + group * heads_once * HD, heads_once),
                turned_ref[:, :passage_keys],
                preferred_element_type=jnp.float32,
            )

        def soften(group):
            expd_ref[group % 2] = jnp.exp2(score_ref[group % 2]).astype(jnp.bfloat16)

        def finish(group):
            summed = jnp.dot(
                expd_ref[group % 2], value_ref[:passage_keys, :], preferred_element_type=jnp.float32
            )
            weights = weight_ref[rows, columns(head * HD)]
            for i in range(heads_once):
                at = group * heads_once + i
                both = summed[i * QLEN : (i + 1) * QLEN]
                weight = both[:, HD:] + weights[:, at : at + 1]
                inverse = pl.reciprocal(weight, approx=True)
                inverse = inverse * (2.0 - weight * inverse)
                total = both[:, :HD] + sum_ref[rows, columns(head * wide + at * HD)].astype(jnp.float32)
                result_ref[slot, :, at * HD : (at + 1) * HD] = (total * inverse).astype(jnp.bfloat16)

        @pl.when(small)
        def unshifted():
            score(0)
            for group in range(groups):
                if group + 1 < groups:
                    score(group + 1)
                soften(group)
                if group > 0:
                    finish(group - 1)
            finish(groups - 1)

        @pl.when(jnp.logical_not(small))
        def shifted():
            visible = causal(heads_once * QLEN)
            for group in range(groups):
                scores = jnp.dot(
                    head_rows(q_ref, rows, column * wide + group * heads_once * HD, heads_once),
                    turned_ref[...],
                    preferred_element_type=jnp.float32,
                )
                scores = jnp.concatenate(
                    [scores[:, :passage_keys], jnp.where(visible, scores[:, passage_keys:], -jnp.inf)], axis=1
                )
                peak = jnp.max(scores, axis=1, keepdims=True)
                expd = jnp.exp2(scores - peak).astype(jnp.bfloat16)
                summed = jnp.dot(expd, value_ref[...], preferred_element_type=jnp.float32)
                ratio = (summed[:, :HD] / summed[:, HD:]).astype(jnp.bfloat16)
                for i in range(heads_once):
                    at = group * heads_once + i
                    result_ref[slot, :, at * HD : (at + 1) * HD] = ratio[i * QLEN : (i + 1) * QLEN]

        leave(step).start()
        return carry

    lax.fori_loop(0, steps, one, 0)
    for step in range(max(steps - 2, 0), steps):
        leave(step).wait()


def attend(part, info, q_rows, own_kv, kept, near, far, own, earlier=None):
    rows, width = q_rows.shape
    span = TOPP * PLEN + QLEN
    heads_once = 2
    vmem = pl.BlockSpec(memory_space=pltpu.VMEM)
    whole = pl.BlockSpec(memory_space=pl.ANY)
    operands = [info, q_rows, own_kv, kept, near, far, *own]
    aliases = {}
    if earlier is not None:
        aliases = {len(operands): 0}
        operands.append(earlier)
    return pl.pallas_call(
        functools.partial(attend_kernel, rows // QLEN * PAIR_HEADS, heads_once, part),
        in_specs=[pl.BlockSpec(memory_space=pltpu.SMEM)] + [vmem] * 8 + [whole] * len(aliases),
        out_specs=whole,
        out_shape=jax.ShapeDtypeStruct((rows, width), jnp.bfloat16),
        scratch_shapes=[
            pltpu.VMEM((span, HD), jnp.bfloat16),
            pltpu.VMEM((2 * HD, span), jnp.bfloat16),
            pltpu.VMEM((span, 2 * HD), jnp.bfloat16),
            pltpu.VMEM((2, heads_once * QLEN, TOPP * PLEN), jnp.float32),
            pltpu.VMEM((2, heads_once * QLEN, TOPP * PLEN), jnp.bfloat16),
            pltpu.VMEM((2, QLEN, GROUPED * HD), jnp.bfloat16),
            pltpu.SemaphoreType.DMA((2,)),
        ],
        input_output_aliases=aliases,
        compiler_params=pltpu.CompilerParams(vmem_limit_bytes=VMEM_BYTES),
        cost_estimate=LITTLE,
        name="attend",
    )(*operands)


def swap(array, axis, bits):
    size = lax.axis_size(axis)
    return lax.ppermute(array, axis, [(i, i ^ bits) for i in range(size)])


def recompute_general(normed, w_kv, pair):
    whole = lax.all_gather(lax.all_gather(w_kv, "member", axis=0, tiled=True), "group", axis=1, tiled=True)
    result = jnp.dot(normed, whole, preferred_element_type=jnp.float32).astype(jnp.bfloat16)
    result = result.reshape(-1, 2, PAIRS, PAIR_WIDTH)
    first = jnp.where(pair == 0, result[:, :, 0], result[:, :, 1])
    second = jnp.where(pair == 0, result[:, :, 1], result[:, :, 0])
    return [first[:, 0], first[:, 1]], [second[:, 0], second[:, 1]]


def local(q_rows, own_kv, cache, recomp_hidden, w_kv, retrieval, positions):
    queries = retrieval.shape[0]
    requests = queries * TOPP
    holders = lax.axis_size("member")
    groups = lax.axis_size("group")
    pass_local = cache.shape[0]
    capacity = -(-requests // holders)
    member = lax.axis_index("member")
    group = lax.axis_index("group")
    pair = group % PAIRS
    tuned = groups == 4 and holders == 8
    wanted = retrieval.reshape(requests)
    request = jnp.concatenate([wanted, positions.reshape(requests * RECOMP)])
    request = jnp.pad(request, (0, -request.shape[0] % 128)).reshape(1, -1, 128)
    request = jnp.broadcast_to(request, (holders,) + request.shape[1:])
    table = lax.all_to_all(request, "member", split_axis=0, concat_axis=0, tiled=True).reshape(-1)
    hidden = recomp_hidden.reshape(requests * RECOMP, D)
    hops = stack_hops(swap(w_kv, "member", 2), swap(w_kv, "member", 4)) if tuned else []
    normed = normalise(hidden, hops[:1])
    me = jnp.stack([member, pair]).astype(jnp.int32)
    ranks, passages = find_rows(table, me, holders, requests, pass_local, capacity, normed)
    holder_of = wanted // pass_local
    same = holder_of[:, None] == holder_of[None, :]
    before = jnp.arange(requests)[None, :] < jnp.arange(requests)[:, None]
    slot = holder_of * capacity + jnp.sum((same & before).astype(jnp.int32), axis=1)
    flip = group // 2 if tuned else jnp.int32(0)
    info = jnp.concatenate([jnp.stack([pair, flip]), slot]).astype(jnp.int32)
    other_info = jnp.concatenate([jnp.stack([1 - pair, flip]), slot]).astype(jnp.int32)
    first_own = attend_own(info, q_rows, own_kv, [ranks], [])
    q_rows, own_kv = first_own[3:]
    pieces, ahead = [], [first_own[0]]
    if tuned:
        stack, two = hops
        aside, across = swap(w_kv, "member", 1), swap(w_kv, "group", 2)
        three = swap(two, "member", 2)
        stack_aside, stack_across = swap(stack, "member", 1), swap(stack, "group", 2)
        pieces = [stack_aside, three]
        ahead += [across, stack_across]
    sent, *rest = pick_rows(me, passages, ranks, cache, pieces, ahead)
    arrived = lax.all_to_all(
        sent.reshape(holders, capacity * KEPT, 2 * HALF), "member", split_axis=0, concat_axis=0, tiled=True
    ).reshape(sent.shape)
    second_own = attend_own(other_info, q_rows, own_kv, [sent], [aside] if tuned else [])
    q_rows, own_kv, *aside = second_own[3:]
    if tuned:
        aside = aside[0]
        other = swap(normed, "group", 1)
        rest_across = swap(rest[0], "group", 2)
        beside_three = swap(three, "member", 1)
        far_three = swap(beside_three, "group", 2)
        across_aside = swap(aside, "group", 2)
        near, near_other = project(
            member,
            normed,
            other,
            [w_kv, aside, stack, stack_aside, three, beside_three],
            ((0, 0), (1, 0), (2, 0), (3, 0), (2, 1), (3, 1), (4, 0), (5, 0)),
            [],
        )
        far, far_other = project(
            member,
            normed,
            other,
            [across, across_aside, stack_across, rest_across, far_three],
            ((0, 0), (1, 0), (2, 0), (3, 0), (2, 1), (3, 1), (3, 2), (4, 0)),
            [near],
        )
        first = [near, far]
        second = [swap(near_other, "group", 1), swap(far_other, "group", 1)]
    else:
        first, second = recompute_general(normed, w_kv, pair)
    out = attend(0, info, q_rows, own_kv, arrived, *first, first_own[:3])
    return attend(1, other_info, q_rows, own_kv, arrived, *second, second_own[:3], earlier=out)


def solution(mesh):
    rows = P(("group", "member"), None)
    placed = (
        rows,
        rows,
        P(("group", "member"), None, None),
        P(("group", "member"), None, None, None),
        P("member", "group"),
        rows,
        P(("group", "member"), None, None),
    )
    return jax.shard_map(local, mesh=mesh, in_specs=placed, out_specs=rows, check_vma=False)
```

```python
import functools

import jax
import jax.numpy as jnp
from jax import lax
from jax.experimental import pallas as pl
from jax.experimental.pallas import tpu as pltpu
from jax.sharding import PartitionSpec as P

D = 4096
HQ = 64
KVH = 4
HD = 128
TOPP = 8
QLEN = 128
PLEN = 64
RECOMP = 16
KEPT = PLEN - RECOMP
GROUPED = HQ // KVH
PAIRS = 2
PAIR_HEADS = KVH // PAIRS
PAIR_WIDTH = PAIR_HEADS * HD
HALF = KVH * HD

EPSILON = 1e-06
SCORE_FACTOR = 1.4426950408889634 / HD**0.5
SAFE_EXPONENT = 80.0
SMALL_VMEM = 12 * 1024 * 1024
VMEM_BYTES = 24 * 1024 * 1024
LARGE_VMEM = 58 * 1024 * 1024
LITTLE = pl.CostEstimate(flops=1, bytes_accessed=1, transcendentals=0)
LARGE = pl.CostEstimate(flops=1, bytes_accessed=36_000_000, transcendentals=0)


def norm_kernel(tile, hidden_ref, *rest):
    normed_ref = rest[-1]

    def one(step, carry):
        rows = pl.ds(pl.multiple_of(step * tile, tile), tile)
        hidden = hidden_ref[rows, :].astype(jnp.float32)
        mean = jnp.mean(hidden * hidden, axis=1, keepdims=True)
        normed_ref[rows, :] = (hidden * lax.rsqrt(mean + EPSILON)).astype(jnp.bfloat16)
        return carry

    lax.fori_loop(0, hidden_ref.shape[0] // tile, one, 0)


def normalise(hidden, ahead):
    vmem = pl.BlockSpec(memory_space=pltpu.VMEM)
    return pl.pallas_call(
        functools.partial(norm_kernel, 32),
        in_specs=[vmem] + [pl.BlockSpec(memory_space=pl.ANY)] * len(ahead),
        out_specs=vmem,
        out_shape=jax.ShapeDtypeStruct(hidden.shape, jnp.bfloat16),
        compiler_params=pltpu.CompilerParams(vmem_limit_bytes=SMALL_VMEM),
        cost_estimate=LITTLE,
        name="normalise",
    )(hidden, *ahead)


def stack_kernel(one_ref, two_ref, stack_ref, copy_ref):
    depth = one_ref.shape[0]
    stack_ref[:depth, :] = one_ref[...]
    stack_ref[depth:, :] = two_ref[...]
    copy_ref[...] = two_ref[...]


def stack_hops(one, two):
    depth, width = one.shape
    vmem = pl.BlockSpec(memory_space=pltpu.VMEM)
    return pl.pallas_call(
        stack_kernel,
        in_specs=[vmem, vmem],
        out_specs=[vmem, vmem],
        out_shape=[jax.ShapeDtypeStruct((rows, width), jnp.bfloat16) for rows in (2 * depth, depth)],
        compiler_params=pltpu.CompilerParams(vmem_limit_bytes=SMALL_VMEM),
        cost_estimate=LITTLE,
        name="stack_hops",
    )(one, two)


def find_kernel(holders, requests, pass_local, capacity, me_ref, table_ref, *rest):
    rank_ref, passage_ref, slot_ref, kept_ref = rest[-4:]
    me = me_ref[0]
    stride = table_ref.shape[0] // holders
    for k in range(holders):
        base = k * (capacity + 1)
        for rank in range(capacity + 1):
            slot_ref[base + rank] = 0
        count = jnp.int32(0)
        for request in range(requests):
            slot_ref[base + count] = request
            mine = (table_ref[k * stride + request] // pass_local == me).astype(jnp.int32)
            count = jnp.minimum(count + mine, capacity)
    spot = lax.broadcasted_iota(jnp.int32, (1, PLEN), 1)
    for k in range(holders):
        for rank in range(capacity):
            at = k * capacity + rank
            request = slot_ref[k * (capacity + 1) + rank]
            passage_ref[at] = lax.rem(table_ref[k * stride + request], pass_local)
            start = k * stride + requests + request * RECOMP
            covered = spot < 0
            for r in range(RECOMP):
                covered = covered | (spot == table_ref[start + r])
            kept_ref[at : at + 1, :] = jnp.where(covered, 0.0, 1.0)
    kept = kept_ref[...]
    upto = lax.broadcasted_iota(jnp.int32, (PLEN, PLEN), 0) <= lax.broadcasted_iota(jnp.int32, (PLEN, PLEN), 1)
    rank_of = jnp.dot(
        kept.astype(jnp.bfloat16), upto.astype(jnp.bfloat16), preferred_element_type=jnp.float32
    )
    rank_ref[...] = jnp.where(kept > 0, rank_of, 0.0)


def find_rows(table, me, holders, requests, pass_local, capacity, normed):
    slots = holders * capacity
    smem = pl.BlockSpec(memory_space=pltpu.SMEM)
    whole = pl.BlockSpec(memory_space=pl.ANY)
    return pl.pallas_call(
        functools.partial(find_kernel, holders, requests, pass_local, capacity),
        in_specs=[smem, smem, whole],
        out_specs=[pl.BlockSpec(memory_space=pltpu.VMEM), smem],
        out_shape=[jax.ShapeDtypeStruct((slots, PLEN), jnp.float32), jax.ShapeDtypeStruct((slots,), jnp.int32)],
        scratch_shapes=[pltpu.SMEM((holders * (capacity + 1),), jnp.int32), pltpu.VMEM((slots, PLEN), jnp.float32)],
        compiler_params=pltpu.CompilerParams(vmem_limit_bytes=SMALL_VMEM),
        cost_estimate=LARGE,
        name="find_rows",
    )(me, table, normed)


def pick_kernel(pieces, me_ref, passage_ref, rank_ref, cache_ref, *rest):
    out_ref = rest[-2] if pieces else rest[-1]
    start = 0
    for piece in rest[:pieces]:
        rest[-1][start : start + piece.shape[0], :] = piece[...]
        start += piece.shape[0]
    pair = me_ref[1]
    row = (lax.broadcasted_iota(jnp.int32, (KEPT, PLEN), 0) + 1).astype(jnp.float32)
    for at in range(out_ref.shape[0]):
        passage = passage_ref[at]
        select = (rank_ref[at : at + 1, :] == row).astype(jnp.bfloat16)
        for place, part in ((0, pair), (1, 1 - pair)):
            for half in range(2):
                start = pl.multiple_of(half * HALF + part * PAIR_WIDTH, PAIR_WIDTH)
                end = (place * 2 + half) * PAIR_WIDTH
                out_ref[at, :, end : end + PAIR_WIDTH] = jnp.dot(
                    select, cache_ref[passage, :, pl.ds(start, PAIR_WIDTH)], preferred_element_type=jnp.float32
                ).astype(jnp.bfloat16)


def pick_rows(me, passages, ranks, cache, pieces, ahead):
    shapes = [jax.ShapeDtypeStruct((passages.shape[0], KEPT, 2 * HALF), jnp.bfloat16)]
    if pieces:
        rows = sum(piece.shape[0] for piece in pieces)
        shapes.append(jax.ShapeDtypeStruct((rows, pieces[0].shape[1]), jnp.bfloat16))
    smem = pl.BlockSpec(memory_space=pltpu.SMEM)
    vmem = pl.BlockSpec(memory_space=pltpu.VMEM)
    return pl.pallas_call(
        functools.partial(pick_kernel, len(pieces)),
        in_specs=[smem, smem] + [vmem] * (2 + len(pieces)) + [pl.BlockSpec(memory_space=pl.ANY)] * len(ahead),
        out_specs=[vmem] * len(shapes),
        out_shape=shapes,
        compiler_params=pltpu.CompilerParams(vmem_limit_bytes=SMALL_VMEM),
        cost_estimate=LITTLE,
        name="pick_rows",
    )(me, passages, ranks, cache, *pieces, *ahead)


def project_kernel(layout, member_ref, mine_ref, other_ref, *refs):
    mine_out, other_out = refs[-2:]
    rows = mine_ref.shape[0]
    depth = D // len(layout)
    total = None
    for k, (array, start) in enumerate(layout):
        chunk = pl.ds(pl.multiple_of((member_ref[0] ^ k) * depth, depth), depth)
        both = jnp.concatenate([mine_ref[:, chunk], other_ref[:, chunk]], axis=0)
        weights = refs[array][start * depth : (start + 1) * depth, :]
        term = jnp.dot(both, weights, preferred_element_type=jnp.float32)
        total = term if total is None else total + term
    mine_out[...] = total[:rows].astype(jnp.bfloat16)
    other_out[...] = total[rows:].astype(jnp.bfloat16)


def project(member, mine, other, arrays, layout, ahead):
    rows, width = mine.shape[0], arrays[0].shape[1]
    shape = jax.ShapeDtypeStruct((rows, width), jnp.bfloat16)
    vmem = pl.BlockSpec(memory_space=pltpu.VMEM)
    return pl.pallas_call(
        functools.partial(project_kernel, layout),
        in_specs=[pl.BlockSpec(memory_space=pltpu.SMEM)]
        + [vmem] * (2 + len(arrays))
        + [pl.BlockSpec(memory_space=pl.ANY)] * len(ahead),
        out_specs=[vmem, vmem],
        out_shape=[shape, shape],
        compiler_params=pltpu.CompilerParams(vmem_limit_bytes=SMALL_VMEM),
        cost_estimate=LITTLE,
        name="project",
    )(member.reshape(1), mine, other, *arrays, *ahead)


def scaled_keys(keys, turned_ref):
    scaled = keys.astype(jnp.float32) * SCORE_FACTOR
    high = scaled.astype(jnp.bfloat16)
    turned_ref[:HD, :] = high.T
    turned_ref[HD:, :] = (scaled - high.astype(jnp.float32)).astype(jnp.bfloat16).T
    return jnp.max(jnp.sum(scaled * scaled, axis=1, keepdims=True))


def head_rows(q_ref, rows, column, heads_once):
    block = jnp.concatenate(
        [q_ref[rows, pl.ds(pl.multiple_of(column + i * HD, HD), HD)] for i in range(heads_once)], axis=0
    )
    return jnp.concatenate([block, block], axis=1)


def causal(rows):
    token = lax.broadcasted_iota(jnp.int32, (rows, QLEN), 0) % QLEN
    return lax.broadcasted_iota(jnp.int32, (rows, QLEN), 1) <= token


def place(step, pair):
    query, head = step // PAIR_HEADS, step % PAIR_HEADS
    rows = pl.ds(pl.multiple_of(query * QLEN, QLEN), QLEN)
    return query, head, rows, pair * PAIR_HEADS + head


def columns(start, width=HD):
    return pl.ds(pl.multiple_of(start, HD), width)


def own_kernel(steps, heads_once, passing, info_ref, q_ref, own_ref, *rest):
    sum_ref, weight_ref, bound_ref = rest[-5 - passing : -2 - passing]
    turned_ref, wide_ref = rest[-2:]
    bound_ref[...] = jnp.zeros_like(bound_ref)
    shown = jnp.where(causal(heads_once * QLEN), 1.0, 0.0).astype(jnp.bfloat16)
    lane = lax.broadcasted_iota(jnp.int32, (QLEN, HD), 1)

    def one(step, carry):
        _, head, rows, column = place(step, info_ref[0])
        scaled_keys(own_ref[rows, columns(column * HD)], turned_ref)
        wide_ref[:, :HD] = own_ref[rows, columns(HALF + column * HD)]
        wide_ref[:, HD:] = jnp.ones((QLEN, HD), jnp.bfloat16)
        weights = jnp.zeros((QLEN, HD), jnp.float32)
        peak = jnp.zeros((QLEN, 1), jnp.float32)
        for first in range(0, GROUPED, heads_once):
            start = (column * GROUPED + first) * HD
            scores = jnp.dot(
                head_rows(q_ref, rows, start, heads_once), turned_ref[...], preferred_element_type=jnp.float32
            )
            summed = jnp.dot(
                jnp.exp2(scores).astype(jnp.bfloat16) * shown, wide_ref[...], preferred_element_type=jnp.float32
            )
            for i in range(heads_once):
                part = summed[i * QLEN : (i + 1) * QLEN]
                sum_ref[rows, columns((head * GROUPED + first + i) * HD)] = part[:, :HD].astype(jnp.bfloat16)
                weights = jnp.where(lane == first + i, part[:, HD:], weights)
            most = None
            for i in range(heads_once):
                block = q_ref[rows, columns(start + i * HD)].astype(jnp.float32)
                most = block * block if most is None else jnp.maximum(most, block * block)
            peak = jnp.maximum(peak, jnp.sum(most, axis=1, keepdims=True))
        weight_ref[rows, columns(head * HD)] = weights
        bound_ref[...] = jnp.maximum(bound_ref[...], jnp.max(peak))
        return carry

    lax.fori_loop(0, steps, one, 0)


def attend_own(info, q_rows, own_kv, ahead, passing):
    rows = q_rows.shape[0]
    whole = pl.BlockSpec(memory_space=pl.ANY)
    vmem = pl.BlockSpec(memory_space=pltpu.VMEM)
    return pl.pallas_call(
        functools.partial(own_kernel, rows // QLEN * PAIR_HEADS, 4, len(passing)),
        in_specs=[pl.BlockSpec(memory_space=pltpu.SMEM), vmem, vmem] + [whole] * (len(passing) + len(ahead)),
        out_specs=[vmem] * 3 + [whole] * len(passing),
        out_shape=[
            jax.ShapeDtypeStruct((rows, PAIR_HEADS * GROUPED * HD), jnp.bfloat16),
            jax.ShapeDtypeStruct((rows, PAIR_HEADS * HD), jnp.float32),
            jax.ShapeDtypeStruct((8, HD), jnp.float32),
        ]
        + [jax.ShapeDtypeStruct(part.shape, part.dtype) for part in passing],
        scratch_shapes=[pltpu.VMEM((2 * HD, QLEN), jnp.bfloat16), pltpu.VMEM((QLEN, 2 * HD), jnp.bfloat16)],
        input_output_aliases={3 + i: 3 + i for i in range(len(passing))},
        compiler_params=pltpu.CompilerParams(vmem_limit_bytes=VMEM_BYTES),
        cost_estimate=LITTLE,
        name="attend_own",
    )(info, q_rows, own_kv, *passing, *ahead)


def block_rows(q_ref, slot, first, heads_once):
    block = jnp.concatenate(
        [q_ref[slot, :, (first + i) * HD : (first + i + 1) * HD] for i in range(heads_once)], axis=0
    )
    return jnp.concatenate([block, block], axis=1)


def fetch(step, start, array_ref, block_ref, arrived_ref):
    _, _, rows, _ = place(step, 0)
    wide, slot = GROUPED * HD, step % 2
    column = start + (step % PAIR_HEADS) * wide
    return pltpu.make_async_copy(
        array_ref.at[rows, columns(column, wide)], block_ref.at[slot], arrived_ref.at[slot]
    )


def leave(step, start, block_ref, array_ref, done_ref):
    _, _, rows, _ = place(step, 0)
    wide, slot = GROUPED * HD, step % 2
    column = start + (step % PAIR_HEADS) * wide
    return pltpu.make_async_copy(
        block_ref.at[slot], array_ref.at[rows, columns(column, wide)], done_ref.at[slot]
    )


def attend_kernel(
    steps,
    heads_once,
    part,
    info_ref,
    q_ref,
    own_hbm_ref,
    kept_ref,
    near_ref,
    far_ref,
    sum_ref,
    weight_ref,
    bound_ref,
    *rest,
):
    out_ref, key_ref, turned_ref, value_ref, score_ref, expd_ref, result_ref, done_ref = rest[-16:-8]
    block_ref, arrived_ref, cut_ref, cut_done_ref, own_ref, own_done_ref, part_ref, part_done_ref = rest[-8:]
    passage_keys = TOPP * PLEN
    wide = GROUPED * HD
    groups = GROUPED // heads_once
    flip = info_ref[1] > 0
    cut = pltpu.make_async_copy(kept_ref.at[:, :, part * HALF : (part + 1) * HALF], cut_ref, cut_done_ref)
    cut.start()
    own = pltpu.make_async_copy(own_hbm_ref, own_ref, own_done_ref)
    own.start()
    start = info_ref[0] * (PAIR_HEADS * wide)
    fetch(0, start, q_ref, block_ref, arrived_ref).start()
    fetch(0, 0, sum_ref, part_ref, part_done_ref).start()
    value_ref[:, HD:] = jnp.ones((passage_keys + QLEN, HD), jnp.bfloat16)
    cut.wait()
    own.wait()

    def one(step, carry):
        query, head, rows, column = place(step, info_ref[0])
        slot = step % 2

        @pl.when(step >= 2)
        def free():
            leave(step - 2, start, result_ref, out_ref, done_ref).wait()

        @pl.when(step + 1 < steps)
        def prefetch():
            fetch(step + 1, start, q_ref, block_ref, arrived_ref).start()
            fetch(step + 1, 0, sum_ref, part_ref, part_done_ref).start()

        offset = head * HD
        for j in range(TOPP):
            block = info_ref[2 + query * TOPP + j]
            key_ref[j * KEPT : (j + 1) * KEPT, :] = cut_ref[block, :, columns(offset)]
            value_ref[j * KEPT : (j + 1) * KEPT, :HD] = cut_ref[block, :, columns(offset + PAIR_WIDTH)]
        near, far = near_ref[rows, columns(head * HD)], far_ref[rows, columns(head * HD)]
        key_ref[TOPP * KEPT : passage_keys, :] = jnp.where(flip, far, near)
        value_ref[TOPP * KEPT : passage_keys, :HD] = jnp.where(flip, near, far)
        key_ref[passage_keys:, :] = own_ref[rows, columns(column * HD)]
        value_ref[passage_keys:, :HD] = own_ref[rows, columns(HALF + column * HD)]
        key_bound = scaled_keys(key_ref[...], turned_ref)
        small = jnp.max(bound_ref[...]) * key_bound <= SAFE_EXPONENT**2

        fetch(step, start, q_ref, block_ref, arrived_ref).wait()
        fetch(step, 0, sum_ref, part_ref, part_done_ref).wait()

        def score(group):
            score_ref[group % 2] = jnp.dot(
                block_rows(block_ref, slot, group * heads_once, heads_once),
                turned_ref[:, :passage_keys],
                preferred_element_type=jnp.float32,
            )

        def soften(group):
            expd_ref[group % 2] = jnp.exp2(score_ref[group % 2]).astype(jnp.bfloat16)

        def finish(group):
            summed = jnp.dot(
                expd_ref[group % 2], value_ref[:passage_keys, :], preferred_element_type=jnp.float32
            )
            weights = weight_ref[rows, columns(head * HD)]
            for i in range(heads_once):
                at = group * heads_once + i
                both = summed[i * QLEN : (i + 1) * QLEN]
                weight = both[:, HD:] + weights[:, at : at + 1]
                inverse = pl.reciprocal(weight, approx=True)
                inverse = inverse * (2.0 - weight * inverse)
                total = both[:, :HD] + part_ref[slot, :, at * HD : (at + 1) * HD].astype(jnp.float32)
                result_ref[slot, :, at * HD : (at + 1) * HD] = (total * inverse).astype(jnp.bfloat16)

        @pl.when(small)
        def unshifted():
            score(0)
            for group in range(groups):
                if group + 1 < groups:
                    score(group + 1)
                soften(group)
                if group > 0:
                    finish(group - 1)
            finish(groups - 1)

        @pl.when(jnp.logical_not(small))
        def shifted():
            visible = causal(heads_once * QLEN)
            for group in range(groups):
                scores = jnp.dot(
                    block_rows(block_ref, slot, group * heads_once, heads_once),
                    turned_ref[...],
                    preferred_element_type=jnp.float32,
                )
                scores = jnp.concatenate(
                    [scores[:, :passage_keys], jnp.where(visible, scores[:, passage_keys:], -jnp.inf)], axis=1
                )
                peak = jnp.max(scores, axis=1, keepdims=True)
                expd = jnp.exp2(scores - peak).astype(jnp.bfloat16)
                summed = jnp.dot(expd, value_ref[...], preferred_element_type=jnp.float32)
                ratio = (summed[:, :HD] / summed[:, HD:]).astype(jnp.bfloat16)
                for i in range(heads_once):
                    at = group * heads_once + i
                    result_ref[slot, :, at * HD : (at + 1) * HD] = ratio[i * QLEN : (i + 1) * QLEN]

        leave(step, start, result_ref, out_ref, done_ref).start()
        return carry

    lax.fori_loop(0, steps, one, 0)
    for step in range(max(steps - 2, 0), steps):
        leave(step, start, result_ref, out_ref, done_ref).wait()


def attend(part, info, q_rows, own_kv, kept, near, far, own, earlier=None):
    rows, width = q_rows.shape
    span = TOPP * PLEN + QLEN
    heads_once = 2
    vmem = pl.BlockSpec(memory_space=pltpu.VMEM)
    whole = pl.BlockSpec(memory_space=pl.ANY)
    hbm = pl.BlockSpec(memory_space=pltpu.HBM)
    operands = [info, q_rows, own_kv, kept, near, far, *own]
    aliases = {}
    if earlier is not None:
        aliases = {len(operands): 0}
        operands.append(earlier)
    return pl.pallas_call(
        functools.partial(attend_kernel, rows // QLEN * PAIR_HEADS, heads_once, part),
        in_specs=[pl.BlockSpec(memory_space=pltpu.SMEM)] + [hbm] * 3
        + [vmem] * 2
        + [hbm]
        + [vmem] * 2
        + [whole] * len(aliases),
        out_specs=whole,
        out_shape=jax.ShapeDtypeStruct((rows, width), jnp.bfloat16),
        scratch_shapes=[
            pltpu.VMEM((span, HD), jnp.bfloat16),
            pltpu.VMEM((2 * HD, span), jnp.bfloat16),
            pltpu.VMEM((span, 2 * HD), jnp.bfloat16),
            pltpu.VMEM((2, heads_once * QLEN, TOPP * PLEN), jnp.float32),
            pltpu.VMEM((2, heads_once * QLEN, TOPP * PLEN), jnp.bfloat16),
            pltpu.VMEM((2, QLEN, GROUPED * HD), jnp.bfloat16),
            pltpu.SemaphoreType.DMA((2,)),
            pltpu.VMEM((2, QLEN, GROUPED * HD), jnp.bfloat16),
            pltpu.SemaphoreType.DMA((2,)),
            pltpu.VMEM((kept.shape[0], KEPT, HALF), jnp.bfloat16),
            pltpu.SemaphoreType.DMA,
            pltpu.VMEM(own_kv.shape, jnp.bfloat16),
            pltpu.SemaphoreType.DMA,
            pltpu.VMEM((2, QLEN, GROUPED * HD), jnp.bfloat16),
            pltpu.SemaphoreType.DMA((2,)),
        ],
        input_output_aliases=aliases,
        compiler_params=pltpu.CompilerParams(vmem_limit_bytes=LARGE_VMEM),
        cost_estimate=LITTLE,
        name="attend",
    )(*operands)


def swap(array, axis, bits):
    size = lax.axis_size(axis)
    return lax.ppermute(array, axis, [(i, i ^ bits) for i in range(size)])


def recompute_general(normed, w_kv, pair):
    whole = lax.all_gather(lax.all_gather(w_kv, "member", axis=0, tiled=True), "group", axis=1, tiled=True)
    result = jnp.dot(normed, whole, preferred_element_type=jnp.float32).astype(jnp.bfloat16)
    result = result.reshape(-1, 2, PAIRS, PAIR_WIDTH)
    first = jnp.where(pair == 0, result[:, :, 0], result[:, :, 1])
    second = jnp.where(pair == 0, result[:, :, 1], result[:, :, 0])
    return [first[:, 0], first[:, 1]], [second[:, 0], second[:, 1]]


def local(q_rows, own_kv, cache, recomp_hidden, w_kv, retrieval, positions):
    queries = retrieval.shape[0]
    requests = queries * TOPP
    holders = lax.axis_size("member")
    groups = lax.axis_size("group")
    pass_local = cache.shape[0]
    capacity = -(-requests // holders)
    member = lax.axis_index("member")
    group = lax.axis_index("group")
    pair = group % PAIRS
    tuned = groups == 4 and holders == 8
    wanted = retrieval.reshape(requests)
    request = jnp.concatenate([wanted, positions.reshape(requests * RECOMP)])
    request = jnp.pad(request, (0, -request.shape[0] % 128)).reshape(1, -1, 128)
    request = jnp.broadcast_to(request, (holders,) + request.shape[1:])
    table = lax.all_to_all(request, "member", split_axis=0, concat_axis=0, tiled=True).reshape(-1)
    hidden = recomp_hidden.reshape(requests * RECOMP, D)
    hops = stack_hops(swap(w_kv, "member", 2), swap(w_kv, "member", 4)) if tuned else []
    normed = normalise(hidden, hops[:1])
    me = jnp.stack([member, pair]).astype(jnp.int32)
    ranks, passages = find_rows(table, me, holders, requests, pass_local, capacity, normed)
    holder_of = wanted // pass_local
    same = holder_of[:, None] == holder_of[None, :]
    before = jnp.arange(requests)[None, :] < jnp.arange(requests)[:, None]
    slot = holder_of * capacity + jnp.sum((same & before).astype(jnp.int32), axis=1)
    flip = group // 2 if tuned else jnp.int32(0)
    info = jnp.concatenate([jnp.stack([pair, flip]), slot]).astype(jnp.int32)
    other_info = jnp.concatenate([jnp.stack([1 - pair, flip]), slot]).astype(jnp.int32)
    first_own = attend_own(info, q_rows, own_kv, [ranks], [])
    pieces, ahead = [], [first_own[0]]
    if tuned:
        stack, two = hops
        aside, across = swap(w_kv, "member", 1), swap(w_kv, "group", 2)
        three = swap(two, "member", 2)
        stack_aside, stack_across = swap(stack, "member", 1), swap(stack, "group", 2)
        pieces = [stack_aside, three]
        ahead += [across, aside, stack_across]
    sent, *rest = pick_rows(me, passages, ranks, cache, pieces, ahead)
    arrived = lax.all_to_all(
        sent.reshape(holders, capacity * KEPT, 2 * HALF), "member", split_axis=0, concat_axis=0, tiled=True
    ).reshape(sent.shape)
    second_own = attend_own(other_info, q_rows, own_kv, [sent], [aside] if tuned else [])
    if tuned:
        aside = second_own[3]
        other = swap(normed, "group", 1)
        rest_across = swap(rest[0], "group", 2)
        beside_three = swap(three, "member", 1)
        far_three = swap(beside_three, "group", 2)
        across_aside = swap(aside, "group", 2)
        near, near_other = project(
            member,
            normed,
            other,
            [w_kv, aside, stack, stack_aside, three, beside_three],
            ((0, 0), (1, 0), (2, 0), (3, 0), (2, 1), (3, 1), (4, 0), (5, 0)),
            [],
        )
        far, far_other = project(
            member,
            normed,
            other,
            [across, across_aside, stack_across, rest_across, far_three],
            ((0, 0), (1, 0), (2, 0), (3, 0), (2, 1), (3, 1), (3, 2), (4, 0)),
            [near],
        )
        first = [near, far]
        second = [swap(near_other, "group", 1), swap(far_other, "group", 1)]
    else:
        first, second = recompute_general(normed, w_kv, pair)
    out = attend(0, info, q_rows, own_kv, arrived, *first, first_own[:3])
    return attend(1, other_info, q_rows, own_kv, arrived, *second, second_own[:3], earlier=out)


def solution(mesh):
    rows = P(("group", "member"), None)
    placed = (
        rows,
        rows,
        P(("group", "member"), None, None),
        P(("group", "member"), None, None, None),
        P("member", "group"),
        rows,
        P(("group", "member"), None, None),
    )
    return jax.shard_map(local, mesh=mesh, in_specs=placed, out_specs=rows, check_vma=False)
```

```python
import functools

import jax
import jax.numpy as jnp
from jax import lax
from jax.experimental import pallas as pl
from jax.experimental.pallas import tpu as pltpu
from jax.sharding import PartitionSpec as P

D = 4096
HQ = 64
KVH = 4
HD = 128
TOPP = 8
QLEN = 128
PLEN = 64
RECOMP = 16
KEPT = PLEN - RECOMP
GROUPED = HQ // KVH
PAIRS = 2
PAIR_HEADS = KVH // PAIRS
PAIR_WIDTH = PAIR_HEADS * HD
HALF = KVH * HD

EPSILON = 1e-06
SCORE_FACTOR = 1.4426950408889634 / HD**0.5
SAFE_EXPONENT = 80.0
SMALL_VMEM = 12 * 1024 * 1024
VMEM_BYTES = 24 * 1024 * 1024
LARGE_VMEM = 58 * 1024 * 1024
PIECES = 4
LITTLE = pl.CostEstimate(flops=1, bytes_accessed=1, transcendentals=0)
LARGE = pl.CostEstimate(flops=1, bytes_accessed=36_000_000, transcendentals=0)


def norm_kernel(tile, hidden_ref, *rest):
    normed_ref = rest[-1]

    def one(step, carry):
        rows = pl.ds(pl.multiple_of(step * tile, tile), tile)
        hidden = hidden_ref[rows, :].astype(jnp.float32)
        mean = jnp.mean(hidden * hidden, axis=1, keepdims=True)
        normed_ref[rows, :] = (hidden * lax.rsqrt(mean + EPSILON)).astype(jnp.bfloat16)
        return carry

    lax.fori_loop(0, hidden_ref.shape[0] // tile, one, 0)


def normalise(hidden, ahead):
    vmem = pl.BlockSpec(memory_space=pltpu.VMEM)
    return pl.pallas_call(
        functools.partial(norm_kernel, 32),
        in_specs=[vmem] + [pl.BlockSpec(memory_space=pl.ANY)] * len(ahead),
        out_specs=vmem,
        out_shape=jax.ShapeDtypeStruct(hidden.shape, jnp.bfloat16),
        compiler_params=pltpu.CompilerParams(vmem_limit_bytes=SMALL_VMEM),
        cost_estimate=LITTLE,
        name="normalise",
    )(hidden, *ahead)


def stack_kernel(one_ref, two_ref, stack_ref, copy_ref):
    depth = one_ref.shape[0]
    stack_ref[:depth, :] = one_ref[...]
    stack_ref[depth:, :] = two_ref[...]
    copy_ref[...] = two_ref[...]


def stack_hops(one, two):
    depth, width = one.shape
    vmem = pl.BlockSpec(memory_space=pltpu.VMEM)
    return pl.pallas_call(
        stack_kernel,
        in_specs=[vmem, vmem],
        out_specs=[vmem, vmem],
        out_shape=[jax.ShapeDtypeStruct((rows, width), jnp.bfloat16) for rows in (2 * depth, depth)],
        compiler_params=pltpu.CompilerParams(vmem_limit_bytes=SMALL_VMEM),
        cost_estimate=LITTLE,
        name="stack_hops",
    )(one, two)


def find_kernel(holders, requests, pass_local, capacity, me_ref, table_ref, *rest):
    rank_ref, passage_ref, slot_ref, kept_ref = rest[-4:]
    me = me_ref[0]
    stride = table_ref.shape[0] // holders
    for k in range(holders):
        base = k * (capacity + 1)
        for rank in range(capacity + 1):
            slot_ref[base + rank] = 0
        count = jnp.int32(0)
        for request in range(requests):
            slot_ref[base + count] = request
            mine = (table_ref[k * stride + request] // pass_local == me).astype(jnp.int32)
            count = jnp.minimum(count + mine, capacity)
    spot = lax.broadcasted_iota(jnp.int32, (1, PLEN), 1)
    for k in range(holders):
        for rank in range(capacity):
            at = k * capacity + rank
            request = slot_ref[k * (capacity + 1) + rank]
            passage_ref[at] = lax.rem(table_ref[k * stride + request], pass_local)
            start = k * stride + requests + request * RECOMP
            covered = spot < 0
            for r in range(RECOMP):
                covered = covered | (spot == table_ref[start + r])
            kept_ref[at : at + 1, :] = jnp.where(covered, 0.0, 1.0)
    kept = kept_ref[...]
    upto = lax.broadcasted_iota(jnp.int32, (PLEN, PLEN), 0) <= lax.broadcasted_iota(jnp.int32, (PLEN, PLEN), 1)
    rank_of = jnp.dot(
        kept.astype(jnp.bfloat16), upto.astype(jnp.bfloat16), preferred_element_type=jnp.float32
    )
    rank_ref[...] = jnp.where(kept > 0, rank_of, 0.0)


def find_rows(table, me, holders, requests, pass_local, capacity, normed):
    slots = holders * capacity
    smem = pl.BlockSpec(memory_space=pltpu.SMEM)
    whole = pl.BlockSpec(memory_space=pl.ANY)
    return pl.pallas_call(
        functools.partial(find_kernel, holders, requests, pass_local, capacity),
        in_specs=[smem, smem, whole],
        out_specs=[pl.BlockSpec(memory_space=pltpu.VMEM), smem],
        out_shape=[jax.ShapeDtypeStruct((slots, PLEN), jnp.float32), jax.ShapeDtypeStruct((slots,), jnp.int32)],
        scratch_shapes=[pltpu.SMEM((holders * (capacity + 1),), jnp.int32), pltpu.VMEM((slots, PLEN), jnp.float32)],
        compiler_params=pltpu.CompilerParams(vmem_limit_bytes=SMALL_VMEM),
        cost_estimate=LARGE,
        name="find_rows",
    )(me, table, normed)


def pick_kernel(pieces, me_ref, passage_ref, rank_ref, cache_ref, *rest):
    out_ref = rest[-2] if pieces else rest[-1]
    start = 0
    for piece in rest[:pieces]:
        rest[-1][start : start + piece.shape[0], :] = piece[...]
        start += piece.shape[0]
    pair = me_ref[1]
    row = (lax.broadcasted_iota(jnp.int32, (KEPT, PLEN), 0) + 1).astype(jnp.float32)
    for at in range(out_ref.shape[0]):
        passage = passage_ref[at]
        select = (rank_ref[at : at + 1, :] == row).astype(jnp.bfloat16)
        for place, part in ((0, pair), (1, 1 - pair)):
            for half in range(2):
                start = pl.multiple_of(half * HALF + part * PAIR_WIDTH, PAIR_WIDTH)
                end = (place * 2 + half) * PAIR_WIDTH
                out_ref[at, :, end : end + PAIR_WIDTH] = jnp.dot(
                    select, cache_ref[passage, :, pl.ds(start, PAIR_WIDTH)], preferred_element_type=jnp.float32
                ).astype(jnp.bfloat16)


def pick_rows(me, passages, ranks, cache, pieces, ahead):
    shapes = [jax.ShapeDtypeStruct((passages.shape[0], KEPT, 2 * HALF), jnp.bfloat16)]
    if pieces:
        rows = sum(piece.shape[0] for piece in pieces)
        shapes.append(jax.ShapeDtypeStruct((rows, pieces[0].shape[1]), jnp.bfloat16))
    smem = pl.BlockSpec(memory_space=pltpu.SMEM)
    vmem = pl.BlockSpec(memory_space=pltpu.VMEM)
    return pl.pallas_call(
        functools.partial(pick_kernel, len(pieces)),
        in_specs=[smem, smem] + [vmem] * (2 + len(pieces)) + [pl.BlockSpec(memory_space=pl.ANY)] * len(ahead),
        out_specs=[vmem] * len(shapes),
        out_shape=shapes,
        compiler_params=pltpu.CompilerParams(vmem_limit_bytes=SMALL_VMEM),
        cost_estimate=LITTLE,
        name="pick_rows",
    )(me, passages, ranks, cache, *pieces, *ahead)


def project_kernel(chunks, layout, carried, last, member_ref, mine_ref, other_ref, *refs):
    rows = mine_ref.shape[0]
    depth = D // chunks
    total = refs[-3 if last else -2][...] if carried else None
    for k, array, start in layout:
        chunk = pl.ds(pl.multiple_of((member_ref[0] ^ k) * depth, depth), depth)
        both = jnp.concatenate([mine_ref[:, chunk], other_ref[:, chunk]], axis=0)
        weights = refs[array][start * depth : (start + 1) * depth, :]
        term = jnp.dot(both, weights, preferred_element_type=jnp.float32)
        total = term if total is None else total + term
    if last:
        refs[-2][...] = total[:rows].astype(jnp.bfloat16)
        refs[-1][...] = total[rows:].astype(jnp.bfloat16)
    else:
        refs[-1][...] = total


def project(member, mine, other, arrays, layout, ahead=(), carry=None, last=True):
    rows, width = mine.shape[0], arrays[0].shape[1]
    chunks = D // arrays[0].shape[0]
    vmem = pl.BlockSpec(memory_space=pltpu.VMEM)
    carried = [] if carry is None else [carry]
    shape = [jax.ShapeDtypeStruct((rows, width), jnp.bfloat16)] * 2
    if not last:
        shape = [jax.ShapeDtypeStruct((2 * rows, width), jnp.float32)]
    return pl.pallas_call(
        functools.partial(project_kernel, chunks, layout, bool(carried), last),
        in_specs=[pl.BlockSpec(memory_space=pltpu.SMEM)]
        + [vmem] * (2 + len(arrays))
        + [pl.BlockSpec(memory_space=pl.ANY)] * len(ahead)
        + [vmem] * len(carried),
        out_specs=[vmem] * len(shape),
        out_shape=shape,
        compiler_params=pltpu.CompilerParams(vmem_limit_bytes=SMALL_VMEM),
        cost_estimate=LITTLE,
        name="project",
    )(member.reshape(1), mine, other, *arrays, *ahead, *carried)


def scaled_keys(keys, turned_ref):
    scaled = keys.astype(jnp.float32) * SCORE_FACTOR
    high = scaled.astype(jnp.bfloat16)
    turned_ref[:HD, :] = high.T
    turned_ref[HD:, :] = (scaled - high.astype(jnp.float32)).astype(jnp.bfloat16).T
    return jnp.max(jnp.sum(scaled * scaled, axis=1, keepdims=True))


def head_rows(q_ref, rows, column, heads_once):
    block = jnp.concatenate(
        [q_ref[rows, pl.ds(pl.multiple_of(column + i * HD, HD), HD)] for i in range(heads_once)], axis=0
    )
    return jnp.concatenate([block, block], axis=1)


def causal(rows):
    token = lax.broadcasted_iota(jnp.int32, (rows, QLEN), 0) % QLEN
    return lax.broadcasted_iota(jnp.int32, (rows, QLEN), 1) <= token


def place(step, pair):
    query, head = step // PAIR_HEADS, step % PAIR_HEADS
    rows = pl.ds(pl.multiple_of(query * QLEN, QLEN), QLEN)
    return query, head, rows, pair * PAIR_HEADS + head


def columns(start, width=HD):
    return pl.ds(pl.multiple_of(start, HD), width)


def own_kernel(steps, heads_once, passing, info_ref, q_ref, own_ref, *rest):
    sum_ref, weight_ref, bound_ref = rest[-5 - passing : -2 - passing]
    turned_ref, wide_ref = rest[-2:]
    bound_ref[...] = jnp.zeros_like(bound_ref)
    shown = jnp.where(causal(heads_once * QLEN), 1.0, 0.0).astype(jnp.bfloat16)
    lane = lax.broadcasted_iota(jnp.int32, (QLEN, HD), 1)

    def one(step, carry):
        _, head, rows, column = place(step, info_ref[0])
        scaled_keys(own_ref[rows, columns(column * HD)], turned_ref)
        wide_ref[:, :HD] = own_ref[rows, columns(HALF + column * HD)]
        wide_ref[:, HD:] = jnp.ones((QLEN, HD), jnp.bfloat16)
        weights = jnp.zeros((QLEN, HD), jnp.float32)
        peak = jnp.zeros((QLEN, 1), jnp.float32)
        for first in range(0, GROUPED, heads_once):
            start = (column * GROUPED + first) * HD
            scores = jnp.dot(
                head_rows(q_ref, rows, start, heads_once), turned_ref[...], preferred_element_type=jnp.float32
            )
            summed = jnp.dot(
                jnp.exp2(scores).astype(jnp.bfloat16) * shown, wide_ref[...], preferred_element_type=jnp.float32
            )
            for i in range(heads_once):
                part = summed[i * QLEN : (i + 1) * QLEN]
                sum_ref[rows, columns((head * GROUPED + first + i) * HD)] = part[:, :HD].astype(jnp.bfloat16)
                weights = jnp.where(lane == first + i, part[:, HD:], weights)
            most = None
            for i in range(heads_once):
                block = q_ref[rows, columns(start + i * HD)].astype(jnp.float32)
                most = block * block if most is None else jnp.maximum(most, block * block)
            peak = jnp.maximum(peak, jnp.sum(most, axis=1, keepdims=True))
        weight_ref[rows, columns(head * HD)] = weights
        bound_ref[...] = jnp.maximum(bound_ref[...], jnp.max(peak))
        return carry

    lax.fori_loop(0, steps, one, 0)


def attend_own(info, q_rows, own_kv, ahead, passing):
    rows = q_rows.shape[0]
    whole = pl.BlockSpec(memory_space=pl.ANY)
    vmem = pl.BlockSpec(memory_space=pltpu.VMEM)
    return pl.pallas_call(
        functools.partial(own_kernel, rows // QLEN * PAIR_HEADS, 4, len(passing)),
        in_specs=[pl.BlockSpec(memory_space=pltpu.SMEM), vmem, vmem] + [whole] * (len(passing) + len(ahead)),
        out_specs=[vmem] * 3 + [whole] * len(passing),
        out_shape=[
            jax.ShapeDtypeStruct((rows, PAIR_HEADS * GROUPED * HD), jnp.bfloat16),
            jax.ShapeDtypeStruct((rows, PAIR_HEADS * HD), jnp.float32),
            jax.ShapeDtypeStruct((8, HD), jnp.float32),
        ]
        + [jax.ShapeDtypeStruct(part.shape, part.dtype) for part in passing],
        scratch_shapes=[pltpu.VMEM((2 * HD, QLEN), jnp.bfloat16), pltpu.VMEM((QLEN, 2 * HD), jnp.bfloat16)],
        input_output_aliases={3 + i: 3 + i for i in range(len(passing))},
        compiler_params=pltpu.CompilerParams(vmem_limit_bytes=VMEM_BYTES),
        cost_estimate=LITTLE,
        name="attend_own",
    )(info, q_rows, own_kv, *passing, *ahead)


def block_rows(q_ref, slot, first, heads_once):
    block = jnp.concatenate(
        [q_ref[slot, :, (first + i) * HD : (first + i + 1) * HD] for i in range(heads_once)], axis=0
    )
    return jnp.concatenate([block, block], axis=1)


def block_copies(step, start, array_ref, block_ref, signal_ref, inward):
    wide, slot = GROUPED * HD, step % 2
    column = columns(start + (step % PAIR_HEADS) * wide, wide)
    height = QLEN // PIECES
    copies = []
    for i in range(PIECES):
        outer = array_ref.at[pl.ds(pl.multiple_of(step // PAIR_HEADS * QLEN + i * height, height), height), column]
        inner = block_ref.at[slot, i * height : (i + 1) * height]
        ends = (outer, inner) if inward else (inner, outer)
        copies.append(pltpu.make_async_copy(*ends, signal_ref.at[slot, i]))
    return copies


def start_all(copies):
    for copy in copies:
        copy.start()


def wait_all(copies):
    for copy in copies:
        copy.wait()


def attend_kernel(
    steps,
    heads_once,
    part,
    info_ref,
    q_ref,
    own_hbm_ref,
    kept_ref,
    near_ref,
    far_ref,
    sum_ref,
    weight_ref,
    bound_ref,
    *rest,
):
    out_ref, key_ref, turned_ref, value_ref, score_ref, expd_ref, result_ref, done_ref = rest[-16:-8]
    block_ref, arrived_ref, cut_ref, cut_done_ref, own_ref, own_done_ref, part_ref, part_done_ref = rest[-8:]
    passage_keys = TOPP * PLEN
    wide = GROUPED * HD
    groups = GROUPED // heads_once
    flip = info_ref[1] > 0
    cuts = []
    for i in range(2 * PAIR_HEADS):
        head, half = divmod(i, 2)
        first = part * HALF + half * PAIR_WIDTH + head * HD
        cuts.append(
            pltpu.make_async_copy(kept_ref.at[:, :, first : first + HD], cut_ref.at[i], cut_done_ref.at[i])
        )
    own = pltpu.make_async_copy(own_hbm_ref, own_ref, own_done_ref)
    own.start()
    start = info_ref[0] * (PAIR_HEADS * wide)

    def fetch(step):
        return block_copies(step, start, q_ref, block_ref, arrived_ref, True) + block_copies(
            step, 0, sum_ref, part_ref, part_done_ref, True
        )

    def leave(step):
        return block_copies(step, start, out_ref, result_ref, done_ref, False)

    start_all(cuts[:2])
    start_all(fetch(0))
    start_all(cuts[2:])
    value_ref[:, HD:] = jnp.ones((passage_keys + QLEN, HD), jnp.bfloat16)
    own.wait()

    def one(step, carry):
        query, head, rows, column = place(step, info_ref[0])
        slot = step % 2

        @pl.when(step >= 2)
        def free():
            wait_all(leave(step - 2))

        @pl.when(step + 1 < steps)
        def prefetch():
            start_all(fetch(step + 1))

        for turn in range(PAIR_HEADS):

            @pl.when(step == turn)
            def columns_here(turn=turn):
                wait_all(cuts[2 * turn : 2 * turn + 2])

        for j in range(TOPP):
            block = info_ref[2 + query * TOPP + j]
            key_ref[j * KEPT : (j + 1) * KEPT, :] = cut_ref[2 * head, block]
            value_ref[j * KEPT : (j + 1) * KEPT, :HD] = cut_ref[2 * head + 1, block]
        near, far = near_ref[rows, columns(head * HD)], far_ref[rows, columns(head * HD)]
        key_ref[TOPP * KEPT : passage_keys, :] = jnp.where(flip, far, near)
        value_ref[TOPP * KEPT : passage_keys, :HD] = jnp.where(flip, near, far)
        key_ref[passage_keys:, :] = own_ref[rows, columns(column * HD)]
        value_ref[passage_keys:, :HD] = own_ref[rows, columns(HALF + column * HD)]
        key_bound = scaled_keys(key_ref[...], turned_ref)
        small = jnp.max(bound_ref[...]) * key_bound <= SAFE_EXPONENT**2

        wait_all(fetch(step))

        def score(group):
            score_ref[group % 2] = jnp.dot(
                block_rows(block_ref, slot, group * heads_once, heads_once),
                turned_ref[:, :passage_keys],
                preferred_element_type=jnp.float32,
            )

        def soften(group):
            expd_ref[group % 2] = jnp.exp2(score_ref[group % 2]).astype(jnp.bfloat16)

        def finish(group):
            summed = jnp.dot(
                expd_ref[group % 2], value_ref[:passage_keys, :], preferred_element_type=jnp.float32
            )
            weights = weight_ref[rows, columns(head * HD)]
            for i in range(heads_once):
                at = group * heads_once + i
                both = summed[i * QLEN : (i + 1) * QLEN]
                weight = both[:, HD:] + weights[:, at : at + 1]
                inverse = pl.reciprocal(weight, approx=True)
                inverse = inverse * (2.0 - weight * inverse)
                total = both[:, :HD] + part_ref[slot, :, at * HD : (at + 1) * HD].astype(jnp.float32)
                result_ref[slot, :, at * HD : (at + 1) * HD] = (total * inverse).astype(jnp.bfloat16)

        @pl.when(small)
        def unshifted():
            score(0)
            for group in range(groups):
                if group + 1 < groups:
                    score(group + 1)
                soften(group)
                if group > 0:
                    finish(group - 1)
            finish(groups - 1)

        @pl.when(jnp.logical_not(small))
        def shifted():
            visible = causal(heads_once * QLEN)
            for group in range(groups):
                scores = jnp.dot(
                    block_rows(block_ref, slot, group * heads_once, heads_once),
                    turned_ref[...],
                    preferred_element_type=jnp.float32,
                )
                scores = jnp.concatenate(
                    [scores[:, :passage_keys], jnp.where(visible, scores[:, passage_keys:], -jnp.inf)], axis=1
                )
                peak = jnp.max(scores, axis=1, keepdims=True)
                expd = jnp.exp2(scores - peak).astype(jnp.bfloat16)
                summed = jnp.dot(expd, value_ref[...], preferred_element_type=jnp.float32)
                ratio = (summed[:, :HD] / summed[:, HD:]).astype(jnp.bfloat16)
                for i in range(heads_once):
                    at = group * heads_once + i
                    result_ref[slot, :, at * HD : (at + 1) * HD] = ratio[i * QLEN : (i + 1) * QLEN]

        start_all(leave(step))
        return carry

    lax.fori_loop(0, steps, one, 0)
    for step in range(max(steps - 2, 0), steps):
        wait_all(leave(step))


def attend(part, info, q_rows, own_kv, kept, near, far, own, earlier=None):
    rows, width = q_rows.shape
    span = TOPP * PLEN + QLEN
    heads_once = 2
    vmem = pl.BlockSpec(memory_space=pltpu.VMEM)
    whole = pl.BlockSpec(memory_space=pl.ANY)
    hbm = pl.BlockSpec(memory_space=pltpu.HBM)
    operands = [info, q_rows, own_kv, kept, near, far, *own]
    aliases = {}
    if earlier is not None:
        aliases = {len(operands): 0}
        operands.append(earlier)
    return pl.pallas_call(
        functools.partial(attend_kernel, rows // QLEN * PAIR_HEADS, heads_once, part),
        in_specs=[pl.BlockSpec(memory_space=pltpu.SMEM)] + [hbm] * 3
        + [vmem] * 2
        + [hbm]
        + [vmem] * 2
        + [whole] * len(aliases),
        out_specs=whole,
        out_shape=jax.ShapeDtypeStruct((rows, width), jnp.bfloat16),
        scratch_shapes=[
            pltpu.VMEM((span, HD), jnp.bfloat16),
            pltpu.VMEM((2 * HD, span), jnp.bfloat16),
            pltpu.VMEM((span, 2 * HD), jnp.bfloat16),
            pltpu.VMEM((2, heads_once * QLEN, TOPP * PLEN), jnp.float32),
            pltpu.VMEM((2, heads_once * QLEN, TOPP * PLEN), jnp.bfloat16),
            pltpu.VMEM((2, QLEN, GROUPED * HD), jnp.bfloat16),
            pltpu.SemaphoreType.DMA((2, PIECES)),
            pltpu.VMEM((2, QLEN, GROUPED * HD), jnp.bfloat16),
            pltpu.SemaphoreType.DMA((2, PIECES)),
            pltpu.VMEM((2 * PAIR_HEADS, kept.shape[0], KEPT, HD), jnp.bfloat16),
            pltpu.SemaphoreType.DMA((2 * PAIR_HEADS,)),
            pltpu.VMEM(own_kv.shape, jnp.bfloat16),
            pltpu.SemaphoreType.DMA,
            pltpu.VMEM((2, QLEN, GROUPED * HD), jnp.bfloat16),
            pltpu.SemaphoreType.DMA((2, PIECES)),
        ],
        input_output_aliases=aliases,
        compiler_params=pltpu.CompilerParams(vmem_limit_bytes=LARGE_VMEM),
        cost_estimate=LITTLE,
        name="attend",
    )(*operands)


def swap(array, axis, bits):
    size = lax.axis_size(axis)
    return lax.ppermute(array, axis, [(i, i ^ bits) for i in range(size)])


def recompute_general(normed, w_kv, pair):
    whole = lax.all_gather(lax.all_gather(w_kv, "member", axis=0, tiled=True), "group", axis=1, tiled=True)
    result = jnp.dot(normed, whole, preferred_element_type=jnp.float32).astype(jnp.bfloat16)
    result = result.reshape(-1, 2, PAIRS, PAIR_WIDTH)
    first = jnp.where(pair == 0, result[:, :, 0], result[:, :, 1])
    second = jnp.where(pair == 0, result[:, :, 1], result[:, :, 0])
    return [first[:, 0], first[:, 1]], [second[:, 0], second[:, 1]]


def local(q_rows, own_kv, cache, recomp_hidden, w_kv, retrieval, positions):
    queries = retrieval.shape[0]
    requests = queries * TOPP
    holders = lax.axis_size("member")
    groups = lax.axis_size("group")
    pass_local = cache.shape[0]
    capacity = -(-requests // holders)
    member = lax.axis_index("member")
    group = lax.axis_index("group")
    pair = group % PAIRS
    tuned = groups == 4 and holders == 8
    wanted = retrieval.reshape(requests)
    request = jnp.concatenate([wanted, positions.reshape(requests * RECOMP)])
    request = jnp.pad(request, (0, -request.shape[0] % 128)).reshape(1, -1, 128)
    request = jnp.broadcast_to(request, (holders,) + request.shape[1:])
    table = lax.all_to_all(request, "member", split_axis=0, concat_axis=0, tiled=True).reshape(-1)
    hidden = recomp_hidden.reshape(requests * RECOMP, D)
    hops = stack_hops(swap(w_kv, "member", 2), swap(w_kv, "member", 4)) if tuned else []
    normed = normalise(hidden, hops[:1])
    me = jnp.stack([member, pair]).astype(jnp.int32)
    ranks, passages = find_rows(table, me, holders, requests, pass_local, capacity, normed)
    holder_of = wanted // pass_local
    same = holder_of[:, None] == holder_of[None, :]
    before = jnp.arange(requests)[None, :] < jnp.arange(requests)[:, None]
    slot = holder_of * capacity + jnp.sum((same & before).astype(jnp.int32), axis=1)
    flip = group // 2 if tuned else jnp.int32(0)
    info = jnp.concatenate([jnp.stack([pair, flip]), slot]).astype(jnp.int32)
    other_info = jnp.concatenate([jnp.stack([1 - pair, flip]), slot]).astype(jnp.int32)
    first_own = attend_own(info, q_rows, own_kv, [ranks], [])
    pieces, ahead = [], [first_own[0]]
    if tuned:
        stack, two = hops
        aside, across = swap(w_kv, "member", 1), swap(w_kv, "group", 2)
        three = swap(two, "member", 2)
        stack_aside, stack_across = swap(stack, "member", 1), swap(stack, "group", 2)
        pieces = [stack_aside, three]
        ahead += [across, aside, stack_across]
    sent, *rest = pick_rows(me, passages, ranks, cache, pieces, ahead)
    arrived = lax.all_to_all(
        sent.reshape(holders, capacity * KEPT, 2 * HALF), "member", split_axis=0, concat_axis=0, tiled=True
    ).reshape(sent.shape)
    second_own = attend_own(other_info, q_rows, own_kv, [sent], [aside] if tuned else [])
    if tuned:
        aside = second_own[3]
        other = swap(normed, "group", 1)
        rest_across = swap(rest[0], "group", 2)
        beside_three = swap(three, "member", 1)
        far_three = swap(beside_three, "group", 2)
        across_aside = swap(aside, "group", 2)
        near, near_other = project(
            member,
            normed,
            other,
            [w_kv, aside, stack, stack_aside, three, beside_three],
            ((0, 0, 0), (1, 1, 0), (2, 2, 0), (3, 3, 0), (4, 2, 1), (5, 3, 1), (6, 4, 0), (7, 5, 0)),
        )
        (begun,) = project(
            member,
            normed,
            other,
            [across, across_aside, stack_across, rest_across],
            ((0, 0, 0), (1, 1, 0), (2, 2, 0), (3, 3, 0), (4, 2, 1), (5, 3, 1), (6, 3, 2)),
            [near],
            last=False,
        )
        far, far_other = project(member, normed, other, [far_three], ((7, 0, 0),), carry=begun)
        first = [near, far]
        second = [swap(near_other, "group", 1), swap(far_other, "group", 1)]
    else:
        first, second = recompute_general(normed, w_kv, pair)
    out = attend(0, info, q_rows, own_kv, arrived, *first, first_own[:3])
    return attend(1, other_info, q_rows, own_kv, arrived, *second, second_own[:3], earlier=out)


def solution(mesh):
    rows = P(("group", "member"), None)
    placed = (
        rows,
        rows,
        P(("group", "member"), None, None),
        P(("group", "member"), None, None, None),
        P("member", "group"),
        rows,
        P(("group", "member"), None, None),
    )
    return jax.shard_map(local, mesh=mesh, in_specs=placed, out_specs=rows, check_vma=False)
```

```python
import functools

import jax
import jax.numpy as jnp
from jax import lax
from jax.experimental import pallas as pl
from jax.experimental.pallas import tpu as pltpu
from jax.sharding import PartitionSpec as P

D = 4096
HQ = 64
KVH = 4
HD = 128
TOPP = 8
QLEN = 128
PLEN = 64
RECOMP = 16
KEPT = PLEN - RECOMP
GROUPED = HQ // KVH
PAIRS = 2
PAIR_HEADS = KVH // PAIRS
PAIR_WIDTH = PAIR_HEADS * HD
HALF = KVH * HD

EPSILON = 1e-06
SCORE_FACTOR = 1.4426950408889634 / HD**0.5
SAFE_EXPONENT = 80.0
SMALL_VMEM = 12 * 1024 * 1024
VMEM_BYTES = 24 * 1024 * 1024
LARGE_VMEM = 58 * 1024 * 1024
LITTLE = pl.CostEstimate(flops=1, bytes_accessed=1, transcendentals=0)
LARGE = pl.CostEstimate(flops=1, bytes_accessed=36_000_000, transcendentals=0)


def norm_kernel(tile, hidden_ref, *rest):
    normed_ref = rest[-1]

    def one(step, carry):
        rows = pl.ds(pl.multiple_of(step * tile, tile), tile)
        hidden = hidden_ref[rows, :].astype(jnp.float32)
        mean = jnp.mean(hidden * hidden, axis=1, keepdims=True)
        normed_ref[rows, :] = (hidden * lax.rsqrt(mean + EPSILON)).astype(jnp.bfloat16)
        return carry

    lax.fori_loop(0, hidden_ref.shape[0] // tile, one, 0)


def normalise(hidden, ahead):
    vmem = pl.BlockSpec(memory_space=pltpu.VMEM)
    return pl.pallas_call(
        functools.partial(norm_kernel, 32),
        in_specs=[vmem] + [pl.BlockSpec(memory_space=pl.ANY)] * len(ahead),
        out_specs=vmem,
        out_shape=jax.ShapeDtypeStruct(hidden.shape, jnp.bfloat16),
        compiler_params=pltpu.CompilerParams(vmem_limit_bytes=SMALL_VMEM),
        cost_estimate=LITTLE,
        name="normalise",
    )(hidden, *ahead)


def stack_kernel(one_ref, two_ref, stack_ref, copy_ref):
    depth = one_ref.shape[0]
    stack_ref[:depth, :] = one_ref[...]
    stack_ref[depth:, :] = two_ref[...]
    copy_ref[...] = two_ref[...]


def stack_hops(one, two):
    depth, width = one.shape
    vmem = pl.BlockSpec(memory_space=pltpu.VMEM)
    return pl.pallas_call(
        stack_kernel,
        in_specs=[vmem, vmem],
        out_specs=[vmem, vmem],
        out_shape=[jax.ShapeDtypeStruct((rows, width), jnp.bfloat16) for rows in (2 * depth, depth)],
        compiler_params=pltpu.CompilerParams(vmem_limit_bytes=SMALL_VMEM),
        cost_estimate=LITTLE,
        name="stack_hops",
    )(one, two)


def find_kernel(holders, requests, pass_local, capacity, me_ref, table_ref, *rest):
    rank_ref, passage_ref, slot_ref, kept_ref = rest[-4:]
    me = me_ref[0]
    stride = table_ref.shape[0] // holders
    for k in range(holders):
        base = k * (capacity + 1)
        for rank in range(capacity + 1):
            slot_ref[base + rank] = 0
        count = jnp.int32(0)
        for request in range(requests):
            slot_ref[base + count] = request
            mine = (table_ref[k * stride + request] // pass_local == me).astype(jnp.int32)
            count = jnp.minimum(count + mine, capacity)
    spot = lax.broadcasted_iota(jnp.int32, (1, PLEN), 1)
    for k in range(holders):
        for rank in range(capacity):
            at = k * capacity + rank
            request = slot_ref[k * (capacity + 1) + rank]
            passage_ref[at] = lax.rem(table_ref[k * stride + request], pass_local)
            start = k * stride + requests + request * RECOMP
            covered = spot < 0
            for r in range(RECOMP):
                covered = covered | (spot == table_ref[start + r])
            kept_ref[at : at + 1, :] = jnp.where(covered, 0.0, 1.0)
    kept = kept_ref[...]
    upto = lax.broadcasted_iota(jnp.int32, (PLEN, PLEN), 0) <= lax.broadcasted_iota(jnp.int32, (PLEN, PLEN), 1)
    rank_of = jnp.dot(
        kept.astype(jnp.bfloat16), upto.astype(jnp.bfloat16), preferred_element_type=jnp.float32
    )
    rank_ref[...] = jnp.where(kept > 0, rank_of, 0.0)


def find_rows(table, me, holders, requests, pass_local, capacity, normed):
    slots = holders * capacity
    smem = pl.BlockSpec(memory_space=pltpu.SMEM)
    whole = pl.BlockSpec(memory_space=pl.ANY)
    return pl.pallas_call(
        functools.partial(find_kernel, holders, requests, pass_local, capacity),
        in_specs=[smem, smem, whole],
        out_specs=[pl.BlockSpec(memory_space=pltpu.VMEM), smem],
        out_shape=[jax.ShapeDtypeStruct((slots, PLEN), jnp.float32), jax.ShapeDtypeStruct((slots,), jnp.int32)],
        scratch_shapes=[pltpu.SMEM((holders * (capacity + 1),), jnp.int32), pltpu.VMEM((slots, PLEN), jnp.float32)],
        compiler_params=pltpu.CompilerParams(vmem_limit_bytes=SMALL_VMEM),
        cost_estimate=LARGE,
        name="find_rows",
    )(me, table, normed)


def pick_kernel(me_ref, passage_ref, rank_ref, cache_ref, *rest):
    out_ref = rest[-1]
    pair = me_ref[1]
    row = (lax.broadcasted_iota(jnp.int32, (KEPT, PLEN), 0) + 1).astype(jnp.float32)
    for at in range(out_ref.shape[0]):
        passage = passage_ref[at]
        select = (rank_ref[at : at + 1, :] == row).astype(jnp.bfloat16)
        for place, part in ((0, pair), (1, 1 - pair)):
            for half in range(2):
                start = pl.multiple_of(half * HALF + part * PAIR_WIDTH, PAIR_WIDTH)
                end = (place * 2 + half) * PAIR_WIDTH
                out_ref[at, :, end : end + PAIR_WIDTH] = jnp.dot(
                    select, cache_ref[passage, :, pl.ds(start, PAIR_WIDTH)], preferred_element_type=jnp.float32
                ).astype(jnp.bfloat16)


def pick_rows(me, passages, ranks, cache, ahead):
    smem = pl.BlockSpec(memory_space=pltpu.SMEM)
    vmem = pl.BlockSpec(memory_space=pltpu.VMEM)
    return pl.pallas_call(
        pick_kernel,
        in_specs=[smem, smem, vmem, vmem] + [pl.BlockSpec(memory_space=pl.ANY)] * len(ahead),
        out_specs=vmem,
        out_shape=jax.ShapeDtypeStruct((passages.shape[0], KEPT, 2 * HALF), jnp.bfloat16),
        compiler_params=pltpu.CompilerParams(vmem_limit_bytes=SMALL_VMEM),
        cost_estimate=LITTLE,
        name="pick_rows",
    )(me, passages, ranks, cache, *ahead)


def project_kernel(chunks, layout, carried, last, member_ref, mine_ref, other_ref, *refs):
    rows = mine_ref.shape[0]
    depth = D // chunks
    total = refs[-3 if last else -2][...] if carried else None
    for k, array, start in layout:
        chunk = pl.ds(pl.multiple_of((member_ref[0] ^ k) * depth, depth), depth)
        both = jnp.concatenate([mine_ref[:, chunk], other_ref[:, chunk]], axis=0)
        weights = refs[array][start * depth : (start + 1) * depth, :]
        term = jnp.dot(both, weights, preferred_element_type=jnp.float32)
        total = term if total is None else total + term
    if last:
        refs[-2][...] = total[:rows].astype(jnp.bfloat16)
        refs[-1][...] = total[rows:].astype(jnp.bfloat16)
    else:
        refs[-1][...] = total


def project(member, mine, other, arrays, layout, ahead=(), carry=None, last=True):
    rows, width = mine.shape[0], arrays[0].shape[1]
    chunks = D // arrays[0].shape[0]
    vmem = pl.BlockSpec(memory_space=pltpu.VMEM)
    carried = [] if carry is None else [carry]
    shape = [jax.ShapeDtypeStruct((rows, width), jnp.bfloat16)] * 2
    if not last:
        shape = [jax.ShapeDtypeStruct((2 * rows, width), jnp.float32)]
    return pl.pallas_call(
        functools.partial(project_kernel, chunks, layout, bool(carried), last),
        in_specs=[pl.BlockSpec(memory_space=pltpu.SMEM)]
        + [vmem] * (2 + len(arrays))
        + [pl.BlockSpec(memory_space=pl.ANY)] * len(ahead)
        + [vmem] * len(carried),
        out_specs=[vmem] * len(shape),
        out_shape=shape,
        compiler_params=pltpu.CompilerParams(vmem_limit_bytes=SMALL_VMEM),
        cost_estimate=LITTLE,
        name="project",
    )(member.reshape(1), mine, other, *arrays, *ahead, *carried)


def scaled_keys(keys, turned_ref):
    scaled = keys.astype(jnp.float32) * SCORE_FACTOR
    high = scaled.astype(jnp.bfloat16)
    turned_ref[:HD, :] = high.T
    turned_ref[HD:, :] = (scaled - high.astype(jnp.float32)).astype(jnp.bfloat16).T
    return jnp.max(jnp.sum(scaled * scaled, axis=1, keepdims=True))


def head_rows(q_ref, rows, column, heads_once):
    block = jnp.concatenate(
        [q_ref[rows, pl.ds(pl.multiple_of(column + i * HD, HD), HD)] for i in range(heads_once)], axis=0
    )
    return jnp.concatenate([block, block], axis=1)


def causal(rows):
    token = lax.broadcasted_iota(jnp.int32, (rows, QLEN), 0) % QLEN
    return lax.broadcasted_iota(jnp.int32, (rows, QLEN), 1) <= token


def place(step, pair):
    query, head = step // PAIR_HEADS, step % PAIR_HEADS
    rows = pl.ds(pl.multiple_of(query * QLEN, QLEN), QLEN)
    return query, head, rows, pair * PAIR_HEADS + head


def columns(start, width=HD):
    return pl.ds(pl.multiple_of(start, HD), width)


def own_kernel(steps, heads_once, passing, info_ref, q_ref, own_ref, *rest):
    sum_ref, weight_ref, bound_ref = rest[-5 - passing : -2 - passing]
    turned_ref, wide_ref = rest[-2:]
    bound_ref[...] = jnp.zeros_like(bound_ref)
    shown = jnp.where(causal(heads_once * QLEN), 1.0, 0.0).astype(jnp.bfloat16)
    lane = lax.broadcasted_iota(jnp.int32, (QLEN, HD), 1)

    def one(step, carry):
        _, head, rows, column = place(step, info_ref[0])
        scaled_keys(own_ref[rows, columns(column * HD)], turned_ref)
        wide_ref[:, :HD] = own_ref[rows, columns(HALF + column * HD)]
        wide_ref[:, HD:] = jnp.ones((QLEN, HD), jnp.bfloat16)
        weights = jnp.zeros((QLEN, HD), jnp.float32)
        peak = jnp.zeros((QLEN, 1), jnp.float32)
        for first in range(0, GROUPED, heads_once):
            start = (column * GROUPED + first) * HD
            scores = jnp.dot(
                head_rows(q_ref, rows, start, heads_once), turned_ref[...], preferred_element_type=jnp.float32
            )
            summed = jnp.dot(
                jnp.exp2(scores).astype(jnp.bfloat16) * shown, wide_ref[...], preferred_element_type=jnp.float32
            )
            for i in range(heads_once):
                part = summed[i * QLEN : (i + 1) * QLEN]
                sum_ref[rows, columns((head * GROUPED + first + i) * HD)] = part[:, :HD].astype(jnp.bfloat16)
                weights = jnp.where(lane == first + i, part[:, HD:], weights)
            most = None
            for i in range(heads_once):
                block = q_ref[rows, columns(start + i * HD)].astype(jnp.float32)
                most = block * block if most is None else jnp.maximum(most, block * block)
            peak = jnp.maximum(peak, jnp.sum(most, axis=1, keepdims=True))
        weight_ref[rows, columns(head * HD)] = weights
        bound_ref[...] = jnp.maximum(bound_ref[...], jnp.max(peak))
        return carry

    lax.fori_loop(0, steps, one, 0)


def attend_own(info, q_rows, own_kv, ahead, passing):
    rows = q_rows.shape[0]
    whole = pl.BlockSpec(memory_space=pl.ANY)
    vmem = pl.BlockSpec(memory_space=pltpu.VMEM)
    return pl.pallas_call(
        functools.partial(own_kernel, rows // QLEN * PAIR_HEADS, 4, len(passing)),
        in_specs=[pl.BlockSpec(memory_space=pltpu.SMEM), vmem, vmem] + [whole] * (len(passing) + len(ahead)),
        out_specs=[vmem] * 3 + [whole] * len(passing),
        out_shape=[
            jax.ShapeDtypeStruct((rows, PAIR_HEADS * GROUPED * HD), jnp.bfloat16),
            jax.ShapeDtypeStruct((rows, PAIR_HEADS * HD), jnp.float32),
            jax.ShapeDtypeStruct((8, HD), jnp.float32),
        ]
        + [jax.ShapeDtypeStruct(part.shape, part.dtype) for part in passing],
        scratch_shapes=[pltpu.VMEM((2 * HD, QLEN), jnp.bfloat16), pltpu.VMEM((QLEN, 2 * HD), jnp.bfloat16)],
        input_output_aliases={3 + i: 3 + i for i in range(len(passing))},
        compiler_params=pltpu.CompilerParams(vmem_limit_bytes=VMEM_BYTES),
        cost_estimate=LITTLE,
        name="attend_own",
    )(info, q_rows, own_kv, *passing, *ahead)


def block_rows(q_ref, slot, first, heads_once):
    block = jnp.concatenate(
        [q_ref[slot, :, (first + i) * HD : (first + i + 1) * HD] for i in range(heads_once)], axis=0
    )
    return jnp.concatenate([block, block], axis=1)


def fetch(step, start, array_ref, block_ref, arrived_ref):
    _, _, rows, _ = place(step, 0)
    wide, slot = GROUPED * HD, step % 2
    column = start + (step % PAIR_HEADS) * wide
    return pltpu.make_async_copy(
        array_ref.at[rows, columns(column, wide)], block_ref.at[slot], arrived_ref.at[slot]
    )


def leave(step, start, block_ref, array_ref, done_ref):
    _, _, rows, _ = place(step, 0)
    wide, slot = GROUPED * HD, step % 2
    column = start + (step % PAIR_HEADS) * wide
    return pltpu.make_async_copy(
        block_ref.at[slot], array_ref.at[rows, columns(column, wide)], done_ref.at[slot]
    )


def attend_kernel(
    steps,
    heads_once,
    part,
    info_ref,
    q_ref,
    own_hbm_ref,
    kept_ref,
    near_ref,
    far_ref,
    sum_ref,
    weight_ref,
    bound_ref,
    *rest,
):
    out_ref, key_ref, turned_ref, value_ref, score_ref, expd_ref, result_ref, done_ref = rest[-16:-8]
    block_ref, arrived_ref, cut_ref, cut_done_ref, own_ref, own_done_ref, part_ref, part_done_ref = rest[-8:]
    passage_keys = TOPP * PLEN
    wide = GROUPED * HD
    groups = GROUPED // heads_once
    flip = info_ref[1] > 0
    cut = pltpu.make_async_copy(kept_ref.at[:, :, part * HALF : (part + 1) * HALF], cut_ref, cut_done_ref)
    cut.start()
    own = pltpu.make_async_copy(own_hbm_ref, own_ref, own_done_ref)
    own.start()
    start = info_ref[0] * (PAIR_HEADS * wide)
    fetch(0, start, q_ref, block_ref, arrived_ref).start()
    fetch(0, 0, sum_ref, part_ref, part_done_ref).start()
    value_ref[:, HD:] = jnp.ones((passage_keys + QLEN, HD), jnp.bfloat16)
    cut.wait()
    own.wait()

    def one(step, carry):
        query, head, rows, column = place(step, info_ref[0])
        slot = step % 2

        @pl.when(step >= 2)
        def free():
            leave(step - 2, start, result_ref, out_ref, done_ref).wait()

        @pl.when(step + 1 < steps)
        def prefetch():
            fetch(step + 1, start, q_ref, block_ref, arrived_ref).start()
            fetch(step + 1, 0, sum_ref, part_ref, part_done_ref).start()

        offset = head * HD
        for j in range(TOPP):
            block = info_ref[2 + query * TOPP + j]
            key_ref[j * KEPT : (j + 1) * KEPT, :] = cut_ref[block, :, columns(offset)]
            value_ref[j * KEPT : (j + 1) * KEPT, :HD] = cut_ref[block, :, columns(offset + PAIR_WIDTH)]
        near, far = near_ref[rows, columns(head * HD)], far_ref[rows, columns(head * HD)]
        key_ref[TOPP * KEPT : passage_keys, :] = jnp.where(flip, far, near)
        value_ref[TOPP * KEPT : passage_keys, :HD] = jnp.where(flip, near, far)
        key_ref[passage_keys:, :] = own_ref[rows, columns(column * HD)]
        value_ref[passage_keys:, :HD] = own_ref[rows, columns(HALF + column * HD)]
        key_bound = scaled_keys(key_ref[...], turned_ref)
        small = jnp.max(bound_ref[...]) * key_bound <= SAFE_EXPONENT**2

        fetch(step, start, q_ref, block_ref, arrived_ref).wait()
        fetch(step, 0, sum_ref, part_ref, part_done_ref).wait()

        def score(group):
            score_ref[group % 2] = jnp.dot(
                block_rows(block_ref, slot, group * heads_once, heads_once),
                turned_ref[:, :passage_keys],
                preferred_element_type=jnp.float32,
            )

        def soften(group):
            expd_ref[group % 2] = jnp.exp2(score_ref[group % 2]).astype(jnp.bfloat16)

        def finish(group):
            summed = jnp.dot(
                expd_ref[group % 2], value_ref[:passage_keys, :], preferred_element_type=jnp.float32
            )
            weights = weight_ref[rows, columns(head * HD)]
            for i in range(heads_once):
                at = group * heads_once + i
                both = summed[i * QLEN : (i + 1) * QLEN]
                weight = both[:, HD:] + weights[:, at : at + 1]
                inverse = pl.reciprocal(weight, approx=True)
                inverse = inverse * (2.0 - weight * inverse)
                total = both[:, :HD] + part_ref[slot, :, at * HD : (at + 1) * HD].astype(jnp.float32)
                result_ref[slot, :, at * HD : (at + 1) * HD] = (total * inverse).astype(jnp.bfloat16)

        @pl.when(small)
        def unshifted():
            score(0)
            for group in range(groups):
                if group + 1 < groups:
                    score(group + 1)
                soften(group)
                if group > 0:
                    finish(group - 1)
            finish(groups - 1)

        @pl.when(jnp.logical_not(small))
        def shifted():
            visible = causal(heads_once * QLEN)
            for group in range(groups):
                scores = jnp.dot(
                    block_rows(block_ref, slot, group * heads_once, heads_once),
                    turned_ref[...],
                    preferred_element_type=jnp.float32,
                )
                scores = jnp.concatenate(
                    [scores[:, :passage_keys], jnp.where(visible, scores[:, passage_keys:], -jnp.inf)], axis=1
                )
                peak = jnp.max(scores, axis=1, keepdims=True)
                expd = jnp.exp2(scores - peak).astype(jnp.bfloat16)
                summed = jnp.dot(expd, value_ref[...], preferred_element_type=jnp.float32)
                ratio = (summed[:, :HD] / summed[:, HD:]).astype(jnp.bfloat16)
                for i in range(heads_once):
                    at = group * heads_once + i
                    result_ref[slot, :, at * HD : (at + 1) * HD] = ratio[i * QLEN : (i + 1) * QLEN]

        leave(step, start, result_ref, out_ref, done_ref).start()
        return carry

    lax.fori_loop(0, steps, one, 0)
    for step in range(max(steps - 2, 0), steps):
        leave(step, start, result_ref, out_ref, done_ref).wait()


def attend(part, info, q_rows, own_kv, kept, near, far, own, earlier=None):
    rows, width = q_rows.shape
    span = TOPP * PLEN + QLEN
    heads_once = 2
    vmem = pl.BlockSpec(memory_space=pltpu.VMEM)
    whole = pl.BlockSpec(memory_space=pl.ANY)
    hbm = pl.BlockSpec(memory_space=pltpu.HBM)
    operands = [info, q_rows, own_kv, kept, near, far, *own]
    aliases = {}
    if earlier is not None:
        aliases = {len(operands): 0}
        operands.append(earlier)
    return pl.pallas_call(
        functools.partial(attend_kernel, rows // QLEN * PAIR_HEADS, heads_once, part),
        in_specs=[pl.BlockSpec(memory_space=pltpu.SMEM)] + [hbm] * 3
        + [vmem] * 2
        + [hbm]
        + [vmem] * 2
        + [whole] * len(aliases),
        out_specs=whole,
        out_shape=jax.ShapeDtypeStruct((rows, width), jnp.bfloat16),
        scratch_shapes=[
            pltpu.VMEM((span, HD), jnp.bfloat16),
            pltpu.VMEM((2 * HD, span), jnp.bfloat16),
            pltpu.VMEM((span, 2 * HD), jnp.bfloat16),
            pltpu.VMEM((2, heads_once * QLEN, TOPP * PLEN), jnp.float32),
            pltpu.VMEM((2, heads_once * QLEN, TOPP * PLEN), jnp.bfloat16),
            pltpu.VMEM((2, QLEN, GROUPED * HD), jnp.bfloat16),
            pltpu.SemaphoreType.DMA((2,)),
            pltpu.VMEM((2, QLEN, GROUPED * HD), jnp.bfloat16),
            pltpu.SemaphoreType.DMA((2,)),
            pltpu.VMEM((kept.shape[0], KEPT, HALF), jnp.bfloat16),
            pltpu.SemaphoreType.DMA,
            pltpu.VMEM(own_kv.shape, jnp.bfloat16),
            pltpu.SemaphoreType.DMA,
            pltpu.VMEM((2, QLEN, GROUPED * HD), jnp.bfloat16),
            pltpu.SemaphoreType.DMA((2,)),
        ],
        input_output_aliases=aliases,
        compiler_params=pltpu.CompilerParams(vmem_limit_bytes=LARGE_VMEM),
        cost_estimate=LITTLE,
        name="attend",
    )(*operands)


def swap(array, axis, bits):
    size = lax.axis_size(axis)
    return lax.ppermute(array, axis, [(i, i ^ bits) for i in range(size)])


def recompute_general(normed, w_kv, pair):
    whole = lax.all_gather(lax.all_gather(w_kv, "member", axis=0, tiled=True), "group", axis=1, tiled=True)
    result = jnp.dot(normed, whole, preferred_element_type=jnp.float32).astype(jnp.bfloat16)
    result = result.reshape(-1, 2, PAIRS, PAIR_WIDTH)
    first = jnp.where(pair == 0, result[:, :, 0], result[:, :, 1])
    second = jnp.where(pair == 0, result[:, :, 1], result[:, :, 0])
    return [first[:, 0], first[:, 1]], [second[:, 0], second[:, 1]]


def local(q_rows, own_kv, cache, recomp_hidden, w_kv, retrieval, positions):
    queries = retrieval.shape[0]
    requests = queries * TOPP
    holders = lax.axis_size("member")
    groups = lax.axis_size("group")
    pass_local = cache.shape[0]
    capacity = -(-requests // holders)
    member = lax.axis_index("member")
    group = lax.axis_index("group")
    pair = group % PAIRS
    tuned = groups == 4 and holders == 8
    wanted = retrieval.reshape(requests)
    request = jnp.concatenate([wanted, positions.reshape(requests * RECOMP)])
    request = jnp.pad(request, (0, -request.shape[0] % 128)).reshape(1, -1, 128)
    request = jnp.broadcast_to(request, (holders,) + request.shape[1:])
    table = lax.all_to_all(request, "member", split_axis=0, concat_axis=0, tiled=True).reshape(-1)
    hidden = recomp_hidden.reshape(requests * RECOMP, D)
    hops = stack_hops(swap(w_kv, "member", 2), swap(w_kv, "member", 4)) if tuned else []
    normed = normalise(hidden, hops[:1])
    me = jnp.stack([member, pair]).astype(jnp.int32)
    ranks, passages = find_rows(table, me, holders, requests, pass_local, capacity, normed)
    holder_of = wanted // pass_local
    same = holder_of[:, None] == holder_of[None, :]
    before = jnp.arange(requests)[None, :] < jnp.arange(requests)[:, None]
    slot = holder_of * capacity + jnp.sum((same & before).astype(jnp.int32), axis=1)
    flip = group // 2 if tuned else jnp.int32(0)
    info = jnp.concatenate([jnp.stack([pair, flip]), slot]).astype(jnp.int32)
    other_info = jnp.concatenate([jnp.stack([1 - pair, flip]), slot]).astype(jnp.int32)
    first_own = attend_own(info, q_rows, own_kv, [ranks], [])
    ahead = [first_own[0]]
    if tuned:
        stack, two = hops
        aside, across = swap(w_kv, "member", 1), swap(w_kv, "group", 2)
        three = swap(two, "member", 2)
        stack_aside, stack_across = swap(stack, "member", 1), swap(stack, "group", 2)
        ahead += [across, aside, stack_across, stack_aside, three]
    sent = pick_rows(me, passages, ranks, cache, ahead)
    arrived = lax.all_to_all(
        sent.reshape(holders, capacity * KEPT, 2 * HALF), "member", split_axis=0, concat_axis=0, tiled=True
    ).reshape(sent.shape)
    second_own = attend_own(other_info, q_rows, own_kv, [sent], [aside] if tuned else [])
    if tuned:
        aside = second_own[3]
        other = swap(normed, "group", 1)
        rest_across, across_three = swap(stack_aside, "group", 2), swap(three, "group", 2)
        beside_three = swap(three, "member", 1)
        far_three = swap(beside_three, "group", 2)
        across_aside = swap(aside, "group", 2)
        near, near_other = project(
            member,
            normed,
            other,
            [w_kv, aside, stack, stack_aside, three, beside_three],
            ((0, 0, 0), (1, 1, 0), (2, 2, 0), (3, 3, 0), (4, 2, 1), (5, 3, 1), (6, 4, 0), (7, 5, 0)),
        )
        (begun,) = project(
            member,
            normed,
            other,
            [across, across_aside, stack_across, rest_across, across_three],
            ((0, 0, 0), (1, 1, 0), (2, 2, 0), (3, 3, 0), (4, 2, 1), (5, 3, 1), (6, 4, 0)),
            [near],
            last=False,
        )
        far, far_other = project(member, normed, other, [far_three], ((7, 0, 0),), carry=begun)
        first = [near, far]
        second = [swap(near_other, "group", 1), swap(far_other, "group", 1)]
    else:
        first, second = recompute_general(normed, w_kv, pair)
    out = attend(0, info, q_rows, own_kv, arrived, *first, first_own[:3])
    return attend(1, other_info, q_rows, own_kv, arrived, *second, second_own[:3], earlier=out)


def solution(mesh):
    rows = P(("group", "member"), None)
    placed = (
        rows,
        rows,
        P(("group", "member"), None, None),
        P(("group", "member"), None, None, None),
        P("member", "group"),
        rows,
        P(("group", "member"), None, None),
    )
    return jax.shard_map(local, mesh=mesh, in_specs=placed, out_specs=rows, check_vma=False)
```

```python
import functools

import jax
import jax.numpy as jnp
from jax import lax
from jax.experimental import pallas as pl
from jax.experimental.pallas import tpu as pltpu
from jax.sharding import PartitionSpec as P

D = 4096
HQ = 64
KVH = 4
HD = 128
TOPP = 8
QLEN = 128
PLEN = 64
RECOMP = 16
KEPT = PLEN - RECOMP
GROUPED = HQ // KVH
PAIRS = 2
PAIR_HEADS = KVH // PAIRS
PAIR_WIDTH = PAIR_HEADS * HD
HALF = KVH * HD

EPSILON = 1e-06
SCORE_FACTOR = 1.4426950408889634 / HD**0.5
SAFE_EXPONENT = 80.0
SMALL_VMEM = 12 * 1024 * 1024
VMEM_BYTES = 24 * 1024 * 1024
LARGE_VMEM = 58 * 1024 * 1024
LITTLE = pl.CostEstimate(flops=1, bytes_accessed=1, transcendentals=0)
LARGE = pl.CostEstimate(flops=1, bytes_accessed=36_000_000, transcendentals=0)


def norm_kernel(tile, hidden_ref, *rest):
    normed_ref = rest[-1]

    def one(step, carry):
        rows = pl.ds(pl.multiple_of(step * tile, tile), tile)
        hidden = hidden_ref[rows, :].astype(jnp.float32)
        mean = jnp.mean(hidden * hidden, axis=1, keepdims=True)
        normed_ref[rows, :] = (hidden * lax.rsqrt(mean + EPSILON)).astype(jnp.bfloat16)
        return carry

    lax.fori_loop(0, hidden_ref.shape[0] // tile, one, 0)


def normalise(hidden, ahead):
    vmem = pl.BlockSpec(memory_space=pltpu.VMEM)
    return pl.pallas_call(
        functools.partial(norm_kernel, 32),
        in_specs=[vmem] + [pl.BlockSpec(memory_space=pl.ANY)] * len(ahead),
        out_specs=vmem,
        out_shape=jax.ShapeDtypeStruct(hidden.shape, jnp.bfloat16),
        compiler_params=pltpu.CompilerParams(vmem_limit_bytes=SMALL_VMEM),
        cost_estimate=LITTLE,
        name="normalise",
    )(hidden, *ahead)


def stack_kernel(one_ref, two_ref, stack_ref, copy_ref):
    depth = one_ref.shape[0]
    stack_ref[:depth, :] = one_ref[...]
    stack_ref[depth:, :] = two_ref[...]
    copy_ref[...] = two_ref[...]


def stack_hops(one, two):
    depth, width = one.shape
    vmem = pl.BlockSpec(memory_space=pltpu.VMEM)
    return pl.pallas_call(
        stack_kernel,
        in_specs=[vmem, vmem],
        out_specs=[vmem, vmem],
        out_shape=[jax.ShapeDtypeStruct((rows, width), jnp.bfloat16) for rows in (2 * depth, depth)],
        compiler_params=pltpu.CompilerParams(vmem_limit_bytes=SMALL_VMEM),
        cost_estimate=LITTLE,
        name="stack_hops",
    )(one, two)


def find_kernel(holders, requests, pass_local, capacity, me_ref, table_ref, *rest):
    rank_ref, passage_ref, slot_ref, kept_ref = rest[-4:]
    me = me_ref[0]
    stride = table_ref.shape[0] // holders
    for k in range(holders):
        base = k * (capacity + 1)
        for rank in range(capacity + 1):
            slot_ref[base + rank] = 0
        count = jnp.int32(0)
        for request in range(requests):
            slot_ref[base + count] = request
            mine = (table_ref[k * stride + request] // pass_local == me).astype(jnp.int32)
            count = jnp.minimum(count + mine, capacity)
    spot = lax.broadcasted_iota(jnp.int32, (1, PLEN), 1)
    for k in range(holders):
        for rank in range(capacity):
            at = k * capacity + rank
            request = slot_ref[k * (capacity + 1) + rank]
            passage_ref[at] = lax.rem(table_ref[k * stride + request], pass_local)
            start = k * stride + requests + request * RECOMP
            covered = spot < 0
            for r in range(RECOMP):
                covered = covered | (spot == table_ref[start + r])
            kept_ref[at : at + 1, :] = jnp.where(covered, 0.0, 1.0)
    kept = kept_ref[...]
    upto = lax.broadcasted_iota(jnp.int32, (PLEN, PLEN), 0) <= lax.broadcasted_iota(jnp.int32, (PLEN, PLEN), 1)
    rank_of = jnp.dot(
        kept.astype(jnp.bfloat16), upto.astype(jnp.bfloat16), preferred_element_type=jnp.float32
    )
    rank_ref[...] = jnp.where(kept > 0, rank_of, 0.0)


def find_rows(table, me, holders, requests, pass_local, capacity, normed):
    slots = holders * capacity
    smem = pl.BlockSpec(memory_space=pltpu.SMEM)
    whole = pl.BlockSpec(memory_space=pl.ANY)
    return pl.pallas_call(
        functools.partial(find_kernel, holders, requests, pass_local, capacity),
        in_specs=[smem, smem, whole],
        out_specs=[pl.BlockSpec(memory_space=pltpu.VMEM), smem],
        out_shape=[jax.ShapeDtypeStruct((slots, PLEN), jnp.float32), jax.ShapeDtypeStruct((slots,), jnp.int32)],
        scratch_shapes=[pltpu.SMEM((holders * (capacity + 1),), jnp.int32), pltpu.VMEM((slots, PLEN), jnp.float32)],
        compiler_params=pltpu.CompilerParams(vmem_limit_bytes=SMALL_VMEM),
        cost_estimate=LARGE,
        name="find_rows",
    )(me, table, normed)


def pick_kernel(me_ref, passage_ref, rank_ref, cache_ref, *rest):
    out_ref = rest[-1]
    pair = me_ref[1]
    row = (lax.broadcasted_iota(jnp.int32, (KEPT, PLEN), 0) + 1).astype(jnp.float32)
    for at in range(out_ref.shape[0]):
        passage = passage_ref[at]
        select = (rank_ref[at : at + 1, :] == row).astype(jnp.bfloat16)
        for place, part in ((0, pair), (1, 1 - pair)):
            for half in range(2):
                start = pl.multiple_of(half * HALF + part * PAIR_WIDTH, PAIR_WIDTH)
                end = (place * 2 + half) * PAIR_WIDTH
                out_ref[at, :, end : end + PAIR_WIDTH] = jnp.dot(
                    select, cache_ref[passage, :, pl.ds(start, PAIR_WIDTH)], preferred_element_type=jnp.float32
                ).astype(jnp.bfloat16)


def pick_rows(me, passages, ranks, cache, ahead):
    smem = pl.BlockSpec(memory_space=pltpu.SMEM)
    vmem = pl.BlockSpec(memory_space=pltpu.VMEM)
    return pl.pallas_call(
        pick_kernel,
        in_specs=[smem, smem, vmem, vmem] + [pl.BlockSpec(memory_space=pl.ANY)] * len(ahead),
        out_specs=vmem,
        out_shape=jax.ShapeDtypeStruct((passages.shape[0], KEPT, 2 * HALF), jnp.bfloat16),
        compiler_params=pltpu.CompilerParams(vmem_limit_bytes=SMALL_VMEM),
        cost_estimate=LITTLE,
        name="pick_rows",
    )(me, passages, ranks, cache, *ahead)


def project_kernel(chunks, layout, carried, last, member_ref, mine_ref, other_ref, *refs):
    rows = mine_ref.shape[0]
    depth = D // chunks
    total = refs[-3 if last else -2][...] if carried else None
    for k, array, start in layout:
        chunk = pl.ds(pl.multiple_of((member_ref[0] ^ k) * depth, depth), depth)
        both = jnp.concatenate([mine_ref[:, chunk], other_ref[:, chunk]], axis=0)
        weights = refs[array][start * depth : (start + 1) * depth, :]
        term = jnp.dot(both, weights, preferred_element_type=jnp.float32)
        total = term if total is None else total + term
    if last:
        refs[-2][...] = total[:rows].astype(jnp.bfloat16)
        refs[-1][...] = total[rows:].astype(jnp.bfloat16)
    else:
        refs[-1][...] = total


def project(member, mine, other, arrays, layout, ahead=(), carry=None, last=True):
    rows, width = mine.shape[0], arrays[0].shape[1]
    chunks = D // arrays[0].shape[0]
    vmem = pl.BlockSpec(memory_space=pltpu.VMEM)
    carried = [] if carry is None else [carry]
    shape = [jax.ShapeDtypeStruct((rows, width), jnp.bfloat16)] * 2
    if not last:
        shape = [jax.ShapeDtypeStruct((2 * rows, width), jnp.float32)]
    return pl.pallas_call(
        functools.partial(project_kernel, chunks, layout, bool(carried), last),
        in_specs=[pl.BlockSpec(memory_space=pltpu.SMEM)]
        + [vmem] * (2 + len(arrays))
        + [pl.BlockSpec(memory_space=pl.ANY)] * len(ahead)
        + [vmem] * len(carried),
        out_specs=[vmem] * len(shape),
        out_shape=shape,
        compiler_params=pltpu.CompilerParams(vmem_limit_bytes=SMALL_VMEM),
        cost_estimate=LITTLE,
        name="project",
    )(member.reshape(1), mine, other, *arrays, *ahead, *carried)


def scaled_keys(keys, turned_ref):
    scaled = keys.astype(jnp.float32) * SCORE_FACTOR
    high = scaled.astype(jnp.bfloat16)
    turned_ref[:HD, :] = high.T
    turned_ref[HD:, :] = (scaled - high.astype(jnp.float32)).astype(jnp.bfloat16).T
    return jnp.max(jnp.sum(scaled * scaled, axis=1, keepdims=True))


def head_rows(q_ref, rows, column, heads_once):
    block = jnp.concatenate(
        [q_ref[rows, pl.ds(pl.multiple_of(column + i * HD, HD), HD)] for i in range(heads_once)], axis=0
    )
    return jnp.concatenate([block, block], axis=1)


def causal(rows):
    token = lax.broadcasted_iota(jnp.int32, (rows, QLEN), 0) % QLEN
    return lax.broadcasted_iota(jnp.int32, (rows, QLEN), 1) <= token


def place(step, pair):
    query, head = step // PAIR_HEADS, step % PAIR_HEADS
    rows = pl.ds(pl.multiple_of(query * QLEN, QLEN), QLEN)
    return query, head, rows, pair * PAIR_HEADS + head


def columns(start, width=HD):
    return pl.ds(pl.multiple_of(start, HD), width)


def own_kernel(steps, heads_once, passing, info_ref, q_ref, own_ref, *rest):
    sum_ref, weight_ref, bound_ref = rest[-5 - passing : -2 - passing]
    turned_ref, wide_ref = rest[-2:]
    bound_ref[...] = jnp.zeros_like(bound_ref)
    shown = jnp.where(causal(heads_once * QLEN), 1.0, 0.0).astype(jnp.bfloat16)
    lane = lax.broadcasted_iota(jnp.int32, (QLEN, HD), 1)

    def one(step, carry):
        _, head, rows, column = place(step, info_ref[0])
        keys = scaled_keys(own_ref[rows, columns(column * HD)], turned_ref)
        wide_ref[:, :HD] = own_ref[rows, columns(HALF + column * HD)]
        wide_ref[:, HD:] = jnp.ones((QLEN, HD), jnp.bfloat16)
        weights = jnp.zeros((QLEN, HD), jnp.float32)
        peak = jnp.zeros((QLEN, 1), jnp.float32)
        for first in range(0, GROUPED, heads_once):
            start = (column * GROUPED + first) * HD
            scores = jnp.dot(
                head_rows(q_ref, rows, start, heads_once), turned_ref[...], preferred_element_type=jnp.float32
            )
            summed = jnp.dot(
                jnp.exp2(scores).astype(jnp.bfloat16) * shown, wide_ref[...], preferred_element_type=jnp.float32
            )
            for i in range(heads_once):
                part = summed[i * QLEN : (i + 1) * QLEN]
                sum_ref[rows, columns((head * GROUPED + first + i) * HD)] = part[:, :HD].astype(jnp.bfloat16)
                weights = jnp.where(lane == first + i, part[:, HD:], weights)
            most = None
            for i in range(heads_once):
                block = q_ref[rows, columns(start + i * HD)].astype(jnp.float32)
                most = block * block if most is None else jnp.maximum(most, block * block)
            peak = jnp.maximum(peak, jnp.sum(most, axis=1, keepdims=True))
        weight_ref[rows, columns(head * HD)] = weights
        bound_ref[:8, :] = jnp.maximum(bound_ref[:8, :], jnp.max(peak))
        bound_ref[8:, :] = jnp.maximum(bound_ref[8:, :], keys)
        return carry

    lax.fori_loop(0, steps, one, 0)


def attend_own(info, q_rows, own_kv, ahead, passing):
    rows = q_rows.shape[0]
    whole = pl.BlockSpec(memory_space=pl.ANY)
    vmem = pl.BlockSpec(memory_space=pltpu.VMEM)
    return pl.pallas_call(
        functools.partial(own_kernel, rows // QLEN * PAIR_HEADS, 4, len(passing)),
        in_specs=[pl.BlockSpec(memory_space=pltpu.SMEM), vmem, vmem] + [whole] * (len(passing) + len(ahead)),
        out_specs=[vmem] * 3 + [whole] * len(passing),
        out_shape=[
            jax.ShapeDtypeStruct((rows, PAIR_HEADS * GROUPED * HD), jnp.bfloat16),
            jax.ShapeDtypeStruct((rows, PAIR_HEADS * HD), jnp.float32),
            jax.ShapeDtypeStruct((16, HD), jnp.float32),
        ]
        + [jax.ShapeDtypeStruct(part.shape, part.dtype) for part in passing],
        scratch_shapes=[pltpu.VMEM((2 * HD, QLEN), jnp.bfloat16), pltpu.VMEM((QLEN, 2 * HD), jnp.bfloat16)],
        input_output_aliases={3 + i: 3 + i for i in range(len(passing))},
        compiler_params=pltpu.CompilerParams(vmem_limit_bytes=VMEM_BYTES),
        cost_estimate=LITTLE,
        name="attend_own",
    )(info, q_rows, own_kv, *passing, *ahead)


def block_rows(q_ref, slot, first, heads_once):
    block = jnp.concatenate(
        [q_ref[slot, :, (first + i) * HD : (first + i + 1) * HD] for i in range(heads_once)], axis=0
    )
    return jnp.concatenate([block, block], axis=1)


def fetch(step, start, array_ref, block_ref, arrived_ref):
    _, _, rows, _ = place(step, 0)
    wide, slot = GROUPED * HD, step % 2
    column = start + (step % PAIR_HEADS) * wide
    return pltpu.make_async_copy(
        array_ref.at[rows, columns(column, wide)], block_ref.at[slot], arrived_ref.at[slot]
    )


def leave(step, start, block_ref, array_ref, done_ref):
    _, _, rows, _ = place(step, 0)
    wide, slot = GROUPED * HD, step % 2
    column = start + (step % PAIR_HEADS) * wide
    return pltpu.make_async_copy(
        block_ref.at[slot], array_ref.at[rows, columns(column, wide)], done_ref.at[slot]
    )


def attend_kernel(
    steps,
    heads_once,
    part,
    info_ref,
    q_ref,
    own_hbm_ref,
    kept_ref,
    near_ref,
    far_ref,
    sum_ref,
    weight_ref,
    bound_ref,
    *rest,
):
    out_ref, key_ref, turned_ref, value_ref, score_ref, expd_ref, result_ref, done_ref = rest[-16:-8]
    block_ref, arrived_ref, cut_ref, cut_done_ref, own_ref, own_done_ref, part_ref, part_done_ref = rest[-8:]
    passage_keys = TOPP * PLEN
    wide = GROUPED * HD
    groups = GROUPED // heads_once
    flip = info_ref[1] > 0
    cut = pltpu.make_async_copy(kept_ref.at[:, :, part * HALF : (part + 1) * HALF], cut_ref, cut_done_ref)
    cut.start()
    start = info_ref[0] * (PAIR_HEADS * wide)
    fetch(0, start, q_ref, block_ref, arrived_ref).start()
    fetch(0, 0, sum_ref, part_ref, part_done_ref).start()
    value_ref[:, HD:] = jnp.ones((passage_keys + QLEN, HD), jnp.bfloat16)
    cut.wait()

    def one(step, carry):
        query, head, rows, column = place(step, info_ref[0])
        slot = step % 2

        @pl.when(step >= 2)
        def free():
            leave(step - 2, start, result_ref, out_ref, done_ref).wait()

        @pl.when(step + 1 < steps)
        def prefetch():
            fetch(step + 1, start, q_ref, block_ref, arrived_ref).start()
            fetch(step + 1, 0, sum_ref, part_ref, part_done_ref).start()

        offset = head * HD
        for j in range(TOPP):
            block = info_ref[2 + query * TOPP + j]
            key_ref[j * KEPT : (j + 1) * KEPT, :] = cut_ref[block, :, columns(offset)]
            value_ref[j * KEPT : (j + 1) * KEPT, :HD] = cut_ref[block, :, columns(offset + PAIR_WIDTH)]
        near, far = near_ref[rows, columns(head * HD)], far_ref[rows, columns(head * HD)]
        key_ref[TOPP * KEPT : passage_keys, :] = jnp.where(flip, far, near)
        value_ref[TOPP * KEPT : passage_keys, :HD] = jnp.where(flip, near, far)
        key_bound = scaled_keys(key_ref[...], turned_ref.at[:, :passage_keys])
        key_bound = jnp.maximum(key_bound, jnp.max(bound_ref[8:, :]))
        small = jnp.max(bound_ref[:8, :]) * key_bound <= SAFE_EXPONENT**2

        fetch(step, start, q_ref, block_ref, arrived_ref).wait()
        fetch(step, 0, sum_ref, part_ref, part_done_ref).wait()

        def score(group):
            score_ref[group % 2] = jnp.dot(
                block_rows(block_ref, slot, group * heads_once, heads_once),
                turned_ref[:, :passage_keys],
                preferred_element_type=jnp.float32,
            )

        def soften(group):
            expd_ref[group % 2] = jnp.exp2(score_ref[group % 2]).astype(jnp.bfloat16)

        def finish(group):
            summed = jnp.dot(
                expd_ref[group % 2], value_ref[:passage_keys, :], preferred_element_type=jnp.float32
            )
            weights = weight_ref[rows, columns(head * HD)]
            for i in range(heads_once):
                at = group * heads_once + i
                both = summed[i * QLEN : (i + 1) * QLEN]
                weight = both[:, HD:] + weights[:, at : at + 1]
                inverse = pl.reciprocal(weight, approx=True)
                inverse = inverse * (2.0 - weight * inverse)
                total = both[:, :HD] + part_ref[slot, :, at * HD : (at + 1) * HD].astype(jnp.float32)
                result_ref[slot, :, at * HD : (at + 1) * HD] = (total * inverse).astype(jnp.bfloat16)

        @pl.when(small)
        def unshifted():
            score(0)
            for group in range(groups):
                if group + 1 < groups:
                    score(group + 1)
                soften(group)
                if group > 0:
                    finish(group - 1)
            finish(groups - 1)

        @pl.when(jnp.logical_not(small))
        def shifted():
            for i in range(2):
                source = own_hbm_ref.at[rows, columns(i * HALF + column * HD)]
                copy = pltpu.make_async_copy(source, own_ref.at[i], own_done_ref.at[i])
                copy.start()
                copy.wait()
            scaled_keys(own_ref[0], turned_ref.at[:, passage_keys:])
            value_ref[passage_keys:, :HD] = own_ref[1]
            visible = causal(heads_once * QLEN)
            for group in range(groups):
                scores = jnp.dot(
                    block_rows(block_ref, slot, group * heads_once, heads_once),
                    turned_ref[...],
                    preferred_element_type=jnp.float32,
                )
                scores = jnp.concatenate(
                    [scores[:, :passage_keys], jnp.where(visible, scores[:, passage_keys:], -jnp.inf)], axis=1
                )
                peak = jnp.max(scores, axis=1, keepdims=True)
                expd = jnp.exp2(scores - peak).astype(jnp.bfloat16)
                summed = jnp.dot(expd, value_ref[...], preferred_element_type=jnp.float32)
                ratio = (summed[:, :HD] / summed[:, HD:]).astype(jnp.bfloat16)
                for i in range(heads_once):
                    at = group * heads_once + i
                    result_ref[slot, :, at * HD : (at + 1) * HD] = ratio[i * QLEN : (i + 1) * QLEN]

        leave(step, start, result_ref, out_ref, done_ref).start()
        return carry

    lax.fori_loop(0, steps, one, 0)
    for step in range(max(steps - 2, 0), steps):
        leave(step, start, result_ref, out_ref, done_ref).wait()


def attend(part, info, q_rows, own_kv, kept, near, far, own, earlier=None):
    rows, width = q_rows.shape
    span = TOPP * PLEN + QLEN
    heads_once = 2
    vmem = pl.BlockSpec(memory_space=pltpu.VMEM)
    whole = pl.BlockSpec(memory_space=pl.ANY)
    hbm = pl.BlockSpec(memory_space=pltpu.HBM)
    operands = [info, q_rows, own_kv, kept, near, far, *own]
    aliases = {}
    if earlier is not None:
        aliases = {len(operands): 0}
        operands.append(earlier)
    return pl.pallas_call(
        functools.partial(attend_kernel, rows // QLEN * PAIR_HEADS, heads_once, part),
        in_specs=[pl.BlockSpec(memory_space=pltpu.SMEM)] + [hbm] * 3
        + [vmem] * 2
        + [hbm]
        + [vmem] * 2
        + [whole] * len(aliases),
        out_specs=whole,
        out_shape=jax.ShapeDtypeStruct((rows, width), jnp.bfloat16),
        scratch_shapes=[
            pltpu.VMEM((TOPP * PLEN, HD), jnp.bfloat16),
            pltpu.VMEM((2 * HD, span), jnp.bfloat16),
            pltpu.VMEM((span, 2 * HD), jnp.bfloat16),
            pltpu.VMEM((2, heads_once * QLEN, TOPP * PLEN), jnp.float32),
            pltpu.VMEM((2, heads_once * QLEN, TOPP * PLEN), jnp.bfloat16),
            pltpu.VMEM((2, QLEN, GROUPED * HD), jnp.bfloat16),
            pltpu.SemaphoreType.DMA((2,)),
            pltpu.VMEM((2, QLEN, GROUPED * HD), jnp.bfloat16),
            pltpu.SemaphoreType.DMA((2,)),
            pltpu.VMEM((kept.shape[0], KEPT, HALF), jnp.bfloat16),
            pltpu.SemaphoreType.DMA,
            pltpu.VMEM((2, QLEN, HD), jnp.bfloat16),
            pltpu.SemaphoreType.DMA((2,)),
            pltpu.VMEM((2, QLEN, GROUPED * HD), jnp.bfloat16),
            pltpu.SemaphoreType.DMA((2,)),
        ],
        input_output_aliases=aliases,
        compiler_params=pltpu.CompilerParams(vmem_limit_bytes=LARGE_VMEM),
        cost_estimate=LITTLE,
        name="attend",
    )(*operands)


def swap(array, axis, bits):
    size = lax.axis_size(axis)
    return lax.ppermute(array, axis, [(i, i ^ bits) for i in range(size)])


def recompute_general(normed, w_kv, pair):
    whole = lax.all_gather(lax.all_gather(w_kv, "member", axis=0, tiled=True), "group", axis=1, tiled=True)
    result = jnp.dot(normed, whole, preferred_element_type=jnp.float32).astype(jnp.bfloat16)
    result = result.reshape(-1, 2, PAIRS, PAIR_WIDTH)
    first = jnp.where(pair == 0, result[:, :, 0], result[:, :, 1])
    second = jnp.where(pair == 0, result[:, :, 1], result[:, :, 0])
    return [first[:, 0], first[:, 1]], [second[:, 0], second[:, 1]]


def local(q_rows, own_kv, cache, recomp_hidden, w_kv, retrieval, positions):
    queries = retrieval.shape[0]
    requests = queries * TOPP
    holders = lax.axis_size("member")
    groups = lax.axis_size("group")
    pass_local = cache.shape[0]
    capacity = -(-requests // holders)
    member = lax.axis_index("member")
    group = lax.axis_index("group")
    pair = group % PAIRS
    tuned = groups == 4 and holders == 8
    wanted = retrieval.reshape(requests)
    request = jnp.concatenate([wanted, positions.reshape(requests * RECOMP)])
    request = jnp.pad(request, (0, -request.shape[0] % 128)).reshape(1, -1, 128)
    request = jnp.broadcast_to(request, (holders,) + request.shape[1:])
    table = lax.all_to_all(request, "member", split_axis=0, concat_axis=0, tiled=True).reshape(-1)
    hidden = recomp_hidden.reshape(requests * RECOMP, D)
    hops = stack_hops(swap(w_kv, "member", 2), swap(w_kv, "member", 4)) if tuned else []
    normed = normalise(hidden, hops[:1])
    me = jnp.stack([member, pair]).astype(jnp.int32)
    ranks, passages = find_rows(table, me, holders, requests, pass_local, capacity, normed)
    holder_of = wanted // pass_local
    same = holder_of[:, None] == holder_of[None, :]
    before = jnp.arange(requests)[None, :] < jnp.arange(requests)[:, None]
    slot = holder_of * capacity + jnp.sum((same & before).astype(jnp.int32), axis=1)
    flip = group // 2 if tuned else jnp.int32(0)
    info = jnp.concatenate([jnp.stack([pair, flip]), slot]).astype(jnp.int32)
    other_info = jnp.concatenate([jnp.stack([1 - pair, flip]), slot]).astype(jnp.int32)
    first_own = attend_own(info, q_rows, own_kv, [ranks], [])
    ahead = [first_own[0]]
    if tuned:
        stack, two = hops
        aside, across = swap(w_kv, "member", 1), swap(w_kv, "group", 2)
        three = swap(two, "member", 2)
        stack_aside, stack_across = swap(stack, "member", 1), swap(stack, "group", 2)
        ahead += [across, aside, stack_across, stack_aside, three]
    sent = pick_rows(me, passages, ranks, cache, ahead)
    arrived = lax.all_to_all(
        sent.reshape(holders, capacity * KEPT, 2 * HALF), "member", split_axis=0, concat_axis=0, tiled=True
    ).reshape(sent.shape)
    second_own = attend_own(other_info, q_rows, own_kv, [sent], [aside] if tuned else [])
    if tuned:
        aside = second_own[3]
        other = swap(normed, "group", 1)
        rest_across, across_three = swap(stack_aside, "group", 2), swap(three, "group", 2)
        beside_three = swap(three, "member", 1)
        far_three = swap(beside_three, "group", 2)
        across_aside = swap(aside, "group", 2)
        near, near_other = project(
            member,
            normed,
            other,
            [w_kv, aside, stack, stack_aside, three, beside_three],
            ((0, 0, 0), (1, 1, 0), (2, 2, 0), (3, 3, 0), (4, 2, 1), (5, 3, 1), (6, 4, 0), (7, 5, 0)),
        )
        (begun,) = project(
            member,
            normed,
            other,
            [across, across_aside, stack_across, rest_across, across_three],
            ((0, 0, 0), (1, 1, 0), (2, 2, 0), (3, 3, 0), (4, 2, 1), (5, 3, 1), (6, 4, 0)),
            [near],
            last=False,
        )
        far, far_other = project(member, normed, other, [far_three], ((7, 0, 0),), carry=begun)
        first = [near, far]
        second = [swap(near_other, "group", 1), swap(far_other, "group", 1)]
    else:
        first, second = recompute_general(normed, w_kv, pair)
    out = attend(0, info, q_rows, own_kv, arrived, *first, first_own[:3])
    return attend(1, other_info, q_rows, own_kv, arrived, *second, second_own[:3], earlier=out)


def solution(mesh):
    rows = P(("group", "member"), None)
    placed = (
        rows,
        rows,
        P(("group", "member"), None, None),
        P(("group", "member"), None, None, None),
        P("member", "group"),
        rows,
        P(("group", "member"), None, None),
    )
    return jax.shard_map(local, mesh=mesh, in_specs=placed, out_specs=rows, check_vma=False)
```

```python
import functools

import jax
import jax.numpy as jnp
from jax import lax
from jax.experimental import pallas as pl
from jax.experimental.pallas import tpu as pltpu
from jax.sharding import PartitionSpec as P

D = 4096
HQ = 64
KVH = 4
HD = 128
TOPP = 8
QLEN = 128
PLEN = 64
RECOMP = 16
KEPT = PLEN - RECOMP
GROUPED = HQ // KVH
PAIRS = 2
PAIR_HEADS = KVH // PAIRS
PAIR_WIDTH = PAIR_HEADS * HD
HALF = KVH * HD

EPSILON = 1e-06
SCORE_FACTOR = 1.4426950408889634 / HD**0.5
SAFE_EXPONENT = 80.0
SMALL_VMEM = 12 * 1024 * 1024
VMEM_BYTES = 24 * 1024 * 1024
LARGE_VMEM = 58 * 1024 * 1024
LITTLE = pl.CostEstimate(flops=1, bytes_accessed=1, transcendentals=0)
LARGE = pl.CostEstimate(flops=1, bytes_accessed=36_000_000, transcendentals=0)


def norm_kernel(tile, hidden_ref, *rest):
    normed_ref = rest[-1]

    def one(step, carry):
        rows = pl.ds(pl.multiple_of(step * tile, tile), tile)
        hidden = hidden_ref[rows, :].astype(jnp.float32)
        mean = jnp.mean(hidden * hidden, axis=1, keepdims=True)
        normed_ref[rows, :] = (hidden * lax.rsqrt(mean + EPSILON)).astype(jnp.bfloat16)
        return carry

    lax.fori_loop(0, hidden_ref.shape[0] // tile, one, 0)


def normalise(hidden, ahead):
    vmem = pl.BlockSpec(memory_space=pltpu.VMEM)
    return pl.pallas_call(
        functools.partial(norm_kernel, 32),
        in_specs=[vmem] + [pl.BlockSpec(memory_space=pl.ANY)] * len(ahead),
        out_specs=vmem,
        out_shape=jax.ShapeDtypeStruct(hidden.shape, jnp.bfloat16),
        compiler_params=pltpu.CompilerParams(vmem_limit_bytes=SMALL_VMEM),
        cost_estimate=LITTLE,
        name="normalise",
    )(hidden, *ahead)


def stack_kernel(one_ref, two_ref, stack_ref, copy_ref):
    depth = one_ref.shape[0]
    stack_ref[:depth, :] = one_ref[...]
    stack_ref[depth:, :] = two_ref[...]
    copy_ref[...] = two_ref[...]


def stack_hops(one, two):
    depth, width = one.shape
    vmem = pl.BlockSpec(memory_space=pltpu.VMEM)
    return pl.pallas_call(
        stack_kernel,
        in_specs=[vmem, vmem],
        out_specs=[vmem, vmem],
        out_shape=[jax.ShapeDtypeStruct((rows, width), jnp.bfloat16) for rows in (2 * depth, depth)],
        compiler_params=pltpu.CompilerParams(vmem_limit_bytes=SMALL_VMEM),
        cost_estimate=LITTLE,
        name="stack_hops",
    )(one, two)


def find_kernel(holders, requests, pass_local, capacity, me_ref, table_ref, *rest):
    rank_ref, passage_ref, slot_ref, kept_ref = rest[-4:]
    me = me_ref[0]
    stride = table_ref.shape[0] // holders
    for k in range(holders):
        base = k * (capacity + 1)
        for rank in range(capacity + 1):
            slot_ref[base + rank] = 0
        count = jnp.int32(0)
        for request in range(requests):
            slot_ref[base + count] = request
            mine = (table_ref[k * stride + request] // pass_local == me).astype(jnp.int32)
            count = jnp.minimum(count + mine, capacity)
    spot = lax.broadcasted_iota(jnp.int32, (1, PLEN), 1)
    for k in range(holders):
        for rank in range(capacity):
            at = k * capacity + rank
            request = slot_ref[k * (capacity + 1) + rank]
            passage_ref[at] = lax.rem(table_ref[k * stride + request], pass_local)
            start = k * stride + requests + request * RECOMP
            covered = spot < 0
            for r in range(RECOMP):
                covered = covered | (spot == table_ref[start + r])
            kept_ref[at : at + 1, :] = jnp.where(covered, 0.0, 1.0)
    kept = kept_ref[...]
    upto = lax.broadcasted_iota(jnp.int32, (PLEN, PLEN), 0) <= lax.broadcasted_iota(jnp.int32, (PLEN, PLEN), 1)
    rank_of = jnp.dot(
        kept.astype(jnp.bfloat16), upto.astype(jnp.bfloat16), preferred_element_type=jnp.float32
    )
    rank_ref[...] = jnp.where(kept > 0, rank_of, 0.0)


def find_rows(table, me, holders, requests, pass_local, capacity, normed):
    slots = holders * capacity
    smem = pl.BlockSpec(memory_space=pltpu.SMEM)
    whole = pl.BlockSpec(memory_space=pl.ANY)
    return pl.pallas_call(
        functools.partial(find_kernel, holders, requests, pass_local, capacity),
        in_specs=[smem, smem, whole],
        out_specs=[pl.BlockSpec(memory_space=pltpu.VMEM), smem],
        out_shape=[jax.ShapeDtypeStruct((slots, PLEN), jnp.float32), jax.ShapeDtypeStruct((slots,), jnp.int32)],
        scratch_shapes=[pltpu.SMEM((holders * (capacity + 1),), jnp.int32), pltpu.VMEM((slots, PLEN), jnp.float32)],
        compiler_params=pltpu.CompilerParams(vmem_limit_bytes=SMALL_VMEM),
        cost_estimate=LARGE,
        name="find_rows",
    )(me, table, normed)


def pick_kernel(me_ref, passage_ref, rank_ref, cache_ref, *rest):
    out_ref = rest[-1]
    pair = me_ref[1]
    row = (lax.broadcasted_iota(jnp.int32, (KEPT, PLEN), 0) + 1).astype(jnp.float32)
    for at in range(out_ref.shape[0]):
        passage = passage_ref[at]
        select = (rank_ref[at : at + 1, :] == row).astype(jnp.bfloat16)
        for place, part in ((0, pair), (1, 1 - pair)):
            for half in range(2):
                start = pl.multiple_of(half * HALF + part * PAIR_WIDTH, PAIR_WIDTH)
                end = (place * 2 + half) * PAIR_WIDTH
                out_ref[at, :, end : end + PAIR_WIDTH] = jnp.dot(
                    select, cache_ref[passage, :, pl.ds(start, PAIR_WIDTH)], preferred_element_type=jnp.float32
                ).astype(jnp.bfloat16)


def pick_rows(me, passages, ranks, cache, ahead):
    smem = pl.BlockSpec(memory_space=pltpu.SMEM)
    vmem = pl.BlockSpec(memory_space=pltpu.VMEM)
    return pl.pallas_call(
        pick_kernel,
        in_specs=[smem, smem, vmem, vmem] + [pl.BlockSpec(memory_space=pl.ANY)] * len(ahead),
        out_specs=vmem,
        out_shape=jax.ShapeDtypeStruct((passages.shape[0], KEPT, 2 * HALF), jnp.bfloat16),
        compiler_params=pltpu.CompilerParams(vmem_limit_bytes=SMALL_VMEM),
        cost_estimate=LITTLE,
        name="pick_rows",
    )(me, passages, ranks, cache, *ahead)


def project_kernel(chunks, layout, carried, last, member_ref, mine_ref, other_ref, *refs):
    rows = mine_ref.shape[0]
    depth = D // chunks
    total = refs[-3 if last else -2][...] if carried else None
    for k, array, start in layout:
        chunk = pl.ds(pl.multiple_of((member_ref[0] ^ k) * depth, depth), depth)
        both = jnp.concatenate([mine_ref[:, chunk], other_ref[:, chunk]], axis=0)
        weights = refs[array][start * depth : (start + 1) * depth, :]
        term = jnp.dot(both, weights, preferred_element_type=jnp.float32)
        total = term if total is None else total + term
    if last:
        refs[-2][...] = total[:rows].astype(jnp.bfloat16)
        refs[-1][...] = total[rows:].astype(jnp.bfloat16)
    else:
        refs[-1][...] = total


def project(member, mine, other, arrays, layout, ahead=(), carry=None, last=True):
    rows, width = mine.shape[0], arrays[0].shape[1]
    chunks = D // arrays[0].shape[0]
    vmem = pl.BlockSpec(memory_space=pltpu.VMEM)
    carried = [] if carry is None else [carry]
    shape = [jax.ShapeDtypeStruct((rows, width), jnp.bfloat16)] * 2
    if not last:
        shape = [jax.ShapeDtypeStruct((2 * rows, width), jnp.float32)]
    return pl.pallas_call(
        functools.partial(project_kernel, chunks, layout, bool(carried), last),
        in_specs=[pl.BlockSpec(memory_space=pltpu.SMEM)]
        + [vmem] * (2 + len(arrays))
        + [pl.BlockSpec(memory_space=pl.ANY)] * len(ahead)
        + [vmem] * len(carried),
        out_specs=[vmem] * len(shape),
        out_shape=shape,
        compiler_params=pltpu.CompilerParams(vmem_limit_bytes=SMALL_VMEM),
        cost_estimate=LITTLE,
        name="project",
    )(member.reshape(1), mine, other, *arrays, *ahead, *carried)


def scaled_keys(keys, turned_ref):
    scaled = keys.astype(jnp.float32) * SCORE_FACTOR
    high = scaled.astype(jnp.bfloat16)
    turned_ref[:HD, :] = high.T
    turned_ref[HD:, :] = (scaled - high.astype(jnp.float32)).astype(jnp.bfloat16).T
    return jnp.max(jnp.sum(scaled * scaled, axis=1, keepdims=True))


def head_rows(q_ref, rows, column, heads_once):
    block = jnp.concatenate(
        [q_ref[rows, pl.ds(pl.multiple_of(column + i * HD, HD), HD)] for i in range(heads_once)], axis=0
    )
    return jnp.concatenate([block, block], axis=1)


def causal(rows):
    token = lax.broadcasted_iota(jnp.int32, (rows, QLEN), 0) % QLEN
    return lax.broadcasted_iota(jnp.int32, (rows, QLEN), 1) <= token


def place(step, pair):
    query, head = step // PAIR_HEADS, step % PAIR_HEADS
    rows = pl.ds(pl.multiple_of(query * QLEN, QLEN), QLEN)
    return query, head, rows, pair * PAIR_HEADS + head


def columns(start, width=HD):
    return pl.ds(pl.multiple_of(start, HD), width)


def own_kernel(steps, heads_once, passing, info_ref, q_ref, own_ref, *rest):
    sum_ref, weight_ref, bound_ref = rest[-5 - passing : -2 - passing]
    turned_ref, wide_ref = rest[-2:]
    bound_ref[...] = jnp.zeros_like(bound_ref)
    shown = jnp.where(causal(heads_once * QLEN), 1.0, 0.0).astype(jnp.bfloat16)
    lane = lax.broadcasted_iota(jnp.int32, (QLEN, HD), 1)

    def one(step, carry):
        _, head, rows, column = place(step, info_ref[0])
        keys = scaled_keys(own_ref[rows, columns(column * HD)], turned_ref)
        wide_ref[:, :HD] = own_ref[rows, columns(HALF + column * HD)]
        wide_ref[:, HD:] = jnp.ones((QLEN, HD), jnp.bfloat16)
        weights = jnp.zeros((QLEN, HD), jnp.float32)
        peak = jnp.zeros((QLEN, 1), jnp.float32)
        for first in range(0, GROUPED, heads_once):
            start = (column * GROUPED + first) * HD
            scores = jnp.dot(
                head_rows(q_ref, rows, start, heads_once), turned_ref[...], preferred_element_type=jnp.float32
            )
            summed = jnp.dot(
                jnp.exp2(scores).astype(jnp.bfloat16) * shown, wide_ref[...], preferred_element_type=jnp.float32
            )
            for i in range(heads_once):
                part = summed[i * QLEN : (i + 1) * QLEN]
                sum_ref[rows, columns((head * GROUPED + first + i) * HD)] = part[:, :HD].astype(jnp.bfloat16)
                weights = jnp.where(lane == first + i, part[:, HD:], weights)
            most = None
            for i in range(heads_once):
                block = q_ref[rows, columns(start + i * HD)].astype(jnp.float32)
                most = block * block if most is None else jnp.maximum(most, block * block)
            peak = jnp.maximum(peak, jnp.sum(most, axis=1, keepdims=True))
        weight_ref[rows, columns(head * HD)] = weights
        bound_ref[:8, :] = jnp.maximum(bound_ref[:8, :], jnp.max(peak))
        bound_ref[8:, :] = jnp.maximum(bound_ref[8:, :], keys)
        return carry

    lax.fori_loop(0, steps, one, 0)


def attend_own(info, q_rows, own_kv, ahead, passing):
    rows = q_rows.shape[0]
    whole = pl.BlockSpec(memory_space=pl.ANY)
    vmem = pl.BlockSpec(memory_space=pltpu.VMEM)
    return pl.pallas_call(
        functools.partial(own_kernel, rows // QLEN * PAIR_HEADS, 4, len(passing)),
        in_specs=[pl.BlockSpec(memory_space=pltpu.SMEM), vmem, vmem] + [whole] * (len(passing) + len(ahead)),
        out_specs=[vmem] * 3 + [whole] * len(passing),
        out_shape=[
            jax.ShapeDtypeStruct((rows, PAIR_HEADS * GROUPED * HD), jnp.bfloat16),
            jax.ShapeDtypeStruct((rows, PAIR_HEADS * HD), jnp.float32),
            jax.ShapeDtypeStruct((16, HD), jnp.float32),
        ]
        + [jax.ShapeDtypeStruct(part.shape, part.dtype) for part in passing],
        scratch_shapes=[pltpu.VMEM((2 * HD, QLEN), jnp.bfloat16), pltpu.VMEM((QLEN, 2 * HD), jnp.bfloat16)],
        input_output_aliases={3 + i: 3 + i for i in range(len(passing))},
        compiler_params=pltpu.CompilerParams(vmem_limit_bytes=VMEM_BYTES),
        cost_estimate=LITTLE,
        name="attend_own",
    )(info, q_rows, own_kv, *passing, *ahead)


def block_rows(q_ref, slot, first, heads_once):
    block = jnp.concatenate(
        [q_ref[slot, :, (first + i) * HD : (first + i + 1) * HD] for i in range(heads_once)], axis=0
    )
    return jnp.concatenate([block, block], axis=1)


def fetch(step, start, array_ref, block_ref, arrived_ref):
    _, _, rows, _ = place(step, 0)
    wide, slot = GROUPED * HD, step % 2
    column = start + (step % PAIR_HEADS) * wide
    return pltpu.make_async_copy(
        array_ref.at[rows, columns(column, wide)], block_ref.at[slot], arrived_ref.at[slot]
    )


def leave(step, start, block_ref, array_ref, done_ref):
    _, _, rows, _ = place(step, 0)
    wide, slot = GROUPED * HD, step % 2
    column = start + (step % PAIR_HEADS) * wide
    return pltpu.make_async_copy(
        block_ref.at[slot], array_ref.at[rows, columns(column, wide)], done_ref.at[slot]
    )


def attend_kernel(
    steps,
    heads_once,
    part,
    info_ref,
    q_ref,
    own_hbm_ref,
    kept_ref,
    near_ref,
    far_ref,
    sum_ref,
    weight_ref,
    bound_ref,
    *rest,
):
    out_ref, key_ref, turned_ref, value_ref, score_ref, expd_ref, result_ref, done_ref = rest[-16:-8]
    block_ref, arrived_ref, cut_ref, cut_done_ref, own_ref, own_done_ref, part_ref, part_done_ref = rest[-8:]
    passage_keys = TOPP * PLEN
    wide = GROUPED * HD
    groups = GROUPED // heads_once
    flip = info_ref[1] > 0
    cut = pltpu.make_async_copy(kept_ref.at[:, :, part * HALF : (part + 1) * HALF], cut_ref, cut_done_ref)
    cut.start()
    start = info_ref[0] * (PAIR_HEADS * wide)
    fetch(0, start, q_ref, block_ref, arrived_ref).start()
    fetch(0, 0, sum_ref, part_ref, part_done_ref).start()
    value_ref[:, HD:] = jnp.ones((passage_keys + QLEN, HD), jnp.bfloat16)
    cut.wait()

    def one(step, carry):
        query, head, rows, column = place(step, info_ref[0])
        slot = step % 2

        @pl.when(step >= 2)
        def free():
            leave(step - 2, start, result_ref, out_ref, done_ref).wait()

        @pl.when(step + 1 < steps)
        def prefetch():
            fetch(step + 1, start, q_ref, block_ref, arrived_ref).start()
            fetch(step + 1, 0, sum_ref, part_ref, part_done_ref).start()

        offset = head * HD
        for j in range(TOPP):
            block = info_ref[2 + query * TOPP + j]
            key_ref[j * KEPT : (j + 1) * KEPT, :] = cut_ref[block, :, columns(offset)]
            value_ref[j * KEPT : (j + 1) * KEPT, :HD] = cut_ref[block, :, columns(offset + PAIR_WIDTH)]
        near, far = near_ref[rows, columns(head * HD)], far_ref[rows, columns(head * HD)]
        key_ref[TOPP * KEPT : passage_keys, :] = jnp.where(flip, far, near)
        value_ref[TOPP * KEPT : passage_keys, :HD] = jnp.where(flip, near, far)
        key_bound = scaled_keys(key_ref[...], turned_ref.at[:, :passage_keys])
        key_bound = jnp.maximum(key_bound, jnp.max(bound_ref[8:, :]))
        small = jnp.max(bound_ref[:8, :]) * key_bound <= SAFE_EXPONENT**2

        fetch(step, start, q_ref, block_ref, arrived_ref).wait()
        fetch(step, 0, sum_ref, part_ref, part_done_ref).wait()

        def score(group):
            score_ref[group % 2] = jnp.dot(
                block_rows(block_ref, slot, group * heads_once, heads_once),
                turned_ref[:, :passage_keys],
                preferred_element_type=jnp.float32,
            )

        def soften(group):
            expd_ref[group % 2] = jnp.exp2(score_ref[group % 2]).astype(jnp.bfloat16)

        def finish(group):
            summed = jnp.dot(
                expd_ref[group % 2], value_ref[:passage_keys, :], preferred_element_type=jnp.float32
            )
            weights = weight_ref[rows, columns(head * HD)]
            for i in range(heads_once):
                at = group * heads_once + i
                both = summed[i * QLEN : (i + 1) * QLEN]
                weight = both[:, HD:] + weights[:, at : at + 1]
                inverse = pl.reciprocal(weight, approx=True)
                inverse = inverse * (2.0 - weight * inverse)
                total = both[:, :HD] + part_ref[slot, :, at * HD : (at + 1) * HD].astype(jnp.float32)
                result_ref[slot, :, at * HD : (at + 1) * HD] = (total * inverse).astype(jnp.bfloat16)

        @pl.when(small)
        def unshifted():
            score(0)
            for group in range(groups):
                if group + 1 < groups:
                    score(group + 1)
                soften(group)
                if group > 0:
                    finish(group - 1)
            finish(groups - 1)

        @pl.when(jnp.logical_not(small))
        def shifted():
            for i in range(2):
                source = own_hbm_ref.at[rows, columns(i * HALF + column * HD)]
                copy = pltpu.make_async_copy(source, own_ref.at[i], own_done_ref.at[i])
                copy.start()
                copy.wait()
            scaled_keys(own_ref[0], turned_ref.at[:, passage_keys:])
            value_ref[passage_keys:, :HD] = own_ref[1]
            visible = causal(heads_once * QLEN)
            for group in range(groups):
                scores = jnp.dot(
                    block_rows(block_ref, slot, group * heads_once, heads_once),
                    turned_ref[...],
                    preferred_element_type=jnp.float32,
                )
                scores = jnp.concatenate(
                    [scores[:, :passage_keys], jnp.where(visible, scores[:, passage_keys:], -jnp.inf)], axis=1
                )
                peak = jnp.max(scores, axis=1, keepdims=True)
                expd = jnp.exp2(scores - peak).astype(jnp.bfloat16)
                summed = jnp.dot(expd, value_ref[...], preferred_element_type=jnp.float32)
                ratio = (summed[:, :HD] / summed[:, HD:]).astype(jnp.bfloat16)
                for i in range(heads_once):
                    at = group * heads_once + i
                    result_ref[slot, :, at * HD : (at + 1) * HD] = ratio[i * QLEN : (i + 1) * QLEN]

        leave(step, start, result_ref, out_ref, done_ref).start()
        return carry

    lax.fori_loop(0, steps, one, 0)
    for step in range(max(steps - 2, 0), steps):
        leave(step, start, result_ref, out_ref, done_ref).wait()


def attend(part, info, q_rows, own_kv, kept, near, far, own, earlier=None):
    rows, width = q_rows.shape
    span = TOPP * PLEN + QLEN
    heads_once = 4
    vmem = pl.BlockSpec(memory_space=pltpu.VMEM)
    whole = pl.BlockSpec(memory_space=pl.ANY)
    hbm = pl.BlockSpec(memory_space=pltpu.HBM)
    operands = [info, q_rows, own_kv, kept, near, far, *own]
    aliases = {}
    if earlier is not None:
        aliases = {len(operands): 0}
        operands.append(earlier)
    return pl.pallas_call(
        functools.partial(attend_kernel, rows // QLEN * PAIR_HEADS, heads_once, part),
        in_specs=[pl.BlockSpec(memory_space=pltpu.SMEM)] + [hbm] * 3
        + [vmem] * 2
        + [hbm]
        + [vmem] * 2
        + [whole] * len(aliases),
        out_specs=whole,
        out_shape=jax.ShapeDtypeStruct((rows, width), jnp.bfloat16),
        scratch_shapes=[
            pltpu.VMEM((TOPP * PLEN, HD), jnp.bfloat16),
            pltpu.VMEM((2 * HD, span), jnp.bfloat16),
            pltpu.VMEM((span, 2 * HD), jnp.bfloat16),
            pltpu.VMEM((2, heads_once * QLEN, TOPP * PLEN), jnp.float32),
            pltpu.VMEM((2, heads_once * QLEN, TOPP * PLEN), jnp.bfloat16),
            pltpu.VMEM((2, QLEN, GROUPED * HD), jnp.bfloat16),
            pltpu.SemaphoreType.DMA((2,)),
            pltpu.VMEM((2, QLEN, GROUPED * HD), jnp.bfloat16),
            pltpu.SemaphoreType.DMA((2,)),
            pltpu.VMEM((kept.shape[0], KEPT, HALF), jnp.bfloat16),
            pltpu.SemaphoreType.DMA,
            pltpu.VMEM((2, QLEN, HD), jnp.bfloat16),
            pltpu.SemaphoreType.DMA((2,)),
            pltpu.VMEM((2, QLEN, GROUPED * HD), jnp.bfloat16),
            pltpu.SemaphoreType.DMA((2,)),
        ],
        input_output_aliases=aliases,
        compiler_params=pltpu.CompilerParams(vmem_limit_bytes=LARGE_VMEM),
        cost_estimate=LITTLE,
        name="attend",
    )(*operands)


def swap(array, axis, bits):
    size = lax.axis_size(axis)
    return lax.ppermute(array, axis, [(i, i ^ bits) for i in range(size)])


def recompute_general(normed, w_kv, pair):
    whole = lax.all_gather(lax.all_gather(w_kv, "member", axis=0, tiled=True), "group", axis=1, tiled=True)
    result = jnp.dot(normed, whole, preferred_element_type=jnp.float32).astype(jnp.bfloat16)
    result = result.reshape(-1, 2, PAIRS, PAIR_WIDTH)
    first = jnp.where(pair == 0, result[:, :, 0], result[:, :, 1])
    second = jnp.where(pair == 0, result[:, :, 1], result[:, :, 0])
    return [first[:, 0], first[:, 1]], [second[:, 0], second[:, 1]]


def local(q_rows, own_kv, cache, recomp_hidden, w_kv, retrieval, positions):
    queries = retrieval.shape[0]
    requests = queries * TOPP
    holders = lax.axis_size("member")
    groups = lax.axis_size("group")
    pass_local = cache.shape[0]
    capacity = -(-requests // holders)
    member = lax.axis_index("member")
    group = lax.axis_index("group")
    pair = group % PAIRS
    tuned = groups == 4 and holders == 8
    wanted = retrieval.reshape(requests)
    request = jnp.concatenate([wanted, positions.reshape(requests * RECOMP)])
    request = jnp.pad(request, (0, -request.shape[0] % 128)).reshape(1, -1, 128)
    request = jnp.broadcast_to(request, (holders,) + request.shape[1:])
    table = lax.all_to_all(request, "member", split_axis=0, concat_axis=0, tiled=True).reshape(-1)
    hidden = recomp_hidden.reshape(requests * RECOMP, D)
    hops = stack_hops(swap(w_kv, "member", 2), swap(w_kv, "member", 4)) if tuned else []
    normed = normalise(hidden, hops[:1])
    me = jnp.stack([member, pair]).astype(jnp.int32)
    ranks, passages = find_rows(table, me, holders, requests, pass_local, capacity, normed)
    holder_of = wanted // pass_local
    same = holder_of[:, None] == holder_of[None, :]
    before = jnp.arange(requests)[None, :] < jnp.arange(requests)[:, None]
    slot = holder_of * capacity + jnp.sum((same & before).astype(jnp.int32), axis=1)
    flip = group // 2 if tuned else jnp.int32(0)
    info = jnp.concatenate([jnp.stack([pair, flip]), slot]).astype(jnp.int32)
    other_info = jnp.concatenate([jnp.stack([1 - pair, flip]), slot]).astype(jnp.int32)
    first_own = attend_own(info, q_rows, own_kv, [ranks], [])
    ahead = [first_own[0]]
    if tuned:
        stack, two = hops
        aside, across = swap(w_kv, "member", 1), swap(w_kv, "group", 2)
        three = swap(two, "member", 2)
        stack_aside, stack_across = swap(stack, "member", 1), swap(stack, "group", 2)
        ahead += [across, aside, stack_across, stack_aside, three]
    sent = pick_rows(me, passages, ranks, cache, ahead)
    arrived = lax.all_to_all(
        sent.reshape(holders, capacity * KEPT, 2 * HALF), "member", split_axis=0, concat_axis=0, tiled=True
    ).reshape(sent.shape)
    second_own = attend_own(other_info, q_rows, own_kv, [sent], [aside] if tuned else [])
    if tuned:
        aside = second_own[3]
        other = swap(normed, "group", 1)
        rest_across, across_three = swap(stack_aside, "group", 2), swap(three, "group", 2)
        beside_three = swap(three, "member", 1)
        far_three = swap(beside_three, "group", 2)
        across_aside = swap(aside, "group", 2)
        near, near_other = project(
            member,
            normed,
            other,
            [w_kv, aside, stack, stack_aside, three, beside_three],
            ((0, 0, 0), (1, 1, 0), (2, 2, 0), (3, 3, 0), (4, 2, 1), (5, 3, 1), (6, 4, 0), (7, 5, 0)),
        )
        (begun,) = project(
            member,
            normed,
            other,
            [across, across_aside, stack_across, rest_across, across_three],
            ((0, 0, 0), (1, 1, 0), (2, 2, 0), (3, 3, 0), (4, 2, 1), (5, 3, 1), (6, 4, 0)),
            [near],
            last=False,
        )
        far, far_other = project(member, normed, other, [far_three], ((7, 0, 0),), carry=begun)
        first = [near, far]
        second = [swap(near_other, "group", 1), swap(far_other, "group", 1)]
    else:
        first, second = recompute_general(normed, w_kv, pair)
    out = attend(0, info, q_rows, own_kv, arrived, *first, first_own[:3])
    return attend(1, other_info, q_rows, own_kv, arrived, *second, second_own[:3], earlier=out)


def solution(mesh):
    rows = P(("group", "member"), None)
    placed = (
        rows,
        rows,
        P(("group", "member"), None, None),
        P(("group", "member"), None, None, None),
        P("member", "group"),
        rows,
        P(("group", "member"), None, None),
    )
    return jax.shard_map(local, mesh=mesh, in_specs=placed, out_specs=rows, check_vma=False)
```
